32 devices in a mesh: dp: 8 (over z, y), frames: 4 (over x, core).
Axes of the slice: x: 2, y: 2, z: 4, core: 2. Of those that a mesh axis runs over, the one named last changes fastest.
Arguments:
- tokens: float32 [32, 128, 1024], P(('dp', 'frames')), may hold values from -6 to 6
- memory: bfloat16 [32, 1504, 1024], P('dp', 'frames'), may hold values from -6 to 6
- cotangent: float32 [32, 128, 1024], P(('dp', 'frames')), may hold values from -6 to 6
- self_project: bfloat16 [1024, 3072], P(('dp', 'frames')), may hold values from -0.1875 to 0.1875
- self_output: bfloat16 [1024, 1024], P(('dp', 'frames')), may hold values from -1 to 1
- cross_query: bfloat16 [1024, 1024], P(('dp', 'frames')), may hold values from -0.1875 to 0.1875
- cross_memory: bfloat16 [1024, 2048], P(('dp', 'frames')), may hold values from -0.1875 to 0.1875
- cross_output: bfloat16 [1024, 1024], P(('dp', 'frames')), may hold values from -3.5 to 3.5
- expand: bfloat16 [1024, 4096], P(('dp', 'frames')), may hold values from -0.1875 to 0.1875
- contract: bfloat16 [4096, 1024], P(('dp', 'frames')), may hold values from -0.09375 to 0.09375
- norm_gains: bfloat16 [4, 1024], P(None, ('dp', 'frames')), may hold values from 0.25 to 1.75
- norm_shifts: bfloat16 [4, 1024], P(None, ('dp', 'frames')), may hold values from -1.5 to 1.5
- target_length: int32 [32], P(('dp', 'frames')), may hold values from 42 to 128, as said below
- memory_length: int32 [32], P('dp'), may hold values from 100 to 1504, as said below
- cross_mask: int32 [32, 1504], P('dp'), may hold values 0 or 1
Outputs:
- result: float32 [32, 128, 1024], P(('dp', 'frames'))
- tokens_grad: float32 [32, 128, 1024], P(('dp', 'frames'))
- memory_grad: float32 [32, 1504, 1024], P('dp', 'frames')
- self_project_grad: float32 [1024, 3072], P(('dp', 'frames'))
- self_output_grad: float32 [1024, 1024], P(('dp', 'frames'))
- cross_query_grad: float32 [1024, 1024], P(('dp', 'frames'))
- cross_memory_grad: float32 [1024, 2048], P(('dp', 'frames'))
- cross_output_grad: float32 [1024, 1024], P(('dp', 'frames'))
- expand_grad: float32 [1024, 4096], P(('dp', 'frames'))
- contract_grad: float32 [4096, 1024], P(('dp', 'frames'))
- norm_gains_grad: float32 [4, 1024], P(None, ('dp', 'frames'))
- norm_shifts_grad: float32 [4, 1024], P(None, ('dp', 'frames'))
- branch_rms: float32 [4], replicated
The draws below stay inside these ranges and needn't reach their ends.
Inputs may be any that keep to these rules, and one draw needn't show every extreme that they name: `target_length`: in every draw some sequence has all 128 rows. `memory_length`: in every group of 4 consecutive items one item has all 1504 frames.
All inputs are finite; a program needn't handle non-finite values. No bound on the sum of `cross_mask` on one device may be relied on, other than what follows from the above.
Results may differ from the reference program's by a relative error of at most 0.029.
Values may be sent and summed in bfloat16 or wider, within the bound.
A program may use at most 192 MiB of HBM per device.

```python
import jax
import jax.numpy as jnp
from jax import lax

HEADS = 16
HEAD_DIM = 64
FF = 4096
SEQ = 128
MEMCAP = 1504
D = 1024
MEM_SHORT = 100
ITEMS = 32
N_FRAMES = 4


def draw_target_length(key, part):
    lengths = jax.random.randint(key, (ITEMS,), SEQ // 3, SEQ + 1)
    chosen = jax.random.randint(jax.random.fold_in(key, 7), (), 0, ITEMS)
    return jnp.where(jnp.arange(ITEMS) == chosen, SEQ, lengths).astype(jnp.int32)


def draw_memory_length(key, part):
    groups = ITEMS // N_FRAMES
    lengths = jax.random.randint(key, (groups, N_FRAMES), MEM_SHORT, MEMCAP + 1)
    chosen = jax.random.randint(jax.random.fold_in(key, 11), (groups, 1), 0, N_FRAMES)
    filled = jnp.arange(N_FRAMES)[None, :] == chosen
    return jnp.where(filled, MEMCAP, lengths).reshape(ITEMS).astype(jnp.int32)


def plant(values, rng, low, high):
    shape = values.shape
    index_at = [jax.random.randint(jax.random.fold_in(rng, axis), (), 0, shape[axis]) for axis in range(len(shape))]
    values = values.at[tuple(index_at)].set(low)
    longest = shape.index(max(shape))
    index_at[longest] = (index_at[longest] + 1) % shape[longest]
    return values.at[tuple(index_at)].set(high)


def level_of(stream_key, shape, pieces, least, top_value):
    level = 1.0
    for dim, parts in pieces:
        heights = jax.random.uniform(jax.random.fold_in(jax.random.fold_in(stream_key, 6), dim), (parts,), jnp.float32, least / len(pieces), top_value / len(pieces))
        level = level * jnp.repeat(jnp.exp(heights), shape[dim] // parts).reshape((-1,) + (1,) * (len(shape) - 1 - dim))
    return level


def gaussian(rng, extent, width, reach, split=(), dtype=jnp.bfloat16):
    loudness = level_of(rng, extent, split, -0.22, 0.18) if split else 1.0
    array = jax.random.normal(rng, extent, jnp.float32) * width * loudness
    return jnp.minimum(jnp.maximum(array, -reach), reach).astype(dtype)


def setup_inputs(seed: int = 0) -> dict:
    streams_of = jax.random.split(jax.random.key(seed), 16)
    return {
        "tokens": gaussian(streams_of[0], (ITEMS, SEQ, D), 1.0, 6.0, ((0, 32),), jnp.float32),
        "memory": gaussian(streams_of[1], (ITEMS, MEMCAP, D), 1.0, 6.0, ((0, 8), (1, 4))),
        "cotangent": gaussian(streams_of[2], (ITEMS, SEQ, D), 1.0, 6.0, ((0, 32),), jnp.float32),
        "self_project": gaussian(streams_of[3], (D, 3 * D), D ** -0.5, 0.1875, ((0, 32),)),
        "self_output": gaussian(streams_of[4], (D, D), (5 * D // SEQ) ** -0.5, 1.0, ((0, 32),)),
        "cross_query": gaussian(streams_of[5], (D, D), D ** -0.5, 0.1875, ((0, 32),)),
        "cross_memory": gaussian(streams_of[6], (D, 2 * D), D ** -0.5, 0.1875, ((0, 32),)),
        "cross_output": gaussian(streams_of[7], (D, D), (5 * D // MEMCAP) ** -0.5, 3.5, ((0, 32),)),
        "expand": gaussian(streams_of[8], (D, FF), D ** -0.5, 0.1875, ((0, 32),)),
        "contract": gaussian(streams_of[9], (FF, D), FF ** -0.5, 0.09375, ((0, 32),)),
        "norm_gains": jnp.clip(1.0 + 0.15 * jax.random.normal(streams_of[10], (4, D), jnp.float32), 0.25, 1.75).astype(jnp.bfloat16),
        "norm_shifts": gaussian(streams_of[11], (4, D), 0.3, 1.5, ((1, 32),)),
        "target_length": draw_target_length(jax.random.fold_in(streams_of[15], 71), 0),
        "memory_length": draw_memory_length(jax.random.fold_in(streams_of[15], 71), 0),
        "cross_mask": plant((jax.random.randint(streams_of[14], (ITEMS, MEMCAP), 0, 8) < 7).astype(jnp.int32), jax.random.fold_in(streams_of[14], 1), 0, 1),
    }


@jax.custom_vjp
def low(v):
    return lax.optimization_barrier(v.astype(jnp.bfloat16)).astype(jnp.float32)

@jax.custom_vjp
def low_back(v):
    return v

def low_keep(v):
    return (low(v), None)

def low_pass(kept, grad):
    return (grad,)

def back_keep(v):
    return (v, None)

def back_low(kept, grad):
    return (low(grad),)
low.defvjp(low_keep, low_pass)
low_back.defvjp(back_keep, back_low)

def layer_norm(values, gain_row, shift_row):
    center = values - lax.optimization_barrier(jnp.mean(values, axis=-1, keepdims=True))
    spread = lax.optimization_barrier(jnp.mean(center * center, axis=-1, keepdims=True))
    return center * lax.rsqrt(spread + 1e-05) * gain_row + shift_row

def product(left_side, right_side):
    return jnp.dot(left_side, right_side, precision=lax.Precision.HIGHEST)

def split_heads(rows):
    return rows.reshape(rows.shape[0], HEADS, HEAD_DIM)

def attend(query_rows, key_rows, value_rows, allowed):
    factor = HEAD_DIM ** (-0.5)
    scores = low_back(jnp.einsum('shd,fhd->hsf', query_rows, key_rows, precision=lax.Precision.HIGHEST) * factor)
    masked = jnp.where(allowed[None], scores, -1e+30)
    row_max = lax.optimization_barrier(jnp.max(masked, axis=-1, keepdims=True))
    shifted = jnp.where(allowed[None], jnp.exp(masked - row_max), 0.0)
    weights = low(shifted / lax.optimization_barrier(jnp.sum(shifted, axis=-1, keepdims=True)))
    mixture = jnp.einsum('hsf,fhd->shd', weights, value_rows, precision=lax.Precision.HIGHEST)
    return low(low_back(mixture.reshape(mixture.shape[0], HEADS * HEAD_DIM)))

def forward(params, token_rows, memory_block, row_valid, key_valid):
    self_project, self_output, cross_query, cross_memory, cross_output, expand, contract, gains, shifts = params
    length = token_rows.shape[0]
    normed_one = low(layer_norm(token_rows, gains[0], shifts[0]))
    joint_rows = low(low_back(product(normed_one, self_project)))
    causal = jnp.arange(length)[:, None] >= jnp.arange(length)[None, :]
    self_mix = attend(split_heads(joint_rows[:, :D]), split_heads(joint_rows[:, D:2 * D]), split_heads(joint_rows[:, 2 * D:]), causal)
    self_branch = low_back(product(self_mix, self_output))
    first_sum = token_rows + self_branch
    normed_two = low(layer_norm(first_sum, gains[1], shifts[1]))
    queries = low(low_back(product(normed_two, cross_query)))
    memory_rows = low(low_back(product(memory_block, cross_memory)))
    frame_allowed = jnp.broadcast_to(key_valid[None, :], (length, key_valid.shape[0]))
    cross_mix = attend(split_heads(queries), split_heads(memory_rows[:, :D]), split_heads(memory_rows[:, D:]), frame_allowed)
    cross_branch = low_back(product(cross_mix, cross_output))
    second_sum = first_sum + cross_branch
    normed_three = low(layer_norm(second_sum, gains[2], shifts[2]))
    hidden = low_back(product(normed_three, expand))
    active = low(jax.nn.gelu(hidden, approximate=False))
    feed_branch = low_back(product(active, contract))
    third_sum = second_sum + feed_branch
    result = jnp.where(row_valid[:, None], layer_norm(third_sum, gains[3], shifts[3]), 0.0)
    return (result, (third_sum, self_branch, cross_branch, feed_branch))

def reference(tokens, memory, cotangent, self_project, self_output, cross_query, cross_memory, cross_output, expand, contract, norm_gains, norm_shifts, target_length, memory_length, cross_mask):
    params = tuple((weight.astype(jnp.float32) for weight in (self_project, self_output, cross_query, cross_memory, cross_output, expand, contract, norm_gains, norm_shifts)))
    positions = jnp.arange(SEQ)
    frame_index = jnp.arange(MEMCAP)
    initial = jax.tree.map(jnp.zeros_like, params)

    def per_sequence(running, inputs):
        grad_total, squares, counted = running
        token_rows, memory_block, cotangent_rows, target_count, memory_count, mask_row = inputs
        row_valid = positions < target_count
        key_valid = (frame_index < memory_count) & ((mask_row == 1) | (frame_index == 0))

        def forward_one(weights_in, tokens_in, memory_in):
            return forward(weights_in, tokens_in, memory_in, row_valid, key_valid)
        result, pullback, branches = jax.vjp(forward_one, params, token_rows, memory_block.astype(jnp.float32), has_aux=True)
        grad_params, grad_tokens, grad_memory = pullback(cotangent_rows)
        row_weight = row_valid.astype(jnp.float32)[:, None]
        squares = squares + jnp.stack([jnp.sum(row_weight * member * member) for member in branches])
        grad_total = jax.tree.map(jnp.add, grad_total, grad_params)
        counted = counted + jnp.sum(row_valid.astype(jnp.float32))
        return ((grad_total, squares, counted), (result, grad_tokens, grad_memory))
    initial_state = (initial, jnp.zeros((4,), jnp.float32), jnp.zeros((), jnp.float32))
    final_state, outputs = lax.scan(per_sequence, initial_state, (tokens, memory, cotangent, target_length, memory_length, cross_mask))
    grad_total, squares, counted = final_state
    result, tokens_grad, memory_grad = outputs
    branch_rms = jnp.sqrt(squares / (counted * D))
    return (result, tokens_grad, memory_grad, grad_total[0], grad_total[1], grad_total[2], grad_total[3], grad_total[4], grad_total[5], grad_total[6], grad_total[7], grad_total[8], branch_rms)
```

```python
import functools
from types import SimpleNamespace

import jax
import jax.numpy as jnp
from jax import lax
from jax.experimental import pallas as pl
from jax.experimental.pallas import tpu as pltpu
from jax.sharding import PartitionSpec as P

MESH = pl.DeviceIdType.MESH
F32 = jnp.float32
BF16 = jnp.bfloat16
HEAD_DIM = 64
LANES = 128
TILE = 256


def dot(a, b):
    return jnp.dot(a, b, preferred_element_type=F32)


def dot_nt(a, b):
    return lax.dot_general(a, b, (((1,), (1,)), ((), ())), preferred_element_type=F32)


def place():
    dp, fr = lax.axis_index("dp"), lax.axis_index("frames")
    z, y = lax.div(dp, 2), lax.rem(dp, 2)
    x, c = lax.div(fr, 2), lax.rem(fr, 2)

    def dev(zz, yy, xx, cc):
        return {"dp": zz * 2 + yy, "frames": xx * 2 + cc}

    me = SimpleNamespace(z=z, y=y, x=x, c=c, fr=fr, dev=dev)
    me.xn = dev(z, y, 1 - x, c)
    me.yn = dev(z, 1 - y, x, c)
    me.sib = dev(z, y, x, 1 - c)
    me.diag = dev(z, y, 1 - x, 1 - c)
    me.j = y * 4 + x * 2 + c
    me.jx = y * 4 + (1 - x) * 2 + c
    me.jy = (1 - y) * 4 + x * 2 + c
    me.jxy = (1 - y) * 4 + (1 - x) * 2 + c
    me.flip = 1 - 2 * c
    return me


def remote(src, dst, send, recv, device):
    return pltpu.make_async_remote_copy(
        src_ref=src, dst_ref=dst, send_sem=send, recv_sem=recv, device_id=device, device_id_type=MESH
    )


def gather_steps(me, w, send, recv, nz):
    half = w.shape[2] // 2

    def cp(view, s, device):
        return remote(view, view, send.at[s], recv.at[s], device)

    def step_z():
        for dz in range(1, nz):
            to = me.dev(lax.rem(me.z + dz, nz), me.y, me.x, me.c)
            cp(w.at[me.z, me.j], dz - 1, to).start()

    def step_near():
        for dz in range(1, nz):
            cp(w.at[lax.rem(me.z + nz - dz, nz), me.j], dz - 1, me.xn).wait_recv()
        cp(w.at[:, me.j], nz - 1, me.xn).start()
        cp(w.at[:, me.j], nz, me.yn).start()
        cp(w.at[:, me.j], nz + 1, me.sib).start()

    def step_far():
        cp(w.at[:, me.jx], nz - 1, me.xn).wait_recv()
        cp(w.at[:, me.jx, 0:half], nz + 2, me.yn).start()
        cp(w.at[:, me.jx], nz + 3, me.sib).start()
        cp(w.at[:, me.jy], nz, me.yn).wait_recv()
        cp(w.at[:, me.jy, half:], nz + 4, me.xn).start()
        cp(w.at[:, me.jy], nz + 5, me.sib).start()

    def step_last():
        cp(w.at[:, me.jxy, 0:half], nz + 2, me.yn).wait_recv()
        cp(w.at[:, me.jxy, half:], nz + 4, me.xn).wait_recv()
        cp(w.at[:, me.jxy], nz + 6, me.sib).start()

    def step_done():
        for at, s in ((me.j, nz + 1), (me.jx, nz + 3), (me.jy, nz + 5), (me.jxy, nz + 6)):
            cp(w.at[:, at + me.flip], s, me.sib).wait_recv()

    def drain():
        for dz in range(1, nz):
            cp(w.at[me.z, me.j], dz - 1, me.xn).wait_send()
        for at, s in ((me.j, nz - 1), (me.j, nz), (me.j, nz + 1), (me.jx, nz + 3), (me.jy, nz + 5), (me.jxy, nz + 6)):
            cp(w.at[:, at], s, me.xn).wait_send()
        cp(w.at[:, me.jx, 0:half], nz + 2, me.xn).wait_send()
        cp(w.at[:, me.jy, half:], nz + 4, me.xn).wait_send()

    return SimpleNamespace(z=step_z, near=step_near, far=step_far, last=step_last, done=step_done, drain=drain)


def lane_masks():
    lane = lax.broadcasted_iota(jnp.int32, (1, LANES), 1)
    left = jnp.where(lane < HEAD_DIM, 1.0, 0.0).astype(BF16)
    return left, (1.0 - left.astype(F32)).astype(BF16)


def two_heads(block):
    left, right = lane_masks()
    return jnp.concatenate([block * left, block * right], axis=0)


def one_block(pair):
    rows = pair.shape[0] // 2
    lane = lax.broadcasted_iota(jnp.int32, (rows, LANES), 1)
    return jnp.where(lane < HEAD_DIM, pair[:rows], pair[rows:])


def at128(p, base=0):
    return pl.ds(pl.multiple_of(base + p * LANES, LANES), LANES)


def put_stat(stat, p, pair):
    rows = pair.shape[0] // 2
    lane = lax.broadcasted_iota(jnp.int32, stat.shape, 1)
    stat = jnp.where(lane == 2 * p, pair[:rows], stat)
    return jnp.where(lane == 2 * p + 1, pair[rows:], stat)


def normalise(values):
    center = values - jnp.mean(values, axis=-1, keepdims=True)
    spread = jnp.mean(center * center, axis=-1, keepdims=True)
    return center * lax.rsqrt(spread + 1e-05)


def forward(r, me, nz):
    d = r.tokens.shape[1]
    rows = r.tokens.shape[0]
    items = r.memory.shape[0]
    frames = r.memory.shape[1]
    pairs = d // LANES

    def weight(k, n):
        return r.wg[k, :, :, :, pl.ds(pl.multiple_of(n * TILE, TILE), TILE)].reshape(d, TILE)

    def product(x, k, sink):
        def body(n, carry):
            sink(n, pl.ds(pl.multiple_of(n * TILE, TILE), TILE), dot(x, weight(k, n)))
            return carry

        lax.fori_loop(0, d // TILE, body, 0)

    def ln(values, i):
        return normalise(values) * r.gs[i : i + 1, :] + r.gs[4 + i : 5 + i, :]

    def norms_in():
        for g in range(2 * nz):
            zz, base = g // 2, 4 * (g % 2)
            total = r.ng[zz, base, 0:16, :].astype(F32)
            for f in range(1, 4):
                total = total + r.ng[zz, base + f, 0:16, :].astype(F32)
            r.gs[:, g * LANES : (g + 1) * LANES] = total

    def norm_one():
        r.n1[...] = ln(r.tokens[...], 0).astype(BF16)
        r.n1t[...] = r.n1[...].T

    def joint(q):
        def sink(n, cols, v):
            r.joint[:, pl.ds(pl.multiple_of(q * d + n * TILE, TILE), TILE)] = v.astype(BF16)

        product(r.n1[...], q, sink)

    def self_attention():
        row = lax.rem(lax.broadcasted_iota(jnp.int32, (2 * rows, rows), 0), rows)
        causal = row >= lax.broadcasted_iota(jnp.int32, (2 * rows, rows), 1)

        def body(p, stat):
            q2 = two_heads(r.joint[:, at128(p)] * jnp.asarray(HEAD_DIM**-0.5, BF16))
            s = dot_nt(q2, r.joint[:, at128(p, d)])
            s = jnp.where(causal, s, -1e30)
            m = jnp.max(s, axis=-1, keepdims=True)
            e = jnp.exp(s - m)
            total = jnp.sum(e, axis=-1, keepdims=True)
            o2 = dot(e.astype(BF16), r.joint[:, at128(p, 2 * d)]) / total
            r.smix[:, at128(p)] = one_block(o2).astype(BF16)
            return put_stat(stat, p, m + jnp.log(total))

        stat = lax.fori_loop(0, pairs, body, jnp.zeros((rows, LANES), F32))
        r.slse[...] = stat.T
        r.smixt[...] = r.smix[...].T

    def self_out():
        def sink(n, cols, v):
            r.branch[:, cols] = v

        product(r.smix[...], 3, sink)
        r.first[...] = r.tokens[...] + r.branch[...]
        squares(1, r.branch[...])
        r.n2[...] = ln(r.first[...], 1).astype(BF16)
        r.n2t[...] = r.n2[...].T

    def squares(i, values):
        ok = lax.broadcasted_iota(jnp.int32, (rows, 1), 0) < r.tl[0]
        total = jnp.sum(jnp.where(ok, values * values, 0.0))
        line = lax.broadcasted_iota(jnp.int32, r.sq.shape, 0)
        r.sq[...] = jnp.where(line == i, total, r.sq[...])

    def start_counts():
        line = lax.broadcasted_iota(jnp.int32, r.sq.shape, 0)
        r.sq[...] = jnp.where(line == 4, r.tl[0].astype(F32), 0.0)

    def queries():
        def sink(n, cols, v):
            r.qa[me.fr, :, cols] = v.astype(BF16)

        product(r.n2[...], 4, sink)

    def q_copy(f, s, device):
        return remote(r.qa.at[f], r.qa.at[f], r.q_send.at[s], r.q_recv.at[s], device)

    fx, fs, fd = (1 - me.x) * 2 + me.c, me.x * 2 + 1 - me.c, (1 - me.x) * 2 + 1 - me.c

    def q_start():
        q_copy(me.fr, 0, me.xn).start()
        q_copy(me.fr, 1, me.sib).start()

    def q_forward():
        q_copy(fx, 0, me.xn).wait_recv()
        q_copy(fx, 2, me.sib).start()

    def q_done():
        q_copy(fs, 1, me.sib).wait_recv()
        q_copy(fd, 2, me.sib).wait_recv()

    def mem_copy(t):
        return pltpu.make_async_copy(r.memory.at[t], r.stage.at[t % 2], r.m_sem.at[t % 2])

    def memory_part(which):
        def item(t):
            mem_copy(t).wait()

            def body(n, carry):
                v = dot(r.stage[t % 2], weight(5 + which, n))
                r.kv[t, :, pl.ds(pl.multiple_of(which * d + n * TILE, TILE), TILE)] = v.astype(BF16)
                return carry

            lax.fori_loop(0, d // TILE, body, 0)
            if which == 0:
                r.memt[:, t * frames : (t + 1) * frames] = r.stage[t % 2].T
            if t + 2 < items:
                mem_copy(t + 2).start()

        def run():
            for t in range(items):
                item(t)
            if which == 0:
                for t in range(min(2, items)):
                    mem_copy(t).start()

        return run

    def mem_start():
        for t in range(min(2, items)):
            mem_copy(t).start()

    def cross_item(t):
        def body(p, stat):
            q2 = two_heads(r.qa[t, :, at128(p)] * jnp.asarray(HEAD_DIM**-0.5, BF16))
            s = dot_nt(q2, r.kv[t, :, at128(p)]) + r.bias[pl.ds(t, 1), :]
            m = jnp.max(s, axis=-1, keepdims=True)
            e = jnp.exp(s - m)
            total = jnp.sum(e, axis=-1, keepdims=True)
            o2 = dot(e.astype(BF16), r.kv[t, :, at128(p, d)]) / total
            r.op[t, :, at128(p)] = one_block(o2).astype(BF16)
            return put_stat(stat, p, m + jnp.log(total))

        stat = lax.fori_loop(0, pairs, body, jnp.zeros((rows, LANES), F32))
        r.opl[t] = stat.T

    def o_copies(t, slot, device):
        return (
            remote(r.op.at[t], r.orv.at[slot], r.o_send.at[slot], r.o_recv.at[slot], device),
            remote(r.opl.at[t, 0:16], r.orl.at[slot, 0:16], r.o_send.at[3 + slot], r.o_recv.at[3 + slot], device),
        )

    def o_start(t, slot, device):
        for cp in o_copies(t, slot, device):
            cp.start()

    def o_wait(t, slot, device):
        for cp in o_copies(t, slot, device):
            cp.wait_recv()

    def merge(parts, sink):
        lses = [lse[0:16] for _, lse in parts]
        top = functools.reduce(jnp.maximum, lses)
        shares = [jnp.exp(v - top) for v in lses]
        total = functools.reduce(jnp.add, shares)
        flat = jnp.concatenate([v / total for v in shares] + [jnp.zeros((LANES - 16 * len(parts), LANES), F32)], axis=0)
        r.wcol[...] = flat.T
        lane = lax.broadcasted_iota(jnp.int32, (rows, LANES), 1)
        for p in range(pairs):
            value = jnp.zeros((rows, LANES), F32)
            for i, (mix, _) in enumerate(parts):
                left = r.wcol[:, 16 * i + 2 * p : 16 * i + 2 * p + 1]
                right = r.wcol[:, 16 * i + 2 * p + 1 : 16 * i + 2 * p + 2]
                share = jnp.where(lane < HEAD_DIM, left, right)
                value = value + share * mix[:, p * LANES : (p + 1) * LANES].astype(F32)
            sink(p, value)
        return top + jnp.log(total)

    def cross_a():
        cross_item(fd)
        o_start(fd, 0, me.sib)
        cross_item(fs)
        o_start(fs, 1, me.sib)

    def cross_b():
        cross_item(fx)
        o_wait(fd, 0, me.sib)

        def sink(p, v):
            r.op[fx, :, p * LANES : (p + 1) * LANES] = v.astype(BF16)

        lse = merge([(r.op.at[fx], r.opl.at[fx]), (r.orv.at[0], r.orl.at[0])], sink)
        r.opl[fx, 0:16] = lse
        o_start(fx, 2, me.xn)
        cross_item(me.fr)

    def cross_c():
        o_wait(fs, 1, me.sib)
        o_wait(fx, 2, me.xn)

        def sink(p, v):
            r.cmix[:, p * LANES : (p + 1) * LANES] = v

        parts = [(r.op.at[me.fr], r.opl.at[me.fr]), (r.orv.at[1], r.orl.at[1]), (r.orv.at[2], r.orl.at[2])]
        r.clse[0:16] = merge(parts, sink)
        r.cmixt[...] = r.cmix[...].T.astype(BF16)

    def cross_out():
        def sink(n, cols, v):
            r.branch[:, cols] = v

        product(r.cmix[...].astype(BF16), 7, sink)
        squares(2, r.branch[...])
        r.second[...] = r.first[...] + r.branch[...]
        r.n3[...] = ln(r.second[...], 2).astype(BF16)
        r.n3t[...] = r.n3[...].T

    def expand(q):
        def sink(n, cols, v):
            at = pl.ds(pl.multiple_of(q * d + n * TILE, TILE), TILE)
            half = 0.5 * (1.0 + lax.erf(v * (2.0**-0.5)))
            r.active[:, at] = (v * half).astype(BF16)
            r.slope[:, at] = (half + v * jnp.exp(-0.5 * v * v) * 0.3989422804014327).astype(BF16)

        product(r.n3[...], 8 + q, sink)
        r.activet[q * d : (q + 1) * d, :] = r.active[:, q * d : (q + 1) * d].T

    def contract(q):
        def sink(n, cols, v):
            r.branch[:, cols] = v if q == 0 else r.branch[:, cols] + v

        product(r.active[:, q * d : (q + 1) * d], 12 + q, sink)

    def finish():
        squares(3, r.branch[...])
        r.third[...] = r.second[...] + r.branch[...]
        squares(0, r.third[...])
        ok = lax.broadcasted_iota(jnp.int32, (rows, 1), 0) < r.tl[0]
        r.result[...] = jnp.where(ok, ln(r.third[...], 3), 0.0)

    def at(k):
        return k + 3

    tasks = {}

    def add(tick, *fs):
        tasks.setdefault(tick, []).extend(fs)

    add(0, start_counts, mem_start)
    add(2, norms_in, norm_one)
    for q in range(3):
        add(at(q), functools.partial(joint, q))
    add(at(2), self_attention)
    add(at(3), self_out)
    add(at(4), queries, q_start)
    add(at(5), q_forward, memory_part(0))
    add(at(6), memory_part(1), q_done, cross_a)
    add(at(7), cross_b)
    add(at(8), cross_c, cross_out)
    for q in range(4):
        add(at(8 + q), functools.partial(expand, q))
        add(at(12 + q), functools.partial(contract, q))
    add(at(15), finish)

    def drain():
        q_copy(me.fr, 0, me.xn).wait_send()
        q_copy(me.fr, 1, me.sib).wait_send()
        q_copy(fx, 2, me.sib).wait_send()
        for t, slot, device in ((fd, 0, me.sib), (fs, 1, me.sib), (fx, 2, me.xn)):
            for cp in o_copies(t, slot, device):
                cp.wait_send()

    return tasks, drain


def run_forward(r, me, nz, chunks):
    own = pltpu.make_async_copy(r.shards, r.wg.at[:, me.z, me.j], r.own_sem.at[0])
    own.start()
    r.ng[me.z, me.j] = r.norms[...]
    barrier = pltpu.get_barrier_semaphore()
    peers = [me.xn, me.yn, me.sib, me.diag]
    peers += [me.dev(lax.rem(me.z + dz, nz), me.y, me.x, me.c) for dz in range(1, nz)]
    for device in peers:
        pl.semaphore_signal(barrier, inc=1, device_id=device, device_id_type=MESH)
    pl.semaphore_wait(barrier, len(peers))
    norm = gather_steps(me, r.ng, r.g_send.at[chunks], r.g_recv.at[chunks], nz)
    steps = [gather_steps(me, r.wg.at[k], r.g_send.at[k], r.g_recv.at[k], nz) for k in range(chunks)]
    norm.z()
    own.wait()
    steps[0].z()
    steps[1].z()
    norm.near()
    norm.far()
    norm.last()
    tasks, drain = forward(r, me, nz)
    for tick in range(chunks + 3):
        if tick + 2 < chunks:
            steps[tick + 2].z()
        if tick < chunks:
            steps[tick].near()
        if 0 <= tick - 1 < chunks:
            steps[tick - 1].far()
        if 0 <= tick - 2 < chunks:
            steps[tick - 2].last()
        if 0 <= tick - 3 < chunks:
            steps[tick - 3].done()
        if tick == 1:
            norm.done()
        for task in tasks.get(tick, ()):
            task()
    drain()
    norm.drain()
    for s in steps:
        s.drain()
CHUNKS = 16
def f_call(nz, tl, tokens, mem_pad, shards, norms, bias):
    rows, d = tokens.shape
    items, frames, _ = mem_pad.shape
    outs = dict(
        result=((rows, d), F32), wg=((CHUNKS, nz, 8, 32, d), BF16), gs=((16, d), F32),
        n1t=((d, rows), BF16), joint=((rows, 3 * d), BF16), smixt=((d, rows), BF16), slse=((LANES, LANES), F32),
        first=((rows, d), F32), n2t=((d, rows), BF16), qa=((items, rows, d), BF16), kv=((items, frames, 2 * d), BF16),
        memt=((d, items * frames), BF16), cmix=((rows, d), F32), clse=((LANES, LANES), F32), second=((rows, d), F32), n3t=((d, rows), BF16),
        activet=((4 * d, rows), BF16), slope=((rows, 4 * d), BF16), third=((rows, d), F32), sq=((8, LANES), F32),
    )
    scratch = dict(
        ng=pltpu.VMEM((nz, 8, 32, LANES), BF16), n1=pltpu.VMEM((rows, d), BF16), smix=pltpu.VMEM((rows, d), BF16),
        branch=pltpu.VMEM((rows, d), F32), n2=pltpu.VMEM((rows, d), BF16), stage=pltpu.VMEM((2, frames, d), BF16),
        op=pltpu.VMEM((items, rows, d), BF16), opl=pltpu.VMEM((items, LANES, LANES), F32), orv=pltpu.VMEM((3, rows, d), BF16),
        orl=pltpu.VMEM((3, LANES, LANES), F32), wcol=pltpu.VMEM((LANES, LANES), F32), cmixt=pltpu.VMEM((d, rows), BF16),
        n3=pltpu.VMEM((rows, d), BF16), active=pltpu.VMEM((rows, 4 * d), BF16),
        own_sem=pltpu.SemaphoreType.DMA((1,)), m_sem=pltpu.SemaphoreType.DMA((2,)),
        g_send=pltpu.SemaphoreType.DMA((CHUNKS + 1, nz + 7)), g_recv=pltpu.SemaphoreType.DMA((CHUNKS + 1, nz + 7)),
        q_send=pltpu.SemaphoreType.DMA((3,)), q_recv=pltpu.SemaphoreType.DMA((3,)),
        o_send=pltpu.SemaphoreType.DMA((6,)), o_recv=pltpu.SemaphoreType.DMA((6,)),
    )
    ins = ["tl", "tokens", "memory", "shards", "norms", "bias"]
    names = ins + list(outs) + list(scratch)

    def kernel(*refs):
        r = SimpleNamespace(**dict(zip(names, refs)))
        run_forward(r, place(), nz, CHUNKS)

    vm = pl.BlockSpec(memory_space=pltpu.VMEM)
    res = pl.pallas_call(
        kernel,
        out_shape=[jax.ShapeDtypeStruct(s, t) for s, t in outs.values()],
        in_specs=[pl.BlockSpec(memory_space=pltpu.SMEM), vm, pl.BlockSpec(memory_space=pl.ANY), pl.BlockSpec(memory_space=pl.ANY), vm, vm],
        out_specs=[vm] * len(outs),
        scratch_shapes=list(scratch.values()),
        compiler_params=pltpu.CompilerParams(collective_id=0, has_side_effects=True, vmem_limit_bytes=63 * 2**20),
    )(tl, tokens, mem_pad, shards, norms, bias)
    return dict(zip(outs, res))

def pack_weights(ws):
    self_project, self_output, cross_query, cross_memory, cross_output, expand, contract = ws
    rows, d = self_output.shape
    ndev = d // rows
    cut = lambda w: jnp.transpose(w.reshape(rows, -1, d), (1, 0, 2))
    q = contract.shape[0] // rows
    ex = jnp.transpose(expand.reshape(rows, ndev, q, rows), (2, 0, 1, 3)).reshape(q, rows, d)
    return jnp.concatenate([cut(self_project), cut(self_output), cut(cross_query), cut(cross_memory), cut(cross_output), ex, contract.reshape(q, rows, d)], axis=0)

def pack_norms(gains, shifts):
    own = jnp.concatenate([gains, shifts], axis=0)
    lane = (lax.axis_index("frames")) * own.shape[1]
    return lax.dynamic_update_slice(jnp.zeros((32, LANES), BF16), own, (0, lane))

def frame_bias(cross_mask, memory_length, frame_count, padded):
    start = lax.axis_index("frames") * frame_count
    at = start + jnp.arange(frame_count)
    mask = lax.dynamic_slice_in_dim(cross_mask, start, frame_count, 1)
    ok = (at[None] < memory_length[:, None]) & ((mask == 1) | (at[None] == 0))
    return jnp.pad(jnp.where(ok, 0.0, -1e30), ((0, 0), (0, padded - frame_count)), constant_values=-1e30).astype(F32)

NZ = 4
block_heads = 4


def layer_norm(values, gain_row, shift_row):
    center = values - jnp.mean(values, axis=-1, keepdims=True)
    spread = jnp.mean(center * center, axis=-1, keepdims=True)
    return center * lax.rsqrt(spread + 1e-05) * gain_row + shift_row


def exact_gelu(values):
    return jax.nn.gelu(values, approximate=False)


def matmul(left_side, right_side):
    return jnp.dot(left_side, right_side, preferred_element_type=jnp.float32)


def split_heads(rows):
    return rows.reshape(rows.shape[:-1] + (rows.shape[-1] // HEAD_DIM, HEAD_DIM))


def to_blocks(rows):
    row_count, head_count, head_width = rows.shape
    return rows.reshape(row_count, head_count // block_heads, block_heads, head_width).transpose(
        1, 0, 2, 3
    )


def from_blocks(blocks):
    group_count, row_count, head_count, head_width = blocks.shape
    return blocks.transpose(1, 0, 2, 3).reshape(row_count, group_count * head_count * head_width)


def block_scores(query_block, key_block, allowed):
    factor = query_block.shape[-1] ** (-0.5)
    raw_scores = (
        jnp.einsum("shd,fhd->hsf", query_block, key_block, preferred_element_type=jnp.float32)
        * factor
    )
    return jnp.where(allowed[None], raw_scores, -1e30)


def block_probs(query_block, key_block, allowed, max_block, total_block):
    scores = block_scores(query_block, key_block, allowed)
    shifted = jnp.where(allowed[None], jnp.exp(scores - max_block[..., None]), 0.0)
    return shifted / total_block[..., None]


def block_grads(query_block, key_block, grad_block, probs, grad_probs, row_dot):
    factor = query_block.shape[-1] ** (-0.5)
    score_grad = (probs * (grad_probs - row_dot)).astype(jnp.bfloat16)
    query_grad = (
        jnp.einsum("hsf,fhd->shd", score_grad, key_block, preferred_element_type=jnp.float32)
        * factor
    )
    key_grad = (
        jnp.einsum("hsf,shd->fhd", score_grad, query_block, preferred_element_type=jnp.float32)
        * factor
    )
    value_grad = jnp.einsum(
        "hsf,shd->fhd", probs.astype(jnp.bfloat16), grad_block, preferred_element_type=jnp.float32
    )
    return (query_grad, key_grad, value_grad)


def attend_whole(query_rows, key_rows, value_rows, allowed):

    def one_group(blocks):
        query_block, key_block, value_block = blocks
        scores = block_scores(query_block, key_block, allowed)
        max_block = jnp.max(scores, axis=-1)
        shifted = jnp.where(allowed[None], jnp.exp(scores - max_block[..., None]), 0.0)
        total_block = jnp.sum(shifted, axis=-1)
        weights = (shifted / total_block[..., None]).astype(jnp.bfloat16)
        mixture = jnp.einsum(
            "hsf,fhd->shd", weights, value_block, preferred_element_type=jnp.float32
        )
        return (mixture, max_block, total_block)

    mixture, row_max, totals = lax.map(
        one_group, (to_blocks(query_rows), to_blocks(key_rows), to_blocks(value_rows))
    )
    return (from_blocks(mixture), row_max, totals)


def attend_whole_back(query_rows, key_rows, value_rows, allowed, grad_rows, row_max, totals):

    def one_group(blocks):
        query_block, key_block, value_block, grad_block, max_block, total_block = blocks
        probs = block_probs(query_block, key_block, allowed, max_block, total_block)
        grad_probs = jnp.einsum(
            "shd,fhd->hsf", grad_block, value_block, preferred_element_type=jnp.float32
        )
        row_dot = jnp.sum(probs * grad_probs, axis=-1, keepdims=True)
        return block_grads(query_block, key_block, grad_block, probs, grad_probs, row_dot)

    query_grad, key_grad, value_grad = lax.map(
        one_group,
        (
            to_blocks(query_rows),
            to_blocks(key_rows),
            to_blocks(value_rows),
            to_blocks(grad_rows),
            row_max,
            totals,
        ),
    )
    return (from_blocks(query_grad), from_blocks(key_grad), from_blocks(value_grad))


def cross_stats(query_rows, key_rows, allowed):

    def one_group(blocks):
        query_block, key_block = blocks
        scores = block_scores(query_block, key_block, allowed)
        max_block = jnp.max(scores, axis=-1)
        total_block = jnp.sum(
            jnp.where(allowed[None], jnp.exp(scores - max_block[..., None]), 0.0), axis=-1
        )
        return (max_block, total_block)

    return lax.map(one_group, (to_blocks(query_rows), to_blocks(key_rows)))


def cross_partial(query_rows, key_rows, value_rows, allowed, row_max, totals):

    def one_group(blocks):
        query_block, key_block, value_block, max_block, total_block = blocks
        probs = block_probs(query_block, key_block, allowed, max_block, total_block)
        return jnp.einsum(
            "hsf,fhd->shd",
            probs.astype(jnp.bfloat16),
            value_block,
            preferred_element_type=jnp.float32,
        )

    return from_blocks(
        lax.map(
            one_group,
            (to_blocks(query_rows), to_blocks(key_rows), to_blocks(value_rows), row_max, totals),
        )
    )


def cross_row_dot(query_rows, key_rows, value_rows, allowed, grad_rows, row_max, totals):

    def one_group(blocks):
        query_block, key_block, value_block, grad_block, max_block, total_block = blocks
        probs = block_probs(query_block, key_block, allowed, max_block, total_block)
        grad_probs = jnp.einsum(
            "shd,fhd->hsf", grad_block, value_block, preferred_element_type=jnp.float32
        )
        return jnp.sum(probs * grad_probs, axis=-1)

    return lax.map(
        one_group,
        (
            to_blocks(query_rows),
            to_blocks(key_rows),
            to_blocks(value_rows),
            to_blocks(grad_rows),
            row_max,
            totals,
        ),
    )


def cross_partial_grads(
    query_rows, key_rows, value_rows, allowed, grad_rows, row_max, totals, row_dot
):

    def one_group(blocks):
        query_block, key_block, value_block, grad_block, max_block, total_block, dot_block = blocks
        probs = block_probs(query_block, key_block, allowed, max_block, total_block)
        grad_probs = jnp.einsum(
            "shd,fhd->hsf", grad_block, value_block, preferred_element_type=jnp.float32
        )
        return block_grads(
            query_block, key_block, grad_block, probs, grad_probs, dot_block[..., None]
        )

    query_grad, key_grad, value_grad = lax.map(
        one_group,
        (
            to_blocks(query_rows),
            to_blocks(key_rows),
            to_blocks(value_rows),
            to_blocks(grad_rows),
            row_max,
            totals,
            row_dot,
        ),
    )
    return (from_blocks(query_grad), from_blocks(key_grad), from_blocks(value_grad))


def unmix(part, q):
    rows, ff = part.shape
    return jnp.transpose(part.reshape(rows, q, ff // (q * rows), rows), (0, 2, 1, 3)).reshape(rows, ff)


def natural(grad, q, rows):
    ff, d = grad.shape
    return jnp.transpose(grad.reshape(q, ff // (q * rows), rows, d), (1, 0, 2, 3)).reshape(ff, d)


def ln_back(values, gain_row, shift_row, grad):
    return jax.vjp(layer_norm, values, gain_row, shift_row)[1](grad)


def local_fast(
    tokens,
    memory,
    cotangent,
    self_project,
    self_output,
    cross_query,
    cross_memory,
    cross_output,
    expand,
    contract,
    norm_gains,
    norm_shifts,
    target_length,
    memory_length,
    cross_mask,
):
    residual_in = tokens[0]
    length, model_width = residual_in.shape
    row_valid = jnp.arange(length) < target_length[0]
    causal = jnp.arange(length)[:, None] >= jnp.arange(length)[None, :]
    item_count, frame_count = memory.shape[:2]
    padded = -(-frame_count // LANES) * LANES
    weights = (self_project, self_output, cross_query, cross_memory, cross_output, expand, contract)
    bias = frame_bias(cross_mask, memory_length, frame_count, padded)
    o = f_call(NZ, target_length, residual_in, jnp.pad(memory, ((0, 0), (0, padded - frame_count), (0, 0))), pack_weights(weights), pack_norms(norm_gains, norm_shifts), bias)
    wg = o["wg"].reshape(CHUNKS, model_width, model_width)
    join = lambda lo, hi: jnp.concatenate([wg[k] for k in range(lo, hi)], axis=1)
    w_self, w_self_out, w_query, w_memory, w_cross_out, w_expand = join(0, 3), wg[3], wg[4], join(5, 7), wg[7], join(8, 12)
    w_contract = jnp.concatenate([wg[k] for k in range(12, 16)], axis=0)
    gains, shifts = o["gs"][:4], o["gs"][4:8]
    normed_one, self_mix_low, normed_two, cross_mix_low, normed_three = (
        o["n1t"].T, o["smixt"].T, o["n2t"].T, o["cmix"].astype(BF16), o["n3t"].T)
    first_sum, second_sum, third_sum, cross_mix, active, slope = o["first"], o["second"], o["third"], o["cmix"], o["activet"].T, o["slope"].astype(F32)
    joint_rows = o["joint"]
    self_queries, self_keys, self_values = (split_heads(joint_rows[:, k * model_width : (k + 1) * model_width]) for k in range(3))
    heads = model_width // HEAD_DIM
    self_max = o["slse"][:heads].reshape(-1, block_heads, length)
    self_totals = jnp.ones_like(self_max)
    query_heads = split_heads(o["qa"])
    kv = o["kv"][:, :frame_count]
    memory_keys, memory_values = split_heads(kv[..., :model_width]), split_heads(kv[..., model_width:])
    cross_max = lax.all_gather(o["clse"][None, :heads], "frames", axis=0, tiled=True).reshape(item_count, -1, block_heads, length)
    cross_totals = jnp.ones_like(cross_max)
    frame_ok = bias[:, :frame_count] == 0.0
    result = o["result"]
    total = lax.psum(o["sq"][:5, 0], ("dp", "frames"))
    squares_all, counted = total[:4], total[4]
    branch_rms = jnp.sqrt(squares_all / (counted * model_width))
    grad_result = jnp.where(row_valid[:, None], cotangent[0], 0.0)
    grad_third, gain_grad_three, shift_grad_three = ln_back(third_sum, gains[3], shifts[3], grad_result)
    feed_low = grad_third.astype(jnp.bfloat16)
    contract_grad = matmul(active.T, feed_low)
    grad_active = matmul(feed_low, w_contract.T)
    grad_hidden = (grad_active * slope).astype(jnp.bfloat16)
    expand_grad = matmul(normed_three.T, grad_hidden)
    grad_normed_three = matmul(grad_hidden, w_expand.T)
    grad_second_part, gain_grad_two, shift_grad_two = ln_back(second_sum, gains[2], shifts[2], grad_normed_three)
    grad_second = grad_third + grad_second_part
    cross_low = grad_second.astype(jnp.bfloat16)
    cross_output_grad = matmul(cross_mix_low.T, cross_low)
    grad_cross_mix = matmul(cross_low, w_cross_out.T).astype(jnp.bfloat16)
    every_grad = split_heads(lax.all_gather(grad_cross_mix[None], "frames", axis=0, tiled=True))

    own_dot = jnp.sum((grad_cross_mix.astype(jnp.float32) * cross_mix).reshape(length, -1, HEAD_DIM), axis=-1).T
    row_dot = lax.all_gather(own_dot[None], "frames", axis=0, tiled=True).reshape(item_count, -1, block_heads, length)

    def item_grads(inputs):
        query_item, key_item, value_item, frame_item, grad_item, max_item, total_item, dot_item = (
            inputs
        )
        allowed = jnp.broadcast_to(frame_item[None, :], (length, frame_count))
        return cross_partial_grads(
            query_item, key_item, value_item, allowed, grad_item, max_item, total_item, dot_item
        )

    query_parts, key_parts, value_parts = lax.map(
        item_grads,
        (
            query_heads,
            memory_keys,
            memory_values,
            frame_ok,
            every_grad,
            cross_max,
            cross_totals,
            row_dot,
        ),
    )
    query_grad = lax.psum_scatter(
        query_parts.astype(jnp.bfloat16), "frames", scatter_dimension=0, tiled=True
    ).astype(jnp.float32)[0]
    memory_low = (
        jnp.concatenate([key_parts, value_parts], axis=2)
        .astype(jnp.bfloat16)
        .reshape(item_count * frame_count, 2 * model_width)
    )
    cross_memory_grad = matmul(memory.reshape(item_count * frame_count, model_width).T, memory_low)
    memory_grad = matmul(memory_low, w_memory.T).reshape(item_count, frame_count, model_width)
    query_low = query_grad.astype(jnp.bfloat16)
    cross_query_grad = matmul(normed_two.T, query_low)
    grad_normed_two = matmul(query_low, w_query.T)
    grad_first_part, gain_grad_one, shift_grad_one = ln_back(first_sum, gains[1], shifts[1], grad_normed_two)
    grad_first = grad_second + grad_first_part
    self_low = grad_first.astype(jnp.bfloat16)
    self_output_grad = matmul(self_mix_low.T, self_low)
    grad_self_mix = matmul(self_low, w_self_out.T).astype(jnp.bfloat16)
    self_query_grad, self_key_grad, self_value_grad = attend_whole_back(
        self_queries,
        self_keys,
        self_values,
        causal,
        split_heads(grad_self_mix),
        self_max,
        self_totals,
    )
    joint_grad = jnp.concatenate([self_query_grad, self_key_grad, self_value_grad], axis=1).astype(
        jnp.bfloat16
    )
    self_project_grad = matmul(normed_one.T, joint_grad)
    grad_normed_one = matmul(joint_grad, w_self.T)
    grad_input_part, gain_grad_zero, shift_grad_zero = ln_back(residual_in, gains[0], shifts[0], grad_normed_one)
    tokens_grad = grad_first + grad_input_part
    gain_grads = jnp.stack([gain_grad_zero, gain_grad_one, gain_grad_two, gain_grad_three])
    shift_grads = jnp.stack([shift_grad_zero, shift_grad_one, shift_grad_two, shift_grad_three])
    reduced = (
        lax.psum_scatter(self_project_grad, ("dp", "frames"), scatter_dimension=0, tiled=True),
        lax.psum_scatter(self_output_grad, ("dp", "frames"), scatter_dimension=0, tiled=True),
        lax.psum_scatter(cross_query_grad, ("dp", "frames"), scatter_dimension=0, tiled=True),
        lax.psum_scatter(cross_memory_grad, ("dp", "frames"), scatter_dimension=0, tiled=True),
        lax.psum_scatter(cross_output_grad, ("dp", "frames"), scatter_dimension=0, tiled=True),
        lax.psum_scatter(expand_grad, ("dp", "frames"), scatter_dimension=0, tiled=True),
        lax.psum_scatter(natural(contract_grad, contract.shape[0] // expand.shape[0], expand.shape[0]), ("dp", "frames"), scatter_dimension=0, tiled=True),
        lax.psum_scatter(gain_grads, ("dp", "frames"), scatter_dimension=1, tiled=True),
        lax.psum_scatter(shift_grads, ("dp", "frames"), scatter_dimension=1, tiled=True),
    )
    (
        project_part,
        output_part,
        query_part,
        memory_part,
        cross_out_part,
        expand_part,
        contract_part,
        gains_part,
        shifts_part,
    ) = reduced
    return (
        result[None],
        tokens_grad[None],
        memory_grad,
        project_part,
        output_part,
        query_part,
        memory_part,
        cross_out_part,
        unmix(expand_part, contract.shape[0] // expand.shape[0]),
        contract_part,
        gains_part,
        shifts_part,
        branch_rms,
    )


def local(
    tokens,
    memory,
    cotangent,
    self_project,
    self_output,
    cross_query,
    cross_memory,
    cross_output,
    expand,
    contract,
    norm_gains,
    norm_shifts,
    target_length,
    memory_length,
    cross_mask,
):
    gathered = (
        lax.all_gather(self_project, ("dp", "frames"), axis=0, tiled=True),
        lax.all_gather(self_output, ("dp", "frames"), axis=0, tiled=True),
        lax.all_gather(cross_query, ("dp", "frames"), axis=0, tiled=True),
        lax.all_gather(cross_memory, ("dp", "frames"), axis=0, tiled=True),
        lax.all_gather(cross_output, ("dp", "frames"), axis=0, tiled=True),
        lax.all_gather(expand, ("dp", "frames"), axis=0, tiled=True),
        lax.all_gather(contract, ("dp", "frames"), axis=0, tiled=True),
        lax.all_gather(norm_gains, ("dp", "frames"), axis=1, tiled=True),
        lax.all_gather(norm_shifts, ("dp", "frames"), axis=1, tiled=True),
    )
    (
        w_self,
        w_self_out,
        w_query,
        w_memory,
        w_cross_out,
        w_expand,
        w_contract,
        gains_low,
        shifts_low,
    ) = gathered
    gains = gains_low.astype(jnp.float32)
    shifts = shifts_low.astype(jnp.float32)
    model_width = w_self_out.shape[0]
    residual_in = tokens[0]
    length = residual_in.shape[0]
    positions = jnp.arange(length)
    row_valid = positions < target_length[0]
    causal = positions[:, None] >= positions[None, :]
    item_count = memory.shape[0]
    frame_count = memory.shape[1]
    own_item = lax.axis_index("frames")
    normed_one_f, back_one = jax.vjp(layer_norm, residual_in, gains[0], shifts[0])
    normed_one = normed_one_f.astype(jnp.bfloat16)
    joint_rows = matmul(normed_one, w_self).astype(jnp.bfloat16)
    self_queries = split_heads(joint_rows[:, :model_width])
    self_keys = split_heads(joint_rows[:, model_width : 2 * model_width])
    self_values = split_heads(joint_rows[:, 2 * model_width :])
    self_mix, self_max, self_totals = attend_whole(self_queries, self_keys, self_values, causal)
    self_mix_low = self_mix.astype(jnp.bfloat16)
    self_branch = matmul(self_mix_low, w_self_out)
    first_sum = residual_in + self_branch
    normed_two_f, back_two = jax.vjp(layer_norm, first_sum, gains[1], shifts[1])
    normed_two = normed_two_f.astype(jnp.bfloat16)
    cross_queries = matmul(normed_two, w_query).astype(jnp.bfloat16)
    every_query = lax.all_gather(cross_queries[None], "frames", axis=0, tiled=True)
    query_heads = split_heads(every_query)
    frame_start = own_item * frame_count
    local_frames = frame_start + jnp.arange(frame_count)
    local_mask = lax.dynamic_slice_in_dim(cross_mask, frame_start, frame_count, 1)
    frame_ok = (local_frames[None, :] < memory_length[:, None]) & (
        (local_mask == 1) | (local_frames[None, :] == 0)
    )
    memory_rows = matmul(memory.reshape(item_count * frame_count, model_width), w_memory).astype(
        jnp.bfloat16
    )
    memory_rows = memory_rows.reshape(item_count, frame_count, 2 * model_width)
    memory_keys = split_heads(memory_rows[..., :model_width])
    memory_values = split_heads(memory_rows[..., model_width:])

    def item_stats(inputs):
        query_item, key_item, frame_item = inputs
        return cross_stats(
            query_item, key_item, jnp.broadcast_to(frame_item[None, :], (length, frame_count))
        )

    local_max, local_totals = lax.map(item_stats, (query_heads, memory_keys, frame_ok))
    cross_max = lax.pmax(local_max.astype(jnp.bfloat16), "frames").astype(local_max.dtype)
    cross_totals = lax.psum(
        (local_totals * jnp.exp(local_max - cross_max)).astype(jnp.bfloat16), "frames"
    ).astype(jnp.float32)

    def item_partial(inputs):
        query_item, key_item, value_item, frame_item, max_item, total_item = inputs
        allowed = jnp.broadcast_to(frame_item[None, :], (length, frame_count))
        return cross_partial(query_item, key_item, value_item, allowed, max_item, total_item)

    partial_mix = lax.map(
        item_partial, (query_heads, memory_keys, memory_values, frame_ok, cross_max, cross_totals)
    )
    cross_mix = lax.psum_scatter(
        partial_mix.astype(jnp.bfloat16), "frames", scatter_dimension=0, tiled=True
    ).astype(jnp.float32)[0]
    cross_mix_low = cross_mix.astype(jnp.bfloat16)
    cross_branch = matmul(cross_mix_low, w_cross_out)
    second_sum = first_sum + cross_branch
    normed_three_f, back_three = jax.vjp(layer_norm, second_sum, gains[2], shifts[2])
    normed_three = normed_three_f.astype(jnp.bfloat16)
    hidden = matmul(normed_three, w_expand)
    active_f, gelu_back = jax.vjp(exact_gelu, hidden)
    active = active_f.astype(jnp.bfloat16)
    feed_branch = matmul(active, w_contract)
    third_sum = second_sum + feed_branch
    final_rows, back_final = jax.vjp(layer_norm, third_sum, gains[3], shifts[3])
    result = jnp.where(row_valid[:, None], final_rows, 0.0)
    row_weight = row_valid.astype(jnp.float32)[:, None]
    squares = jnp.stack(
        [
            jnp.sum(row_weight * member * member)
            for member in (third_sum, self_branch, cross_branch, feed_branch)
        ]
    )
    squares_all, counted = lax.psum((squares, jnp.sum(row_weight)), ("dp", "frames"))
    branch_rms = jnp.sqrt(squares_all / (counted * model_width))
    grad_result = jnp.where(row_valid[:, None], cotangent[0], 0.0)
    grad_third, gain_grad_three, shift_grad_three = back_final(grad_result)
    feed_low = grad_third.astype(jnp.bfloat16)
    contract_grad = matmul(active.T, feed_low)
    grad_active = matmul(feed_low, w_contract.T)
    grad_hidden = gelu_back(grad_active)[0].astype(jnp.bfloat16)
    expand_grad = matmul(normed_three.T, grad_hidden)
    grad_normed_three = matmul(grad_hidden, w_expand.T)
    grad_second_part, gain_grad_two, shift_grad_two = back_three(grad_normed_three)
    grad_second = grad_third + grad_second_part
    cross_low = grad_second.astype(jnp.bfloat16)
    cross_output_grad = matmul(cross_mix_low.T, cross_low)
    grad_cross_mix = matmul(cross_low, w_cross_out.T).astype(jnp.bfloat16)
    every_grad = split_heads(lax.all_gather(grad_cross_mix[None], "frames", axis=0, tiled=True))

    def item_dot(inputs):
        query_item, key_item, value_item, frame_item, grad_item, max_item, total_item = inputs
        allowed = jnp.broadcast_to(frame_item[None, :], (length, frame_count))
        return cross_row_dot(
            query_item, key_item, value_item, allowed, grad_item, max_item, total_item
        )

    local_dot = lax.map(
        item_dot,
        (query_heads, memory_keys, memory_values, frame_ok, every_grad, cross_max, cross_totals),
    )
    row_dot = lax.psum(local_dot.astype(jnp.bfloat16), "frames").astype(jnp.float32)

    def item_grads(inputs):
        query_item, key_item, value_item, frame_item, grad_item, max_item, total_item, dot_item = (
            inputs
        )
        allowed = jnp.broadcast_to(frame_item[None, :], (length, frame_count))
        return cross_partial_grads(
            query_item, key_item, value_item, allowed, grad_item, max_item, total_item, dot_item
        )

    query_parts, key_parts, value_parts = lax.map(
        item_grads,
        (
            query_heads,
            memory_keys,
            memory_values,
            frame_ok,
            every_grad,
            cross_max,
            cross_totals,
            row_dot,
        ),
    )
    query_grad = lax.psum_scatter(
        query_parts.astype(jnp.bfloat16), "frames", scatter_dimension=0, tiled=True
    ).astype(jnp.float32)[0]
    memory_low = (
        jnp.concatenate([key_parts, value_parts], axis=2)
        .astype(jnp.bfloat16)
        .reshape(item_count * frame_count, 2 * model_width)
    )
    cross_memory_grad = matmul(memory.reshape(item_count * frame_count, model_width).T, memory_low)
    memory_grad = matmul(memory_low, w_memory.T).reshape(item_count, frame_count, model_width)
    query_low = query_grad.astype(jnp.bfloat16)
    cross_query_grad = matmul(normed_two.T, query_low)
    grad_normed_two = matmul(query_low, w_query.T)
    grad_first_part, gain_grad_one, shift_grad_one = back_two(grad_normed_two)
    grad_first = grad_second + grad_first_part
    self_low = grad_first.astype(jnp.bfloat16)
    self_output_grad = matmul(self_mix_low.T, self_low)
    grad_self_mix = matmul(self_low, w_self_out.T).astype(jnp.bfloat16)
    self_query_grad, self_key_grad, self_value_grad = attend_whole_back(
        self_queries,
        self_keys,
        self_values,
        causal,
        split_heads(grad_self_mix),
        self_max,
        self_totals,
    )
    joint_grad = jnp.concatenate([self_query_grad, self_key_grad, self_value_grad], axis=1).astype(
        jnp.bfloat16
    )
    self_project_grad = matmul(normed_one.T, joint_grad)
    grad_normed_one = matmul(joint_grad, w_self.T)
    grad_input_part, gain_grad_zero, shift_grad_zero = back_one(grad_normed_one)
    tokens_grad = grad_first + grad_input_part
    gain_grads = jnp.stack([gain_grad_zero, gain_grad_one, gain_grad_two, gain_grad_three])
    shift_grads = jnp.stack([shift_grad_zero, shift_grad_one, shift_grad_two, shift_grad_three])
    reduced = (
        lax.psum_scatter(self_project_grad, ("dp", "frames"), scatter_dimension=0, tiled=True),
        lax.psum_scatter(self_output_grad, ("dp", "frames"), scatter_dimension=0, tiled=True),
        lax.psum_scatter(cross_query_grad, ("dp", "frames"), scatter_dimension=0, tiled=True),
        lax.psum_scatter(cross_memory_grad, ("dp", "frames"), scatter_dimension=0, tiled=True),
        lax.psum_scatter(cross_output_grad, ("dp", "frames"), scatter_dimension=0, tiled=True),
        lax.psum_scatter(expand_grad, ("dp", "frames"), scatter_dimension=0, tiled=True),
        lax.psum_scatter(contract_grad, ("dp", "frames"), scatter_dimension=0, tiled=True),
        lax.psum_scatter(gain_grads, ("dp", "frames"), scatter_dimension=1, tiled=True),
        lax.psum_scatter(shift_grads, ("dp", "frames"), scatter_dimension=1, tiled=True),
    )
    (
        project_part,
        output_part,
        query_part,
        memory_part,
        cross_out_part,
        expand_part,
        contract_part,
        gains_part,
        shifts_part,
    ) = reduced
    return (
        result[None],
        tokens_grad[None],
        memory_grad,
        project_part,
        output_part,
        query_part,
        memory_part,
        cross_out_part,
        expand_part,
        contract_part,
        gains_part,
        shifts_part,
        branch_rms,
    )


def solution(mesh):
    return jax.shard_map(
        local_fast if (mesh.shape['dp'], mesh.shape['frames']) == (2 * NZ, 4) else local,
        mesh=mesh,
        in_specs=(
            P(("dp", "frames"), None, None),
            P("dp", "frames", None),
            P(("dp", "frames"), None, None),
            P(("dp", "frames"), None),
            P(("dp", "frames"), None),
            P(("dp", "frames"), None),
            P(("dp", "frames"), None),
            P(("dp", "frames"), None),
            P(("dp", "frames"), None),
            P(("dp", "frames"), None),
            P(None, ("dp", "frames")),
            P(None, ("dp", "frames")),
            P(("dp", "frames")),
            P("dp"),
            P("dp", None),
        ),
        out_specs=(
            P(("dp", "frames"), None, None),
            P(("dp", "frames"), None, None),
            P("dp", "frames", None),
            P(("dp", "frames"), None),
            P(("dp", "frames"), None),
            P(("dp", "frames"), None),
            P(("dp", "frames"), None),
            P(("dp", "frames"), None),
            P(("dp", "frames"), None),
            P(("dp", "frames"), None),
            P(None, ("dp", "frames")),
            P(None, ("dp", "frames")),
            P(),
        ),
        check_vma=False,
    )
```

```python
import functools
from types import SimpleNamespace

import jax
import jax.numpy as jnp
from jax import lax
from jax.experimental import pallas as pl
from jax.experimental.pallas import tpu as pltpu
from jax.sharding import PartitionSpec as P

MESH = pl.DeviceIdType.MESH
F32 = jnp.float32
BF16 = jnp.bfloat16
HEAD_DIM = 64
LANES = 128
TILE = 256


def dot(a, b):
    return jnp.dot(a, b, preferred_element_type=F32)


def dot_nt(a, b):
    return lax.dot_general(a, b, (((1,), (1,)), ((), ())), preferred_element_type=F32)


def place():
    dp, fr = lax.axis_index("dp"), lax.axis_index("frames")
    z, y = lax.div(dp, 2), lax.rem(dp, 2)
    x, c = lax.div(fr, 2), lax.rem(fr, 2)

    def dev(zz, yy, xx, cc):
        return {"dp": zz * 2 + yy, "frames": xx * 2 + cc}

    me = SimpleNamespace(z=z, y=y, x=x, c=c, fr=fr, dev=dev)
    me.xn = dev(z, y, 1 - x, c)
    me.yn = dev(z, 1 - y, x, c)
    me.sib = dev(z, y, x, 1 - c)
    me.diag = dev(z, y, 1 - x, 1 - c)
    return me


def remote(src, dst, send, recv, device):
    return pltpu.make_async_remote_copy(
        src_ref=src, dst_ref=dst, send_sem=send, recv_sem=recv, device_id=device, device_id_type=MESH
    )


def gather_steps(me, w, send, recv, nz):
    half = w.shape[4] // 2
    xo, yo, co = 1 - me.x, 1 - me.y, 1 - me.c

    def cp(view, s, device):
        return remote(view, view, send.at[s], recv.at[s], device)

    def spot(y, x, c):
        return w.at[:, y, x, c]

    def own(z):
        return w.at[z, me.y, me.x, me.c]

    def part(y, x, lower):
        return w.at[:, y, x, me.c, 0:half] if lower else w.at[:, y, x, me.c, half:]

    def step_z():
        for dz in range(1, nz):
            cp(own(me.z), dz - 1, me.dev(lax.rem(me.z + dz, nz), me.y, me.x, me.c)).start()

    def step_near():
        for dz in range(1, nz):
            cp(own(lax.rem(me.z + nz - dz, nz)), dz - 1, me.xn).wait_recv()
        cp(spot(me.y, me.x, me.c), nz - 1, me.xn).start()
        cp(spot(me.y, me.x, me.c), nz, me.yn).start()
        cp(spot(me.y, me.x, me.c), nz + 1, me.sib).start()

    def step_far():
        cp(spot(me.y, xo, me.c), nz - 1, me.xn).wait_recv()
        cp(part(me.y, xo, True), nz + 2, me.yn).start()
        cp(spot(me.y, xo, me.c), nz + 3, me.sib).start()
        cp(spot(yo, me.x, me.c), nz, me.yn).wait_recv()
        cp(part(yo, me.x, False), nz + 4, me.xn).start()
        cp(spot(yo, me.x, me.c), nz + 5, me.sib).start()

    def step_last():
        cp(part(yo, xo, True), nz + 2, me.yn).wait_recv()
        cp(part(yo, xo, False), nz + 4, me.xn).wait_recv()
        cp(spot(yo, xo, me.c), nz + 6, me.sib).start()

    def step_done():
        for y, x, s in ((me.y, me.x, nz + 1), (me.y, xo, nz + 3), (yo, me.x, nz + 5), (yo, xo, nz + 6)):
            cp(spot(y, x, co), s, me.sib).wait_recv()

    def drain():
        for dz in range(1, nz):
            cp(own(me.z), dz - 1, me.xn).wait_send()
        for y, x, s in (
            (me.y, me.x, nz - 1),
            (me.y, me.x, nz),
            (me.y, me.x, nz + 1),
            (me.y, xo, nz + 3),
            (yo, me.x, nz + 5),
            (yo, xo, nz + 6),
        ):
            cp(spot(y, x, me.c), s, me.xn).wait_send()
        cp(part(me.y, xo, True), nz + 2, me.xn).wait_send()
        cp(part(yo, me.x, False), nz + 4, me.xn).wait_send()

    return SimpleNamespace(z=step_z, near=step_near, far=step_far, last=step_last, done=step_done, drain=drain)


def scatter_steps(me, w, box, send, recv, credit, nz, turn, slots, turns, sink):
    half = w.shape[4] // 2
    xo, yo, co = 1 - me.x, 1 - me.y, 1 - me.c
    slot = turn % slots
    core, y1, x1, x2, y2, zs = (b.at[slot] for b in box)

    def above(dz):
        return me.dev(lax.rem(me.z + dz, nz), me.y, me.x, me.c)

    def below(dz):
        return me.dev(lax.rem(me.z + nz - dz, nz), me.y, me.x, me.c)

    moves = [
        (w.at[:, :, :, co], core, me.sib, me.sib),
        (w.at[:, yo, :, me.c, 0:half], y1, me.yn, me.yn),
        (w.at[:, :, xo, me.c, half:], x1, me.xn, me.xn),
        (w.at[:, me.y, xo, me.c, 0:half], x2, me.xn, me.xn),
        (w.at[:, yo, me.x, me.c, half:], y2, me.yn, me.yn),
    ]
    for dz in range(1, nz):
        moves.append((w.at[lax.rem(me.z + dz, nz), me.y, me.x, me.c], zs.at[dz - 1], above(dz), below(dz)))

    def cp(i):
        src, dst, to, _ = moves[i]
        return remote(src, dst, send.at[i], recv.at[i], to)

    def go(i):
        if turn >= slots:
            pl.semaphore_wait(credit.at[i], 1)
        cp(i).start()

    def free(i):
        if turn + slots < turns:
            pl.semaphore_signal(credit.at[i], inc=1, device_id=moves[i][3], device_id_type=MESH)

    def add(view, arrived):
        view[...] = (view[...].astype(F32) + arrived[...].astype(F32)).astype(w.dtype)

    def step_a():
        go(0)

    def step_b():
        cp(0).wait_recv()

        def body(zz, carry):
            for y in range(2):
                for x in range(2):
                    add(w.at[zz, y, x, me.c], core.at[zz, y, x])
            return carry

        lax.fori_loop(0, nz, body, 0)
        free(0)
        go(1)
        go(2)

    def step_c():
        cp(1).wait_recv()
        cp(2).wait_recv()

        def body(zz, carry):
            for o in range(2):
                add(w.at[zz, me.y, o, me.c, 0:half], y1.at[zz, o])
                add(w.at[zz, o, me.x, me.c, half:], x1.at[zz, o])
            return carry

        lax.fori_loop(0, nz, body, 0)
        free(1)
        free(2)
        go(3)
        go(4)

    def step_d():
        cp(3).wait_recv()
        cp(4).wait_recv()

        def body(zz, carry):
            add(w.at[zz, me.y, me.x, me.c, 0:half], x2.at[zz])
            add(w.at[zz, me.y, me.x, me.c, half:], y2.at[zz])
            return carry

        lax.fori_loop(0, nz, body, 0)
        free(3)
        free(4)
        for dz in range(1, nz):
            go(4 + dz)

    def step_e():
        total = w[me.z, me.y, me.x, me.c].astype(F32)
        for dz in range(1, nz):
            cp(4 + dz).wait_recv()
            total = total + zs[dz - 1].astype(F32)
        sink(total)
        for dz in range(1, nz):
            free(4 + dz)

    def drain():
        for i in range(len(moves)):
            cp(i).wait_send()

    return SimpleNamespace(a=step_a, b=step_b, c=step_c, d=step_d, e=step_e, drain=drain)


def lane_masks():
    lane = lax.broadcasted_iota(jnp.int32, (1, LANES), 1)
    left = jnp.where(lane < HEAD_DIM, 1.0, 0.0).astype(BF16)
    return left, (1.0 - left.astype(F32)).astype(BF16)


def two_heads(block):
    left, right = lane_masks()
    return jnp.concatenate([block * left, block * right], axis=0)


def one_block(pair):
    rows = pair.shape[0] // 2
    lane = lax.broadcasted_iota(jnp.int32, (rows, LANES), 1)
    return jnp.where(lane < HEAD_DIM, pair[:rows], pair[rows:])


def at128(p, base=0):
    return pl.ds(pl.multiple_of(base + p * LANES, LANES), LANES)


def put_stat(stat, p, pair):
    rows = pair.shape[0] // 2
    lane = lax.broadcasted_iota(jnp.int32, stat.shape, 1)
    stat = jnp.where(lane == 2 * p, pair[:rows], stat)
    return jnp.where(lane == 2 * p + 1, pair[rows:], stat)


def normalise(values):
    center = values - jnp.mean(values, axis=-1, keepdims=True)
    spread = jnp.mean(center * center, axis=-1, keepdims=True)
    return center * lax.rsqrt(spread + 1e-05)


def forward(r, me, nz):
    rows, d = r.tokens.shape
    items, frames = r.kv.shape[:2]
    pairs = d // LANES

    def weight(k, n):
        return r.wg[k, :, :, :, :, :, pl.ds(pl.multiple_of(n * TILE, TILE), TILE)].reshape(d, TILE)

    def product(x, k, sink):
        def body(n, carry):
            sink(n, pl.ds(pl.multiple_of(n * TILE, TILE), TILE), dot(x, weight(k, n)))
            return carry

        lax.fori_loop(0, d // TILE, body, 0)

    def ln(values, i):
        return normalise(values) * r.gs[i : i + 1, :] + r.gs[4 + i : 5 + i, :]

    def norms_in():
        for g in range(2 * nz):
            total = r.ng[g // 2, g % 2, 0, 0, 0:16, :].astype(F32)
            for f in range(1, 4):
                total = total + r.ng[g // 2, g % 2, f // 2, f % 2, 0:16, :].astype(F32)
            r.gs[:, g * LANES : (g + 1) * LANES] = total

    def norm_one():
        pltpu.make_async_copy(r.tokens, r.first, r.own_sem.at[1]).wait()
        r.xb[...] = ln(r.first[...], 0).astype(BF16)
        r.n1t[...] = r.xb[...].T

    def joint(q):
        def sink(n, cols, v):
            r.joint[:, pl.ds(pl.multiple_of(q * d + n * TILE, TILE), TILE)] = v.astype(BF16)

        product(r.xb[...], q, sink)

    def self_attention():
        row = lax.rem(lax.broadcasted_iota(jnp.int32, (2 * rows, rows), 0), rows)
        causal = row >= lax.broadcasted_iota(jnp.int32, (2 * rows, rows), 1)

        def body(p, stat):
            q2 = two_heads(r.joint[:, at128(p)] * jnp.asarray(HEAD_DIM**-0.5, BF16))
            s = dot_nt(q2, r.joint[:, at128(p, d)])
            s = jnp.where(causal, s, -1e30)
            m = jnp.max(s, axis=-1, keepdims=True)
            e = jnp.exp(s - m)
            total = jnp.sum(e, axis=-1, keepdims=True)
            o2 = dot(e.astype(BF16), r.joint[:, at128(p, 2 * d)]) / total
            r.xb[:, at128(p)] = one_block(o2).astype(BF16)
            return put_stat(stat, p, m + jnp.log(total))

        stat = lax.fori_loop(0, pairs, body, jnp.zeros((rows, LANES), F32))
        r.slse[...] = stat.T
        r.smixt[...] = r.xb[...].T

    def self_out():
        def sink(n, cols, v):
            r.branch[:, cols] = v

        product(r.xb[...], 3, sink)
        r.first[...] = r.first[...] + r.branch[...]
        squares(1, r.branch[...])
        r.xb[...] = ln(r.first[...], 1).astype(BF16)
        r.n2t[...] = r.xb[...].T

    def squares(i, values):
        ok = lax.broadcasted_iota(jnp.int32, (rows, 1), 0) < r.tl[0]
        total = jnp.sum(jnp.where(ok, values * values, 0.0))
        line = lax.broadcasted_iota(jnp.int32, r.sq.shape, 0)
        r.sq[...] = jnp.where(line == i, total, r.sq[...])

    def start_counts():
        line = lax.broadcasted_iota(jnp.int32, r.sq.shape, 0)
        r.sq[...] = jnp.where(line == 4, r.tl[0].astype(F32), 0.0)

    def queries():
        def sink(n, cols, v):
            r.qa[me.fr, :, cols] = v.astype(BF16)

        product(r.xb[...], 4, sink)

    def q_copy(f, s, device):
        return remote(r.qa.at[f], r.qa.at[f], r.q_send.at[s], r.q_recv.at[s], device)

    fx, fs, fd = (1 - me.x) * 2 + me.c, me.x * 2 + 1 - me.c, (1 - me.x) * 2 + 1 - me.c

    def q_start():
        q_copy(me.fr, 0, me.xn).start()
        q_copy(me.fr, 1, me.sib).start()

    def q_forward():
        q_copy(fx, 0, me.xn).wait_recv()
        q_copy(fx, 2, me.sib).start()

    def q_done():
        q_copy(fs, 1, me.sib).wait_recv()
        q_copy(fd, 2, me.sib).wait_recv()

    def mem_copy(t):
        return pltpu.make_async_copy(r.memory.at[t], r.rc.at[t % 2, 0 : r.memory.shape[1]], r.m_sem.at[t % 2])

    def memory_part(which):
        def item(t):
            mem_copy(t).wait()
            stage = r.rc.at[t % 2, 0 : r.memory.shape[1]]

            def body(n, carry):
                v = dot(stage[...].reshape(frames, d), weight(5 + which, n))
                r.kv[t, :, pl.ds(pl.multiple_of(which * d + n * TILE, TILE), TILE)] = v.astype(BF16)
                return carry

            lax.fori_loop(0, d // TILE, body, 0)
            if which == 0:
                r.memt[:, t * frames : (t + 1) * frames] = stage[...].reshape(frames, d).T
            if t + 2 < items:
                mem_copy(t + 2).start()

        def run():
            for t in range(items):
                item(t)
            if which == 0:
                for t in range(min(2, items)):
                    mem_copy(t).start()

        return run

    def mem_start():
        for t in range(min(2, items)):
            mem_copy(t).start()

    def cross_item(t):
        def body(p, stat):
            q2 = two_heads(r.qa[t, :, at128(p)] * jnp.asarray(HEAD_DIM**-0.5, BF16))
            s = dot_nt(q2, r.kv[t, :, at128(p)]) + r.bias[pl.ds(t, 1), :]
            m = jnp.max(s, axis=-1, keepdims=True)
            e = jnp.exp(s - m)
            total = jnp.sum(e, axis=-1, keepdims=True)
            o2 = dot(e.astype(BF16), r.kv[t, :, at128(p, d)]) / total
            r.op[t, :, at128(p)] = one_block(o2).astype(BF16)
            return put_stat(stat, p, m + jnp.log(total))

        stat = lax.fori_loop(0, pairs, body, jnp.zeros((rows, LANES), F32))
        r.opl[t] = stat.T

    def o_copies(t, slot, device):
        return (
            remote(r.op.at[t], r.orv.at[slot], r.o_send.at[slot], r.o_recv.at[slot], device),
            remote(r.opl.at[t, 0:16], r.orl.at[slot, 0:16], r.o_send.at[3 + slot], r.o_recv.at[3 + slot], device),
        )

    def o_start(t, slot, device):
        for cp in o_copies(t, slot, device):
            cp.start()

    def o_wait(t, slot, device):
        for cp in o_copies(t, slot, device):
            cp.wait_recv()

    def merge(parts, sink):
        lses = [lse[0:16] for _, lse in parts]
        top = functools.reduce(jnp.maximum, lses)
        shares = [jnp.exp(v - top) for v in lses]
        total = functools.reduce(jnp.add, shares)
        flat = jnp.concatenate([v / total for v in shares] + [jnp.zeros((LANES - 16 * len(parts), LANES), F32)], axis=0)
        r.wcol[...] = flat.T
        lane = lax.broadcasted_iota(jnp.int32, (rows, LANES), 1)
        for p in range(pairs):
            value = jnp.zeros((rows, LANES), F32)
            for i, (mix, _) in enumerate(parts):
                left = r.wcol[:, 16 * i + 2 * p : 16 * i + 2 * p + 1]
                right = r.wcol[:, 16 * i + 2 * p + 1 : 16 * i + 2 * p + 2]
                share = jnp.where(lane < HEAD_DIM, left, right)
                value = value + share * mix[:, p * LANES : (p + 1) * LANES].astype(F32)
            sink(p, value)
        return top + jnp.log(total)

    def cross_a():
        cross_item(fd)
        o_start(fd, 0, me.sib)
        cross_item(fs)
        o_start(fs, 1, me.sib)

    def cross_b():
        cross_item(fx)
        o_wait(fd, 0, me.sib)

        def sink(p, v):
            r.op[fx, :, p * LANES : (p + 1) * LANES] = v.astype(BF16)

        lse = merge([(r.op.at[fx], r.opl.at[fx]), (r.orv.at[0], r.orl.at[0])], sink)
        r.opl[fx, 0:16] = lse
        o_start(fx, 2, me.xn)
        cross_item(me.fr)

    def cross_c():
        o_wait(fs, 1, me.sib)
        o_wait(fx, 2, me.xn)

        def sink(p, v):
            r.xb[:, p * LANES : (p + 1) * LANES] = v.astype(BF16)

        parts = [(r.op.at[me.fr], r.opl.at[me.fr]), (r.orv.at[1], r.orl.at[1]), (r.orv.at[2], r.orl.at[2])]
        r.clse[0:16] = merge(parts, sink)
        r.cmixt[...] = r.xb[...].T

    def cross_out():
        def sink(n, cols, v):
            r.branch[:, cols] = v

        product(r.xb[...], 7, sink)
        squares(2, r.branch[...])
        r.second[...] = r.first[...] + r.branch[...]
        r.xb[...] = ln(r.second[...], 2).astype(BF16)
        r.n3t[...] = r.xb[...].T

    def expand(q):
        def sink(n, cols, v):
            at = pl.ds(pl.multiple_of(q * d + n * TILE, TILE), TILE)
            half = 0.5 * (1.0 + lax.erf(v * (2.0**-0.5)))
            r.active[:, at] = (v * half).astype(BF16)
            r.slope[:, at] = (half + v * jnp.exp(-0.5 * v * v) * 0.3989422804014327).astype(BF16)

        product(r.xb[...], 8 + q, sink)
        r.activet[q * d : (q + 1) * d, :] = r.active[:, q * d : (q + 1) * d].T

    def contract(q):
        def sink(n, cols, v):
            r.branch[:, cols] = v if q == 0 else r.branch[:, cols] + v

        product(r.active[:, q * d : (q + 1) * d], 12 + q, sink)

    def finish():
        squares(3, r.branch[...])
        r.third[...] = r.second[...] + r.branch[...]
        squares(0, r.third[...])
        ok = lax.broadcasted_iota(jnp.int32, (rows, 1), 0) < r.tl[0]
        r.result[...] = jnp.where(ok, ln(r.third[...], 3), 0.0)

    def at(k):
        return k + 3

    tasks = {}

    def add(tick, *fs):
        tasks.setdefault(tick, []).extend(fs)

    add(0, start_counts, mem_start)
    add(2, norms_in, norm_one)
    for q in range(3):
        add(at(q), functools.partial(joint, q))
    add(at(2), self_attention)
    add(at(3), self_out)
    add(at(4), queries, q_start)
    add(at(5), q_forward, memory_part(0))
    add(at(6), memory_part(1), q_done, cross_a)
    add(at(7), cross_b)
    add(at(8), cross_c, cross_out)
    for q in range(4):
        add(at(8 + q), functools.partial(expand, q))
        add(at(12 + q), functools.partial(contract, q))
    add(at(15), finish)

    def drain():
        q_copy(me.fr, 0, me.xn).wait_send()
        q_copy(me.fr, 1, me.sib).wait_send()
        q_copy(fx, 2, me.sib).wait_send()
        for t, slot, device in ((fd, 0, me.sib), (fs, 1, me.sib), (fx, 2, me.xn)):
            for cp in o_copies(t, slot, device):
                cp.wait_send()

    return tasks, drain, (fx, fs, fd)


def ln_back(values, gain_row, grad):
    center = values - jnp.mean(values, axis=-1, keepdims=True)
    scale = lax.rsqrt(jnp.mean(center * center, axis=-1, keepdims=True) + 1e-05)
    unit = center * scale
    gain_grad = jnp.sum(grad * unit, axis=0, keepdims=True)
    shift_grad = jnp.sum(grad, axis=0, keepdims=True)
    lifted = grad * gain_row
    inner = jnp.mean(lifted * unit, axis=-1, keepdims=True)
    back = scale * (lifted - jnp.mean(lifted, axis=-1, keepdims=True) - unit * inner)
    return back, gain_grad, shift_grad


def backward(r, me, nz, fronts):
    rows, d = r.first.shape
    items, frames = r.kv.shape[:2]
    pairs = d // LANES
    depth = d // nz
    fx, fs, fd = fronts
    t = {}

    def cols(n):
        return pl.ds(pl.multiple_of(n * TILE, TILE), TILE)

    def weight_rows(k, zz):
        return r.wg[k, zz].reshape(depth, d)

    def grad_into(k, left, right):
        def body(n, carry):
            v = dot(left, right(cols(n))).astype(BF16)
            r.wg[k, :, :, :, :, :, cols(n)] = v.reshape(nz, 2, 2, 2, d // (8 * nz), TILE)
            return carry

        lax.fori_loop(0, d // TILE, body, 0)

    def through(k, grad, sink):
        def body(zz, carry):
            sink(zz, pl.ds(pl.multiple_of(zz * depth, depth), depth), dot_nt(grad, weight_rows(k, zz)))
            return carry

        lax.fori_loop(0, nz, body, 0)

    def ln_step(i, values, grad, first=False):
        back, gain, shift = ln_back(values, r.gs[i : i + 1, :], grad)
        r.gr[...] = back if first else r.gr[...] + back
        r.nrow[i : i + 1, :] = gain
        r.nrow[4 + i : 5 + i, :] = shift

    def start():
        pltpu.make_async_copy(r.cotangent, r.gr, r.own_sem.at[2]).wait()
        r.biast[...] = jnp.concatenate([r.bias[...], jnp.zeros((LANES - r.bias.shape[0], frames), F32)], axis=0).T
        for g in range(d // LANES):
            r.nrow[8:16, g * LANES : (g + 1) * LANES] = r.sq[...]
        ok = lax.broadcasted_iota(jnp.int32, (rows, 1), 0) < r.tl[0]
        ln_step(3, r.third[...], jnp.where(ok, r.gr[...], 0.0), True)
        r.xb[...] = r.gr[...].astype(BF16)
        pltpu.make_async_copy(r.tokens, r.third, r.own_sem.at[1]).start()

    def contract(q):
        def sink(zz, at, v):
            at = pl.ds(pl.multiple_of(q * d + zz * depth, depth), depth)
            r.active[:, at] = (v * r.slope[:, at].astype(F32)).astype(BF16)

        through(12 + q, r.xb[...], sink)
        grad_into(12 + q, r.activet[q * d : (q + 1) * d, :], lambda at: r.xb[:, at])

    def adder(fresh):
        def sink(zz, at, v):
            r.branch[:, at] = v if fresh else r.branch[:, at] + v

        return sink

    def expand(q):
        through(8 + q, r.active[:, q * d : (q + 1) * d], adder(q == 0))
        grad_into(8 + q, r.n3t[...], lambda at: r.active[:, pl.ds(pl.multiple_of(q * d + at.start, TILE), TILE)])

    def cross_out():
        ln_step(2, r.second[...], r.branch[...])
        r.xb[...] = r.gr[...].astype(BF16)

        def sink(zz, at, v):
            r.ga[me.fr, :, at] = v.astype(BF16)

        through(7, r.xb[...], sink)
        r.gl[me.fr, 0:16] = r.clse[0:16]

        def body(p, carry):
            left, right = row_dots(r.ga[me.fr, :, at128(p)], r.cmixt[at128(p), :])
            r.gl[me.fr, pl.ds(16 + 2 * p, 1), :] = left
            r.gl[me.fr, pl.ds(17 + 2 * p, 1), :] = right
            return carry

        lax.fori_loop(0, pairs, body, 0)

    def cross_out_grad():
        grad_into(7, r.cmixt[...], lambda at: r.xb[:, at])

    def row_dots(grad, mixt):
        prod = grad.astype(F32).T * mixt.astype(F32)
        return jnp.sum(prod[:HEAD_DIM], axis=0, keepdims=True), jnp.sum(prod[HEAD_DIM:], axis=0, keepdims=True)

    def g_copies(f, s, device):
        return (
            remote(r.ga.at[f], r.ga.at[f], r.g2_send.at[s], r.g2_recv.at[s], device),
            remote(r.gl.at[f], r.gl.at[f], r.g2_send.at[3 + s], r.g2_recv.at[3 + s], device),
        )

    def each(copies, what):
        for cp in copies:
            getattr(cp, what)()

    def g_start():
        each(g_copies(me.fr, 0, me.xn), "start")
        each(g_copies(me.fr, 1, me.sib), "start")

    def g_forward():
        each(g_copies(fx, 0, me.xn), "wait_recv")
        each(g_copies(fx, 2, me.sib), "start")

    def g_drain():
        each(g_copies(me.fr, 0, me.xn), "wait_send")
        each(g_copies(me.fr, 1, me.sib), "wait_send")
        each(g_copies(fx, 2, me.sib), "wait_send")

    scale = HEAD_DIM**-0.5

    def pair_back(q, k, v, g, hide, lse, dots):
        q2, g2 = two_heads(q * jnp.asarray(scale, BF16)), two_heads(g)
        probs = jnp.exp(hide(dot_nt(k, q2)) - lse)
        ds = (probs * (dot_nt(v, g2) - dots)).astype(BF16)
        dq = one_block(dot(ds.T, k)) * scale
        return dq, dot(ds, q2), dot(probs.astype(BF16), g2)

    def cross_item(f):
        lane = lax.broadcasted_iota(jnp.int32, (frames, LANES), 1)
        column = jnp.sum(jnp.where(lane == f, r.biast[...], 0.0), axis=-1, keepdims=True)

        def body(p, carry):
            stats = [
                jnp.concatenate([r.gl[f, pl.ds(b + 2 * p, 1), :], r.gl[f, pl.ds(b + 1 + 2 * p, 1), :]], axis=1)
                for b in (0, 16)
            ]
            dq, dk, dv = pair_back(
                r.qa[f, :, at128(p)],
                r.kv[f, :, at128(p)],
                r.kv[f, :, at128(p, d)],
                r.ga[f, :, at128(p)],
                lambda s: s + column,
                *stats,
            )
            r.op[f, :, at128(p)] = dq.astype(BF16)
            r.kv[f, :, at128(p)] = dk.astype(BF16)
            r.kv[f, :, at128(p, d)] = dv.astype(BF16)
            return carry

        lax.fori_loop(0, pairs, body, 0)

    def d_copy(f, slot, device):
        return remote(r.op.at[f], r.orv.at[slot], r.o2_send.at[slot], r.o2_recv.at[slot], device)

    def cross_one():
        cross_item(me.fr)

    def cross_two():
        each(g_copies(fs, 1, me.sib), "wait_recv")
        cross_item(fs)
        d_copy(fs, 1, me.sib).start()

    def cross_three():
        each(g_copies(fd, 2, me.sib), "wait_recv")
        cross_item(fd)
        d_copy(fd, 0, me.sib).start()

    def cross_four():
        cross_item(fx)
        d_copy(fd, 0, me.sib).wait_recv()
        r.op[fx] = (r.op[fx].astype(F32) + r.orv[0].astype(F32)).astype(BF16)
        d_copy(fx, 2, me.xn).start()

    def tile_copy(i, f, zz):
        return pltpu.make_async_copy(
            r.mst.at[i, 0 : r.memory_grad.shape[1]],
            r.memory_grad.at[f, :, pl.ds(pl.multiple_of(zz * depth, depth), depth)],
            r.t_sem.at[i],
        )

    def memory_grad(half):
        def body(n, carry):
            f, pair = lax.div(n, nz // 2), lax.rem(n, nz // 2)
            for i in range(2):
                zz = 2 * pair + i

                @pl.when(n > half * items * nz // 4)
                def _():
                    tile_copy(i, f, zz).wait()

                v = dot_nt(r.kv[f, :, 0:d], weight_rows(5, zz)) + dot_nt(r.kv[f, :, d : 2 * d], weight_rows(6, zz))
                r.mst[i] = v
                tile_copy(i, f, zz).start()
            return carry

        count = items * nz // 4
        lax.fori_loop(half * count, (half + 1) * count, body, 0)
        for i in range(2):
            tile_copy(i, 0, i).wait()

    def memory_weights(which):
        grad_into(
            5 + which,
            r.memt[...],
            lambda at: r.kv[:, :, pl.ds(pl.multiple_of(which * d + at.start, TILE), TILE)].reshape(items * frames, TILE),
        )

    def query():
        d_copy(fs, 1, me.sib).wait_recv()
        d_copy(fx, 2, me.xn).wait_recv()
        r.xb[...] = (r.op[me.fr].astype(F32) + r.orv[1].astype(F32) + r.orv[2].astype(F32)).astype(BF16)
        through(4, r.xb[...], adder(True))
        grad_into(4, r.n2t[...], lambda at: r.xb[:, at])

    def d_drain():
        for f, slot, device in ((fd, 0, me.sib), (fs, 1, me.sib), (fx, 2, me.xn)):
            d_copy(f, slot, device).wait_send()

    def self_out():
        ln_step(1, r.first[...], r.branch[...])
        r.xb[...] = r.gr[...].astype(BF16)

        def sink(zz, at, v):
            r.ga[me.fr, :, at] = v.astype(BF16)

        through(3, r.xb[...], sink)
        grad_into(3, r.smixt[...], lambda at: r.xb[:, at])

    def self_attention():
        key = lax.broadcasted_iota(jnp.int32, (rows, 2 * rows), 0)
        causal = key <= lax.rem(lax.broadcasted_iota(jnp.int32, (rows, 2 * rows), 1), rows)

        def body(p, carry):
            g = r.ga[me.fr, :, at128(p)]
            lse = jnp.concatenate([r.slse[pl.ds(2 * p, 1), :], r.slse[pl.ds(2 * p + 1, 1), :]], axis=1)
            dots = jnp.concatenate(row_dots(g, r.smixt[at128(p), :]), axis=1)
            dq, dk, dv = pair_back(
                r.joint[:, at128(p)],
                r.joint[:, at128(p, d)],
                r.joint[:, at128(p, 2 * d)],
                g,
                lambda s: jnp.where(causal, s, -1e30),
                lse,
                dots,
            )
            r.joint[:, at128(p)] = dq.astype(BF16)
            r.joint[:, at128(p, d)] = dk.astype(BF16)
            r.joint[:, at128(p, 2 * d)] = dv.astype(BF16)
            return carry

        lax.fori_loop(0, pairs, body, 0)

    def project(q):
        through(q, r.joint[:, q * d : (q + 1) * d], adder(q == 0))
        grad_into(q, r.n1t[...], lambda at: r.joint[:, pl.ds(pl.multiple_of(q * d + at.start, TILE), TILE)])

    def finish():
        pltpu.make_async_copy(r.tokens, r.third, r.own_sem.at[1]).wait()
        ln_step(0, r.third[...], r.branch[...])
        pltpu.make_async_copy(r.gr, r.tokens_grad, r.own_sem.at[2]).start()
        for g in range(d // LANES):
            for f in range(4):
                r.nw[g // 2, g % 2, f // 2, f % 2] = r.nrow[:, g * LANES : (g + 1) * LANES]

    def close():
        pltpu.make_async_copy(r.gr, r.tokens_grad, r.own_sem.at[2]).wait()

    return SimpleNamespace(**{k: v for k, v in locals().items() if callable(v)})


GRAD_ORDER = (12, 13, 14, 15, 8, 9, 10, 11, 7, 5, 6, 4, 3, 0, 1, 2)
SLOTS = 2


def run(r, nz, chunks):
    me = place()
    own = pltpu.make_async_copy(r.shards, r.wg.at[:, me.z, me.y, me.x, me.c], r.own_sem.at[0])
    own.start()
    pltpu.make_async_copy(r.tokens, r.first, r.own_sem.at[1]).start()
    pltpu.make_async_copy(r.cotangent, r.gr, r.own_sem.at[2]).start()
    r.ng[me.z, me.y, me.x, me.c] = r.norms[...]
    barrier = pltpu.get_barrier_semaphore()
    peers = [me.xn, me.yn, me.sib, me.diag]
    peers += [me.dev(lax.rem(me.z + dz, nz), me.y, me.x, me.c) for dz in range(1, nz)]
    for device in peers:
        pl.semaphore_signal(barrier, inc=1, device_id=device, device_id_type=MESH)
    pl.semaphore_wait(barrier, len(peers))
    norm = gather_steps(me, r.ng, r.g_send.at[chunks], r.g_recv.at[chunks], nz)
    steps = [gather_steps(me, r.wg.at[k], r.g_send.at[k], r.g_recv.at[k], nz) for k in range(chunks)]
    norm.z()
    own.wait()
    steps[0].z()
    steps[1].z()
    norm.near()
    norm.far()
    norm.last()
    tasks, drain, fronts = forward(r, me, nz)
    for tick in range(chunks + 3):
        if tick + 2 < chunks:
            steps[tick + 2].z()
        if tick < chunks:
            steps[tick].near()
        if 0 <= tick - 1 < chunks:
            steps[tick - 1].far()
        if 0 <= tick - 2 < chunks:
            steps[tick - 2].last()
        if 0 <= tick - 3 < chunks:
            steps[tick - 3].done()
        if tick == 1:
            norm.done()
        for task in tasks.get(tick, ()):
            task()
    drain()
    norm.drain()
    for s in steps:
        s.drain()

    b = backward(r, me, nz, fronts)

    def out_copy(turn):
        return pltpu.make_async_copy(r.ost.at[turn % 2], r.grads.at[GRAD_ORDER[turn]], r.e_sem.at[turn % 2])

    def keep(turn):
        def sink(total):
            if turn >= 2:
                out_copy(turn - 2).wait()
            r.ost[turn % 2] = total
            out_copy(turn).start()

        return sink

    def keep_norms(total):
        r.norm_out[...] = total

    boxes = (r.rc, r.y1, r.x1, r.x2, r.y2, r.zs)
    adds = [
        scatter_steps(me, r.wg.at[k], boxes, r.s_send.at[m], r.s_recv.at[m], r.credit, nz, m, SLOTS, chunks, keep(m))
        for m, k in enumerate(GRAD_ORDER)
    ]
    norm_boxes = (r.nrc, r.ny1, r.nx1, r.nx2, r.ny2, r.nzs)
    adds.append(
        scatter_steps(me, r.nw, norm_boxes, r.s_send.at[chunks], r.s_recv.at[chunks], r.credit, nz, 0, 1, 1, keep_norms)
    )
    part = functools.partial
    work = {
        -1: [b.start, part(b.contract, 0)],
        0: [part(b.contract, 1)],
        1: [part(b.contract, 2), part(b.contract, 3)],
        2: [part(b.expand, 0), part(b.expand, 1)],
        3: [part(b.expand, 2), part(b.expand, 3)],
        4: [b.cross_out, b.g_start, b.cross_out_grad, b.cross_one],
        5: [b.g_forward, b.cross_two, b.cross_three],
        6: [b.cross_four, b.g_drain, part(b.memory_grad, 0)],
        7: [part(b.memory_grad, 1), part(b.memory_weights, 0)],
        8: [part(b.memory_weights, 1), b.query],
        9: [b.d_drain, b.self_out],
        10: [b.self_attention, part(b.project, 0)],
        11: [part(b.project, 1), part(b.project, 2)],
        12: [b.finish],
    }
    extra = chunks + 1
    for tick in range(-1, extra + 3):
        for task in work.get(tick, ()):
            task()
        if tick + 1 < extra:
            adds[tick + 1].a()
        if 0 <= tick < extra:
            adds[tick].b()
        if 0 <= tick - 1 < extra:
            adds[tick - 1].c()
        if 0 <= tick - 2 < extra:
            adds[tick - 2].d()
        if 0 <= tick - 3 < extra:
            adds[tick - 3].e()
    b.close()
    out_copy(chunks - 2).wait()
    out_copy(chunks - 1).wait()
    for s in adds:
        s.drain()


VMEM_BYTES = 127 * 2**19


def fused(nz, chunks, frame_count, tl, tokens, cotangent, memory, shards, norms, bias):
    rows, d = tokens.shape
    items, parts = memory.shape[0], memory.shape[1]
    slab = shards.shape[1]
    padded = parts * 4 * slab
    half = slab // 2
    outs = dict(
        result=((rows, d), F32, pltpu.VMEM),
        tokens_grad=((rows, d), F32, pl.ANY),
        memory_grad=((items, frame_count, d), F32, pl.ANY),
        grads=((chunks, slab, d), F32, pl.ANY),
        norm_out=((16, LANES), F32, pltpu.VMEM),
    )
    vm = pltpu.VMEM
    dma = pltpu.SemaphoreType.DMA
    scratch = dict(
        wg=vm((chunks, nz, 2, 2, 2, slab, d), BF16),
        ng=vm((nz, 2, 2, 2, 32, LANES), BF16),
        gs=vm((16, d), F32),
        n1t=vm((d, rows), BF16),
        joint=vm((rows, 3 * d), BF16),
        smixt=vm((d, rows), BF16),
        slse=vm((LANES, LANES), F32),
        first=vm((rows, d), F32),
        n2t=vm((d, rows), BF16),
        qa=vm((items, rows, d), BF16),
        kv=vm((items, padded, 2 * d), BF16),
        memt=vm((d, items * padded), BF16),
        clse=vm((LANES, LANES), F32),
        second=vm((rows, d), F32),
        n3t=vm((d, rows), BF16),
        activet=vm((4 * d, rows), BF16),
        active=vm((rows, 4 * d), BF16),
        slope=vm((rows, 4 * d), BF16),
        third=vm((rows, d), F32),
        sq=vm((8, LANES), F32),
        xb=vm((rows, d), BF16),
        branch=vm((rows, d), F32),
        op=vm((items, rows, d), BF16),
        opl=vm((items, LANES, LANES), F32),
        orv=vm((3, rows, d), BF16),
        orl=vm((3, LANES, LANES), F32),
        wcol=vm((LANES, LANES), F32),
        cmixt=vm((d, rows), BF16),
        gr=vm((rows, d), F32),
        ga=vm((items, rows, d), BF16),
        gl=vm((items, 32, LANES), F32),
        nrow=vm((16, d), F32),
        biast=vm((padded, LANES), F32),
        mst=vm((2, padded, d // nz), F32),
        ost=vm((2, slab, d), F32),
        nw=vm((nz, 2, 2, 2, 16, LANES), F32),
        rc=vm((SLOTS, nz, 2, 2, slab, d), BF16),
        y1=vm((SLOTS, nz, 2, half, d), BF16),
        x1=vm((SLOTS, nz, 2, half, d), BF16),
        x2=vm((SLOTS, nz, half, d), BF16),
        y2=vm((SLOTS, nz, half, d), BF16),
        zs=vm((SLOTS, nz - 1, slab, d), BF16),
        nrc=vm((1, nz, 2, 2, 16, LANES), F32),
        ny1=vm((1, nz, 2, 8, LANES), F32),
        nx1=vm((1, nz, 2, 8, LANES), F32),
        nx2=vm((1, nz, 8, LANES), F32),
        ny2=vm((1, nz, 8, LANES), F32),
        nzs=vm((1, nz - 1, 16, LANES), F32),
        own_sem=dma((3,)),
        m_sem=dma((2,)),
        t_sem=dma((2,)),
        e_sem=dma((2,)),
        g_send=dma((chunks + 1, nz + 7)),
        g_recv=dma((chunks + 1, nz + 7)),
        s_send=dma((chunks + 1, nz + 4)),
        s_recv=dma((chunks + 1, nz + 4)),
        credit=pltpu.SemaphoreType.REGULAR((nz + 4,)),
        q_send=dma((3,)),
        q_recv=dma((3,)),
        o_send=dma((6,)),
        o_recv=dma((6,)),
        g2_send=dma((6,)),
        g2_recv=dma((6,)),
        o2_send=dma((3,)),
        o2_recv=dma((3,)),
    )
    ins = ["tl", "tokens", "cotangent", "memory", "shards", "norms", "bias"]
    names = ins + list(outs) + list(scratch)

    def kernel(*refs):
        run(SimpleNamespace(**dict(zip(names, refs))), nz, chunks)

    def at(space):
        return pl.BlockSpec(memory_space=space)

    res = pl.pallas_call(
        kernel,
        out_shape=[jax.ShapeDtypeStruct(s, t) for s, t, _ in outs.values()],
        in_specs=[at(s) for s in (pltpu.SMEM, pl.ANY, pl.ANY, pl.ANY, pl.ANY, pltpu.VMEM, pltpu.VMEM)],
        out_specs=[at(s) for _, _, s in outs.values()],
        scratch_shapes=list(scratch.values()),
        compiler_params=pltpu.CompilerParams(collective_id=0, has_side_effects=True, vmem_limit_bytes=VMEM_BYTES),
    )(tl, tokens, cotangent, memory, shards, norms, bias)
    return dict(zip(outs, res))


CHUNKS = 16
Z_CHIPS = 4


def pack_weights(weights):
    self_project, self_output, cross_query, cross_memory, cross_output, expand, contract = weights
    slab, d = self_output.shape
    devices = d // slab
    blocks = contract.shape[0] // slab

    def cut(w):
        return jnp.transpose(w.reshape(slab, -1, d), (1, 0, 2))

    wide = jnp.transpose(expand.reshape(slab, devices, blocks, slab), (2, 0, 1, 3)).reshape(blocks, slab, d)
    return jnp.concatenate(
        [cut(w) for w in (self_project, self_output, cross_query, cross_memory, cross_output)]
        + [wide, contract.reshape(blocks, slab, d)],
        axis=0,
    )


def pack_norms(gains, shifts):
    own = jnp.concatenate([gains, shifts], axis=0)
    lane = lax.axis_index("frames") * own.shape[1]
    return lax.dynamic_update_slice(jnp.zeros((32, LANES), BF16), own, (0, lane))


def frame_bias(cross_mask, memory_length, frame_count, padded):
    start = lax.axis_index("frames") * frame_count
    at = start + jnp.arange(frame_count)
    mask = lax.dynamic_slice_in_dim(cross_mask, start, frame_count, 1)
    ok = (at[None] < memory_length[:, None]) & ((mask == 1) | (at[None] == 0))
    bias = jnp.where(ok, 0.0, -1e30).astype(F32)
    return jnp.pad(bias, ((0, 8 - bias.shape[0]), (0, padded - frame_count)), constant_values=-1e30)


def local_fused(
    tokens,
    memory,
    cotangent,
    self_project,
    self_output,
    cross_query,
    cross_memory,
    cross_output,
    expand,
    contract,
    norm_gains,
    norm_shifts,
    target_length,
    memory_length,
    cross_mask,
):
    items, frame_count, d = memory.shape
    slab = self_output.shape[0]
    group = 4 * slab
    parts = -(-frame_count // group)
    padded = parts * group
    rolled = jnp.pad(memory, ((0, 0), (0, padded - frame_count), (0, 0))).reshape(items, parts, 2, 2, slab, d)
    weights = (self_project, self_output, cross_query, cross_memory, cross_output, expand, contract)
    o = fused(
        Z_CHIPS,
        CHUNKS,
        frame_count,
        target_length,
        tokens[0],
        cotangent[0],
        rolled,
        pack_weights(weights),
        pack_norms(norm_gains, norm_shifts),
        frame_bias(cross_mask, memory_length, frame_count, padded),
    )
    g = o["grads"]
    blocks = contract.shape[0] // slab

    def side(lo, hi):
        return jnp.concatenate([g[k] for k in range(lo, hi)], axis=1)

    wide = g[8:12].reshape(blocks, slab, d // slab, slab)
    expand_grad = jnp.transpose(wide, (1, 2, 0, 3)).reshape(slab, blocks * d)
    n = o["norm_out"]
    width = norm_gains.shape[1]
    mine = lax.dynamic_slice_in_dim(n, lax.axis_index("frames") * width, width, 1)
    counts = n[8:13, 0]
    branch_rms = jnp.sqrt(counts[:4] / (counts[4] * d))
    return (
        o["result"][None],
        o["tokens_grad"][None],
        o["memory_grad"],
        side(0, 3),
        g[3],
        g[4],
        side(5, 7),
        g[7],
        expand_grad,
        g[12:16].reshape(blocks * slab, d),
        mine[0:4],
        mine[4:8],
        branch_rms,
    )


block_heads = 4


def layer_norm(values, gain_row, shift_row):
    center = values - jnp.mean(values, axis=-1, keepdims=True)
    spread = jnp.mean(center * center, axis=-1, keepdims=True)
    return center * lax.rsqrt(spread + 1e-05) * gain_row + shift_row


def exact_gelu(values):
    return jax.nn.gelu(values, approximate=False)


def matmul(left_side, right_side):
    return jnp.dot(left_side, right_side, preferred_element_type=jnp.float32)


def split_heads(rows):
    return rows.reshape(rows.shape[:-1] + (rows.shape[-1] // HEAD_DIM, HEAD_DIM))


def to_blocks(rows):
    row_count, head_count, head_width = rows.shape
    return rows.reshape(row_count, head_count // block_heads, block_heads, head_width).transpose(
        1, 0, 2, 3
    )


def from_blocks(blocks):
    group_count, row_count, head_count, head_width = blocks.shape
    return blocks.transpose(1, 0, 2, 3).reshape(row_count, group_count * head_count * head_width)


def block_scores(query_block, key_block, allowed):
    factor = query_block.shape[-1] ** (-0.5)
    raw_scores = (
        jnp.einsum("shd,fhd->hsf", query_block, key_block, preferred_element_type=jnp.float32)
        * factor
    )
    return jnp.where(allowed[None], raw_scores, -1e30)


def block_probs(query_block, key_block, allowed, max_block, total_block):
    scores = block_scores(query_block, key_block, allowed)
    shifted = jnp.where(allowed[None], jnp.exp(scores - max_block[..., None]), 0.0)
    return shifted / total_block[..., None]


def block_grads(query_block, key_block, grad_block, probs, grad_probs, row_dot):
    factor = query_block.shape[-1] ** (-0.5)
    score_grad = (probs * (grad_probs - row_dot)).astype(jnp.bfloat16)
    query_grad = (
        jnp.einsum("hsf,fhd->shd", score_grad, key_block, preferred_element_type=jnp.float32)
        * factor
    )
    key_grad = (
        jnp.einsum("hsf,shd->fhd", score_grad, query_block, preferred_element_type=jnp.float32)
        * factor
    )
    value_grad = jnp.einsum(
        "hsf,shd->fhd", probs.astype(jnp.bfloat16), grad_block, preferred_element_type=jnp.float32
    )
    return (query_grad, key_grad, value_grad)


def attend_whole(query_rows, key_rows, value_rows, allowed):

    def one_group(blocks):
        query_block, key_block, value_block = blocks
        scores = block_scores(query_block, key_block, allowed)
        max_block = jnp.max(scores, axis=-1)
        shifted = jnp.where(allowed[None], jnp.exp(scores - max_block[..., None]), 0.0)
        total_block = jnp.sum(shifted, axis=-1)
        weights = (shifted / total_block[..., None]).astype(jnp.bfloat16)
        mixture = jnp.einsum(
            "hsf,fhd->shd", weights, value_block, preferred_element_type=jnp.float32
        )
        return (mixture, max_block, total_block)

    mixture, row_max, totals = lax.map(
        one_group, (to_blocks(query_rows), to_blocks(key_rows), to_blocks(value_rows))
    )
    return (from_blocks(mixture), row_max, totals)


def attend_whole_back(query_rows, key_rows, value_rows, allowed, grad_rows, row_max, totals):

    def one_group(blocks):
        query_block, key_block, value_block, grad_block, max_block, total_block = blocks
        probs = block_probs(query_block, key_block, allowed, max_block, total_block)
        grad_probs = jnp.einsum(
            "shd,fhd->hsf", grad_block, value_block, preferred_element_type=jnp.float32
        )
        row_dot = jnp.sum(probs * grad_probs, axis=-1, keepdims=True)
        return block_grads(query_block, key_block, grad_block, probs, grad_probs, row_dot)

    query_grad, key_grad, value_grad = lax.map(
        one_group,
        (
            to_blocks(query_rows),
            to_blocks(key_rows),
            to_blocks(value_rows),
            to_blocks(grad_rows),
            row_max,
            totals,
        ),
    )
    return (from_blocks(query_grad), from_blocks(key_grad), from_blocks(value_grad))


def cross_stats(query_rows, key_rows, allowed):

    def one_group(blocks):
        query_block, key_block = blocks
        scores = block_scores(query_block, key_block, allowed)
        max_block = jnp.max(scores, axis=-1)
        total_block = jnp.sum(
            jnp.where(allowed[None], jnp.exp(scores - max_block[..., None]), 0.0), axis=-1
        )
        return (max_block, total_block)

    return lax.map(one_group, (to_blocks(query_rows), to_blocks(key_rows)))


def cross_partial(query_rows, key_rows, value_rows, allowed, row_max, totals):

    def one_group(blocks):
        query_block, key_block, value_block, max_block, total_block = blocks
        probs = block_probs(query_block, key_block, allowed, max_block, total_block)
        return jnp.einsum(
            "hsf,fhd->shd",
            probs.astype(jnp.bfloat16),
            value_block,
            preferred_element_type=jnp.float32,
        )

    return from_blocks(
        lax.map(
            one_group,
            (to_blocks(query_rows), to_blocks(key_rows), to_blocks(value_rows), row_max, totals),
        )
    )


def cross_row_dot(query_rows, key_rows, value_rows, allowed, grad_rows, row_max, totals):

    def one_group(blocks):
        query_block, key_block, value_block, grad_block, max_block, total_block = blocks
        probs = block_probs(query_block, key_block, allowed, max_block, total_block)
        grad_probs = jnp.einsum(
            "shd,fhd->hsf", grad_block, value_block, preferred_element_type=jnp.float32
        )
        return jnp.sum(probs * grad_probs, axis=-1)

    return lax.map(
        one_group,
        (
            to_blocks(query_rows),
            to_blocks(key_rows),
            to_blocks(value_rows),
            to_blocks(grad_rows),
            row_max,
            totals,
        ),
    )


def cross_partial_grads(
    query_rows, key_rows, value_rows, allowed, grad_rows, row_max, totals, row_dot
):

    def one_group(blocks):
        query_block, key_block, value_block, grad_block, max_block, total_block, dot_block = blocks
        probs = block_probs(query_block, key_block, allowed, max_block, total_block)
        grad_probs = jnp.einsum(
            "shd,fhd->hsf", grad_block, value_block, preferred_element_type=jnp.float32
        )
        return block_grads(
            query_block, key_block, grad_block, probs, grad_probs, dot_block[..., None]
        )

    query_grad, key_grad, value_grad = lax.map(
        one_group,
        (
            to_blocks(query_rows),
            to_blocks(key_rows),
            to_blocks(value_rows),
            to_blocks(grad_rows),
            row_max,
            totals,
            row_dot,
        ),
    )
    return (from_blocks(query_grad), from_blocks(key_grad), from_blocks(value_grad))


def local(
    tokens,
    memory,
    cotangent,
    self_project,
    self_output,
    cross_query,
    cross_memory,
    cross_output,
    expand,
    contract,
    norm_gains,
    norm_shifts,
    target_length,
    memory_length,
    cross_mask,
):
    gathered = (
        lax.all_gather(self_project, ("dp", "frames"), axis=0, tiled=True),
        lax.all_gather(self_output, ("dp", "frames"), axis=0, tiled=True),
        lax.all_gather(cross_query, ("dp", "frames"), axis=0, tiled=True),
        lax.all_gather(cross_memory, ("dp", "frames"), axis=0, tiled=True),
        lax.all_gather(cross_output, ("dp", "frames"), axis=0, tiled=True),
        lax.all_gather(expand, ("dp", "frames"), axis=0, tiled=True),
        lax.all_gather(contract, ("dp", "frames"), axis=0, tiled=True),
        lax.all_gather(norm_gains, ("dp", "frames"), axis=1, tiled=True),
        lax.all_gather(norm_shifts, ("dp", "frames"), axis=1, tiled=True),
    )
    (
        w_self,
        w_self_out,
        w_query,
        w_memory,
        w_cross_out,
        w_expand,
        w_contract,
        gains_low,
        shifts_low,
    ) = gathered
    gains = gains_low.astype(jnp.float32)
    shifts = shifts_low.astype(jnp.float32)
    model_width = w_self_out.shape[0]
    residual_in = tokens[0]
    length = residual_in.shape[0]
    positions = jnp.arange(length)
    row_valid = positions < target_length[0]
    causal = positions[:, None] >= positions[None, :]
    item_count = memory.shape[0]
    frame_count = memory.shape[1]
    own_item = lax.axis_index("frames")
    normed_one_f, back_one = jax.vjp(layer_norm, residual_in, gains[0], shifts[0])
    normed_one = normed_one_f.astype(jnp.bfloat16)
    joint_rows = matmul(normed_one, w_self).astype(jnp.bfloat16)
    self_queries = split_heads(joint_rows[:, :model_width])
    self_keys = split_heads(joint_rows[:, model_width : 2 * model_width])
    self_values = split_heads(joint_rows[:, 2 * model_width :])
    self_mix, self_max, self_totals = attend_whole(self_queries, self_keys, self_values, causal)
    self_mix_low = self_mix.astype(jnp.bfloat16)
    self_branch = matmul(self_mix_low, w_self_out)
    first_sum = residual_in + self_branch
    normed_two_f, back_two = jax.vjp(layer_norm, first_sum, gains[1], shifts[1])
    normed_two = normed_two_f.astype(jnp.bfloat16)
    cross_queries = matmul(normed_two, w_query).astype(jnp.bfloat16)
    every_query = lax.all_gather(cross_queries[None], "frames", axis=0, tiled=True)
    query_heads = split_heads(every_query)
    frame_start = own_item * frame_count
    local_frames = frame_start + jnp.arange(frame_count)
    local_mask = lax.dynamic_slice_in_dim(cross_mask, frame_start, frame_count, 1)
    frame_ok = (local_frames[None, :] < memory_length[:, None]) & (
        (local_mask == 1) | (local_frames[None, :] == 0)
    )
    memory_rows = matmul(memory.reshape(item_count * frame_count, model_width), w_memory).astype(
        jnp.bfloat16
    )
    memory_rows = memory_rows.reshape(item_count, frame_count, 2 * model_width)
    memory_keys = split_heads(memory_rows[..., :model_width])
    memory_values = split_heads(memory_rows[..., model_width:])

    def item_stats(inputs):
        query_item, key_item, frame_item = inputs
        return cross_stats(
            query_item, key_item, jnp.broadcast_to(frame_item[None, :], (length, frame_count))
        )

    local_max, local_totals = lax.map(item_stats, (query_heads, memory_keys, frame_ok))
    cross_max = lax.pmax(local_max.astype(jnp.bfloat16), "frames").astype(local_max.dtype)
    cross_totals = lax.psum(
        (local_totals * jnp.exp(local_max - cross_max)).astype(jnp.bfloat16), "frames"
    ).astype(jnp.float32)

    def item_partial(inputs):
        query_item, key_item, value_item, frame_item, max_item, total_item = inputs
        allowed = jnp.broadcast_to(frame_item[None, :], (length, frame_count))
        return cross_partial(query_item, key_item, value_item, allowed, max_item, total_item)

    partial_mix = lax.map(
        item_partial, (query_heads, memory_keys, memory_values, frame_ok, cross_max, cross_totals)
    )
    cross_mix = lax.psum_scatter(
        partial_mix.astype(jnp.bfloat16), "frames", scatter_dimension=0, tiled=True
    ).astype(jnp.float32)[0]
    cross_mix_low = cross_mix.astype(jnp.bfloat16)
    cross_branch = matmul(cross_mix_low, w_cross_out)
    second_sum = first_sum + cross_branch
    normed_three_f, back_three = jax.vjp(layer_norm, second_sum, gains[2], shifts[2])
    normed_three = normed_three_f.astype(jnp.bfloat16)
    hidden = matmul(normed_three, w_expand)
    active_f, gelu_back = jax.vjp(exact_gelu, hidden)
    active = active_f.astype(jnp.bfloat16)
    feed_branch = matmul(active, w_contract)
    third_sum = second_sum + feed_branch
    final_rows, back_final = jax.vjp(layer_norm, third_sum, gains[3], shifts[3])
    result = jnp.where(row_valid[:, None], final_rows, 0.0)
    row_weight = row_valid.astype(jnp.float32)[:, None]
    squares = jnp.stack(
        [
            jnp.sum(row_weight * member * member)
            for member in (third_sum, self_branch, cross_branch, feed_branch)
        ]
    )
    squares_all, counted = lax.psum((squares, jnp.sum(row_weight)), ("dp", "frames"))
    branch_rms = jnp.sqrt(squares_all / (counted * model_width))
    grad_result = jnp.where(row_valid[:, None], cotangent[0], 0.0)
    grad_third, gain_grad_three, shift_grad_three = back_final(grad_result)
    feed_low = grad_third.astype(jnp.bfloat16)
    contract_grad = matmul(active.T, feed_low)
    grad_active = matmul(feed_low, w_contract.T)
    grad_hidden = gelu_back(grad_active)[0].astype(jnp.bfloat16)
    expand_grad = matmul(normed_three.T, grad_hidden)
    grad_normed_three = matmul(grad_hidden, w_expand.T)
    grad_second_part, gain_grad_two, shift_grad_two = back_three(grad_normed_three)
    grad_second = grad_third + grad_second_part
    cross_low = grad_second.astype(jnp.bfloat16)
    cross_output_grad = matmul(cross_mix_low.T, cross_low)
    grad_cross_mix = matmul(cross_low, w_cross_out.T).astype(jnp.bfloat16)
    every_grad = split_heads(lax.all_gather(grad_cross_mix[None], "frames", axis=0, tiled=True))

    def item_dot(inputs):
        query_item, key_item, value_item, frame_item, grad_item, max_item, total_item = inputs
        allowed = jnp.broadcast_to(frame_item[None, :], (length, frame_count))
        return cross_row_dot(
            query_item, key_item, value_item, allowed, grad_item, max_item, total_item
        )

    local_dot = lax.map(
        item_dot,
        (query_heads, memory_keys, memory_values, frame_ok, every_grad, cross_max, cross_totals),
    )
    row_dot = lax.psum(local_dot.astype(jnp.bfloat16), "frames").astype(jnp.float32)

    def item_grads(inputs):
        query_item, key_item, value_item, frame_item, grad_item, max_item, total_item, dot_item = (
            inputs
        )
        allowed = jnp.broadcast_to(frame_item[None, :], (length, frame_count))
        return cross_partial_grads(
            query_item, key_item, value_item, allowed, grad_item, max_item, total_item, dot_item
        )

    query_parts, key_parts, value_parts = lax.map(
        item_grads,
        (
            query_heads,
            memory_keys,
            memory_values,
            frame_ok,
            every_grad,
            cross_max,
            cross_totals,
            row_dot,
        ),
    )
    query_grad = lax.psum_scatter(
        query_parts.astype(jnp.bfloat16), "frames", scatter_dimension=0, tiled=True
    ).astype(jnp.float32)[0]
    memory_low = (
        jnp.concatenate([key_parts, value_parts], axis=2)
        .astype(jnp.bfloat16)
        .reshape(item_count * frame_count, 2 * model_width)
    )
    cross_memory_grad = matmul(memory.reshape(item_count * frame_count, model_width).T, memory_low)
    memory_grad = matmul(memory_low, w_memory.T).reshape(item_count, frame_count, model_width)
    query_low = query_grad.astype(jnp.bfloat16)
    cross_query_grad = matmul(normed_two.T, query_low)
    grad_normed_two = matmul(query_low, w_query.T)
    grad_first_part, gain_grad_one, shift_grad_one = back_two(grad_normed_two)
    grad_first = grad_second + grad_first_part
    self_low = grad_first.astype(jnp.bfloat16)
    self_output_grad = matmul(self_mix_low.T, self_low)
    grad_self_mix = matmul(self_low, w_self_out.T).astype(jnp.bfloat16)
    self_query_grad, self_key_grad, self_value_grad = attend_whole_back(
        self_queries,
        self_keys,
        self_values,
        causal,
        split_heads(grad_self_mix),
        self_max,
        self_totals,
    )
    joint_grad = jnp.concatenate([self_query_grad, self_key_grad, self_value_grad], axis=1).astype(
        jnp.bfloat16
    )
    self_project_grad = matmul(normed_one.T, joint_grad)
    grad_normed_one = matmul(joint_grad, w_self.T)
    grad_input_part, gain_grad_zero, shift_grad_zero = back_one(grad_normed_one)
    tokens_grad = grad_first + grad_input_part
    gain_grads = jnp.stack([gain_grad_zero, gain_grad_one, gain_grad_two, gain_grad_three])
    shift_grads = jnp.stack([shift_grad_zero, shift_grad_one, shift_grad_two, shift_grad_three])
    reduced = (
        lax.psum_scatter(self_project_grad, ("dp", "frames"), scatter_dimension=0, tiled=True),
        lax.psum_scatter(self_output_grad, ("dp", "frames"), scatter_dimension=0, tiled=True),
        lax.psum_scatter(cross_query_grad, ("dp", "frames"), scatter_dimension=0, tiled=True),
        lax.psum_scatter(cross_memory_grad, ("dp", "frames"), scatter_dimension=0, tiled=True),
        lax.psum_scatter(cross_output_grad, ("dp", "frames"), scatter_dimension=0, tiled=True),
        lax.psum_scatter(expand_grad, ("dp", "frames"), scatter_dimension=0, tiled=True),
        lax.psum_scatter(contract_grad, ("dp", "frames"), scatter_dimension=0, tiled=True),
        lax.psum_scatter(gain_grads, ("dp", "frames"), scatter_dimension=1, tiled=True),
        lax.psum_scatter(shift_grads, ("dp", "frames"), scatter_dimension=1, tiled=True),
    )
    (
        project_part,
        output_part,
        query_part,
        memory_part,
        cross_out_part,
        expand_part,
        contract_part,
        gains_part,
        shifts_part,
    ) = reduced
    return (
        result[None],
        tokens_grad[None],
        memory_grad,
        project_part,
        output_part,
        query_part,
        memory_part,
        cross_out_part,
        expand_part,
        contract_part,
        gains_part,
        shifts_part,
        branch_rms,
    )


def solution(mesh):
    fits = (mesh.shape["dp"], mesh.shape["frames"]) == (2 * Z_CHIPS, 4)
    return jax.shard_map(
        local_fused if fits else local,
        mesh=mesh,
        in_specs=(
            P(("dp", "frames"), None, None),
            P("dp", "frames", None),
            P(("dp", "frames"), None, None),
            P(("dp", "frames"), None),
            P(("dp", "frames"), None),
            P(("dp", "frames"), None),
            P(("dp", "frames"), None),
            P(("dp", "frames"), None),
            P(("dp", "frames"), None),
            P(("dp", "frames"), None),
            P(None, ("dp", "frames")),
            P(None, ("dp", "frames")),
            P(("dp", "frames")),
            P("dp"),
            P("dp", None),
        ),
        out_specs=(
            P(("dp", "frames"), None, None),
            P(("dp", "frames"), None, None),
            P("dp", "frames", None),
            P(("dp", "frames"), None),
            P(("dp", "frames"), None),
            P(("dp", "frames"), None),
            P(("dp", "frames"), None),
            P(("dp", "frames"), None),
            P(("dp", "frames"), None),
            P(("dp", "frames"), None),
            P(None, ("dp", "frames")),
            P(None, ("dp", "frames")),
            P(),
        ),
        check_vma=False,
    )
```

```python
import functools
from types import SimpleNamespace

import jax
import jax.numpy as jnp
from jax import lax
from jax.experimental import pallas as pl
from jax.experimental.pallas import tpu as pltpu
from jax.sharding import PartitionSpec as P

MESH = pl.DeviceIdType.MESH
F32 = jnp.float32
BF16 = jnp.bfloat16
HEAD_DIM = 64
LANES = 128
WIDE = 512


def dot(a, b):
    return jnp.dot(a, b, preferred_element_type=F32)


def dot_nt(a, b):
    return lax.dot_general(a, b, (((1,), (1,)), ((), ())), preferred_element_type=F32)


def place():
    dp, fr = lax.axis_index("dp"), lax.axis_index("frames")
    z, y = lax.div(dp, 2), lax.rem(dp, 2)
    x, c = lax.div(fr, 2), lax.rem(fr, 2)

    def dev(zz, yy, xx, cc):
        return {"dp": zz * 2 + yy, "frames": xx * 2 + cc}

    me = SimpleNamespace(z=z, y=y, x=x, c=c, fr=fr, dev=dev)
    me.xn = dev(z, y, 1 - x, c)
    me.yn = dev(z, 1 - y, x, c)
    me.sib = dev(z, y, x, 1 - c)
    me.diag = dev(z, y, 1 - x, 1 - c)
    return me


def remote(src, dst, send, recv, device):
    return pltpu.make_async_remote_copy(
        src_ref=src, dst_ref=dst, send_sem=send, recv_sem=recv, device_id=device, device_id_type=MESH
    )


def gather_steps(me, w, send, recv, nz, tilt=False):
    half = w.shape[4] if tilt else w.shape[4] // 2
    xo, yo, co = 1 - me.x, 1 - me.y, 1 - me.c

    def cp(view, s, device):
        return remote(view, view, send.at[s], recv.at[s], device)

    def spot(y, x, c):
        return w.at[:, y, x, c]

    def one(dz, y, x):
        return w.at[lax.rem(me.z + nz - dz, nz), y, x, me.c]

    def part(y, x, lower):
        return w.at[:, y, x, me.c, 0:half] if lower else w.at[:, y, x, me.c, half:]

    def step_z():
        for dz in range(1, nz):
            cp(one(0, me.y, me.x), dz - 1, me.dev(lax.rem(me.z + dz, nz), me.y, me.x, me.c)).start()

    def step_near():
        for dz in range(1, nz):
            cp(one(dz, me.y, me.x), dz - 1, me.xn).wait_recv()
        cp(spot(me.y, me.x, me.c), nz - 1, me.xn).start()
        cp(spot(me.y, me.x, me.c), nz, me.yn).start()
        cp(spot(me.y, me.x, me.c), nz + 1, me.sib).start()

    def step_far():
        cp(spot(me.y, xo, me.c), nz - 1, me.xn).wait_recv()
        cp(part(me.y, xo, True), nz + 2, me.yn).start()
        cp(spot(me.y, xo, me.c), nz + 3, me.sib).start()
        cp(spot(yo, me.x, me.c), nz, me.yn).wait_recv()
        if not tilt:
            cp(part(yo, me.x, False), nz + 4, me.xn).start()
        cp(spot(yo, me.x, me.c), nz + 5, me.sib).start()

    def step_last():
        cp(part(yo, xo, True), nz + 2, me.yn).wait_recv()
        if not tilt:
            cp(part(yo, xo, False), nz + 4, me.xn).wait_recv()
        cp(spot(yo, xo, me.c), nz + 6, me.sib).start()

    def step_done():
        for y, x, s in ((me.y, me.x, nz + 1), (me.y, xo, nz + 3), (yo, me.x, nz + 5), (yo, xo, nz + 6)):
            cp(spot(y, x, co), s, me.sib).wait_recv()

    def drain():
        for dz in range(1, nz):
            cp(one(0, me.y, me.x), dz - 1, me.xn).wait_send()
        for s in (nz - 1, nz):
            cp(spot(me.y, me.x, me.c), s, me.xn).wait_send()
        for y, x, s in ((me.y, me.x, nz + 1), (me.y, xo, nz + 3), (yo, me.x, nz + 5), (yo, xo, nz + 6)):
            cp(spot(y, x, me.c), s, me.xn).wait_send()
        cp(part(me.y, xo, True), nz + 2, me.xn).wait_send()
        if not tilt:
            cp(part(yo, me.x, False), nz + 4, me.xn).wait_send()

    return SimpleNamespace(
        z=step_z, near=step_near, far=step_far, last=step_last, done=step_done, drain=drain
    )


def gather_late_steps(me, w, send, recv, nz):
    half = w.shape[4] // 2
    xo, yo, co = 1 - me.x, 1 - me.y, 1 - me.c

    def cp(view, s, device):
        return remote(view, view, send.at[s], recv.at[s], device)

    def one(y, x):
        return w.at[me.z, y, x, me.c]

    def part(y, x, lower):
        return w.at[me.z, y, x, me.c, 0:half] if lower else w.at[me.z, y, x, me.c, half:]

    def layer(dz, c):
        return w.at[lax.rem(me.z + nz - dz, nz), :, :, c]

    def step_near():
        cp(one(me.y, me.x), 0, me.xn).start()
        cp(one(me.y, me.x), 1, me.yn).start()

    def step_far():
        cp(one(me.y, xo), 0, me.xn).wait_recv()
        cp(part(me.y, xo, True), 2, me.yn).start()
        cp(one(yo, me.x), 1, me.yn).wait_recv()
        cp(part(yo, me.x, False), 3, me.xn).start()

    def step_square():
        cp(part(yo, xo, True), 2, me.yn).wait_recv()
        cp(part(yo, xo, False), 3, me.xn).wait_recv()
        cp(layer(0, me.c), 4, me.sib).start()

    def step_z(dz):
        cp(layer(0, me.c), 4 + dz, me.dev(lax.rem(me.z + dz, nz), me.y, me.x, me.c)).start()

    def step_pass(dz):
        cp(layer(dz, me.c), 4 + dz, me.xn).wait_recv()
        cp(layer(dz, me.c), 3 + nz + dz, me.sib).start()

    def step_done():
        cp(layer(0, co), 4, me.sib).wait_recv()
        for dz in range(1, nz):
            cp(layer(dz, co), 3 + nz + dz, me.sib).wait_recv()

    def drain():
        cp(one(me.y, me.x), 0, me.xn).wait_send()
        cp(one(me.y, me.x), 1, me.xn).wait_send()
        cp(part(me.y, xo, True), 2, me.xn).wait_send()
        cp(part(yo, me.x, False), 3, me.xn).wait_send()
        cp(layer(0, me.c), 4, me.xn).wait_send()
        for dz in range(1, nz):
            cp(layer(0, me.c), 4 + dz, me.xn).wait_send()
            cp(layer(dz, me.c), 3 + nz + dz, me.xn).wait_send()

    return SimpleNamespace(
        near=step_near, far=step_far, square=step_square, z=step_z, pass_on=step_pass, done=step_done, drain=drain
    )


class Moves:
    def __init__(self, moves, send, recv, core_recv):
        self.moves, self.send, self.recv, self.core_recv = moves, send, recv, core_recv

    def cp(self, i):
        src, dst, to = self.moves[i][:3]
        return remote(src, dst, self.send.at[i], self.recv.at[i - 1] if i else self.core_recv, to)

    def go(self, i):
        _, _, _, _, credit, turn, slots, _ = self.moves[i]
        if turn >= slots:
            pl.semaphore_wait(credit, 1)
        self.cp(i).start()

    def free(self, i):
        _, _, _, giver, credit, turn, slots, turns = self.moves[i]
        if turn + slots < turns:
            pl.semaphore_signal(credit, inc=1, device_id=giver, device_id_type=MESH)

    def arrive(self, *at):
        for i in at:
            self.cp(i).wait_recv()

    def drain(self):
        for i in range(len(self.moves)):
            self.cp(i).wait_send()


def add(view, arrived):
    view[...] = (view[...].astype(F32) + arrived[...].astype(F32)).astype(view.dtype)


def add_core(me, w, core, nz):
    def body(zz, carry):
        for y in range(2):
            for x in range(2):
                add(w.at[zz, y, x, me.c], core.at[zz, y, x])
        return carry

    lax.fori_loop(0, nz, body, 0)


def scatter_steps(me, w, box, sems, credit, nz, core_turn, turn, sink):
    half = w.shape[4] // 2
    xo, yo, co = 1 - me.x, 1 - me.y, 1 - me.c
    core = box[0].at[core_turn[0] % core_turn[1]]
    y1, x1, x2, y2, zs = (b.at[turn[0] % turn[1]] for b in box[1:])

    def at_z(dz):
        return me.dev(lax.rem(me.z + nz + dz, nz), me.y, me.x, me.c)

    moves = [
        (w.at[:, :, :, co], core, me.sib, me.sib, credit.at[0], *core_turn),
        (w.at[:, yo, :, me.c, 0:half], y1, me.yn, me.yn, credit.at[1], *turn),
        (w.at[:, :, xo, me.c, half:], x1, me.xn, me.xn, credit.at[2], *turn),
        (w.at[:, me.y, xo, me.c, 0:half], x2, me.xn, me.xn, credit.at[3], *turn),
        (w.at[:, yo, me.x, me.c, half:], y2, me.yn, me.yn, credit.at[4], *turn),
    ]
    for dz in range(1, nz):
        slab = w.at[lax.rem(me.z + dz, nz), me.y, me.x, me.c]
        moves.append((slab, zs.at[dz - 1], at_z(dz), at_z(-dz), credit.at[4 + dz], *turn))
    m = Moves(moves, *sems)

    def step_a():
        m.go(0)

    def step_b():
        m.arrive(0)
        add_core(me, w, core, nz)
        m.free(0)
        m.go(1)
        m.go(2)

    def step_c():
        m.arrive(1, 2)

        def body(zz, carry):
            for o in range(2):
                add(w.at[zz, me.y, o, me.c, 0:half], y1.at[zz, o])
                add(w.at[zz, o, me.x, me.c, half:], x1.at[zz, o])
            return carry

        lax.fori_loop(0, nz, body, 0)
        m.free(1)
        m.free(2)
        m.go(3)
        m.go(4)

    def step_d():
        m.arrive(3, 4)

        def body(zz, carry):
            add(w.at[zz, me.y, me.x, me.c, 0:half], x2.at[zz])
            add(w.at[zz, me.y, me.x, me.c, half:], y2.at[zz])
            return carry

        lax.fori_loop(0, nz, body, 0)
        m.free(3)
        m.free(4)
        for dz in range(1, nz):
            m.go(4 + dz)

    def step_e():
        total = w[me.z, me.y, me.x, me.c].astype(F32)
        for dz in range(1, nz):
            m.arrive(4 + dz)
            total = total + zs[dz - 1].astype(F32)
        sink(total)
        for dz in range(1, nz):
            m.free(4 + dz)

    return SimpleNamespace(a=step_a, b=step_b, c=step_c, d=step_d, e=step_e, drain=m.drain)


def scatter_early_steps(me, w, box, sems, credit, nz, core_turn, turn, sink):
    half = w.shape[4] // 2
    xo, yo, co = 1 - me.x, 1 - me.y, 1 - me.c
    core = box[0].at[core_turn[0] % core_turn[1]]
    y1, x1, x2, y2, zs = (b.at[turn[0] % turn[1]] for b in box[1:])

    def at_z(dz):
        return me.dev(lax.rem(me.z + nz + dz, nz), me.y, me.x, me.c)

    moves = [
        (w.at[:, :, :, co], core, me.sib, me.sib, credit.at[0], *core_turn),
        (w.at[me.z, yo, :, me.c, 0:half], y1, me.yn, me.yn, credit.at[nz + 4], *turn),
        (w.at[me.z, :, xo, me.c, half:], x1, me.xn, me.xn, credit.at[nz + 5], *turn),
        (w.at[me.z, me.y, xo, me.c, 0:half], x2, me.xn, me.xn, credit.at[nz + 6], *turn),
        (w.at[me.z, yo, me.x, me.c, half:], y2, me.yn, me.yn, credit.at[nz + 7], *turn),
    ]
    for dz in range(1, nz):
        layer = w.at[lax.rem(me.z + dz, nz), :, :, me.c]
        moves.append((layer, zs.at[dz - 1], at_z(dz), at_z(-dz), credit.at[nz + 7 + dz], *turn))
    m = Moves(moves, *sems)

    def step_a():
        m.go(0)

    def step_b():
        m.arrive(0)
        add_core(me, w, core, nz)
        m.free(0)

    def step_z(dz):
        m.go(4 + dz)

    def step_c():
        for dz in range(1, nz):
            m.arrive(4 + dz)
            for y in range(2):
                for x in range(2):
                    add(w.at[me.z, y, x, me.c], zs.at[dz - 1, y, x])
            m.free(4 + dz)
        m.go(1)
        m.go(2)

    def step_d():
        m.arrive(1, 2)
        for o in range(2):
            add(w.at[me.z, me.y, o, me.c, 0:half], y1.at[o])
            add(w.at[me.z, o, me.x, me.c, half:], x1.at[o])
        m.free(1)
        m.free(2)
        m.go(3)
        m.go(4)

    def step_e():
        m.arrive(3, 4)
        late = jnp.concatenate([x2[...].astype(F32), y2[...].astype(F32)], axis=0)
        sink(w[me.z, me.y, me.x, me.c].astype(F32) + late)
        m.free(3)
        m.free(4)

    return SimpleNamespace(a=step_a, b=step_b, z=step_z, c=step_c, d=step_d, e=step_e, drain=m.drain)


def lane_masks():
    lane = lax.broadcasted_iota(jnp.int32, (1, LANES), 1)
    left = jnp.where(lane < HEAD_DIM, 1.0, 0.0).astype(BF16)
    return left, (1.0 - left.astype(F32)).astype(BF16)


def two_heads(block):
    left, right = lane_masks()
    return jnp.concatenate([block * left, block * right], axis=0)


def one_block(pair):
    rows = pair.shape[0] // 2
    lane = lax.broadcasted_iota(jnp.int32, (rows, LANES), 1)
    return jnp.where(lane < HEAD_DIM, pair[:rows], pair[rows:])


def at128(p, base=0):
    return pl.ds(pl.multiple_of(base + p * LANES, LANES), LANES)


def put_stat(stat, p, pair):
    rows = pair.shape[0] // 2
    lane = lax.broadcasted_iota(jnp.int32, stat.shape, 1)
    stat = jnp.where(lane == 2 * p, pair[:rows], stat)
    return jnp.where(lane == 2 * p + 1, pair[rows:], stat)


def normalise(values):
    center = values - jnp.mean(values, axis=-1, keepdims=True)
    spread = jnp.mean(center * center, axis=-1, keepdims=True)
    return center * lax.rsqrt(spread + 1e-05)


def forward(r, me, nz):
    rows, d = r.tokens.shape
    items, frames = r.kv.shape[:2]
    pairs = d // LANES

    def weight(k, n, size=WIDE):
        return r.wg[k, :, :, :, :, :, n * size : (n + 1) * size].reshape(d, size)

    def product(x, k, sink):
        sink(dot(x, weight(k, 0, d)))

    def ln(values, i):
        return normalise(values) * r.gs[i : i + 1, :] + r.gs[4 + i : 5 + i, :]

    def norms_in():
        for g in range(2 * nz):
            total = r.ng[g // 2, g % 2, 0, 0, 0:16, :].astype(F32)
            for f in range(1, 4):
                total = total + r.ng[g // 2, g % 2, f // 2, f % 2, 0:16, :].astype(F32)
            r.gs[:, g * LANES : (g + 1) * LANES] = total

    def norm_one():
        pltpu.make_async_copy(r.tokens, r.first, r.own_sem.at[1]).wait()
        r.xb[...] = ln(r.first[...], 0).astype(BF16)
        r.n1t[...] = r.xb[...].T

    def joint(q):
        def sink(v):
            r.joint[:, q * d : (q + 1) * d] = v.astype(BF16)

        product(r.xb[...], q, sink)

    def self_attention(half):
        row = lax.rem(lax.broadcasted_iota(jnp.int32, (2 * rows, rows), 0), rows)
        causal = row >= lax.broadcasted_iota(jnp.int32, (2 * rows, rows), 1)

        def body(p, stat):
            q2 = two_heads(r.joint[:, at128(p)] * jnp.asarray(HEAD_DIM**-0.5, BF16))
            s = dot_nt(q2, r.joint[:, at128(p, d)])
            s = jnp.where(causal, s, -1e30)
            m = jnp.max(s, axis=-1, keepdims=True)
            e = jnp.exp(s - m)
            total = jnp.sum(e, axis=-1, keepdims=True)
            o2 = dot(e.astype(BF16), r.joint[:, at128(p, 2 * d)]) / total
            r.xb[:, at128(p)] = one_block(o2).astype(BF16)
            return put_stat(stat, p, m + jnp.log(total))

        first = jnp.zeros((rows, LANES), F32) if half == 0 else r.wcol[...]
        stat = lax.fori_loop(half * pairs // 2, (half + 1) * pairs // 2, body, first)
        if half == 0:
            r.wcol[...] = stat
        else:
            r.slse[...] = stat.T[0:16]
            r.smixt[...] = r.xb[...].T

    def self_out():
        def sink(v):
            r.branch[...] = v

        product(r.xb[...], 3, sink)
        r.first[...] = r.first[...] + r.branch[...]
        squares(1, r.branch[...])
        r.xb[...] = ln(r.first[...], 1).astype(BF16)
        r.n2t[...] = r.xb[...].T

    def squares(i, values):
        ok = lax.broadcasted_iota(jnp.int32, (rows, 1), 0) < r.tl[0]
        total = jnp.sum(jnp.where(ok, values * values, 0.0))
        line = lax.broadcasted_iota(jnp.int32, r.sq.shape, 0)
        r.sq[...] = jnp.where(line == i, total, r.sq[...])

    def start_counts():
        line = lax.broadcasted_iota(jnp.int32, r.sq.shape, 0)
        r.sq[...] = jnp.where(line == 4, r.tl[0].astype(F32), 0.0)

    def queries():
        def sink(v):
            r.qa[me.fr] = v.astype(BF16)

        product(r.xb[...], 4, sink)

    def q_copy(f, s, device):
        return remote(r.qa.at[f], r.qa.at[f], r.q_send.at[s], r.q_recv.at[s], device)

    fx, fs, fd = (1 - me.x) * 2 + me.c, me.x * 2 + 1 - me.c, (1 - me.x) * 2 + 1 - me.c

    def q_start():
        q_copy(me.fr, 0, me.xn).start()
        q_copy(me.fr, 1, me.sib).start()

    def q_forward():
        q_copy(fx, 0, me.xn).wait_recv()
        q_copy(fx, 2, me.sib).start()

    def q_done():
        q_copy(fs, 1, me.sib).wait_recv()
        q_copy(fd, 2, me.sib).wait_recv()

    def mem_copy(t):
        return pltpu.make_async_copy(r.memory.at[t], r.rc.at[t % 2, 0 : r.memory.shape[1]], r.m_sem.at[t % 2])

    def memory_part(which, t):
        mem_copy(t).wait()
        stage = r.rc.at[t % 2, 0 : r.memory.shape[1]]
        for n in range(d // WIDE):
            v = dot(stage[...].reshape(frames, d), weight(5 + which, n))
            r.kv[t, :, which * d + n * WIDE : which * d + (n + 1) * WIDE] = v.astype(BF16)
        if which == 0:
            r.memt[:, t * frames : (t + 1) * frames] = stage[...].reshape(frames, d).T
        if t + 2 < items or which == 0:
            mem_copy((t + 2) % items).start()

    def mem_start():
        for t in range(min(2, items)):
            mem_copy(t).start()

    def cross_half(t, half):
        def body(p, stat):
            q2 = two_heads(r.qa[t, :, at128(p)] * jnp.asarray(HEAD_DIM**-0.5, BF16))
            s = dot_nt(q2, r.kv[t, :, at128(p)]) + r.bias[pl.ds(t, 1), :]
            m = jnp.max(s, axis=-1, keepdims=True)
            e = jnp.exp(s - m)
            total = jnp.sum(e, axis=-1, keepdims=True)
            o2 = dot(e.astype(BF16), r.kv[t, :, at128(p, d)]) / total
            r.op[t, :, at128(p)] = one_block(o2).astype(BF16)
            return put_stat(stat, p, m + jnp.log(total))

        first = jnp.zeros((rows, LANES), F32) if half == 0 else r.wcol[...]
        stat = lax.fori_loop(half * pairs // 2, (half + 1) * pairs // 2, body, first)
        if half == 0:
            r.wcol[...] = stat
        else:
            r.opl[t] = stat.T[0:16]

    def o_copies(t, slot, device):
        return (
            remote(r.op.at[t], r.orv.at[slot], r.o_send.at[slot], r.o_recv.at[slot], device),
            remote(r.opl.at[t], r.orl.at[slot], r.o_send.at[3 + slot], r.o_recv.at[3 + slot], device),
        )

    def o_start(t, slot, device):
        for cp in o_copies(t, slot, device):
            cp.start()

    def o_wait(t, slot, device):
        for cp in o_copies(t, slot, device):
            cp.wait_recv()

    def merge(parts, sink):
        lses = [lse[...] for _, lse in parts]
        top = functools.reduce(jnp.maximum, lses)
        shares = [jnp.exp(v - top) for v in lses]
        total = functools.reduce(jnp.add, shares)
        flat = jnp.concatenate([v / total for v in shares] + [jnp.zeros((LANES - 16 * len(parts), LANES), F32)], axis=0)
        r.wcol[...] = flat.T
        lane = lax.broadcasted_iota(jnp.int32, (rows, LANES), 1)
        for p in range(pairs):
            value = jnp.zeros((rows, LANES), F32)
            for i, (mix, _) in enumerate(parts):
                left = r.wcol[:, 16 * i + 2 * p : 16 * i + 2 * p + 1]
                right = r.wcol[:, 16 * i + 2 * p + 1 : 16 * i + 2 * p + 2]
                share = jnp.where(lane < HEAD_DIM, left, right)
                value = value + share * mix[:, p * LANES : (p + 1) * LANES].astype(F32)
            sink(p, value)
        return top + jnp.log(total)

    def send_far():
        o_start(fd, 0, me.sib)

    def send_side():
        o_start(fs, 1, me.sib)

    def merge_across():
        o_wait(fd, 0, me.sib)

        def sink(p, v):
            r.op[fx, :, p * LANES : (p + 1) * LANES] = v.astype(BF16)

        r.opl[fx] = merge([(r.op.at[fx], r.opl.at[fx]), (r.orv.at[0], r.orl.at[0])], sink)
        o_start(fx, 2, me.xn)

    def merge_own():
        o_wait(fs, 1, me.sib)
        o_wait(fx, 2, me.xn)

        def sink(p, v):
            r.xb[:, p * LANES : (p + 1) * LANES] = v.astype(BF16)

        parts = [(r.op.at[me.fr], r.opl.at[me.fr]), (r.orv.at[1], r.orl.at[1]), (r.orv.at[2], r.orl.at[2])]
        r.clse[...] = merge(parts, sink)
        r.cmixt[...] = r.xb[...].T

    def cross_out():
        def sink(v):
            r.branch[...] = v

        product(r.xb[...], 7, sink)
        squares(2, r.branch[...])
        r.second[...] = r.first[...] + r.branch[...]
        r.xb[...] = ln(r.second[...], 2).astype(BF16)
        r.n3t[...] = r.xb[...].T

    def expand(q):
        for n in range(d // WIDE):
            v = dot(r.xb[...], weight(8 + q, n))
            at = slice(q * d + n * WIDE, q * d + (n + 1) * WIDE)
            half = 0.5 * (1.0 + lax.erf(v * (2.0**-0.5)))
            r.active[:, at] = (v * half).astype(BF16)
            r.slope[:, at] = (half + v * jnp.exp(-0.5 * v * v) * 0.3989422804014327).astype(BF16)
        r.activet[q * d : (q + 1) * d, :] = r.active[:, q * d : (q + 1) * d].T

    def contract(q, fresh=False):
        def sink(v):
            r.branch[...] = v if fresh else r.branch[...] + v

        product(r.active[:, q * d : (q + 1) * d], 12 + q, sink)

    def finish():
        squares(3, r.branch[...])
        r.third[...] = r.second[...] + r.branch[...]
        squares(0, r.third[...])
        ok = lax.broadcasted_iota(jnp.int32, (rows, 1), 0) < r.tl[0]
        r.branch[...] = jnp.where(ok, ln(r.third[...], 3), 0.0)
        pltpu.make_async_copy(r.branch, r.result, r.own_sem.at[3]).start()

    part = functools.partial

    def item(t):
        return [part(cross_half, t, 0), part(cross_half, t, 1)]

    tasks = {
        0: [start_counts, mem_start],
        2: [norms_in, norm_one],
        4: [part(joint, 0)],
        5: [part(joint, 1)],
        6: [part(joint, 2), part(self_attention, 0), part(self_attention, 1)],
        7: [self_out],
        8: [queries, q_start],
        9: [part(memory_part, 0, t) for t in range(items)],
        10: [q_forward] + [part(memory_part, 1, t) for t in range(items)],
        11: [q_done, *item(fd), send_far, *item(fs), send_side],
        12: [*item(fx), merge_across],
        13: item(me.fr),
        14: [merge_own, cross_out, part(expand, 0), part(expand, 1)],
        15: [part(expand, 2), part(expand, 3)],
        16: [part(contract, 3, True), part(contract, 0)],
        17: [part(contract, 1)],
        18: [part(contract, 2), finish],
    }

    def drain():
        q_copy(me.fr, 0, me.xn).wait_send()
        q_copy(me.fr, 1, me.sib).wait_send()
        q_copy(fx, 2, me.sib).wait_send()
        for t, slot, device in ((fd, 0, me.sib), (fs, 1, me.sib), (fx, 2, me.xn)):
            for cp in o_copies(t, slot, device):
                cp.wait_send()

    return tasks, drain, (fx, fs, fd)


def ln_back(values, gain_row, grad):
    center = values - jnp.mean(values, axis=-1, keepdims=True)
    scale = lax.rsqrt(jnp.mean(center * center, axis=-1, keepdims=True) + 1e-05)
    unit = center * scale
    gain_grad = jnp.sum(grad * unit, axis=0, keepdims=True)
    shift_grad = jnp.sum(grad, axis=0, keepdims=True)
    lifted = grad * gain_row
    inner = jnp.mean(lifted * unit, axis=-1, keepdims=True)
    back = scale * (lifted - jnp.mean(lifted, axis=-1, keepdims=True) - unit * inner)
    return back, gain_grad, shift_grad


def backward(r, me, nz, fronts):
    rows, d = r.first.shape
    items, frames = r.kv.shape[:2]
    pairs = d // LANES
    fx, fs, fd = fronts
    t = {}

    def grad_into(k, left, right, into=None):
        for n in range(d // WIDE):
            v = dot(left, right(n * WIDE, (n + 1) * WIDE)).astype(BF16)
            at = slice(n * WIDE, (n + 1) * WIDE)
            r.wg[k if into is None else into, :, :, :, :, :, at] = v.reshape(nz, 2, 2, 2, d // (8 * nz), WIDE)

    def through(k, grad):
        return dot_nt(grad, r.wg[k].reshape(d, d))

    def ln_step(i, values, grad, first=False):
        back, gain, shift = ln_back(values, r.gs[i : i + 1, :], grad)
        r.gr[...] = back if first else r.gr[...] + back
        r.nrow[i : i + 1, :] = gain
        r.nrow[4 + i : 5 + i, :] = shift

    def start():
        pltpu.make_async_copy(r.cotangent, r.gr, r.own_sem.at[2]).wait()
        r.biast[...] = jnp.concatenate([r.bias[...], jnp.zeros((LANES - r.bias.shape[0], frames), F32)], axis=0).T
        for g in range(d // LANES):
            r.nrow[8:16, g * LANES : (g + 1) * LANES] = r.sq[...]
        ok = lax.broadcasted_iota(jnp.int32, (rows, 1), 0) < r.tl[0]
        ln_step(3, r.third[...], jnp.where(ok, r.gr[...], 0.0), True)
        r.xb[...] = r.gr[...].astype(BF16)
        pltpu.make_async_copy(r.tokens, r.third, r.own_sem.at[1]).start()

    def contract(q):
        at = slice(q * d, (q + 1) * d)
        r.active[:, at] = (through(12 + q, r.xb[...]) * r.slope[:, at].astype(F32)).astype(BF16)

    def contract_grad(q):
        grad_into(12 + q, r.activet[q * d : (q + 1) * d, :], lambda lo, hi: r.xb[:, lo:hi])

    def onto(fresh, value):
        r.branch[...] = value if fresh else r.branch[...] + value

    def expand(q):
        if q == 0:
            pltpu.make_async_copy(r.branch, r.result, r.own_sem.at[3]).wait()
        onto(q == 0, through(8 + q, r.active[:, q * d : (q + 1) * d]))

    def expand_grad(q):
        grad_into(8 + q, r.n3t[...], lambda lo, hi: r.active[:, q * d + lo : q * d + hi])

    def cross_out():
        ln_step(2, r.second[...], r.branch[...])
        r.xb[...] = r.gr[...].astype(BF16)
        r.ga[me.fr] = through(7, r.xb[...]).astype(BF16)
        r.gl[me.fr, 0:16] = r.clse[...]

        def body(p, carry):
            left, right = row_dots(r.ga[me.fr, :, at128(p)], r.cmixt[at128(p), :])
            r.gl[me.fr, pl.ds(16 + 2 * p, 1), :] = left
            r.gl[me.fr, pl.ds(17 + 2 * p, 1), :] = right
            return carry

        lax.fori_loop(0, pairs, body, 0)

    def cross_out_grad():
        grad_into(7, r.cmixt[...], lambda lo, hi: r.xb[:, lo:hi])

    def row_dots(grad, mixt):
        prod = grad.astype(F32).T * mixt.astype(F32)
        return jnp.sum(prod[:HEAD_DIM], axis=0, keepdims=True), jnp.sum(prod[HEAD_DIM:], axis=0, keepdims=True)

    def g_copies(f, s, device):
        return (
            remote(r.ga.at[f], r.ga.at[f], r.g2_send.at[s], r.g2_recv.at[s], device),
            remote(r.gl.at[f], r.gl.at[f], r.g2_send.at[3 + s], r.g2_recv.at[3 + s], device),
        )

    def each(copies, what):
        for cp in copies:
            getattr(cp, what)()

    def g_start():
        each(g_copies(me.fr, 0, me.xn), "start")
        each(g_copies(me.fr, 1, me.sib), "start")

    def g_forward():
        each(g_copies(fx, 0, me.xn), "wait_recv")
        each(g_copies(fx, 2, me.sib), "start")

    def g_drain():
        each(g_copies(me.fr, 0, me.xn), "wait_send")
        each(g_copies(me.fr, 1, me.sib), "wait_send")
        each(g_copies(fx, 2, me.sib), "wait_send")

    scale = HEAD_DIM**-0.5

    def pair_back(q, k, v, g, hide, lse, dots):
        q2, g2 = two_heads(q * jnp.asarray(scale, BF16)), two_heads(g)
        probs = jnp.exp(hide(dot_nt(k, q2)) - lse)
        ds = (probs * (dot_nt(v, g2) - dots)).astype(BF16)
        dq = one_block(dot(ds.T, k)) * scale
        return dq, dot(ds, q2), dot(probs.astype(BF16), g2)

    def cross_half(f, half):
        lane = lax.broadcasted_iota(jnp.int32, (frames, LANES), 1)
        column = jnp.sum(jnp.where(lane == f, r.biast[...], 0.0), axis=-1, keepdims=True)

        def body(p, carry):
            stats = [
                jnp.concatenate([r.gl[f, pl.ds(b + 2 * p, 1), :], r.gl[f, pl.ds(b + 1 + 2 * p, 1), :]], axis=1)
                for b in (0, 16)
            ]
            dq, dk, dv = pair_back(
                r.qa[f, :, at128(p)],
                r.kv[f, :, at128(p)],
                r.kv[f, :, at128(p, d)],
                r.ga[f, :, at128(p)],
                lambda s: s + column,
                *stats,
            )
            r.op[f, :, at128(p)] = dq.astype(BF16)
            r.kv[f, :, at128(p)] = dk.astype(BF16)
            r.kv[f, :, at128(p, d)] = dv.astype(BF16)
            return carry

        lax.fori_loop(half * pairs // 2, (half + 1) * pairs // 2, body, 0)

    def d_copy(f, slot, device):
        return remote(r.op.at[f], r.orv.at[slot], r.o2_send.at[slot], r.o2_recv.at[slot], device)

    def side_ready():
        each(g_copies(fs, 1, me.sib), "wait_recv")

    def send_side():
        d_copy(fs, 1, me.sib).start()

    def far_ready():
        each(g_copies(fd, 2, me.sib), "wait_recv")

    def send_far():
        d_copy(fd, 0, me.sib).start()

    def send_across():
        d_copy(fd, 0, me.sib).wait_recv()
        r.op[fx] = (r.op[fx].astype(F32) + r.orv[0].astype(F32)).astype(BF16)
        d_copy(fx, 2, me.xn).start()

    def tile_copy(n):
        f, h = n // 2, n % 2
        return pltpu.make_async_copy(
            r.mst.at[n % 2, 0 : r.memory_grad.shape[1]],
            r.memory_grad.at[f, :, h * WIDE : (h + 1) * WIDE],
            r.t_sem.at[n % 2],
        )

    def memory_grad(n):
        f, h = n // 2, n % 2
        if n >= 2:
            tile_copy(n - 2).wait()
        layers = slice(h * nz // 2, (h + 1) * nz // 2)
        keys, values = (r.wg[k, layers].reshape(WIDE, d) for k in (5, 6))
        r.mst[n % 2] = dot_nt(r.kv[f, :, 0:d], keys) + dot_nt(r.kv[f, :, d : 2 * d], values)
        tile_copy(n).start()

    def memory_done():
        for n in (2 * items - 2, 2 * items - 1):
            tile_copy(n).wait()

    def memory_weights(which, into):
        def rows_of(lo, hi):
            return r.kv[:, :, which * d + lo : which * d + hi].reshape(items * frames, hi - lo)

        grad_into(5 + which, r.memt[...], rows_of, into)

    def query():
        d_copy(fs, 1, me.sib).wait_recv()
        d_copy(fx, 2, me.xn).wait_recv()
        r.xb[...] = (r.op[me.fr].astype(F32) + r.orv[1].astype(F32) + r.orv[2].astype(F32)).astype(BF16)
        onto(True, through(4, r.xb[...]))
        grad_into(4, r.n2t[...], lambda lo, hi: r.xb[:, lo:hi])

    def d_drain():
        for f, slot, device in ((fd, 0, me.sib), (fs, 1, me.sib), (fx, 2, me.xn)):
            d_copy(f, slot, device).wait_send()

    def self_out():
        ln_step(1, r.first[...], r.branch[...])
        r.xb[...] = r.gr[...].astype(BF16)
        r.ga[me.fr] = through(3, r.xb[...]).astype(BF16)
        grad_into(3, r.smixt[...], lambda lo, hi: r.xb[:, lo:hi])

    def self_attention(half):
        key = lax.broadcasted_iota(jnp.int32, (rows, 2 * rows), 0)
        causal = key <= lax.rem(lax.broadcasted_iota(jnp.int32, (rows, 2 * rows), 1), rows)

        def body(p, carry):
            g = r.ga[me.fr, :, at128(p)]
            lse = jnp.concatenate([r.slse[pl.ds(2 * p, 1), :], r.slse[pl.ds(2 * p + 1, 1), :]], axis=1)
            dots = jnp.concatenate(row_dots(g, r.smixt[at128(p), :]), axis=1)
            dq, dk, dv = pair_back(
                r.joint[:, at128(p)],
                r.joint[:, at128(p, d)],
                r.joint[:, at128(p, 2 * d)],
                g,
                lambda s: jnp.where(causal, s, -1e30),
                lse,
                dots,
            )
            r.joint[:, at128(p)] = dq.astype(BF16)
            r.joint[:, at128(p, d)] = dk.astype(BF16)
            r.joint[:, at128(p, 2 * d)] = dv.astype(BF16)
            return carry

        lax.fori_loop(half * pairs // 2, (half + 1) * pairs // 2, body, 0)

    def project(q):
        onto(q == 0, through(q, r.joint[:, q * d : (q + 1) * d]))

    def project_grad(q):
        grad_into(q, r.n1t[...], lambda lo, hi: r.joint[:, q * d + lo : q * d + hi])

    def finish():
        pltpu.make_async_copy(r.tokens, r.third, r.own_sem.at[1]).wait()
        ln_step(0, r.third[...], r.branch[...])
        pltpu.make_async_copy(r.gr, r.tokens_grad, r.own_sem.at[2]).start()
        for g in range(d // LANES):
            for f in range(4):
                r.nw[g // 2, g % 2, f // 2, f % 2] = r.nrow[:, g * LANES : (g + 1) * LANES]

    def close():
        pltpu.make_async_copy(r.gr, r.tokens_grad, r.own_sem.at[2]).wait()

    return SimpleNamespace(**{k: v for k, v in locals().items() if callable(v)})


GRAD_ORDER = (12, 13, 14, 15, 8, 9, 10, 11, 7, 5, 6, 4, 3, 0, 1, 2)
SLOTS = 2


LATE = (15,)
LATE_TICKS = (2, 5, 8)
TILT = ()
EARLY = (1,)
EARLY_END = 8
ROWS = 7
SEND_ROWS = 6
INTO = {5: 12, 6: 14}


def own_blocks(r):
    slab, d = r.self_output.shape
    blocks = {}
    for k in range(3):
        blocks[k] = (r.self_project.at[:, k * d : (k + 1) * d], r.self_project_grad.at[:, k * d : (k + 1) * d])
    for k in range(2):
        blocks[5 + k] = (r.cross_memory.at[:, k * d : (k + 1) * d], r.cross_memory_grad.at[:, k * d : (k + 1) * d])
    blocks[3] = (r.self_output, r.self_output_grad)
    blocks[4] = (r.cross_query, r.cross_query_grad)
    blocks[7] = (r.cross_output, r.cross_output_grad)
    for k in range(4):
        blocks[12 + k] = tuple(a.at[k * slab : (k + 1) * slab] for a in (r.contract, r.contract_grad))
    return blocks


def deal(r, put):
    slab = r.expand.shape[0]
    ways = LANES // slab

    def body(g, carry):
        lane = lax.div(lax.broadcasted_iota(jnp.int32, (slab, LANES), 1), slab)
        source = [r.expand[:, at128(ways * g + a)].astype(F32) for a in range(ways)]
        for q in range(ways):
            total = source[q]
            for a in range(ways):
                if a != q:
                    total = jnp.where(lane == a, pltpu.roll(source[a], (slab * (a - q)) % LANES, 1), total)
            put(q, at128(g), total.astype(BF16))
        return carry

    lax.fori_loop(0, r.expand.shape[1] // (ways * LANES), body, 0)


def undeal(r, q, total):
    slab = total.shape[0]
    ways = LANES // slab
    lane = lax.div(lax.broadcasted_iota(jnp.int32, (slab, LANES), 1), slab)
    for g in range(total.shape[1] // LANES):
        block = total[:, g * LANES : (g + 1) * LANES]
        for a in range(ways):
            line, column = divmod((ways * g + a) * LANES, total.shape[1])
            at = (slice(line * slab, (line + 1) * slab), slice(column, column + LANES))
            moved = block if a == q else pltpu.roll(block, (slab * (q - a)) % LANES, 1)
            r.second[at] = jnp.where(lane == q, moved, r.second[at])


def run(r, nz, chunks):
    me = place()
    barrier = pltpu.get_barrier_semaphore()
    peers = [me.xn, me.yn, me.sib, me.diag]
    peers += [me.dev(lax.rem(me.z + dz, nz), me.y, me.x, me.c) for dz in range(1, nz)]
    for device in peers:
        pl.semaphore_signal(barrier, inc=1, device_id=device, device_id_type=MESH)
    blocks = own_blocks(r)
    owns = {
        k: pltpu.make_async_copy(blocks[k][0], r.wg.at[k, me.z, me.y, me.x, me.c], r.w_sem.at[k]) for k in sorted(blocks)
    }
    for k in (0, 1, *LATE):
        owns[k].start()
    for k in owns:
        if k not in (0, 1, *LATE):
            owns[k].start()
    pltpu.make_async_copy(r.tokens, r.first, r.own_sem.at[1]).start()
    pltpu.make_async_copy(r.cotangent, r.gr, r.own_sem.at[2]).start()
    slab = r.expand.shape[0]
    lane = lax.div(lax.broadcasted_iota(jnp.int32, (8, LANES), 1), slab)
    both = jnp.concatenate([r.norm_gains[...].astype(F32), r.norm_shifts[...].astype(F32)], axis=0)
    wide = jnp.where(lane == me.fr, jnp.concatenate([both] * (LANES // slab), axis=1), 0.0)
    r.ng[me.z, me.y, me.x, me.c] = jnp.concatenate([wide, jnp.zeros((24, LANES), F32)], axis=0).astype(BF16)

    def put(q, at, v):
        r.wg[8 + q, me.z, me.y, me.x, me.c, :, at] = v

    early = [k for k in range(chunks) if k not in LATE]
    count = len(early)
    norm = gather_steps(me, r.ng, r.g_send.at[ROWS], r.g_recv.at[ROWS], nz)
    steps = []
    for k in range(chunks):
        row = ROWS + 1 + LATE.index(k) if k in LATE else early.index(k) % ROWS
        sems = (r.g_send.at[row], r.g_recv.at[row])
        if k in LATE:
            steps.append(gather_late_steps(me, r.wg.at[k], *sems, nz))
        else:
            steps.append(gather_steps(me, r.wg.at[k], *sems, nz, k in TILT))

    def mix(steps, pieces):
        for i, step in enumerate(steps):
            step()
            for piece in pieces[i * len(pieces) // len(steps) : (i + 1) * len(pieces) // len(steps)]:
                piece()

    part = functools.partial
    pl.semaphore_wait(barrier, len(peers))
    norm.z()
    owns[0].wait()
    steps[0].z()
    for k in LATE:
        owns[k].wait()
        steps[k].near()
    for k in owns:
        if k != 0 and k not in LATE:
            owns[k].wait()
    for k in LATE:
        steps[k].far()
    tasks, drain, fronts = forward(r, me, nz)
    lines = {tick: [] for tick in range(count + 4)}
    for tick in lines:
        for step, t in (
            ("done", tick - 4),
            ("near", tick),
            ("drain", tick - 4),
            ("z", tick + 2),
            ("far", tick - 1),
            ("last", tick - 2),
        ):
            if tick == 0 and step == "z":
                lines[tick].append(steps[early[1]].z)
            if 0 <= t < count:
                lines[tick].append(getattr(steps[early[t]], step))
    lines[0].insert(1, norm.near)
    lines[0].append(norm.far)
    lines[1] += [norm.last] + [steps[k].square for k in LATE]
    lines[2].insert(0, norm.done)
    for i, k in enumerate(LATE):
        for dz in range(1, nz):
            tick = LATE_TICKS[i * (nz - 1) + dz - 1]
            lines[tick].append(part(steps[k].z, dz))
            lines[tick + 3].append(part(steps[k].pass_on, dz))
        lines[tick + 5].insert(0, steps[k].done)
    tasks[0] = tasks.get(0, []) + [part(deal, r, put)]
    for tick in lines:
        mix(lines[tick], tasks.get(tick, []))
    drain()
    norm.drain()
    for k in LATE:
        steps[k].drain()

    b = backward(r, me, nz, fronts)

    plain = [m for m in range(chunks) if m not in EARLY]
    ends = {m: i + 3.0 for i, m in enumerate(plain)}
    ends.update({m: EARLY_END + 0.5 for m in EARLY})
    direct = sorted((m for m, k in enumerate(GRAD_ORDER) if k in blocks), key=ends.get)

    def out_copy(i):
        return pltpu.make_async_copy(r.ost.at[i % 2], blocks[GRAD_ORDER[direct[i]]][1], r.e_sem.at[i % 2])

    def keep(turn):
        k = GRAD_ORDER[turn]

        def sink(total):
            if k not in blocks:
                undeal(r, k - 8, total)
                return
            i = direct.index(turn)
            if i >= 2:
                out_copy(i - 2).wait()
            r.ost[i % 2] = total
            out_copy(i).start()

        return sink

    def keep_norms(total):
        rms = jnp.sqrt(total / (total[12:13] * r.first.shape[1]))
        line = lax.broadcasted_iota(jnp.int32, total.shape, 0)
        r.norm_out[...] = jnp.where(line < 8, total, rms)

    boxes = (r.rc, r.y1, r.x1, r.x2, r.y2, r.zs)
    fast_boxes = (r.rc, r.fy1, r.fx1, r.fx2, r.fy2, r.fzs)
    norm_boxes = (r.nrc, r.ny1, r.nx1, r.nx2, r.ny2, r.nzs)
    adds = {}
    for m, k in enumerate(GRAD_ORDER):
        w = r.wg.at[INTO.get(k, k)]
        if m in EARLY:
            build, box, turn = scatter_early_steps, fast_boxes, (EARLY.index(m), 1, len(EARLY))
            at = SEND_ROWS, SLOTS
        else:
            build, box, turn = scatter_steps, boxes, (plain.index(m), SLOTS, len(plain))
            at = turn[0] % SEND_ROWS, turn[0] % SLOTS
        sems = (r.s_send.at[at[0]], r.s_recv.at[at[1]], r.core_recv.at[m % SLOTS])
        adds[m] = build(me, w, box, sems, r.credit, nz, (m, SLOTS, chunks), turn, keep(m))
    once = (0, 1, 1)
    sems = (r.s_send.at[SEND_ROWS + 1], r.s_recv.at[SLOTS + 1], r.core_recv.at[SLOTS])
    adds[chunks] = scatter_steps(me, r.nw, norm_boxes, sems, r.credit, nz, once, once, keep_norms)
    wide_copies = [
        pltpu.make_async_copy(
            r.second.at[i * slab : (i + 1) * slab],
            r.expand_grad.at[:, i * r.second.shape[1] : (i + 1) * r.second.shape[1]],
            r.x_sem.at[i],
        )
        for i in range(4)
    ]

    def wide_start():
        for cp in wide_copies:
            cp.start()

    def pair(f):
        return [part(b.cross_half, f, 0), part(b.cross_half, f, 1)]

    fx, fs, fd = fronts
    mg = [part(b.memory_grad, n) for n in range(8)]
    work = {
        -1: [b.start, part(b.contract, 0), part(b.contract_grad, 0)],
        0: [part(b.contract, 1), part(b.contract_grad, 1), part(b.contract, 2), part(b.contract_grad, 2)],
        1: [part(b.contract, 3), part(b.contract_grad, 3), part(b.expand, 0), part(b.expand_grad, 0)],
        2: [part(b.expand, 1), part(b.expand_grad, 1), part(b.expand, 2), part(b.expand_grad, 2)],
        3: [part(b.expand, 3), part(b.expand_grad, 3), b.cross_out, b.g_start, b.cross_out_grad],
        4: pair(me.fr) + [b.side_ready, part(b.cross_half, fs, 0)],
        5: [part(b.cross_half, fs, 1), b.send_side, b.g_forward, b.far_ready, part(b.cross_half, fd, 0)],
        6: [part(b.cross_half, fd, 1), b.send_far, *pair(fx)],
        7: [b.send_across, part(b.memory_weights, 0, INTO[5]), b.g_drain],
        8: [part(b.memory_weights, 1, INTO[6]), mg[0]],
        9: [b.query, mg[1], mg[2]],
        10: [b.d_drain, b.self_out, mg[3]],
        11: [part(b.self_attention, 0), part(b.self_attention, 1), part(b.project, 0), part(b.project_grad, 0)],
        12: [part(b.project, 1), part(b.project_grad, 1), mg[4]],
        13: [part(b.project, 2), part(b.project_grad, 2), b.finish],
        14: [mg[5]],
        15: [mg[6], mg[7]],
        16: [b.memory_done],
    }
    starts, named = {}, {}
    for i, m in enumerate(plain):
        starts.setdefault(i - 1, []).append(m)
        for late, name in enumerate("bcde"):
            named.setdefault(i + late, {})[name] = getattr(adds[m], name)
    steps = {tick: [by[n] for n in "bcde" if n in by] for tick, by in named.items()}
    for i, m in enumerate(plain[:-SEND_ROWS]):
        steps[i + SEND_ROWS - 1].insert(0, adds[m].drain)
    (first,) = (adds[m] for m in EARLY)
    starts[0].insert(0, EARLY[0])
    steps[1].insert(0, first.b)
    for dz in range(1, nz):
        steps[dz].append(part(first.z, dz))
    for back, step in enumerate((first.e, first.d, first.c)):
        steps[EARLY_END - back].append(step)
    last = len(plain) - 1
    for tick, name in zip(range(last, last + 4), "bcde"):
        steps.setdefault(tick, []).append(getattr(adds[chunks], name))
    starts[last - 1].append(chunks)
    for tick in range(-1, last + 4):
        mix(steps.get(tick, []) or [lambda: None], work.get(tick, []))
        if tick == 10:
            wide_start()
        for m in starts.get(tick, []):
            adds[m].a()
    b.close()
    for cp in wide_copies:
        cp.wait()
    out_copy(len(direct) - 2).wait()
    out_copy(len(direct) - 1).wait()
    for m in (*plain[-SEND_ROWS:], *EARLY, chunks):
        adds[m].drain()


VMEM_BYTES = 127 * 2**19


INPUTS = (
    "tl",
    "tokens",
    "cotangent",
    "memory",
    "self_project",
    "self_output",
    "cross_query",
    "cross_memory",
    "cross_output",
    "expand",
    "contract",
    "norm_gains",
    "norm_shifts",
    "bias",
)
GRADS = ("self_project", "self_output", "cross_query", "cross_memory", "cross_output", "expand", "contract")


def at(space):
    return pl.BlockSpec(memory_space=space)


def fused(nz, chunks, frame_count, **given):
    rows, d = given["tokens"].shape
    items, parts = given["memory"].shape[:2]
    slab = given["self_output"].shape[0]
    padded = parts * 4 * slab
    half = slab // 2
    outs = dict(
        result=((rows, d), pl.ANY),
        tokens_grad=((rows, d), pl.ANY),
        memory_grad=((items, frame_count, d), pl.ANY),
        **{k + "_grad": (given[k].shape, pl.ANY) for k in GRADS},
        norm_out=((16, LANES), pltpu.VMEM),
    )
    vm = pltpu.VMEM
    dma = pltpu.SemaphoreType.DMA
    scratch = dict(
        wg=vm((chunks, nz, 2, 2, 2, slab, d), BF16),
        ng=vm((nz, 2, 2, 2, 32, LANES), BF16),
        gs=vm((16, d), F32),
        n1t=vm((d, rows), BF16),
        joint=vm((rows, 3 * d), BF16),
        smixt=vm((d, rows), BF16),
        slse=vm((16, LANES), F32),
        first=vm((rows, d), F32),
        n2t=vm((d, rows), BF16),
        qa=vm((items, rows, d), BF16),
        kv=vm((items, padded, 2 * d), BF16),
        memt=vm((d, items * padded), BF16),
        clse=vm((16, LANES), F32),
        second=vm((rows, d), F32),
        n3t=vm((d, rows), BF16),
        activet=vm((4 * d, rows), BF16),
        active=vm((rows, 4 * d), BF16),
        slope=vm((rows, 4 * d), BF16),
        third=vm((rows, d), F32),
        sq=vm((8, LANES), F32),
        xb=vm((rows, d), BF16),
        branch=vm((rows, d), F32),
        op=vm((items, rows, d), BF16),
        opl=vm((items, 16, LANES), F32),
        orv=vm((3, rows, d), BF16),
        orl=vm((3, 16, LANES), F32),
        wcol=vm((LANES, LANES), F32),
        cmixt=vm((d, rows), BF16),
        gr=vm((rows, d), F32),
        ga=vm((items, rows, d), BF16),
        gl=vm((items, 32, LANES), F32),
        nrow=vm((16, d), F32),
        biast=vm((padded, LANES), F32),
        mst=vm((2, padded, WIDE), F32),
        ost=vm((2, slab, d), F32),
        nw=vm((nz, 2, 2, 2, 16, LANES), F32),
        rc=vm((SLOTS, nz, 2, 2, slab, d), BF16),
        y1=vm((SLOTS, nz, 2, half, d), BF16),
        x1=vm((SLOTS, nz, 2, half, d), BF16),
        x2=vm((SLOTS, nz, half, d), BF16),
        y2=vm((SLOTS, nz, half, d), BF16),
        zs=vm((SLOTS, nz - 1, slab, d), BF16),
        fy1=vm((1, 2, half, d), BF16),
        fx1=vm((1, 2, half, d), BF16),
        fx2=vm((1, half, d), BF16),
        fy2=vm((1, half, d), BF16),
        fzs=vm((1, nz - 1, 2, 2, slab, d), BF16),
        nrc=vm((1, nz, 2, 2, 16, LANES), F32),
        ny1=vm((1, nz, 2, 8, LANES), F32),
        nx1=vm((1, nz, 2, 8, LANES), F32),
        nx2=vm((1, nz, 8, LANES), F32),
        ny2=vm((1, nz, 8, LANES), F32),
        nzs=vm((1, nz - 1, 16, LANES), F32),
        own_sem=dma((4,)),
        x_sem=dma((4,)),
        w_sem=dma((chunks,)),
        m_sem=dma((2,)),
        t_sem=dma((2,)),
        e_sem=dma((2,)),
        g_send=dma((ROWS + 1 + len(LATE), nz + 7)),
        g_recv=dma((ROWS + 1 + len(LATE), nz + 7)),
        s_send=dma((SEND_ROWS + 2, nz + 4)),
        s_recv=dma((SLOTS + 2, nz + 3)),
        core_recv=dma((SLOTS + 1,)),
        credit=pltpu.SemaphoreType.REGULAR((2 * nz + 7,)),
        q_send=dma((3,)),
        q_recv=dma((3,)),
        o_send=dma((6,)),
        o_recv=dma((6,)),
        g2_send=dma((6,)),
        g2_recv=dma((6,)),
        o2_send=dma((3,)),
        o2_recv=dma((3,)),
    )
    names = list(INPUTS) + list(outs) + list(scratch)

    def kernel(*refs):
        run(SimpleNamespace(**dict(zip(names, refs))), nz, chunks)

    spaces = {"tl": pltpu.SMEM, "expand": pltpu.VMEM, "norm_gains": pltpu.VMEM, "norm_shifts": pltpu.VMEM, "bias": pltpu.VMEM}
    res = pl.pallas_call(
        kernel,
        out_shape=[jax.ShapeDtypeStruct(s, F32) for s, _ in outs.values()],
        in_specs=[at(spaces.get(k, pl.ANY)) for k in INPUTS],
        out_specs=[at(s) for _, s in outs.values()],
        scratch_shapes=list(scratch.values()),
        compiler_params=pltpu.CompilerParams(collective_id=0, has_side_effects=True, vmem_limit_bytes=VMEM_BYTES),
    )(*(given[k] for k in INPUTS))
    return dict(zip(outs, res))


def settle(arrays, norm_out, width):
    count = len(arrays)
    pieces = []
    for i, a in enumerate(arrays):
        pieces += [(i, k) for k in range(a.shape[0])] if a.ndim == 3 else [(i, None)]

    def kernel(*refs):
        sources, (table, scalars) = refs[:count], refs[count : count + 2]
        targets = refs[count + 2 : 2 * count + 2]
        gains, shifts, rms = refs[2 * count + 2 : 2 * count + 5]
        held = refs[2 * count + 5 : 3 * count + 5]
        in_sem, out_sem = refs[3 * count + 5 :]

        def pick(ref, k):
            return ref if k is None else ref.at[k]

        ins = [pltpu.make_async_copy(pick(sources[i], k), pick(held[i], k), in_sem.at[n]) for n, (i, k) in enumerate(pieces)]
        outs = [pltpu.make_async_copy(pick(held[i], k), pick(targets[i], k), out_sem.at[n]) for n, (i, k) in enumerate(pieces)]
        for cp in ins:
            cp.start()
        fr = lax.axis_index("frames")
        mine = jnp.zeros((8, width), F32)
        for f in range(LANES // width):
            mine = jnp.where(fr == f, table[0:8, f * width : (f + 1) * width], mine)
        gains[...] = mine[0:4]
        shifts[...] = mine[4:8]
        for i in range(4):
            rms[i] = scalars[8 + i, 0]
        for a, b in zip(ins, outs):
            a.wait()
            b.start()
        for b in outs:
            b.wait()

    small = jax.ShapeDtypeStruct((4, width), F32)
    return pl.pallas_call(
        kernel,
        out_shape=[jax.ShapeDtypeStruct(a.shape, a.dtype) for a in arrays] + [small, small, jax.ShapeDtypeStruct((4,), F32)],
        in_specs=[at(pl.ANY)] * count + [at(pltpu.VMEM), at(pltpu.SMEM)],
        out_specs=[at(pl.ANY)] * count + [at(pltpu.VMEM)] * 2 + [at(pltpu.SMEM)],
        scratch_shapes=[pltpu.VMEM(a.shape, a.dtype) for a in arrays]
        + [pltpu.SemaphoreType.DMA((len(pieces),)), pltpu.SemaphoreType.DMA((len(pieces),))],
        compiler_params=pltpu.CompilerParams(vmem_limit_bytes=VMEM_BYTES),
    )(*arrays, norm_out, norm_out)


CHUNKS = 16
Z_CHIPS = 4


def frame_bias(cross_mask, memory_length, frame_count, padded):
    start = lax.axis_index("frames") * frame_count
    items = cross_mask.shape[0]
    wide = jnp.pad(cross_mask, ((0, 8 - items), (0, padded - frame_count)))
    mask = lax.dynamic_slice_in_dim(wide, start, padded, 1)
    lengths = jnp.pad(memory_length, (0, 8 - items))
    offset = jnp.arange(padded)[None]
    at = start + offset
    ok = (offset < frame_count) & (at < lengths[:, None]) & ((mask == 1) | (at == 0))
    return jnp.where(ok, 0.0, -1e30).astype(F32)


def local_fused(
    tokens,
    memory,
    cotangent,
    self_project,
    self_output,
    cross_query,
    cross_memory,
    cross_output,
    expand,
    contract,
    norm_gains,
    norm_shifts,
    target_length,
    memory_length,
    cross_mask,
):
    items, frame_count, d = memory.shape
    slab = self_output.shape[0]
    group = 4 * slab
    parts = -(-frame_count // group)
    padded = parts * group
    rolled = jnp.pad(memory, ((0, 0), (0, padded - frame_count), (0, 0))).reshape(items, parts, 2, 2, slab, d)
    o = fused(
        Z_CHIPS,
        CHUNKS,
        frame_count,
        tl=target_length,
        tokens=tokens[0],
        cotangent=cotangent[0],
        memory=rolled,
        self_project=self_project,
        self_output=self_output,
        cross_query=cross_query,
        cross_memory=cross_memory,
        cross_output=cross_output,
        expand=expand,
        contract=contract,
        norm_gains=norm_gains,
        norm_shifts=norm_shifts,
        bias=frame_bias(cross_mask, memory_length, frame_count, padded),
    )
    large = [o[k] for k in ("result", "tokens_grad", "memory_grad")] + [o[k + "_grad"] for k in GRADS]
    done = settle(large, o["norm_out"], norm_gains.shape[1])
    return (done[0][None], done[1][None], *done[2:])


block_heads = 4


def layer_norm(values, gain_row, shift_row):
    center = values - jnp.mean(values, axis=-1, keepdims=True)
    spread = jnp.mean(center * center, axis=-1, keepdims=True)
    return center * lax.rsqrt(spread + 1e-05) * gain_row + shift_row


def exact_gelu(values):
    return jax.nn.gelu(values, approximate=False)


def matmul(left_side, right_side):
    return jnp.dot(left_side, right_side, preferred_element_type=jnp.float32)


def split_heads(rows):
    return rows.reshape(rows.shape[:-1] + (rows.shape[-1] // HEAD_DIM, HEAD_DIM))


def to_blocks(rows):
    row_count, head_count, head_width = rows.shape
    return rows.reshape(row_count, head_count // block_heads, block_heads, head_width).transpose(
        1, 0, 2, 3
    )


def from_blocks(blocks):
    group_count, row_count, head_count, head_width = blocks.shape
    return blocks.transpose(1, 0, 2, 3).reshape(row_count, group_count * head_count * head_width)


def block_scores(query_block, key_block, allowed):
    factor = query_block.shape[-1] ** (-0.5)
    raw_scores = (
        jnp.einsum("shd,fhd->hsf", query_block, key_block, preferred_element_type=jnp.float32)
        * factor
    )
    return jnp.where(allowed[None], raw_scores, -1e30)


def block_probs(query_block, key_block, allowed, max_block, total_block):
    scores = block_scores(query_block, key_block, allowed)
    shifted = jnp.where(allowed[None], jnp.exp(scores - max_block[..., None]), 0.0)
    return shifted / total_block[..., None]


def block_grads(query_block, key_block, grad_block, probs, grad_probs, row_dot):
    factor = query_block.shape[-1] ** (-0.5)
    score_grad = (probs * (grad_probs - row_dot)).astype(jnp.bfloat16)
    query_grad = (
        jnp.einsum("hsf,fhd->shd", score_grad, key_block, preferred_element_type=jnp.float32)
        * factor
    )
    key_grad = (
        jnp.einsum("hsf,shd->fhd", score_grad, query_block, preferred_element_type=jnp.float32)
        * factor
    )
    value_grad = jnp.einsum(
        "hsf,shd->fhd", probs.astype(jnp.bfloat16), grad_block, preferred_element_type=jnp.float32
    )
    return (query_grad, key_grad, value_grad)


def attend_whole(query_rows, key_rows, value_rows, allowed):

    def one_group(blocks):
        query_block, key_block, value_block = blocks
        scores = block_scores(query_block, key_block, allowed)
        max_block = jnp.max(scores, axis=-1)
        shifted = jnp.where(allowed[None], jnp.exp(scores - max_block[..., None]), 0.0)
        total_block = jnp.sum(shifted, axis=-1)
        weights = (shifted / total_block[..., None]).astype(jnp.bfloat16)
        mixture = jnp.einsum(
            "hsf,fhd->shd", weights, value_block, preferred_element_type=jnp.float32
        )
        return (mixture, max_block, total_block)

    mixture, row_max, totals = lax.map(
        one_group, (to_blocks(query_rows), to_blocks(key_rows), to_blocks(value_rows))
    )
    return (from_blocks(mixture), row_max, totals)


def attend_whole_back(query_rows, key_rows, value_rows, allowed, grad_rows, row_max, totals):

    def one_group(blocks):
        query_block, key_block, value_block, grad_block, max_block, total_block = blocks
        probs = block_probs(query_block, key_block, allowed, max_block, total_block)
        grad_probs = jnp.einsum(
            "shd,fhd->hsf", grad_block, value_block, preferred_element_type=jnp.float32
        )
        row_dot = jnp.sum(probs * grad_probs, axis=-1, keepdims=True)
        return block_grads(query_block, key_block, grad_block, probs, grad_probs, row_dot)

    query_grad, key_grad, value_grad = lax.map(
        one_group,
        (
            to_blocks(query_rows),
            to_blocks(key_rows),
            to_blocks(value_rows),
            to_blocks(grad_rows),
            row_max,
            totals,
        ),
    )
    return (from_blocks(query_grad), from_blocks(key_grad), from_blocks(value_grad))


def cross_stats(query_rows, key_rows, allowed):

    def one_group(blocks):
        query_block, key_block = blocks
        scores = block_scores(query_block, key_block, allowed)
        max_block = jnp.max(scores, axis=-1)
        total_block = jnp.sum(
            jnp.where(allowed[None], jnp.exp(scores - max_block[..., None]), 0.0), axis=-1
        )
        return (max_block, total_block)

    return lax.map(one_group, (to_blocks(query_rows), to_blocks(key_rows)))


def cross_partial(query_rows, key_rows, value_rows, allowed, row_max, totals):

    def one_group(blocks):
        query_block, key_block, value_block, max_block, total_block = blocks
        probs = block_probs(query_block, key_block, allowed, max_block, total_block)
        return jnp.einsum(
            "hsf,fhd->shd",
            probs.astype(jnp.bfloat16),
            value_block,
            preferred_element_type=jnp.float32,
        )

    return from_blocks(
        lax.map(
            one_group,
            (to_blocks(query_rows), to_blocks(key_rows), to_blocks(value_rows), row_max, totals),
        )
    )


def cross_row_dot(query_rows, key_rows, value_rows, allowed, grad_rows, row_max, totals):

    def one_group(blocks):
        query_block, key_block, value_block, grad_block, max_block, total_block = blocks
        probs = block_probs(query_block, key_block, allowed, max_block, total_block)
        grad_probs = jnp.einsum(
            "shd,fhd->hsf", grad_block, value_block, preferred_element_type=jnp.float32
        )
        return jnp.sum(probs * grad_probs, axis=-1)

    return lax.map(
        one_group,
        (
            to_blocks(query_rows),
            to_blocks(key_rows),
            to_blocks(value_rows),
            to_blocks(grad_rows),
            row_max,
            totals,
        ),
    )


def cross_partial_grads(
    query_rows, key_rows, value_rows, allowed, grad_rows, row_max, totals, row_dot
):

    def one_group(blocks):
        query_block, key_block, value_block, grad_block, max_block, total_block, dot_block = blocks
        probs = block_probs(query_block, key_block, allowed, max_block, total_block)
        grad_probs = jnp.einsum(
            "shd,fhd->hsf", grad_block, value_block, preferred_element_type=jnp.float32
        )
        return block_grads(
            query_block, key_block, grad_block, probs, grad_probs, dot_block[..., None]
        )

    query_grad, key_grad, value_grad = lax.map(
        one_group,
        (
            to_blocks(query_rows),
            to_blocks(key_rows),
            to_blocks(value_rows),
            to_blocks(grad_rows),
            row_max,
            totals,
            row_dot,
        ),
    )
    return (from_blocks(query_grad), from_blocks(key_grad), from_blocks(value_grad))


def local(
    tokens,
    memory,
    cotangent,
    self_project,
    self_output,
    cross_query,
    cross_memory,
    cross_output,
    expand,
    contract,
    norm_gains,
    norm_shifts,
    target_length,
    memory_length,
    cross_mask,
):
    gathered = (
        lax.all_gather(self_project, ("dp", "frames"), axis=0, tiled=True),
        lax.all_gather(self_output, ("dp", "frames"), axis=0, tiled=True),
        lax.all_gather(cross_query, ("dp", "frames"), axis=0, tiled=True),
        lax.all_gather(cross_memory, ("dp", "frames"), axis=0, tiled=True),
        lax.all_gather(cross_output, ("dp", "frames"), axis=0, tiled=True),
        lax.all_gather(expand, ("dp", "frames"), axis=0, tiled=True),
        lax.all_gather(contract, ("dp", "frames"), axis=0, tiled=True),
        lax.all_gather(norm_gains, ("dp", "frames"), axis=1, tiled=True),
        lax.all_gather(norm_shifts, ("dp", "frames"), axis=1, tiled=True),
    )
    (
        w_self,
        w_self_out,
        w_query,
        w_memory,
        w_cross_out,
        w_expand,
        w_contract,
        gains_low,
        shifts_low,
    ) = gathered
    gains = gains_low.astype(jnp.float32)
    shifts = shifts_low.astype(jnp.float32)
    model_width = w_self_out.shape[0]
    residual_in = tokens[0]
    length = residual_in.shape[0]
    positions = jnp.arange(length)
    row_valid = positions < target_length[0]
    causal = positions[:, None] >= positions[None, :]
    item_count = memory.shape[0]
    frame_count = memory.shape[1]
    own_item = lax.axis_index("frames")
    normed_one_f, back_one = jax.vjp(layer_norm, residual_in, gains[0], shifts[0])
    normed_one = normed_one_f.astype(jnp.bfloat16)
    joint_rows = matmul(normed_one, w_self).astype(jnp.bfloat16)
    self_queries = split_heads(joint_rows[:, :model_width])
    self_keys = split_heads(joint_rows[:, model_width : 2 * model_width])
    self_values = split_heads(joint_rows[:, 2 * model_width :])
    self_mix, self_max, self_totals = attend_whole(self_queries, self_keys, self_values, causal)
    self_mix_low = self_mix.astype(jnp.bfloat16)
    self_branch = matmul(self_mix_low, w_self_out)
    first_sum = residual_in + self_branch
    normed_two_f, back_two = jax.vjp(layer_norm, first_sum, gains[1], shifts[1])
    normed_two = normed_two_f.astype(jnp.bfloat16)
    cross_queries = matmul(normed_two, w_query).astype(jnp.bfloat16)
    every_query = lax.all_gather(cross_queries[None], "frames", axis=0, tiled=True)
    query_heads = split_heads(every_query)
    frame_start = own_item * frame_count
    local_frames = frame_start + jnp.arange(frame_count)
    local_mask = lax.dynamic_slice_in_dim(cross_mask, frame_start, frame_count, 1)
    frame_ok = (local_frames[None, :] < memory_length[:, None]) & (
        (local_mask == 1) | (local_frames[None, :] == 0)
    )
    memory_rows = matmul(memory.reshape(item_count * frame_count, model_width), w_memory).astype(
        jnp.bfloat16
    )
    memory_rows = memory_rows.reshape(item_count, frame_count, 2 * model_width)
    memory_keys = split_heads(memory_rows[..., :model_width])
    memory_values = split_heads(memory_rows[..., model_width:])

    def item_stats(inputs):
        query_item, key_item, frame_item = inputs
        return cross_stats(
            query_item, key_item, jnp.broadcast_to(frame_item[None, :], (length, frame_count))
        )

    local_max, local_totals = lax.map(item_stats, (query_heads, memory_keys, frame_ok))
    cross_max = lax.pmax(local_max.astype(jnp.bfloat16), "frames").astype(local_max.dtype)
    cross_totals = lax.psum(
        (local_totals * jnp.exp(local_max - cross_max)).astype(jnp.bfloat16), "frames"
    ).astype(jnp.float32)

    def item_partial(inputs):
        query_item, key_item, value_item, frame_item, max_item, total_item = inputs
        allowed = jnp.broadcast_to(frame_item[None, :], (length, frame_count))
        return cross_partial(query_item, key_item, value_item, allowed, max_item, total_item)

    partial_mix = lax.map(
        item_partial, (query_heads, memory_keys, memory_values, frame_ok, cross_max, cross_totals)
    )
    cross_mix = lax.psum_scatter(
        partial_mix.astype(jnp.bfloat16), "frames", scatter_dimension=0, tiled=True
    ).astype(jnp.float32)[0]
    cross_mix_low = cross_mix.astype(jnp.bfloat16)
    cross_branch = matmul(cross_mix_low, w_cross_out)
    second_sum = first_sum + cross_branch
    normed_three_f, back_three = jax.vjp(layer_norm, second_sum, gains[2], shifts[2])
    normed_three = normed_three_f.astype(jnp.bfloat16)
    hidden = matmul(normed_three, w_expand)
    active_f, gelu_back = jax.vjp(exact_gelu, hidden)
    active = active_f.astype(jnp.bfloat16)
    feed_branch = matmul(active, w_contract)
    third_sum = second_sum + feed_branch
    final_rows, back_final = jax.vjp(layer_norm, third_sum, gains[3], shifts[3])
    result = jnp.where(row_valid[:, None], final_rows, 0.0)
    row_weight = row_valid.astype(jnp.float32)[:, None]
    squares = jnp.stack(
        [
            jnp.sum(row_weight * member * member)
            for member in (third_sum, self_branch, cross_branch, feed_branch)
        ]
    )
    squares_all, counted = lax.psum((squares, jnp.sum(row_weight)), ("dp", "frames"))
    branch_rms = jnp.sqrt(squares_all / (counted * model_width))
    grad_result = jnp.where(row_valid[:, None], cotangent[0], 0.0)
    grad_third, gain_grad_three, shift_grad_three = back_final(grad_result)
    feed_low = grad_third.astype(jnp.bfloat16)
    contract_grad = matmul(active.T, feed_low)
    grad_active = matmul(feed_low, w_contract.T)
    grad_hidden = gelu_back(grad_active)[0].astype(jnp.bfloat16)
    expand_grad = matmul(normed_three.T, grad_hidden)
    grad_normed_three = matmul(grad_hidden, w_expand.T)
    grad_second_part, gain_grad_two, shift_grad_two = back_three(grad_normed_three)
    grad_second = grad_third + grad_second_part
    cross_low = grad_second.astype(jnp.bfloat16)
    cross_output_grad = matmul(cross_mix_low.T, cross_low)
    grad_cross_mix = matmul(cross_low, w_cross_out.T).astype(jnp.bfloat16)
    every_grad = split_heads(lax.all_gather(grad_cross_mix[None], "frames", axis=0, tiled=True))

    def item_dot(inputs):
        query_item, key_item, value_item, frame_item, grad_item, max_item, total_item = inputs
        allowed = jnp.broadcast_to(frame_item[None, :], (length, frame_count))
        return cross_row_dot(
            query_item, key_item, value_item, allowed, grad_item, max_item, total_item
        )

    local_dot = lax.map(
        item_dot,
        (query_heads, memory_keys, memory_values, frame_ok, every_grad, cross_max, cross_totals),
    )
    row_dot = lax.psum(local_dot.astype(jnp.bfloat16), "frames").astype(jnp.float32)

    def item_grads(inputs):
        query_item, key_item, value_item, frame_item, grad_item, max_item, total_item, dot_item = (
            inputs
        )
        allowed = jnp.broadcast_to(frame_item[None, :], (length, frame_count))
        return cross_partial_grads(
            query_item, key_item, value_item, allowed, grad_item, max_item, total_item, dot_item
        )

    query_parts, key_parts, value_parts = lax.map(
        item_grads,
        (
            query_heads,
            memory_keys,
            memory_values,
            frame_ok,
            every_grad,
            cross_max,
            cross_totals,
            row_dot,
        ),
    )
    query_grad = lax.psum_scatter(
        query_parts.astype(jnp.bfloat16), "frames", scatter_dimension=0, tiled=True
    ).astype(jnp.float32)[0]
    memory_low = (
        jnp.concatenate([key_parts, value_parts], axis=2)
        .astype(jnp.bfloat16)
        .reshape(item_count * frame_count, 2 * model_width)
    )
    cross_memory_grad = matmul(memory.reshape(item_count * frame_count, model_width).T, memory_low)
    memory_grad = matmul(memory_low, w_memory.T).reshape(item_count, frame_count, model_width)
    query_low = query_grad.astype(jnp.bfloat16)
    cross_query_grad = matmul(normed_two.T, query_low)
    grad_normed_two = matmul(query_low, w_query.T)
    grad_first_part, gain_grad_one, shift_grad_one = back_two(grad_normed_two)
    grad_first = grad_second + grad_first_part
    self_low = grad_first.astype(jnp.bfloat16)
    self_output_grad = matmul(self_mix_low.T, self_low)
    grad_self_mix = matmul(self_low, w_self_out.T).astype(jnp.bfloat16)
    self_query_grad, self_key_grad, self_value_grad = attend_whole_back(
        self_queries,
        self_keys,
        self_values,
        causal,
        split_heads(grad_self_mix),
        self_max,
        self_totals,
    )
    joint_grad = jnp.concatenate([self_query_grad, self_key_grad, self_value_grad], axis=1).astype(
        jnp.bfloat16
    )
    self_project_grad = matmul(normed_one.T, joint_grad)
    grad_normed_one = matmul(joint_grad, w_self.T)
    grad_input_part, gain_grad_zero, shift_grad_zero = back_one(grad_normed_one)
    tokens_grad = grad_first + grad_input_part
    gain_grads = jnp.stack([gain_grad_zero, gain_grad_one, gain_grad_two, gain_grad_three])
    shift_grads = jnp.stack([shift_grad_zero, shift_grad_one, shift_grad_two, shift_grad_three])
    reduced = (
        lax.psum_scatter(self_project_grad, ("dp", "frames"), scatter_dimension=0, tiled=True),
        lax.psum_scatter(self_output_grad, ("dp", "frames"), scatter_dimension=0, tiled=True),
        lax.psum_scatter(cross_query_grad, ("dp", "frames"), scatter_dimension=0, tiled=True),
        lax.psum_scatter(cross_memory_grad, ("dp", "frames"), scatter_dimension=0, tiled=True),
        lax.psum_scatter(cross_output_grad, ("dp", "frames"), scatter_dimension=0, tiled=True),
        lax.psum_scatter(expand_grad, ("dp", "frames"), scatter_dimension=0, tiled=True),
        lax.psum_scatter(contract_grad, ("dp", "frames"), scatter_dimension=0, tiled=True),
        lax.psum_scatter(gain_grads, ("dp", "frames"), scatter_dimension=1, tiled=True),
        lax.psum_scatter(shift_grads, ("dp", "frames"), scatter_dimension=1, tiled=True),
    )
    (
        project_part,
        output_part,
        query_part,
        memory_part,
        cross_out_part,
        expand_part,
        contract_part,
        gains_part,
        shifts_part,
    ) = reduced
    return (
        result[None],
        tokens_grad[None],
        memory_grad,
        project_part,
        output_part,
        query_part,
        memory_part,
        cross_out_part,
        expand_part,
        contract_part,
        gains_part,
        shifts_part,
        branch_rms,
    )


def solution(mesh):
    fits = (mesh.shape["dp"], mesh.shape["frames"]) == (2 * Z_CHIPS, 4)
    return jax.shard_map(
        local_fused if fits else local,
        mesh=mesh,
        in_specs=(
            P(("dp", "frames"), None, None),
            P("dp", "frames", None),
            P(("dp", "frames"), None, None),
            P(("dp", "frames"), None),
            P(("dp", "frames"), None),
            P(("dp", "frames"), None),
            P(("dp", "frames"), None),
            P(("dp", "frames"), None),
            P(("dp", "frames"), None),
            P(("dp", "frames"), None),
            P(None, ("dp", "frames")),
            P(None, ("dp", "frames")),
            P(("dp", "frames")),
            P("dp"),
            P("dp", None),
        ),
        out_specs=(
            P(("dp", "frames"), None, None),
            P(("dp", "frames"), None, None),
            P("dp", "frames", None),
            P(("dp", "frames"), None),
            P(("dp", "frames"), None),
            P(("dp", "frames"), None),
            P(("dp", "frames"), None),
            P(("dp", "frames"), None),
            P(("dp", "frames"), None),
            P(("dp", "frames"), None),
            P(None, ("dp", "frames")),
            P(None, ("dp", "frames")),
            P(),
        ),
        check_vma=False,
    )
```

```python
import functools
from types import SimpleNamespace

import jax
import jax.numpy as jnp
from jax import lax
from jax.experimental import pallas as pl
from jax.experimental.pallas import tpu as pltpu
from jax.sharding import PartitionSpec as P

MESH = pl.DeviceIdType.MESH
F32 = jnp.float32
BF16 = jnp.bfloat16
HEAD_DIM = 64
LANES = 128
WIDE = 512


def dot(a, b):
    return jnp.dot(a, b, preferred_element_type=F32)


def dot_nt(a, b):
    return lax.dot_general(a, b, (((1,), (1,)), ((), ())), preferred_element_type=F32)


def place():
    dp, fr = lax.axis_index("dp"), lax.axis_index("frames")
    z, y = lax.div(dp, 2), lax.rem(dp, 2)
    x, c = lax.div(fr, 2), lax.rem(fr, 2)

    def dev(zz, yy, xx, cc):
        return {"dp": zz * 2 + yy, "frames": xx * 2 + cc}

    me = SimpleNamespace(z=z, y=y, x=x, c=c, fr=fr, dev=dev)
    me.xn = dev(z, y, 1 - x, c)
    me.yn = dev(z, 1 - y, x, c)
    me.sib = dev(z, y, x, 1 - c)
    me.diag = dev(z, y, 1 - x, 1 - c)
    return me


def remote(src, dst, send, recv, device):
    return pltpu.make_async_remote_copy(
        src_ref=src, dst_ref=dst, send_sem=send, recv_sem=recv, device_id=device, device_id_type=MESH
    )


def z_ways(me, nz):
    sends = {dz: (me.z != nz - 1) if dz == 1 else (me.z != 0) if dz == nz - 1 else None for dz in range(1, nz)}
    inner = (me.z == 1) | (me.z == 2)
    upper = me.z == 2
    return sends, inner, lax.rem(me.z + 2, nz), jnp.where(upper, nz - 1, 0), jnp.where(upper, nz - 1, 1)


def when(condition, action):
    if condition is None:
        action()
    else:
        pl.when(condition)(action)


def gather_steps(me, w, send, recv, nz, tilt=False):
    half = w.shape[4] if tilt else w.shape[4] // 2
    xo, yo, co = 1 - me.x, 1 - me.y, 1 - me.c

    def cp(view, s, device):
        return remote(view, view, send.at[s], recv.at[s], device)

    def spot(y, x, c):
        return w.at[:, y, x, c]

    def one(dz, y, x):
        return w.at[lax.rem(me.z + nz - dz, nz), y, x, me.c]

    def part(y, x, lower):
        return w.at[:, y, x, me.c, 0:half] if lower else w.at[:, y, x, me.c, half:]

    sends, inner, source, target, distance = z_ways(me, nz)
    passed = w.at[source, me.y, me.x, me.c]

    def pass_copy():
        to = me.dev(target, me.y, me.x, me.c)
        return remote(passed, passed, send.at[nz + 7], recv.at[distance - 1], to)

    def z_copy(dz):
        return cp(one(0, me.y, me.x), dz - 1, me.dev(lax.rem(me.z + dz, nz), me.y, me.x, me.c))

    def z_arrived(dz):
        cp(one(dz, me.y, me.x), dz - 1, me.xn).wait_recv()

    def step_z():
        for dz in range(1, nz):
            when(sends[dz], lambda: z_copy(dz).start())

    def step_relay():
        @pl.when(inner)
        def _():
            z_arrived(2)
            pass_copy().start()

    def step_near():
        z_arrived(1)
        z_arrived(3)
        pl.when(jnp.logical_not(inner))(lambda: z_arrived(2))
        cp(spot(me.y, me.x, me.c), nz - 1, me.xn).start()
        cp(spot(me.y, me.x, me.c), nz, me.yn).start()
        cp(spot(me.y, me.x, me.c), nz + 1, me.sib).start()

    def step_far():
        cp(spot(me.y, xo, me.c), nz - 1, me.xn).wait_recv()
        cp(part(me.y, xo, True), nz + 2, me.yn).start()
        cp(spot(me.y, xo, me.c), nz + 3, me.sib).start()
        cp(spot(yo, me.x, me.c), nz, me.yn).wait_recv()
        if not tilt:
            cp(part(yo, me.x, False), nz + 4, me.xn).start()
        cp(spot(yo, me.x, me.c), nz + 5, me.sib).start()

    def step_last():
        cp(part(yo, xo, True), nz + 2, me.yn).wait_recv()
        if not tilt:
            cp(part(yo, xo, False), nz + 4, me.xn).wait_recv()
        cp(spot(yo, xo, me.c), nz + 6, me.sib).start()

    def step_done():
        for y, x, s in ((me.y, me.x, nz + 1), (me.y, xo, nz + 3), (yo, me.x, nz + 5), (yo, xo, nz + 6)):
            cp(spot(y, x, co), s, me.sib).wait_recv()

    def drain():
        for dz in range(1, nz):
            when(sends[dz], lambda: z_copy(dz).wait_send())
        pl.when(inner)(lambda: pass_copy().wait_send())
        for s in (nz - 1, nz):
            cp(spot(me.y, me.x, me.c), s, me.xn).wait_send()
        for y, x, s in ((me.y, me.x, nz + 1), (me.y, xo, nz + 3), (yo, me.x, nz + 5), (yo, xo, nz + 6)):
            cp(spot(y, x, me.c), s, me.xn).wait_send()
        cp(part(me.y, xo, True), nz + 2, me.xn).wait_send()
        if not tilt:
            cp(part(yo, me.x, False), nz + 4, me.xn).wait_send()

    return SimpleNamespace(
        z=step_z, relay=step_relay, near=step_near, far=step_far, last=step_last, done=step_done, drain=drain
    )


def gather_late_steps(me, w, send, recv, nz):
    half = w.shape[4] // 2
    xo, yo, co = 1 - me.x, 1 - me.y, 1 - me.c

    def cp(view, s, device):
        return remote(view, view, send.at[s], recv.at[s], device)

    def one(y, x):
        return w.at[me.z, y, x, me.c]

    def part(y, x, lower):
        return w.at[me.z, y, x, me.c, 0:half] if lower else w.at[me.z, y, x, me.c, half:]

    def layer(dz, c):
        return w.at[lax.rem(me.z + nz - dz, nz), :, :, c]

    def step_near():
        cp(one(me.y, me.x), 0, me.xn).start()
        cp(one(me.y, me.x), 1, me.yn).start()

    def step_far():
        cp(one(me.y, xo), 0, me.xn).wait_recv()
        cp(part(me.y, xo, True), 2, me.yn).start()
        cp(one(yo, me.x), 1, me.yn).wait_recv()
        cp(part(yo, me.x, False), 3, me.xn).start()

    def step_square():
        cp(part(yo, xo, True), 2, me.yn).wait_recv()
        cp(part(yo, xo, False), 3, me.xn).wait_recv()
        cp(layer(0, me.c), 4, me.sib).start()

    sends, inner, source, target, distance = z_ways(me, nz)
    passed = w.at[source, :, :, me.c]

    def pass_copy():
        to = me.dev(target, me.y, me.x, me.c)
        return remote(passed, passed, send.at[nz + 7], recv.at[4 + distance], to)

    def z_copy(dz):
        return cp(layer(0, me.c), 4 + dz, me.dev(lax.rem(me.z + dz, nz), me.y, me.x, me.c))

    def step_z(dz):
        when(sends[dz], lambda: z_copy(dz).start())

    def step_pass(dz):
        cp(layer(dz, me.c), 4 + dz, me.xn).wait_recv()
        if dz == 2:
            pl.when(inner)(lambda: pass_copy().start())
        cp(layer(dz, me.c), 3 + nz + dz, me.sib).start()

    def step_done():
        cp(layer(0, co), 4, me.sib).wait_recv()
        for dz in range(1, nz):
            cp(layer(dz, co), 3 + nz + dz, me.sib).wait_recv()

    def drain():
        cp(one(me.y, me.x), 0, me.xn).wait_send()
        cp(one(me.y, me.x), 1, me.xn).wait_send()
        cp(part(me.y, xo, True), 2, me.xn).wait_send()
        cp(part(yo, me.x, False), 3, me.xn).wait_send()
        cp(layer(0, me.c), 4, me.xn).wait_send()
        for dz in range(1, nz):
            when(sends[dz], lambda: z_copy(dz).wait_send())
            cp(layer(dz, me.c), 3 + nz + dz, me.xn).wait_send()
        pl.when(inner)(lambda: pass_copy().wait_send())

    return SimpleNamespace(
        near=step_near, far=step_far, square=step_square, z=step_z, pass_on=step_pass, done=step_done, drain=drain
    )


class Moves:
    def __init__(self, moves, send, recv, core_recv):
        self.moves, self.send, self.recv, self.core_recv = moves, send, recv, core_recv

    def cp(self, i):
        src, dst, to = self.moves[i][:3]
        return remote(src, dst, self.send.at[i], self.recv.at[i - 1] if i else self.core_recv, to)

    def go(self, i):
        _, _, _, _, credit, turn, slots, _ = self.moves[i]
        if turn >= slots:
            pl.semaphore_wait(credit, 1)
        self.cp(i).start()

    def free(self, i):
        _, _, _, giver, credit, turn, slots, turns = self.moves[i]
        if turn + slots < turns:
            pl.semaphore_signal(credit, inc=1, device_id=giver, device_id_type=MESH)

    def arrive(self, *at):
        for i in at:
            self.cp(i).wait_recv()

    def drain(self):
        for i in range(len(self.moves)):
            self.cp(i).wait_send()


def add(view, arrived):
    view[...] = (view[...].astype(F32) + arrived[...].astype(F32)).astype(view.dtype)


def add_core(me, w, core, nz):
    def body(zz, carry):
        for y in range(2):
            for x in range(2):
                add(w.at[zz, y, x, me.c], core.at[zz, y, x])
        return carry

    lax.fori_loop(0, nz, body, 0)


def scatter_steps(me, w, box, sems, credit, nz, core_turn, turn, sink):
    half = w.shape[4] // 2
    xo, yo, co = 1 - me.x, 1 - me.y, 1 - me.c
    core = box[0].at[core_turn[0] % core_turn[1]]
    y1, x1, x2, y2, zs = (b.at[turn[0] % turn[1]] for b in box[1:])

    def at_z(dz):
        return me.dev(lax.rem(me.z + nz + dz, nz), me.y, me.x, me.c)

    moves = [
        (w.at[:, :, :, co], core, me.sib, me.sib, credit.at[0], *core_turn),
        (w.at[:, yo, :, me.c, 0:half], y1, me.yn, me.yn, credit.at[1], *turn),
        (w.at[:, :, xo, me.c, half:], x1, me.xn, me.xn, credit.at[2], *turn),
        (w.at[:, me.y, xo, me.c, 0:half], x2, me.xn, me.xn, credit.at[3], *turn),
        (w.at[:, yo, me.x, me.c, half:], y2, me.yn, me.yn, credit.at[4], *turn),
    ]
    for dz in range(1, nz):
        slab = w.at[lax.rem(me.z + dz, nz), me.y, me.x, me.c]
        moves.append((slab, zs.at[dz - 1], at_z(dz), at_z(-dz), credit.at[4 + dz], *turn))
    m = Moves(moves, *sems)

    def step_a():
        m.go(0)

    def step_b():
        m.arrive(0)
        add_core(me, w, core, nz)
        m.free(0)
        m.go(1)
        m.go(2)

    def step_c():
        m.arrive(1, 2)

        def body(zz, carry):
            for o in range(2):
                add(w.at[zz, me.y, o, me.c, 0:half], y1.at[zz, o])
                add(w.at[zz, o, me.x, me.c, half:], x1.at[zz, o])
            return carry

        lax.fori_loop(0, nz, body, 0)
        m.free(1)
        m.free(2)
        m.go(3)
        m.go(4)

    def step_d():
        m.arrive(3, 4)

        def body(zz, carry):
            add(w.at[zz, me.y, me.x, me.c, 0:half], x2.at[zz])
            add(w.at[zz, me.y, me.x, me.c, half:], y2.at[zz])
            return carry

        lax.fori_loop(0, nz, body, 0)
        m.free(3)
        m.free(4)
        for dz in range(1, nz):
            m.go(4 + dz)

    def step_e():
        total = w[me.z, me.y, me.x, me.c].astype(F32)
        for dz in range(1, nz):
            m.arrive(4 + dz)
            total = total + zs[dz - 1].astype(F32)
        sink(total)
        for dz in range(1, nz):
            m.free(4 + dz)

    return SimpleNamespace(a=step_a, b=step_b, c=step_c, d=step_d, e=step_e, drain=m.drain)


def scatter_early_steps(me, w, box, sems, credit, nz, core_turn, turn, sink):
    half = w.shape[4] // 2
    xo, yo, co = 1 - me.x, 1 - me.y, 1 - me.c
    core = box[0].at[core_turn[0] % core_turn[1]]
    y1, x1, x2, y2, zs = (b.at[turn[0] % turn[1]] for b in box[1:])

    def at_z(dz):
        return me.dev(lax.rem(me.z + nz + dz, nz), me.y, me.x, me.c)

    moves = [
        (w.at[:, :, :, co], core, me.sib, me.sib, credit.at[0], *core_turn),
        (w.at[me.z, yo, :, me.c, 0:half], y1, me.yn, me.yn, credit.at[nz + 4], *turn),
        (w.at[me.z, :, xo, me.c, half:], x1, me.xn, me.xn, credit.at[nz + 5], *turn),
        (w.at[me.z, me.y, xo, me.c, 0:half], x2, me.xn, me.xn, credit.at[nz + 6], *turn),
        (w.at[me.z, yo, me.x, me.c, half:], y2, me.yn, me.yn, credit.at[nz + 7], *turn),
    ]
    for dz in range(1, nz):
        layer = w.at[lax.rem(me.z + dz, nz), :, :, me.c]
        moves.append((layer, zs.at[dz - 1], at_z(dz), at_z(-dz), credit.at[nz + 7 + dz], *turn))
    m = Moves(moves, *sems)

    def step_a():
        m.go(0)

    def step_b():
        m.arrive(0)
        add_core(me, w, core, nz)
        m.free(0)

    def step_z(dz):
        m.go(4 + dz)

    def step_c():
        for dz in range(1, nz):
            m.arrive(4 + dz)
            for y in range(2):
                for x in range(2):
                    add(w.at[me.z, y, x, me.c], zs.at[dz - 1, y, x])
            m.free(4 + dz)
        m.go(1)
        m.go(2)

    def step_d():
        m.arrive(1, 2)
        for o in range(2):
            add(w.at[me.z, me.y, o, me.c, 0:half], y1.at[o])
            add(w.at[me.z, o, me.x, me.c, half:], x1.at[o])
        m.free(1)
        m.free(2)
        m.go(3)
        m.go(4)

    def step_e():
        m.arrive(3, 4)
        late = jnp.concatenate([x2[...].astype(F32), y2[...].astype(F32)], axis=0)
        sink(w[me.z, me.y, me.x, me.c].astype(F32) + late)
        m.free(3)
        m.free(4)

    return SimpleNamespace(a=step_a, b=step_b, z=step_z, c=step_c, d=step_d, e=step_e, drain=m.drain)


def lane_masks():
    lane = lax.broadcasted_iota(jnp.int32, (1, LANES), 1)
    left = jnp.where(lane < HEAD_DIM, 1.0, 0.0).astype(BF16)
    return left, (1.0 - left.astype(F32)).astype(BF16)


def two_heads(block):
    left, right = lane_masks()
    return jnp.concatenate([block * left, block * right], axis=0)


def one_block(pair):
    rows = pair.shape[0] // 2
    lane = lax.broadcasted_iota(jnp.int32, (rows, LANES), 1)
    return jnp.where(lane < HEAD_DIM, pair[:rows], pair[rows:])


def at128(p, base=0):
    return pl.ds(pl.multiple_of(base + p * LANES, LANES), LANES)


def put_stat(stat, p, pair):
    rows = pair.shape[0] // 2
    lane = lax.broadcasted_iota(jnp.int32, stat.shape, 1)
    stat = jnp.where(lane == 2 * p, pair[:rows], stat)
    return jnp.where(lane == 2 * p + 1, pair[rows:], stat)


def normalise(values):
    center = values - jnp.mean(values, axis=-1, keepdims=True)
    spread = jnp.mean(center * center, axis=-1, keepdims=True)
    return center * lax.rsqrt(spread + 1e-05)


def forward(r, me, nz):
    rows, d = r.tokens.shape
    items, frames = r.kv.shape[:2]
    pairs = d // LANES

    def weight(k, n, size=WIDE):
        return r.wg[k, :, :, :, :, :, n * size : (n + 1) * size].reshape(d, size)

    def product(x, k, sink):
        sink(dot(x, weight(k, 0, d)))

    def ln(values, i):
        return normalise(values) * r.gs[i : i + 1, :] + r.gs[4 + i : 5 + i, :]

    def norms_in():
        for g in range(2 * nz):
            total = r.ng[g // 2, g % 2, 0, 0, 0:16, :].astype(F32)
            for f in range(1, 4):
                total = total + r.ng[g // 2, g % 2, f // 2, f % 2, 0:16, :].astype(F32)
            r.gs[:, g * LANES : (g + 1) * LANES] = total

    def norm_one():
        pltpu.make_async_copy(r.tokens, r.first, r.own_sem.at[1]).wait()
        r.xb[...] = ln(r.first[...], 0).astype(BF16)
        r.n1t[...] = r.xb[...].T

    def joint(q):
        def sink(v):
            r.joint[:, q * d : (q + 1) * d] = v.astype(BF16)

        product(r.xb[...], q, sink)

    def self_attention(half):
        row = lax.rem(lax.broadcasted_iota(jnp.int32, (2 * rows, rows), 0), rows)
        causal = row >= lax.broadcasted_iota(jnp.int32, (2 * rows, rows), 1)

        def body(p, stat):
            q2 = two_heads(r.joint[:, at128(p)] * jnp.asarray(HEAD_DIM**-0.5, BF16))
            s = dot_nt(q2, r.joint[:, at128(p, d)])
            s = jnp.where(causal, s, -1e30)
            m = jnp.max(s, axis=-1, keepdims=True)
            e = jnp.exp(s - m)
            total = jnp.sum(e, axis=-1, keepdims=True)
            o2 = dot(e.astype(BF16), r.joint[:, at128(p, 2 * d)]) / total
            r.xb[:, at128(p)] = one_block(o2).astype(BF16)
            return put_stat(stat, p, m + jnp.log(total))

        first = jnp.zeros((rows, LANES), F32) if half == 0 else r.wcol[...]
        stat = lax.fori_loop(half * pairs // 2, (half + 1) * pairs // 2, body, first)
        if half == 0:
            r.wcol[...] = stat
        else:
            r.slse[...] = stat.T[0:16]
            r.smixt[...] = r.xb[...].T

    def self_out():
        def sink(v):
            r.branch[...] = v

        product(r.xb[...], 3, sink)
        r.first[...] = r.first[...] + r.branch[...]
        squares(1, r.branch[...])
        r.xb[...] = ln(r.first[...], 1).astype(BF16)
        r.n2t[...] = r.xb[...].T

    def squares(i, values):
        ok = lax.broadcasted_iota(jnp.int32, (rows, 1), 0) < r.tl[0]
        total = jnp.sum(jnp.where(ok, values * values, 0.0))
        line = lax.broadcasted_iota(jnp.int32, r.sq.shape, 0)
        r.sq[...] = jnp.where(line == i, total, r.sq[...])

    def start_counts():
        line = lax.broadcasted_iota(jnp.int32, r.sq.shape, 0)
        r.sq[...] = jnp.where(line == 4, r.tl[0].astype(F32), 0.0)

    def queries():
        def sink(v):
            r.qa[me.fr] = v.astype(BF16)

        product(r.xb[...], 4, sink)

    def q_copy(f, s, device):
        return remote(r.qa.at[f], r.qa.at[f], r.q_send.at[s], r.q_recv.at[s], device)

    fx, fs, fd = (1 - me.x) * 2 + me.c, me.x * 2 + 1 - me.c, (1 - me.x) * 2 + 1 - me.c

    def q_start():
        q_copy(me.fr, 0, me.xn).start()
        q_copy(me.fr, 1, me.sib).start()

    def q_forward():
        q_copy(fx, 0, me.xn).wait_recv()
        q_copy(fx, 2, me.sib).start()

    def q_done():
        q_copy(fs, 1, me.sib).wait_recv()
        q_copy(fd, 2, me.sib).wait_recv()

    def mem_copy(t):
        return pltpu.make_async_copy(r.memory.at[t], r.rc.at[t % 2, 0 : r.memory.shape[1]], r.m_sem.at[t % 2])

    def memory_part(which, t):
        mem_copy(t).wait()
        stage = r.rc.at[t % 2, 0 : r.memory.shape[1]]
        for n in range(d // WIDE):
            v = dot(stage[...].reshape(frames, d), weight(5 + which, n))
            r.kv[t, :, which * d + n * WIDE : which * d + (n + 1) * WIDE] = v.astype(BF16)
        if which == 0:
            r.memt[:, t * frames : (t + 1) * frames] = stage[...].reshape(frames, d).T
        if t + 2 < items or which == 0:
            mem_copy((t + 2) % items).start()

    def mem_start():
        for t in range(min(2, items)):
            mem_copy(t).start()

    def cross_half(t, half):
        def body(p, stat):
            q2 = two_heads(r.qa[t, :, at128(p)] * jnp.asarray(HEAD_DIM**-0.5, BF16))
            s = dot_nt(q2, r.kv[t, :, at128(p)]) + r.bias[pl.ds(t, 1), :]
            m = jnp.max(s, axis=-1, keepdims=True)
            e = jnp.exp(s - m)
            total = jnp.sum(e, axis=-1, keepdims=True)
            o2 = dot(e.astype(BF16), r.kv[t, :, at128(p, d)]) / total
            r.op[t, :, at128(p)] = one_block(o2).astype(BF16)
            return put_stat(stat, p, m + jnp.log(total))

        first = jnp.zeros((rows, LANES), F32) if half == 0 else r.wcol[...]
        stat = lax.fori_loop(half * pairs // 2, (half + 1) * pairs // 2, body, first)
        if half == 0:
            r.wcol[...] = stat
        else:
            r.opl[t] = stat.T[0:16]

    def o_copies(t, slot, device):
        return (
            remote(r.op.at[t], r.orv.at[slot], r.o_send.at[slot], r.o_recv.at[slot], device),
            remote(r.opl.at[t], r.orl.at[slot], r.o_send.at[3 + slot], r.o_recv.at[3 + slot], device),
        )

    def o_start(t, slot, device):
        for cp in o_copies(t, slot, device):
            cp.start()

    def o_wait(t, slot, device):
        for cp in o_copies(t, slot, device):
            cp.wait_recv()

    def merge(parts, sink):
        lses = [lse[...] for _, lse in parts]
        top = functools.reduce(jnp.maximum, lses)
        shares = [jnp.exp(v - top) for v in lses]
        total = functools.reduce(jnp.add, shares)
        flat = jnp.concatenate([v / total for v in shares] + [jnp.zeros((LANES - 16 * len(parts), LANES), F32)], axis=0)
        r.wcol[...] = flat.T
        lane = lax.broadcasted_iota(jnp.int32, (rows, LANES), 1)
        for p in range(pairs):
            value = jnp.zeros((rows, LANES), F32)
            for i, (mix, _) in enumerate(parts):
                left = r.wcol[:, 16 * i + 2 * p : 16 * i + 2 * p + 1]
                right = r.wcol[:, 16 * i + 2 * p + 1 : 16 * i + 2 * p + 2]
                share = jnp.where(lane < HEAD_DIM, left, right)
                value = value + share * mix[:, p * LANES : (p + 1) * LANES].astype(F32)
            sink(p, value)
        return top + jnp.log(total)

    def send_far():
        o_start(fd, 0, me.sib)

    def send_side():
        o_start(fs, 1, me.sib)

    def merge_across():
        o_wait(fd, 0, me.sib)

        def sink(p, v):
            r.op[fx, :, p * LANES : (p + 1) * LANES] = v.astype(BF16)

        r.opl[fx] = merge([(r.op.at[fx], r.opl.at[fx]), (r.orv.at[0], r.orl.at[0])], sink)
        o_start(fx, 2, me.xn)

    def merge_own():
        o_wait(fs, 1, me.sib)
        o_wait(fx, 2, me.xn)

        def sink(p, v):
            r.xb[:, p * LANES : (p + 1) * LANES] = v.astype(BF16)

        parts = [(r.op.at[me.fr], r.opl.at[me.fr]), (r.orv.at[1], r.orl.at[1]), (r.orv.at[2], r.orl.at[2])]
        r.clse[...] = merge(parts, sink)
        r.cmixt[...] = r.xb[...].T

    def cross_out():
        def sink(v):
            r.branch[...] = v

        product(r.xb[...], 7, sink)
        squares(2, r.branch[...])
        r.second[...] = r.first[...] + r.branch[...]
        r.xb[...] = ln(r.second[...], 2).astype(BF16)
        r.n3t[...] = r.xb[...].T

    def expand(q):
        for n in range(d // WIDE):
            v = dot(r.xb[...], weight(8 + q, n))
            at = slice(q * d + n * WIDE, q * d + (n + 1) * WIDE)
            half = 0.5 * (1.0 + lax.erf(v * (2.0**-0.5)))
            r.active[:, at] = (v * half).astype(BF16)
            r.slope[:, at] = (half + v * jnp.exp(-0.5 * v * v) * 0.3989422804014327).astype(BF16)
        r.activet[q * d : (q + 1) * d, :] = r.active[:, q * d : (q + 1) * d].T

    def contract(q, fresh=False):
        def sink(v):
            r.branch[...] = v if fresh else r.branch[...] + v

        product(r.active[:, q * d : (q + 1) * d], 12 + q, sink)

    def finish():
        squares(3, r.branch[...])
        r.third[...] = r.second[...] + r.branch[...]
        squares(0, r.third[...])
        ok = lax.broadcasted_iota(jnp.int32, (rows, 1), 0) < r.tl[0]
        r.branch[...] = jnp.where(ok, ln(r.third[...], 3), 0.0)
        pltpu.make_async_copy(r.branch, r.result, r.own_sem.at[3]).start()

    part = functools.partial

    def item(t):
        return [part(cross_half, t, 0), part(cross_half, t, 1)]

    tasks = {
        0: [start_counts, mem_start],
        2: [norms_in, norm_one],
        4: [part(joint, 0)],
        5: [part(joint, 1)],
        6: [part(joint, 2), part(self_attention, 0), part(self_attention, 1)],
        7: [self_out],
        8: [queries, q_start],
        9: [part(memory_part, 0, t) for t in range(items)],
        10: [q_forward] + [part(memory_part, 1, t) for t in range(items)],
        11: [q_done, *item(fd), send_far, *item(fs), send_side],
        12: [*item(fx), merge_across],
        13: item(me.fr),
        14: [merge_own, cross_out, part(expand, 0), part(expand, 1), part(contract, LATE[0] - 12, True)],
        15: [part(expand, 2), part(expand, 3), part(contract, LATE[1] - 12)],
        16: [part(contract, LATE[2] - 12), part(contract, 0), finish],
    }

    def drain():
        q_copy(me.fr, 0, me.xn).wait_send()
        q_copy(me.fr, 1, me.sib).wait_send()
        q_copy(fx, 2, me.sib).wait_send()
        for t, slot, device in ((fd, 0, me.sib), (fs, 1, me.sib), (fx, 2, me.xn)):
            for cp in o_copies(t, slot, device):
                cp.wait_send()

    return tasks, drain, (fx, fs, fd)


def ln_back(values, gain_row, grad):
    center = values - jnp.mean(values, axis=-1, keepdims=True)
    scale = lax.rsqrt(jnp.mean(center * center, axis=-1, keepdims=True) + 1e-05)
    unit = center * scale
    gain_grad = jnp.sum(grad * unit, axis=0, keepdims=True)
    shift_grad = jnp.sum(grad, axis=0, keepdims=True)
    lifted = grad * gain_row
    inner = jnp.mean(lifted * unit, axis=-1, keepdims=True)
    back = scale * (lifted - jnp.mean(lifted, axis=-1, keepdims=True) - unit * inner)
    return back, gain_grad, shift_grad


def backward(r, me, nz, fronts):
    rows, d = r.first.shape
    items, frames = r.kv.shape[:2]
    pairs = d // LANES
    fx, fs, fd = fronts
    t = {}

    def grad_into(k, left, right, into=None):
        for n in range(d // WIDE):
            v = dot(left, right(n * WIDE, (n + 1) * WIDE)).astype(BF16)
            at = slice(n * WIDE, (n + 1) * WIDE)
            r.wg[k if into is None else into, :, :, :, :, :, at] = v.reshape(nz, 2, 2, 2, d // (8 * nz), WIDE)

    def through(k, grad):
        return dot_nt(grad, r.wg[k].reshape(d, d))

    def ln_step(i, values, grad, first=False):
        back, gain, shift = ln_back(values, r.gs[i : i + 1, :], grad)
        r.gr[...] = back if first else r.gr[...] + back
        r.nrow[i : i + 1, :] = gain
        r.nrow[4 + i : 5 + i, :] = shift

    def start():
        pltpu.make_async_copy(r.cotangent, r.gr, r.own_sem.at[2]).wait()
        r.biast[...] = jnp.concatenate([r.bias[...], jnp.zeros((LANES - r.bias.shape[0], frames), F32)], axis=0).T
        for g in range(d // LANES):
            r.nrow[8:16, g * LANES : (g + 1) * LANES] = r.sq[...]
        ok = lax.broadcasted_iota(jnp.int32, (rows, 1), 0) < r.tl[0]
        ln_step(3, r.third[...], jnp.where(ok, r.gr[...], 0.0), True)
        r.xb[...] = r.gr[...].astype(BF16)
        pltpu.make_async_copy(r.tokens, r.third, r.own_sem.at[1]).start()

    def contract(q):
        at = slice(q * d, (q + 1) * d)
        r.active[:, at] = (through(12 + q, r.xb[...]) * r.slope[:, at].astype(F32)).astype(BF16)

    def contract_grad(q):
        grad_into(12 + q, r.activet[q * d : (q + 1) * d, :], lambda lo, hi: r.xb[:, lo:hi])

    def onto(fresh, value):
        r.branch[...] = value if fresh else r.branch[...] + value

    def expand(q):
        if q == 0:
            pltpu.make_async_copy(r.branch, r.result, r.own_sem.at[3]).wait()
        onto(q == 0, through(8 + q, r.active[:, q * d : (q + 1) * d]))

    def expand_grad(q):
        grad_into(8 + q, r.n3t[...], lambda lo, hi: r.active[:, q * d + lo : q * d + hi])

    def cross_out():
        ln_step(2, r.second[...], r.branch[...])
        r.xb[...] = r.gr[...].astype(BF16)
        r.ga[me.fr] = through(7, r.xb[...]).astype(BF16)
        r.gl[me.fr, 0:16] = r.clse[...]

        def body(p, carry):
            left, right = row_dots(r.ga[me.fr, :, at128(p)], r.cmixt[at128(p), :])
            r.gl[me.fr, pl.ds(16 + 2 * p, 1), :] = left
            r.gl[me.fr, pl.ds(17 + 2 * p, 1), :] = right
            return carry

        lax.fori_loop(0, pairs, body, 0)

    def cross_out_grad():
        grad_into(7, r.cmixt[...], lambda lo, hi: r.xb[:, lo:hi])

    def row_dots(grad, mixt):
        prod = grad.astype(F32).T * mixt.astype(F32)
        return jnp.sum(prod[:HEAD_DIM], axis=0, keepdims=True), jnp.sum(prod[HEAD_DIM:], axis=0, keepdims=True)

    def g_copies(f, s, device):
        return (
            remote(r.ga.at[f], r.ga.at[f], r.g2_send.at[s], r.g2_recv.at[s], device),
            remote(r.gl.at[f], r.gl.at[f], r.g2_send.at[3 + s], r.g2_recv.at[3 + s], device),
        )

    def each(copies, what):
        for cp in copies:
            getattr(cp, what)()

    def g_start():
        each(g_copies(me.fr, 0, me.xn), "start")
        each(g_copies(me.fr, 1, me.sib), "start")

    def g_forward():
        each(g_copies(fx, 0, me.xn), "wait_recv")
        each(g_copies(fx, 2, me.sib), "start")

    def g_drain():
        each(g_copies(me.fr, 0, me.xn), "wait_send")
        each(g_copies(me.fr, 1, me.sib), "wait_send")
        each(g_copies(fx, 2, me.sib), "wait_send")

    scale = HEAD_DIM**-0.5

    def pair_back(q, k, v, g, hide, lse, dots):
        q2, g2 = two_heads(q * jnp.asarray(scale, BF16)), two_heads(g)
        probs = jnp.exp(hide(dot_nt(k, q2)) - lse)
        ds = (probs * (dot_nt(v, g2) - dots)).astype(BF16)
        dq = one_block(dot(ds.T, k)) * scale
        return dq, dot(ds, q2), dot(probs.astype(BF16), g2)

    def cross_half(f, half):
        lane = lax.broadcasted_iota(jnp.int32, (frames, LANES), 1)
        column = jnp.sum(jnp.where(lane == f, r.biast[...], 0.0), axis=-1, keepdims=True)

        def body(p, carry):
            stats = [
                jnp.concatenate([r.gl[f, pl.ds(b + 2 * p, 1), :], r.gl[f, pl.ds(b + 1 + 2 * p, 1), :]], axis=1)
                for b in (0, 16)
            ]
            dq, dk, dv = pair_back(
                r.qa[f, :, at128(p)],
                r.kv[f, :, at128(p)],
                r.kv[f, :, at128(p, d)],
                r.ga[f, :, at128(p)],
                lambda s: s + column,
                *stats,
            )
            r.op[f, :, at128(p)] = dq.astype(BF16)
            r.kv[f, :, at128(p)] = dk.astype(BF16)
            r.kv[f, :, at128(p, d)] = dv.astype(BF16)
            return carry

        lax.fori_loop(half * pairs // 2, (half + 1) * pairs // 2, body, 0)

    def d_copy(f, slot, device):
        return remote(r.op.at[f], r.orv.at[slot], r.o2_send.at[slot], r.o2_recv.at[slot], device)

    def side_ready():
        each(g_copies(fs, 1, me.sib), "wait_recv")

    def send_side():
        d_copy(fs, 1, me.sib).start()

    def far_ready():
        each(g_copies(fd, 2, me.sib), "wait_recv")

    def send_far():
        d_copy(fd, 0, me.sib).start()

    def send_across():
        d_copy(fd, 0, me.sib).wait_recv()
        r.op[fx] = (r.op[fx].astype(F32) + r.orv[0].astype(F32)).astype(BF16)
        d_copy(fx, 2, me.xn).start()

    def tile_copy(n):
        f, h = n // 2, n % 2
        return pltpu.make_async_copy(
            r.mst.at[n % 2, 0 : r.memory_grad.shape[1]],
            r.memory_grad.at[f, :, h * WIDE : (h + 1) * WIDE],
            r.t_sem.at[n % 2],
        )

    def memory_grad(n):
        f, h = n // 2, n % 2
        if n >= 2:
            tile_copy(n - 2).wait()
        layers = slice(h * nz // 2, (h + 1) * nz // 2)
        keys, values = (r.wg[k, layers].reshape(WIDE, d) for k in (5, 6))
        r.mst[n % 2] = dot_nt(r.kv[f, :, 0:d], keys) + dot_nt(r.kv[f, :, d : 2 * d], values)
        tile_copy(n).start()

    def memory_done():
        for n in (2 * items - 2, 2 * items - 1):
            tile_copy(n).wait()

    def memory_weights(which, into):
        def rows_of(lo, hi):
            return r.kv[:, :, which * d + lo : which * d + hi].reshape(items * frames, hi - lo)

        grad_into(5 + which, r.memt[...], rows_of, into)

    def query():
        d_copy(fs, 1, me.sib).wait_recv()
        d_copy(fx, 2, me.xn).wait_recv()
        r.xb[...] = (r.op[me.fr].astype(F32) + r.orv[1].astype(F32) + r.orv[2].astype(F32)).astype(BF16)
        onto(True, through(4, r.xb[...]))
        grad_into(4, r.n2t[...], lambda lo, hi: r.xb[:, lo:hi])

    def d_drain():
        for f, slot, device in ((fd, 0, me.sib), (fs, 1, me.sib), (fx, 2, me.xn)):
            d_copy(f, slot, device).wait_send()

    def self_out():
        ln_step(1, r.first[...], r.branch[...])
        r.xb[...] = r.gr[...].astype(BF16)
        r.ga[me.fr] = through(3, r.xb[...]).astype(BF16)
        grad_into(3, r.smixt[...], lambda lo, hi: r.xb[:, lo:hi])

    def self_attention(half):
        key = lax.broadcasted_iota(jnp.int32, (rows, 2 * rows), 0)
        causal = key <= lax.rem(lax.broadcasted_iota(jnp.int32, (rows, 2 * rows), 1), rows)

        def body(p, carry):
            g = r.ga[me.fr, :, at128(p)]
            lse = jnp.concatenate([r.slse[pl.ds(2 * p, 1), :], r.slse[pl.ds(2 * p + 1, 1), :]], axis=1)
            dots = jnp.concatenate(row_dots(g, r.smixt[at128(p), :]), axis=1)
            dq, dk, dv = pair_back(
                r.joint[:, at128(p)],
                r.joint[:, at128(p, d)],
                r.joint[:, at128(p, 2 * d)],
                g,
                lambda s: jnp.where(causal, s, -1e30),
                lse,
                dots,
            )
            r.joint[:, at128(p)] = dq.astype(BF16)
            r.joint[:, at128(p, d)] = dk.astype(BF16)
            r.joint[:, at128(p, 2 * d)] = dv.astype(BF16)
            return carry

        lax.fori_loop(half * pairs // 2, (half + 1) * pairs // 2, body, 0)

    def project(q):
        onto(q == 0, through(q, r.joint[:, q * d : (q + 1) * d]))

    def project_grad(q):
        grad_into(q, r.n1t[...], lambda lo, hi: r.joint[:, q * d + lo : q * d + hi])

    def finish():
        pltpu.make_async_copy(r.tokens, r.third, r.own_sem.at[1]).wait()
        ln_step(0, r.third[...], r.branch[...])
        pltpu.make_async_copy(r.gr, r.tokens_grad, r.own_sem.at[2]).start()
        for g in range(d // LANES):
            for f in range(4):
                r.nw[g // 2, g % 2, f // 2, f % 2] = r.nrow[:, g * LANES : (g + 1) * LANES]

    def close():
        pltpu.make_async_copy(r.gr, r.tokens_grad, r.own_sem.at[2]).wait()

    return SimpleNamespace(**{k: v for k, v in locals().items() if callable(v)})


GRAD_ORDER = (12, 13, 14, 15, 8, 9, 10, 11, 7, 5, 6, 4, 3, 0, 1, 2)
SLOTS = 2


LATE = (13, 14, 15)
LATE_TICKS = (1, 4, 8)
TILT = (5, 9)
EARLY = (1,)
EARLY_END = 8
ROWS = 7
SEND_ROWS = 7
INTO = {5: 12, 6: 14}


def own_blocks(r):
    slab, d = r.self_output.shape
    blocks = {}
    for k in range(3):
        blocks[k] = (r.self_project.at[:, k * d : (k + 1) * d], r.self_project_grad.at[:, k * d : (k + 1) * d])
    for k in range(2):
        blocks[5 + k] = (r.cross_memory.at[:, k * d : (k + 1) * d], r.cross_memory_grad.at[:, k * d : (k + 1) * d])
    blocks[3] = (r.self_output, r.self_output_grad)
    blocks[4] = (r.cross_query, r.cross_query_grad)
    blocks[7] = (r.cross_output, r.cross_output_grad)
    for k in range(4):
        blocks[12 + k] = tuple(a.at[k * slab : (k + 1) * slab] for a in (r.contract, r.contract_grad))
    return blocks


def deal(r, put):
    slab = r.expand.shape[0]
    ways = LANES // slab

    def body(g, carry):
        lane = lax.div(lax.broadcasted_iota(jnp.int32, (slab, LANES), 1), slab)
        source = [r.expand[:, at128(ways * g + a)].astype(F32) for a in range(ways)]
        for q in range(ways):
            total = source[q]
            for a in range(ways):
                if a != q:
                    total = jnp.where(lane == a, pltpu.roll(source[a], (slab * (a - q)) % LANES, 1), total)
            put(q, at128(g), total.astype(BF16))
        return carry

    lax.fori_loop(0, r.expand.shape[1] // (ways * LANES), body, 0)


def undeal(r, q, total):
    slab = total.shape[0]
    ways = LANES // slab
    lane = lax.div(lax.broadcasted_iota(jnp.int32, (slab, LANES), 1), slab)
    for g in range(total.shape[1] // LANES):
        block = total[:, g * LANES : (g + 1) * LANES]
        for a in range(ways):
            line, column = divmod((ways * g + a) * LANES, total.shape[1])
            at = (slice(line * slab, (line + 1) * slab), slice(column, column + LANES))
            moved = block if a == q else pltpu.roll(block, (slab * (q - a)) % LANES, 1)
            r.second[at] = jnp.where(lane == q, moved, r.second[at])


def run(r, nz, chunks):
    me = place()
    barrier = pltpu.get_barrier_semaphore()
    peers = [me.xn, me.yn, me.sib, me.diag]
    peers += [me.dev(lax.rem(me.z + dz, nz), me.y, me.x, me.c) for dz in range(1, nz)]
    for device in peers:
        pl.semaphore_signal(barrier, inc=1, device_id=device, device_id_type=MESH)
    blocks = own_blocks(r)
    owns = {
        k: pltpu.make_async_copy(blocks[k][0], r.wg.at[k, me.z, me.y, me.x, me.c], r.w_sem.at[k]) for k in sorted(blocks)
    }
    for k in (0, 1, *LATE):
        owns[k].start()
    for k in owns:
        if k not in (0, 1, *LATE):
            owns[k].start()
    pltpu.make_async_copy(r.tokens, r.first, r.own_sem.at[1]).start()
    pltpu.make_async_copy(r.cotangent, r.gr, r.own_sem.at[2]).start()
    slab = r.expand.shape[0]
    lane = lax.div(lax.broadcasted_iota(jnp.int32, (8, LANES), 1), slab)
    both = jnp.concatenate([r.norm_gains[...].astype(F32), r.norm_shifts[...].astype(F32)], axis=0)
    wide = jnp.where(lane == me.fr, jnp.concatenate([both] * (LANES // slab), axis=1), 0.0)
    r.ng[me.z, me.y, me.x, me.c] = jnp.concatenate([wide, jnp.zeros((24, LANES), F32)], axis=0).astype(BF16)

    def put(q, at, v):
        r.wg[8 + q, me.z, me.y, me.x, me.c, :, at] = v

    early = [k for k in range(chunks) if k not in LATE]
    count = len(early)
    norm = gather_steps(me, r.ng, r.g_send.at[ROWS], r.g_recv.at[ROWS], nz)
    steps = []
    for k in range(chunks):
        row = ROWS + 1 + LATE.index(k) if k in LATE else early.index(k) % ROWS
        sems = (r.g_send.at[row], r.g_recv.at[row])
        if k in LATE:
            steps.append(gather_late_steps(me, r.wg.at[k], *sems, nz))
        else:
            steps.append(gather_steps(me, r.wg.at[k], *sems, nz, k in TILT))

    def mix(steps, pieces):
        for i, step in enumerate(steps):
            step()
            for piece in pieces[i * len(pieces) // len(steps) : (i + 1) * len(pieces) // len(steps)]:
                piece()

    part = functools.partial
    pl.semaphore_wait(barrier, len(peers))
    norm.z()
    owns[0].wait()
    steps[0].z()
    for k in LATE:
        owns[k].wait()
        steps[k].near()
    for k in owns:
        if k != 0 and k not in LATE:
            owns[k].wait()
    for k in LATE:
        steps[k].far()
    steps[0].relay()
    tasks, drain, fronts = forward(r, me, nz)
    lines = {tick: [] for tick in range(count + 4)}
    for tick in lines:
        for step, t in (
            ("done", tick - 4),
            ("near", tick),
            ("drain", tick - 4),
            ("z", tick + 2),
            ("relay", tick + 1),
            ("far", tick - 1),
            ("last", tick - 2),
        ):
            if tick == 0 and step == "z":
                lines[tick].append(steps[early[1]].z)
            if 0 <= t < count:
                lines[tick].append(getattr(steps[early[t]], step))
    lines[0][1:1] = [norm.relay, norm.near]
    lines[0].append(norm.far)
    lines[1] += [norm.last] + [steps[k].square for k in LATE]
    lines[2].insert(0, norm.done)
    for k, first in zip(LATE, LATE_TICKS):
        for dz, go, come in ((2, first, first + 3), (1, first + 2, first + 6), (3, first + 2, first + 6)):
            lines[go].append(part(steps[k].z, dz))
            lines[come].append(part(steps[k].pass_on, dz))
        lines[first + 8].insert(0, steps[k].done)
    tasks[0] = tasks.get(0, []) + [part(deal, r, put)]
    for tick in lines:
        mix(lines[tick], tasks.get(tick, []))
    drain()
    norm.drain()
    for k in LATE:
        steps[k].drain()

    b = backward(r, me, nz, fronts)

    plain = [m for m in range(chunks) if m not in EARLY]
    ends = {m: i + 3.0 for i, m in enumerate(plain)}
    ends.update({m: EARLY_END + 0.5 for m in EARLY})
    direct = sorted((m for m, k in enumerate(GRAD_ORDER) if k in blocks), key=ends.get)

    def out_copy(i):
        return pltpu.make_async_copy(r.ost.at[i % 2], blocks[GRAD_ORDER[direct[i]]][1], r.e_sem.at[i % 2])

    def keep(turn):
        k = GRAD_ORDER[turn]

        def sink(total):
            if k not in blocks:
                undeal(r, k - 8, total)
                return
            i = direct.index(turn)
            if i >= 2:
                out_copy(i - 2).wait()
            r.ost[i % 2] = total
            out_copy(i).start()

        return sink

    def keep_norms(total):
        rms = jnp.sqrt(total / (total[12:13] * r.first.shape[1]))
        line = lax.broadcasted_iota(jnp.int32, total.shape, 0)
        r.norm_out[...] = jnp.where(line < 8, total, rms)

    boxes = (r.rc, r.y1, r.x1, r.x2, r.y2, r.zs)
    fast_boxes = (r.rc, r.fy1, r.fx1, r.fx2, r.fy2, r.fzs)
    norm_boxes = (r.nrc, r.ny1, r.nx1, r.nx2, r.ny2, r.nzs)
    adds = {}
    for m, k in enumerate(GRAD_ORDER):
        w = r.wg.at[INTO.get(k, k)]
        if m in EARLY:
            build, box, turn = scatter_early_steps, fast_boxes, (EARLY.index(m), 1, len(EARLY))
            at = SEND_ROWS, SLOTS
        else:
            build, box, turn = scatter_steps, boxes, (plain.index(m), SLOTS, len(plain))
            at = turn[0] % SEND_ROWS, turn[0] % SLOTS
        sems = (r.s_send.at[at[0]], r.s_recv.at[at[1]], r.core_recv.at[m % SLOTS])
        adds[m] = build(me, w, box, sems, r.credit, nz, (m, SLOTS, chunks), turn, keep(m))
    once = (0, 1, 1)
    sems = (r.s_send.at[SEND_ROWS + 1], r.s_recv.at[SLOTS + 1], r.core_recv.at[SLOTS])
    adds[chunks] = scatter_steps(me, r.nw, norm_boxes, sems, r.credit, nz, once, once, keep_norms)
    wide_copies = [
        pltpu.make_async_copy(
            r.second.at[i * slab : (i + 1) * slab],
            r.expand_grad.at[:, i * r.second.shape[1] : (i + 1) * r.second.shape[1]],
            r.x_sem.at[i],
        )
        for i in range(4)
    ]

    def wide_start():
        for cp in wide_copies:
            cp.start()

    def pair(f):
        return [part(b.cross_half, f, 0), part(b.cross_half, f, 1)]

    fx, fs, fd = fronts
    mg = [part(b.memory_grad, n) for n in range(8)]
    work = {
        -1: [b.start, part(b.contract, 0), part(b.contract_grad, 0)],
        0: [f for q in (1, 2, 3) for f in (part(b.contract, q), part(b.contract_grad, q))],
        1: [f for q in (0, 1, 2) for f in (part(b.expand, q), part(b.expand_grad, q))],
        2: [part(b.expand, 3), part(b.expand_grad, 3), b.cross_out, b.g_start, b.cross_out_grad],
        3: pair(me.fr) + [b.side_ready, part(b.cross_half, fs, 0)],
        4: [part(b.cross_half, fs, 1), b.send_side, b.g_forward, b.far_ready, part(b.cross_half, fd, 0)],
        5: [part(b.cross_half, fd, 1), b.send_far, *pair(fx)],
        6: [b.send_across, part(b.memory_weights, 0, INTO[5]), b.g_drain],
        7: [part(b.memory_weights, 1, INTO[6]), mg[0]],
        8: [b.query, mg[1], mg[2]],
        9: [b.d_drain, b.self_out, mg[3]],
        10: [part(b.self_attention, 0), part(b.self_attention, 1), part(b.project, 0), part(b.project_grad, 0)],
        11: [part(b.project, 1), part(b.project_grad, 1), mg[4]],
        12: [part(b.project, 2), part(b.project_grad, 2), b.finish],
        13: [mg[5]],
        14: [mg[6], mg[7]],
        16: [b.memory_done],
    }
    starts, named = {}, {}
    for i, m in enumerate(plain):
        starts.setdefault(i - 2 if i >= 3 else i - 1, []).append(m)
        for late, name in enumerate("bcde"):
            named.setdefault(i + late, {})[name] = getattr(adds[m], name)
    steps = {tick: [by[n] for n in "bcde" if n in by] for tick, by in named.items()}
    for i, m in enumerate(plain[:-SEND_ROWS]):
        steps[i + SEND_ROWS - 2].insert(0, adds[m].drain)
    (first,) = (adds[m] for m in EARLY)
    starts[0].insert(0, EARLY[0])
    steps[1].insert(0, first.b)
    for dz in range(1, nz):
        steps[dz].append(part(first.z, dz))
    for back, step in enumerate((first.e, first.d, first.c)):
        steps[EARLY_END - back].append(step)
    last = len(plain) - 1
    for tick, name in zip(range(last, last + 4), "bcde"):
        steps.setdefault(tick, []).append(getattr(adds[chunks], name))
    starts[last - 2].append(chunks)
    for tick in range(-1, last + 4):
        mix(steps.get(tick, []) or [lambda: None], work.get(tick, []))
        if tick == 10:
            wide_start()
        for m in starts.get(tick, []):
            adds[m].a()
    b.close()
    for cp in wide_copies:
        cp.wait()
    out_copy(len(direct) - 2).wait()
    out_copy(len(direct) - 1).wait()
    for m in (*plain[-SEND_ROWS:], *EARLY, chunks):
        adds[m].drain()


VMEM_BYTES = 127 * 2**19


INPUTS = (
    "tl",
    "tokens",
    "cotangent",
    "memory",
    "self_project",
    "self_output",
    "cross_query",
    "cross_memory",
    "cross_output",
    "expand",
    "contract",
    "norm_gains",
    "norm_shifts",
    "bias",
)
GRADS = ("self_project", "self_output", "cross_query", "cross_memory", "cross_output", "expand", "contract")


def at(space):
    return pl.BlockSpec(memory_space=space)


def fused(nz, chunks, frame_count, **given):
    rows, d = given["tokens"].shape
    items, parts = given["memory"].shape[:2]
    slab = given["self_output"].shape[0]
    padded = parts * 4 * slab
    half = slab // 2
    outs = dict(
        result=((rows, d), pl.ANY),
        tokens_grad=((rows, d), pl.ANY),
        memory_grad=((items, frame_count, d), pl.ANY),
        **{k + "_grad": (given[k].shape, pl.ANY) for k in GRADS},
        norm_out=((16, LANES), pltpu.VMEM),
    )
    vm = pltpu.VMEM
    dma = pltpu.SemaphoreType.DMA
    scratch = dict(
        wg=vm((chunks, nz, 2, 2, 2, slab, d), BF16),
        ng=vm((nz, 2, 2, 2, 32, LANES), BF16),
        gs=vm((16, d), F32),
        n1t=vm((d, rows), BF16),
        joint=vm((rows, 3 * d), BF16),
        smixt=vm((d, rows), BF16),
        slse=vm((16, LANES), F32),
        first=vm((rows, d), F32),
        n2t=vm((d, rows), BF16),
        qa=vm((items, rows, d), BF16),
        kv=vm((items, padded, 2 * d), BF16),
        memt=vm((d, items * padded), BF16),
        clse=vm((16, LANES), F32),
        second=vm((rows, d), F32),
        n3t=vm((d, rows), BF16),
        activet=vm((4 * d, rows), BF16),
        active=vm((rows, 4 * d), BF16),
        slope=vm((rows, 4 * d), BF16),
        third=vm((rows, d), F32),
        sq=vm((8, LANES), F32),
        xb=vm((rows, d), BF16),
        branch=vm((rows, d), F32),
        op=vm((items, rows, d), BF16),
        opl=vm((items, 16, LANES), F32),
        orv=vm((3, rows, d), BF16),
        orl=vm((3, 16, LANES), F32),
        wcol=vm((LANES, LANES), F32),
        cmixt=vm((d, rows), BF16),
        gr=vm((rows, d), F32),
        ga=vm((items, rows, d), BF16),
        gl=vm((items, 32, LANES), F32),
        nrow=vm((16, d), F32),
        biast=vm((padded, LANES), F32),
        mst=vm((2, padded, WIDE), F32),
        ost=vm((2, slab, d), F32),
        nw=vm((nz, 2, 2, 2, 16, LANES), F32),
        rc=vm((SLOTS, nz, 2, 2, slab, d), BF16),
        y1=vm((SLOTS, nz, 2, half, d), BF16),
        x1=vm((SLOTS, nz, 2, half, d), BF16),
        x2=vm((SLOTS, nz, half, d), BF16),
        y2=vm((SLOTS, nz, half, d), BF16),
        zs=vm((SLOTS, nz - 1, slab, d), BF16),
        fy1=vm((1, 2, half, d), BF16),
        fx1=vm((1, 2, half, d), BF16),
        fx2=vm((1, half, d), BF16),
        fy2=vm((1, half, d), BF16),
        fzs=vm((1, nz - 1, 2, 2, slab, d), BF16),
        nrc=vm((1, nz, 2, 2, 16, LANES), F32),
        ny1=vm((1, nz, 2, 8, LANES), F32),
        nx1=vm((1, nz, 2, 8, LANES), F32),
        nx2=vm((1, nz, 8, LANES), F32),
        ny2=vm((1, nz, 8, LANES), F32),
        nzs=vm((1, nz - 1, 16, LANES), F32),
        own_sem=dma((4,)),
        x_sem=dma((4,)),
        w_sem=dma((chunks,)),
        m_sem=dma((2,)),
        t_sem=dma((2,)),
        e_sem=dma((2,)),
        g_send=dma((ROWS + 1 + len(LATE), nz + 8)),
        g_recv=dma((ROWS + 1 + len(LATE), nz + 7)),
        s_send=dma((SEND_ROWS + 2, nz + 4)),
        s_recv=dma((SLOTS + 2, nz + 3)),
        core_recv=dma((SLOTS + 1,)),
        credit=pltpu.SemaphoreType.REGULAR((2 * nz + 7,)),
        q_send=dma((3,)),
        q_recv=dma((3,)),
        o_send=dma((6,)),
        o_recv=dma((6,)),
        g2_send=dma((6,)),
        g2_recv=dma((6,)),
        o2_send=dma((3,)),
        o2_recv=dma((3,)),
    )
    names = list(INPUTS) + list(outs) + list(scratch)

    def kernel(*refs):
        run(SimpleNamespace(**dict(zip(names, refs))), nz, chunks)

    spaces = {"tl": pltpu.SMEM, "expand": pltpu.VMEM, "norm_gains": pltpu.VMEM, "norm_shifts": pltpu.VMEM, "bias": pltpu.VMEM}
    res = pl.pallas_call(
        kernel,
        out_shape=[jax.ShapeDtypeStruct(s, F32) for s, _ in outs.values()],
        in_specs=[at(spaces.get(k, pl.ANY)) for k in INPUTS],
        out_specs=[at(s) for _, s in outs.values()],
        scratch_shapes=list(scratch.values()),
        compiler_params=pltpu.CompilerParams(collective_id=0, has_side_effects=True, vmem_limit_bytes=VMEM_BYTES),
    )(*(given[k] for k in INPUTS))
    return dict(zip(outs, res))


def settle(arrays, norm_out, width):
    count = len(arrays)
    pieces = []
    for i, a in enumerate(arrays):
        pieces += [(i, k) for k in range(a.shape[0])] if a.ndim == 3 else [(i, None)]

    def kernel(*refs):
        sources, (table, scalars) = refs[:count], refs[count : count + 2]
        targets = refs[count + 2 : 2 * count + 2]
        gains, shifts, rms = refs[2 * count + 2 : 2 * count + 5]
        held = refs[2 * count + 5 : 3 * count + 5]
        in_sem, out_sem = refs[3 * count + 5 :]

        def pick(ref, k):
            return ref if k is None else ref.at[k]

        ins = [pltpu.make_async_copy(pick(sources[i], k), pick(held[i], k), in_sem.at[n]) for n, (i, k) in enumerate(pieces)]
        outs = [pltpu.make_async_copy(pick(held[i], k), pick(targets[i], k), out_sem.at[n]) for n, (i, k) in enumerate(pieces)]
        for cp in ins:
            cp.start()
        fr = lax.axis_index("frames")
        mine = jnp.zeros((8, width), F32)
        for f in range(LANES // width):
            mine = jnp.where(fr == f, table[0:8, f * width : (f + 1) * width], mine)
        gains[...] = mine[0:4]
        shifts[...] = mine[4:8]
        for i in range(4):
            rms[i] = scalars[8 + i, 0]
        for a, b in zip(ins, outs):
            a.wait()
            b.start()
        for b in outs:
            b.wait()

    small = jax.ShapeDtypeStruct((4, width), F32)
    return pl.pallas_call(
        kernel,
        out_shape=[jax.ShapeDtypeStruct(a.shape, a.dtype) for a in arrays] + [small, small, jax.ShapeDtypeStruct((4,), F32)],
        in_specs=[at(pl.ANY)] * count + [at(pltpu.VMEM), at(pltpu.SMEM)],
        out_specs=[at(pl.ANY)] * count + [at(pltpu.VMEM)] * 2 + [at(pltpu.SMEM)],
        scratch_shapes=[pltpu.VMEM(a.shape, a.dtype) for a in arrays]
        + [pltpu.SemaphoreType.DMA((len(pieces),)), pltpu.SemaphoreType.DMA((len(pieces),))],
        compiler_params=pltpu.CompilerParams(vmem_limit_bytes=VMEM_BYTES),
    )(*arrays, norm_out, norm_out)


CHUNKS = 16
Z_CHIPS = 4


def frame_bias(cross_mask, memory_length, frame_count, padded):
    start = lax.axis_index("frames") * frame_count
    items = cross_mask.shape[0]
    wide = jnp.pad(cross_mask, ((0, 8 - items), (0, padded - frame_count)))
    mask = lax.dynamic_slice_in_dim(wide, start, padded, 1)
    lengths = jnp.pad(memory_length, (0, 8 - items))
    offset = jnp.arange(padded)[None]
    at = start + offset
    ok = (offset < frame_count) & (at < lengths[:, None]) & ((mask == 1) | (at == 0))
    return jnp.where(ok, 0.0, -1e30).astype(F32)


def local_fused(
    tokens,
    memory,
    cotangent,
    self_project,
    self_output,
    cross_query,
    cross_memory,
    cross_output,
    expand,
    contract,
    norm_gains,
    norm_shifts,
    target_length,
    memory_length,
    cross_mask,
):
    items, frame_count, d = memory.shape
    slab = self_output.shape[0]
    group = 4 * slab
    parts = -(-frame_count // group)
    padded = parts * group
    rolled = jnp.pad(memory, ((0, 0), (0, padded - frame_count), (0, 0))).reshape(items, parts, 2, 2, slab, d)
    o = fused(
        Z_CHIPS,
        CHUNKS,
        frame_count,
        tl=target_length,
        tokens=tokens[0],
        cotangent=cotangent[0],
        memory=rolled,
        self_project=self_project,
        self_output=self_output,
        cross_query=cross_query,
        cross_memory=cross_memory,
        cross_output=cross_output,
        expand=expand,
        contract=contract,
        norm_gains=norm_gains,
        norm_shifts=norm_shifts,
        bias=frame_bias(cross_mask, memory_length, frame_count, padded),
    )
    large = [o[k] for k in ("result", "tokens_grad", "memory_grad")] + [o[k + "_grad"] for k in GRADS]
    done = settle(large, o["norm_out"], norm_gains.shape[1])
    return (done[0][None], done[1][None], *done[2:])


block_heads = 4


def layer_norm(values, gain_row, shift_row):
    center = values - jnp.mean(values, axis=-1, keepdims=True)
    spread = jnp.mean(center * center, axis=-1, keepdims=True)
    return center * lax.rsqrt(spread + 1e-05) * gain_row + shift_row


def exact_gelu(values):
    return jax.nn.gelu(values, approximate=False)


def matmul(left_side, right_side):
    return jnp.dot(left_side, right_side, preferred_element_type=jnp.float32)


def split_heads(rows):
    return rows.reshape(rows.shape[:-1] + (rows.shape[-1] // HEAD_DIM, HEAD_DIM))


def to_blocks(rows):
    row_count, head_count, head_width = rows.shape
    return rows.reshape(row_count, head_count // block_heads, block_heads, head_width).transpose(
        1, 0, 2, 3
    )


def from_blocks(blocks):
    group_count, row_count, head_count, head_width = blocks.shape
    return blocks.transpose(1, 0, 2, 3).reshape(row_count, group_count * head_count * head_width)


def block_scores(query_block, key_block, allowed):
    factor = query_block.shape[-1] ** (-0.5)
    raw_scores = (
        jnp.einsum("shd,fhd->hsf", query_block, key_block, preferred_element_type=jnp.float32)
        * factor
    )
    return jnp.where(allowed[None], raw_scores, -1e30)


def block_probs(query_block, key_block, allowed, max_block, total_block):
    scores = block_scores(query_block, key_block, allowed)
    shifted = jnp.where(allowed[None], jnp.exp(scores - max_block[..., None]), 0.0)
    return shifted / total_block[..., None]


def block_grads(query_block, key_block, grad_block, probs, grad_probs, row_dot):
    factor = query_block.shape[-1] ** (-0.5)
    score_grad = (probs * (grad_probs - row_dot)).astype(jnp.bfloat16)
    query_grad = (
        jnp.einsum("hsf,fhd->shd", score_grad, key_block, preferred_element_type=jnp.float32)
        * factor
    )
    key_grad = (
        jnp.einsum("hsf,shd->fhd", score_grad, query_block, preferred_element_type=jnp.float32)
        * factor
    )
    value_grad = jnp.einsum(
        "hsf,shd->fhd", probs.astype(jnp.bfloat16), grad_block, preferred_element_type=jnp.float32
    )
    return (query_grad, key_grad, value_grad)


def attend_whole(query_rows, key_rows, value_rows, allowed):

    def one_group(blocks):
        query_block, key_block, value_block = blocks
        scores = block_scores(query_block, key_block, allowed)
        max_block = jnp.max(scores, axis=-1)
        shifted = jnp.where(allowed[None], jnp.exp(scores - max_block[..., None]), 0.0)
        total_block = jnp.sum(shifted, axis=-1)
        weights = (shifted / total_block[..., None]).astype(jnp.bfloat16)
        mixture = jnp.einsum(
            "hsf,fhd->shd", weights, value_block, preferred_element_type=jnp.float32
        )
        return (mixture, max_block, total_block)

    mixture, row_max, totals = lax.map(
        one_group, (to_blocks(query_rows), to_blocks(key_rows), to_blocks(value_rows))
    )
    return (from_blocks(mixture), row_max, totals)


def attend_whole_back(query_rows, key_rows, value_rows, allowed, grad_rows, row_max, totals):

    def one_group(blocks):
        query_block, key_block, value_block, grad_block, max_block, total_block = blocks
        probs = block_probs(query_block, key_block, allowed, max_block, total_block)
        grad_probs = jnp.einsum(
            "shd,fhd->hsf", grad_block, value_block, preferred_element_type=jnp.float32
        )
        row_dot = jnp.sum(probs * grad_probs, axis=-1, keepdims=True)
        return block_grads(query_block, key_block, grad_block, probs, grad_probs, row_dot)

    query_grad, key_grad, value_grad = lax.map(
        one_group,
        (
            to_blocks(query_rows),
            to_blocks(key_rows),
            to_blocks(value_rows),
            to_blocks(grad_rows),
            row_max,
            totals,
        ),
    )
    return (from_blocks(query_grad), from_blocks(key_grad), from_blocks(value_grad))


def cross_stats(query_rows, key_rows, allowed):

    def one_group(blocks):
        query_block, key_block = blocks
        scores = block_scores(query_block, key_block, allowed)
        max_block = jnp.max(scores, axis=-1)
        total_block = jnp.sum(
            jnp.where(allowed[None], jnp.exp(scores - max_block[..., None]), 0.0), axis=-1
        )
        return (max_block, total_block)

    return lax.map(one_group, (to_blocks(query_rows), to_blocks(key_rows)))


def cross_partial(query_rows, key_rows, value_rows, allowed, row_max, totals):

    def one_group(blocks):
        query_block, key_block, value_block, max_block, total_block = blocks
        probs = block_probs(query_block, key_block, allowed, max_block, total_block)
        return jnp.einsum(
            "hsf,fhd->shd",
            probs.astype(jnp.bfloat16),
            value_block,
            preferred_element_type=jnp.float32,
        )

    return from_blocks(
        lax.map(
            one_group,
            (to_blocks(query_rows), to_blocks(key_rows), to_blocks(value_rows), row_max, totals),
        )
    )


def cross_row_dot(query_rows, key_rows, value_rows, allowed, grad_rows, row_max, totals):

    def one_group(blocks):
        query_block, key_block, value_block, grad_block, max_block, total_block = blocks
        probs = block_probs(query_block, key_block, allowed, max_block, total_block)
        grad_probs = jnp.einsum(
            "shd,fhd->hsf", grad_block, value_block, preferred_element_type=jnp.float32
        )
        return jnp.sum(probs * grad_probs, axis=-1)

    return lax.map(
        one_group,
        (
            to_blocks(query_rows),
            to_blocks(key_rows),
            to_blocks(value_rows),
            to_blocks(grad_rows),
            row_max,
            totals,
        ),
    )


def cross_partial_grads(
    query_rows, key_rows, value_rows, allowed, grad_rows, row_max, totals, row_dot
):

    def one_group(blocks):
        query_block, key_block, value_block, grad_block, max_block, total_block, dot_block = blocks
        probs = block_probs(query_block, key_block, allowed, max_block, total_block)
        grad_probs = jnp.einsum(
            "shd,fhd->hsf", grad_block, value_block, preferred_element_type=jnp.float32
        )
        return block_grads(
            query_block, key_block, grad_block, probs, grad_probs, dot_block[..., None]
        )

    query_grad, key_grad, value_grad = lax.map(
        one_group,
        (
            to_blocks(query_rows),
            to_blocks(key_rows),
            to_blocks(value_rows),
            to_blocks(grad_rows),
            row_max,
            totals,
            row_dot,
        ),
    )
    return (from_blocks(query_grad), from_blocks(key_grad), from_blocks(value_grad))


def local(
    tokens,
    memory,
    cotangent,
    self_project,
    self_output,
    cross_query,
    cross_memory,
    cross_output,
    expand,
    contract,
    norm_gains,
    norm_shifts,
    target_length,
    memory_length,
    cross_mask,
):
    gathered = (
        lax.all_gather(self_project, ("dp", "frames"), axis=0, tiled=True),
        lax.all_gather(self_output, ("dp", "frames"), axis=0, tiled=True),
        lax.all_gather(cross_query, ("dp", "frames"), axis=0, tiled=True),
        lax.all_gather(cross_memory, ("dp", "frames"), axis=0, tiled=True),
        lax.all_gather(cross_output, ("dp", "frames"), axis=0, tiled=True),
        lax.all_gather(expand, ("dp", "frames"), axis=0, tiled=True),
        lax.all_gather(contract, ("dp", "frames"), axis=0, tiled=True),
        lax.all_gather(norm_gains, ("dp", "frames"), axis=1, tiled=True),
        lax.all_gather(norm_shifts, ("dp", "frames"), axis=1, tiled=True),
    )
    (
        w_self,
        w_self_out,
        w_query,
        w_memory,
        w_cross_out,
        w_expand,
        w_contract,
        gains_low,
        shifts_low,
    ) = gathered
    gains = gains_low.astype(jnp.float32)
    shifts = shifts_low.astype(jnp.float32)
    model_width = w_self_out.shape[0]
    residual_in = tokens[0]
    length = residual_in.shape[0]
    positions = jnp.arange(length)
    row_valid = positions < target_length[0]
    causal = positions[:, None] >= positions[None, :]
    item_count = memory.shape[0]
    frame_count = memory.shape[1]
    own_item = lax.axis_index("frames")
    normed_one_f, back_one = jax.vjp(layer_norm, residual_in, gains[0], shifts[0])
    normed_one = normed_one_f.astype(jnp.bfloat16)
    joint_rows = matmul(normed_one, w_self).astype(jnp.bfloat16)
    self_queries = split_heads(joint_rows[:, :model_width])
    self_keys = split_heads(joint_rows[:, model_width : 2 * model_width])
    self_values = split_heads(joint_rows[:, 2 * model_width :])
    self_mix, self_max, self_totals = attend_whole(self_queries, self_keys, self_values, causal)
    self_mix_low = self_mix.astype(jnp.bfloat16)
    self_branch = matmul(self_mix_low, w_self_out)
    first_sum = residual_in + self_branch
    normed_two_f, back_two = jax.vjp(layer_norm, first_sum, gains[1], shifts[1])
    normed_two = normed_two_f.astype(jnp.bfloat16)
    cross_queries = matmul(normed_two, w_query).astype(jnp.bfloat16)
    every_query = lax.all_gather(cross_queries[None], "frames", axis=0, tiled=True)
    query_heads = split_heads(every_query)
    frame_start = own_item * frame_count
    local_frames = frame_start + jnp.arange(frame_count)
    local_mask = lax.dynamic_slice_in_dim(cross_mask, frame_start, frame_count, 1)
    frame_ok = (local_frames[None, :] < memory_length[:, None]) & (
        (local_mask == 1) | (local_frames[None, :] == 0)
    )
    memory_rows = matmul(memory.reshape(item_count * frame_count, model_width), w_memory).astype(
        jnp.bfloat16
    )
    memory_rows = memory_rows.reshape(item_count, frame_count, 2 * model_width)
    memory_keys = split_heads(memory_rows[..., :model_width])
    memory_values = split_heads(memory_rows[..., model_width:])

    def item_stats(inputs):
        query_item, key_item, frame_item = inputs
        return cross_stats(
            query_item, key_item, jnp.broadcast_to(frame_item[None, :], (length, frame_count))
        )

    local_max, local_totals = lax.map(item_stats, (query_heads, memory_keys, frame_ok))
    cross_max = lax.pmax(local_max.astype(jnp.bfloat16), "frames").astype(local_max.dtype)
    cross_totals = lax.psum(
        (local_totals * jnp.exp(local_max - cross_max)).astype(jnp.bfloat16), "frames"
    ).astype(jnp.float32)

    def item_partial(inputs):
        query_item, key_item, value_item, frame_item, max_item, total_item = inputs
        allowed = jnp.broadcast_to(frame_item[None, :], (length, frame_count))
        return cross_partial(query_item, key_item, value_item, allowed, max_item, total_item)

    partial_mix = lax.map(
        item_partial, (query_heads, memory_keys, memory_values, frame_ok, cross_max, cross_totals)
    )
    cross_mix = lax.psum_scatter(
        partial_mix.astype(jnp.bfloat16), "frames", scatter_dimension=0, tiled=True
    ).astype(jnp.float32)[0]
    cross_mix_low = cross_mix.astype(jnp.bfloat16)
    cross_branch = matmul(cross_mix_low, w_cross_out)
    second_sum = first_sum + cross_branch
    normed_three_f, back_three = jax.vjp(layer_norm, second_sum, gains[2], shifts[2])
    normed_three = normed_three_f.astype(jnp.bfloat16)
    hidden = matmul(normed_three, w_expand)
    active_f, gelu_back = jax.vjp(exact_gelu, hidden)
    active = active_f.astype(jnp.bfloat16)
    feed_branch = matmul(active, w_contract)
    third_sum = second_sum + feed_branch
    final_rows, back_final = jax.vjp(layer_norm, third_sum, gains[3], shifts[3])
    result = jnp.where(row_valid[:, None], final_rows, 0.0)
    row_weight = row_valid.astype(jnp.float32)[:, None]
    squares = jnp.stack(
        [
            jnp.sum(row_weight * member * member)
            for member in (third_sum, self_branch, cross_branch, feed_branch)
        ]
    )
    squares_all, counted = lax.psum((squares, jnp.sum(row_weight)), ("dp", "frames"))
    branch_rms = jnp.sqrt(squares_all / (counted * model_width))
    grad_result = jnp.where(row_valid[:, None], cotangent[0], 0.0)
    grad_third, gain_grad_three, shift_grad_three = back_final(grad_result)
    feed_low = grad_third.astype(jnp.bfloat16)
    contract_grad = matmul(active.T, feed_low)
    grad_active = matmul(feed_low, w_contract.T)
    grad_hidden = gelu_back(grad_active)[0].astype(jnp.bfloat16)
    expand_grad = matmul(normed_three.T, grad_hidden)
    grad_normed_three = matmul(grad_hidden, w_expand.T)
    grad_second_part, gain_grad_two, shift_grad_two = back_three(grad_normed_three)
    grad_second = grad_third + grad_second_part
    cross_low = grad_second.astype(jnp.bfloat16)
    cross_output_grad = matmul(cross_mix_low.T, cross_low)
    grad_cross_mix = matmul(cross_low, w_cross_out.T).astype(jnp.bfloat16)
    every_grad = split_heads(lax.all_gather(grad_cross_mix[None], "frames", axis=0, tiled=True))

    def item_dot(inputs):
        query_item, key_item, value_item, frame_item, grad_item, max_item, total_item = inputs
        allowed = jnp.broadcast_to(frame_item[None, :], (length, frame_count))
        return cross_row_dot(
            query_item, key_item, value_item, allowed, grad_item, max_item, total_item
        )

    local_dot = lax.map(
        item_dot,
        (query_heads, memory_keys, memory_values, frame_ok, every_grad, cross_max, cross_totals),
    )
    row_dot = lax.psum(local_dot.astype(jnp.bfloat16), "frames").astype(jnp.float32)

    def item_grads(inputs):
        query_item, key_item, value_item, frame_item, grad_item, max_item, total_item, dot_item = (
            inputs
        )
        allowed = jnp.broadcast_to(frame_item[None, :], (length, frame_count))
        return cross_partial_grads(
            query_item, key_item, value_item, allowed, grad_item, max_item, total_item, dot_item
        )

    query_parts, key_parts, value_parts = lax.map(
        item_grads,
        (
            query_heads,
            memory_keys,
            memory_values,
            frame_ok,
            every_grad,
            cross_max,
            cross_totals,
            row_dot,
        ),
    )
    query_grad = lax.psum_scatter(
        query_parts.astype(jnp.bfloat16), "frames", scatter_dimension=0, tiled=True
    ).astype(jnp.float32)[0]
    memory_low = (
        jnp.concatenate([key_parts, value_parts], axis=2)
        .astype(jnp.bfloat16)
        .reshape(item_count * frame_count, 2 * model_width)
    )
    cross_memory_grad = matmul(memory.reshape(item_count * frame_count, model_width).T, memory_low)
    memory_grad = matmul(memory_low, w_memory.T).reshape(item_count, frame_count, model_width)
    query_low = query_grad.astype(jnp.bfloat16)
    cross_query_grad = matmul(normed_two.T, query_low)
    grad_normed_two = matmul(query_low, w_query.T)
    grad_first_part, gain_grad_one, shift_grad_one = back_two(grad_normed_two)
    grad_first = grad_second + grad_first_part
    self_low = grad_first.astype(jnp.bfloat16)
    self_output_grad = matmul(self_mix_low.T, self_low)
    grad_self_mix = matmul(self_low, w_self_out.T).astype(jnp.bfloat16)
    self_query_grad, self_key_grad, self_value_grad = attend_whole_back(
        self_queries,
        self_keys,
        self_values,
        causal,
        split_heads(grad_self_mix),
        self_max,
        self_totals,
    )
    joint_grad = jnp.concatenate([self_query_grad, self_key_grad, self_value_grad], axis=1).astype(
        jnp.bfloat16
    )
    self_project_grad = matmul(normed_one.T, joint_grad)
    grad_normed_one = matmul(joint_grad, w_self.T)
    grad_input_part, gain_grad_zero, shift_grad_zero = back_one(grad_normed_one)
    tokens_grad = grad_first + grad_input_part
    gain_grads = jnp.stack([gain_grad_zero, gain_grad_one, gain_grad_two, gain_grad_three])
    shift_grads = jnp.stack([shift_grad_zero, shift_grad_one, shift_grad_two, shift_grad_three])
    reduced = (
        lax.psum_scatter(self_project_grad, ("dp", "frames"), scatter_dimension=0, tiled=True),
        lax.psum_scatter(self_output_grad, ("dp", "frames"), scatter_dimension=0, tiled=True),
        lax.psum_scatter(cross_query_grad, ("dp", "frames"), scatter_dimension=0, tiled=True),
        lax.psum_scatter(cross_memory_grad, ("dp", "frames"), scatter_dimension=0, tiled=True),
        lax.psum_scatter(cross_output_grad, ("dp", "frames"), scatter_dimension=0, tiled=True),
        lax.psum_scatter(expand_grad, ("dp", "frames"), scatter_dimension=0, tiled=True),
        lax.psum_scatter(contract_grad, ("dp", "frames"), scatter_dimension=0, tiled=True),
        lax.psum_scatter(gain_grads, ("dp", "frames"), scatter_dimension=1, tiled=True),
        lax.psum_scatter(shift_grads, ("dp", "frames"), scatter_dimension=1, tiled=True),
    )
    (
        project_part,
        output_part,
        query_part,
        memory_part,
        cross_out_part,
        expand_part,
        contract_part,
        gains_part,
        shifts_part,
    ) = reduced
    return (
        result[None],
        tokens_grad[None],
        memory_grad,
        project_part,
        output_part,
        query_part,
        memory_part,
        cross_out_part,
        expand_part,
        contract_part,
        gains_part,
        shifts_part,
        branch_rms,
    )


def solution(mesh):
    fits = (mesh.shape["dp"], mesh.shape["frames"]) == (2 * Z_CHIPS, 4)
    return jax.shard_map(
        local_fused if fits else local,
        mesh=mesh,
        in_specs=(
            P(("dp", "frames"), None, None),
            P("dp", "frames", None),
            P(("dp", "frames"), None, None),
            P(("dp", "frames"), None),
            P(("dp", "frames"), None),
            P(("dp", "frames"), None),
            P(("dp", "frames"), None),
            P(("dp", "frames"), None),
            P(("dp", "frames"), None),
            P(("dp", "frames"), None),
            P(None, ("dp", "frames")),
            P(None, ("dp", "frames")),
            P(("dp", "frames")),
            P("dp"),
            P("dp", None),
        ),
        out_specs=(
            P(("dp", "frames"), None, None),
            P(("dp", "frames"), None, None),
            P("dp", "frames", None),
            P(("dp", "frames"), None),
            P(("dp", "frames"), None),
            P(("dp", "frames"), None),
            P(("dp", "frames"), None),
            P(("dp", "frames"), None),
            P(("dp", "frames"), None),
            P(("dp", "frames"), None),
            P(None, ("dp", "frames")),
            P(None, ("dp", "frames")),
            P(),
        ),
        check_vma=False,
    )
```

```python
import functools
from types import SimpleNamespace

import jax
import jax.numpy as jnp
from jax import lax
from jax.experimental import pallas as pl
from jax.experimental.pallas import tpu as pltpu
from jax.sharding import PartitionSpec as P

MESH = pl.DeviceIdType.MESH
F32 = jnp.float32
BF16 = jnp.bfloat16
HEAD_DIM = 64
LANES = 128
WIDE = 512


def dot(a, b):
    return jnp.dot(a, b, preferred_element_type=F32)


def dot_nt(a, b):
    return lax.dot_general(a, b, (((1,), (1,)), ((), ())), preferred_element_type=F32)


def place():
    dp, fr = lax.axis_index("dp"), lax.axis_index("frames")
    z, y = lax.div(dp, 2), lax.rem(dp, 2)
    x, c = lax.div(fr, 2), lax.rem(fr, 2)

    def dev(zz, yy, xx, cc):
        return {"dp": zz * 2 + yy, "frames": xx * 2 + cc}

    me = SimpleNamespace(z=z, y=y, x=x, c=c, fr=fr, dev=dev)
    me.xn = dev(z, y, 1 - x, c)
    me.yn = dev(z, 1 - y, x, c)
    me.sib = dev(z, y, x, 1 - c)
    me.diag = dev(z, y, 1 - x, 1 - c)
    return me


def remote(src, dst, send, recv, device):
    return pltpu.make_async_remote_copy(
        src_ref=src, dst_ref=dst, send_sem=send, recv_sem=recv, device_id=device, device_id_type=MESH
    )


def z_ways(me, nz):
    sends = {dz: (me.z != nz - 1) if dz == 1 else (me.z != 0) if dz == nz - 1 else None for dz in range(1, nz)}
    inner = (me.z == 1) | (me.z == 2)
    upper = me.z == 2
    return sends, inner, lax.rem(me.z + 2, nz), jnp.where(upper, nz - 1, 0), jnp.where(upper, nz - 1, 1)


def when(condition, action):
    if condition is None:
        action()
    else:
        pl.when(condition)(action)


def gather_steps(me, w, send, recv, nz, tilt=False):
    half = w.shape[4] if tilt else w.shape[4] // 2
    xo, yo, co = 1 - me.x, 1 - me.y, 1 - me.c

    def cp(view, s, device):
        return remote(view, view, send.at[s], recv.at[s], device)

    def spot(y, x, c):
        return w.at[:, y, x, c]

    def one(dz, y, x):
        return w.at[lax.rem(me.z + nz - dz, nz), y, x, me.c]

    def part(y, x, lower):
        return w.at[:, y, x, me.c, 0:half] if lower else w.at[:, y, x, me.c, half:]

    sends, inner, source, target, distance = z_ways(me, nz)
    passed = w.at[source, me.y, me.x, me.c]

    def pass_copy():
        to = me.dev(target, me.y, me.x, me.c)
        return remote(passed, passed, send.at[nz + 7], recv.at[distance - 1], to)

    def z_copy(dz):
        return cp(one(0, me.y, me.x), dz - 1, me.dev(lax.rem(me.z + dz, nz), me.y, me.x, me.c))

    def z_arrived(dz):
        cp(one(dz, me.y, me.x), dz - 1, me.xn).wait_recv()

    def step_z():
        for dz in range(1, nz):
            when(sends[dz], lambda: z_copy(dz).start())

    def step_relay():
        @pl.when(inner)
        def _():
            z_arrived(2)
            pass_copy().start()

    def step_near():
        z_arrived(1)
        z_arrived(3)
        pl.when(jnp.logical_not(inner))(lambda: z_arrived(2))
        cp(spot(me.y, me.x, me.c), nz - 1, me.xn).start()
        cp(spot(me.y, me.x, me.c), nz, me.yn).start()
        cp(spot(me.y, me.x, me.c), nz + 1, me.sib).start()

    def step_far():
        cp(spot(me.y, xo, me.c), nz - 1, me.xn).wait_recv()
        cp(part(me.y, xo, True), nz + 2, me.yn).start()
        cp(spot(me.y, xo, me.c), nz + 3, me.sib).start()
        cp(spot(yo, me.x, me.c), nz, me.yn).wait_recv()
        if not tilt:
            cp(part(yo, me.x, False), nz + 4, me.xn).start()
        cp(spot(yo, me.x, me.c), nz + 5, me.sib).start()

    def step_last():
        cp(part(yo, xo, True), nz + 2, me.yn).wait_recv()
        if not tilt:
            cp(part(yo, xo, False), nz + 4, me.xn).wait_recv()
        cp(spot(yo, xo, me.c), nz + 6, me.sib).start()

    def step_done():
        for y, x, s in ((me.y, me.x, nz + 1), (me.y, xo, nz + 3), (yo, me.x, nz + 5), (yo, xo, nz + 6)):
            cp(spot(y, x, co), s, me.sib).wait_recv()

    def drain():
        for dz in range(1, nz):
            when(sends[dz], lambda: z_copy(dz).wait_send())
        pl.when(inner)(lambda: pass_copy().wait_send())
        for s in (nz - 1, nz):
            cp(spot(me.y, me.x, me.c), s, me.xn).wait_send()
        for y, x, s in ((me.y, me.x, nz + 1), (me.y, xo, nz + 3), (yo, me.x, nz + 5), (yo, xo, nz + 6)):
            cp(spot(y, x, me.c), s, me.xn).wait_send()
        cp(part(me.y, xo, True), nz + 2, me.xn).wait_send()
        if not tilt:
            cp(part(yo, me.x, False), nz + 4, me.xn).wait_send()

    return SimpleNamespace(
        z=step_z, relay=step_relay, near=step_near, far=step_far, last=step_last, done=step_done, drain=drain
    )


def gather_late_steps(me, w, send, recv, nz):
    half = w.shape[4] // 2
    xo, yo, co = 1 - me.x, 1 - me.y, 1 - me.c

    def cp(view, s, device):
        return remote(view, view, send.at[s], recv.at[s], device)

    def one(y, x):
        return w.at[me.z, y, x, me.c]

    def part(y, x, lower):
        return w.at[me.z, y, x, me.c, 0:half] if lower else w.at[me.z, y, x, me.c, half:]

    def layer(dz, c):
        return w.at[lax.rem(me.z + nz - dz, nz), :, :, c]

    def step_near():
        cp(one(me.y, me.x), 0, me.xn).start()
        cp(one(me.y, me.x), 1, me.yn).start()

    def step_far():
        cp(one(me.y, xo), 0, me.xn).wait_recv()
        cp(part(me.y, xo, True), 2, me.yn).start()
        cp(one(yo, me.x), 1, me.yn).wait_recv()
        cp(part(yo, me.x, False), 3, me.xn).start()

    def step_square():
        cp(part(yo, xo, True), 2, me.yn).wait_recv()
        cp(part(yo, xo, False), 3, me.xn).wait_recv()
        cp(layer(0, me.c), 4, me.sib).start()

    sends, inner, source, target, distance = z_ways(me, nz)
    passed = w.at[source, :, :, me.c]

    def pass_copy():
        to = me.dev(target, me.y, me.x, me.c)
        return remote(passed, passed, send.at[nz + 7], recv.at[4 + distance], to)

    def z_copy(dz):
        return cp(layer(0, me.c), 4 + dz, me.dev(lax.rem(me.z + dz, nz), me.y, me.x, me.c))

    def step_z(dz):
        when(sends[dz], lambda: z_copy(dz).start())

    def step_pass(dz):
        cp(layer(dz, me.c), 4 + dz, me.xn).wait_recv()
        if dz == 2:
            pl.when(inner)(lambda: pass_copy().start())
        cp(layer(dz, me.c), 3 + nz + dz, me.sib).start()

    def step_done():
        cp(layer(0, co), 4, me.sib).wait_recv()
        for dz in range(1, nz):
            cp(layer(dz, co), 3 + nz + dz, me.sib).wait_recv()

    def drain():
        cp(one(me.y, me.x), 0, me.xn).wait_send()
        cp(one(me.y, me.x), 1, me.xn).wait_send()
        cp(part(me.y, xo, True), 2, me.xn).wait_send()
        cp(part(yo, me.x, False), 3, me.xn).wait_send()
        cp(layer(0, me.c), 4, me.xn).wait_send()
        for dz in range(1, nz):
            when(sends[dz], lambda: z_copy(dz).wait_send())
            cp(layer(dz, me.c), 3 + nz + dz, me.xn).wait_send()
        pl.when(inner)(lambda: pass_copy().wait_send())

    return SimpleNamespace(
        near=step_near, far=step_far, square=step_square, z=step_z, pass_on=step_pass, done=step_done, drain=drain
    )


class Moves:
    def __init__(self, moves, send, recv, core_recv):
        self.moves, self.send, self.recv, self.core_recv = moves, send, recv, core_recv

    def cp(self, i):
        src, dst, to = self.moves[i][:3]
        return remote(src, dst, self.send.at[i], self.recv.at[i - 1] if i else self.core_recv, to)

    def go(self, i):
        _, _, _, _, credit, turn, slots, _, sends, _ = self.moves[i]

        def action():
            if turn >= slots:
                pl.semaphore_wait(credit, 1)
            self.cp(i).start()

        when(sends, action)

    def free(self, i):
        _, _, _, giver, credit, turn, slots, turns, _, receives = self.moves[i]
        if turn + slots < turns:
            when(receives, lambda: pl.semaphore_signal(credit, inc=1, device_id=giver, device_id_type=MESH))

    def arrive(self, *at):
        for i in at:
            when(self.moves[i][9], lambda: self.cp(i).wait_recv())

    def drain(self):
        for i in range(len(self.moves)):
            when(self.moves[i][8], lambda: self.cp(i).wait_send())


def add(view, arrived):
    view[...] = (view[...].astype(F32) + arrived[...].astype(F32)).astype(view.dtype)


def add_core(me, w, core, nz):
    def body(zz, carry):
        for y in range(2):
            for x in range(2):
                add(w.at[zz, y, x, me.c], core.at[zz, y, x])
        return carry

    lax.fori_loop(0, nz, body, 0)


RELAY = 8


def z_moves(me, nz, layer, zs, relay, credit, turn):
    last = nz - 1
    outer = (me.z == 0) | (me.z == last)

    def at_z(zz):
        return me.dev(zz, me.y, me.x, me.c)

    moves = []
    for dz in range(1, nz):
        to, giver = lax.rem(me.z + dz, nz), lax.rem(me.z + nz - dz, nz)
        sends = {1: me.z != last, last: me.z != 0}.get(dz)
        receives = {1: me.z != 0, last: me.z != last}.get(dz)
        moves.append((layer(to), zs.at[dz - 1], at_z(to), at_z(giver), credit.at[dz - 1], *turn, sends, receives))
    near = jnp.where(me.z == last, last - 1, 1)
    back = jnp.where(me.z == last - 1, last, 0)
    moves.append(
        (layer(last - me.z), relay, at_z(near), at_z(back), credit.at[nz - 1], *turn, outer, jnp.logical_not(outer))
    )
    return moves, outer, jnp.where(me.z == last - 1, 0, last)


def scatter_steps(me, w, box, sems, credit, nz, core_turn, turn, sink):
    half = w.shape[4] // 2
    xo, yo, co = 1 - me.x, 1 - me.y, 1 - me.c
    core = box[0].at[core_turn[0] % core_turn[1]]
    y1, x1, x2, y2, zs, relay = (b.at[turn[0] % turn[1]] for b in box[1:7])
    total = box[7]
    both = (None, None)

    def layer(zz):
        return w.at[zz, me.y, me.x, me.c]

    moves = [
        (w.at[:, :, :, co], core, me.sib, me.sib, credit.at[0], *core_turn, *both),
        (w.at[:, yo, :, me.c, 0:half], y1, me.yn, me.yn, credit.at[1], *turn, *both),
        (w.at[:, :, xo, me.c, half:], x1, me.xn, me.xn, credit.at[2], *turn, *both),
        (w.at[:, me.y, xo, me.c, 0:half], x2, me.xn, me.xn, credit.at[3], *turn, *both),
        (w.at[:, yo, me.x, me.c, half:], y2, me.yn, me.yn, credit.at[4], *turn, *both),
    ]
    along, outer, handed = z_moves(me, nz, layer, zs, relay, credit.at[5 : 5 + nz], turn)
    m = Moves(moves + along, *sems)

    def step_a():
        m.go(0)

    def step_b():
        m.arrive(0)
        add_core(me, w, core, nz)
        m.free(0)
        m.go(1)
        m.go(2)

    def step_c():
        m.arrive(1, 2)

        def body(zz, carry):
            for o in range(2):
                add(w.at[zz, me.y, o, me.c, 0:half], y1.at[zz, o])
                add(w.at[zz, o, me.x, me.c, half:], x1.at[zz, o])
            return carry

        lax.fori_loop(0, nz, body, 0)
        m.free(1)
        m.free(2)
        m.go(3)
        m.go(4)

    def step_d():
        m.arrive(3, 4)

        def body(zz, carry):
            add(w.at[zz, me.y, me.x, me.c, 0:half], x2.at[zz])
            add(w.at[zz, me.y, me.x, me.c, half:], y2.at[zz])
            return carry

        lax.fori_loop(0, nz, body, 0)
        m.free(3)
        m.free(4)
        m.go(RELAY)
        m.go(5)
        m.go(7)
        pl.when(outer)(lambda: m.go(6))

    def step_r():
        @pl.when(jnp.logical_not(outer))
        def _():
            m.cp(RELAY).wait_recv()
            add(layer(handed), relay)
            m.go(6)

        m.free(RELAY)

    def step_e():
        m.arrive(5, 6, 7)
        total[...] = layer(me.z)[...].astype(F32) + zs[1].astype(F32)

        @pl.when(me.z != 0)
        def _():
            total[...] += zs[0].astype(F32)

        @pl.when(me.z != nz - 1)
        def _():
            total[...] += zs[2].astype(F32)

        sink(total[...])
        for i in (5, 6, 7):
            m.free(i)

    return SimpleNamespace(a=step_a, b=step_b, c=step_c, d=step_d, r=step_r, e=step_e, drain=m.drain)


def scatter_early_steps(me, w, box, sems, credit, nz, core_turn, turn, sink):
    half = w.shape[4] // 2
    xo, yo, co = 1 - me.x, 1 - me.y, 1 - me.c
    core = box[0].at[core_turn[0] % core_turn[1]]
    y1, x1, x2, y2, zs, relay = (b.at[turn[0] % turn[1]] for b in box[1:7])
    both = (None, None)
    base = 5 + nz

    def layer(zz):
        return w.at[zz, :, :, me.c]

    moves = [
        (w.at[:, :, :, co], core, me.sib, me.sib, credit.at[0], *core_turn, *both),
        (w.at[me.z, yo, :, me.c, 0:half], y1, me.yn, me.yn, credit.at[base], *turn, *both),
        (w.at[me.z, :, xo, me.c, half:], x1, me.xn, me.xn, credit.at[base + 1], *turn, *both),
        (w.at[me.z, me.y, xo, me.c, 0:half], x2, me.xn, me.xn, credit.at[base + 2], *turn, *both),
        (w.at[me.z, yo, me.x, me.c, half:], y2, me.yn, me.yn, credit.at[base + 3], *turn, *both),
    ]
    along, outer, handed = z_moves(me, nz, layer, zs, relay, credit.at[base + 4 : base + 4 + nz], turn)
    m = Moves(moves + along, *sems)

    def add_layer(zz, arrived):
        for y in range(2):
            for x in range(2):
                add(w.at[zz, y, x, me.c], arrived.at[y, x])

    def step_a():
        m.go(0)

    def step_b():
        m.arrive(0)
        add_core(me, w, core, nz)
        m.free(0)

    def step_z():
        m.go(RELAY)
        m.go(5)
        m.go(7)
        pl.when(outer)(lambda: m.go(6))

    def step_r():
        @pl.when(jnp.logical_not(outer))
        def _():
            m.cp(RELAY).wait_recv()
            add_layer(handed, relay)
            m.go(6)

        m.free(RELAY)

    def step_c():
        m.arrive(5, 6, 7)
        add_layer(me.z, zs.at[1])
        pl.when(me.z != 0)(lambda: add_layer(me.z, zs.at[0]))
        pl.when(me.z != nz - 1)(lambda: add_layer(me.z, zs.at[2]))
        for i in (5, 6, 7):
            m.free(i)
        m.go(1)
        m.go(2)

    def step_d():
        m.arrive(1, 2)
        for o in range(2):
            add(w.at[me.z, me.y, o, me.c, 0:half], y1.at[o])
            add(w.at[me.z, o, me.x, me.c, half:], x1.at[o])
        m.free(1)
        m.free(2)
        m.go(3)
        m.go(4)

    def step_e():
        m.arrive(3, 4)
        late = jnp.concatenate([x2[...].astype(F32), y2[...].astype(F32)], axis=0)
        sink(w[me.z, me.y, me.x, me.c].astype(F32) + late)
        m.free(3)
        m.free(4)

    return SimpleNamespace(a=step_a, b=step_b, z=step_z, r=step_r, c=step_c, d=step_d, e=step_e, drain=m.drain)


def lane_masks():
    lane = lax.broadcasted_iota(jnp.int32, (1, LANES), 1)
    left = jnp.where(lane < HEAD_DIM, 1.0, 0.0).astype(BF16)
    return left, (1.0 - left.astype(F32)).astype(BF16)


def two_heads(block):
    left, right = lane_masks()
    return jnp.concatenate([block * left, block * right], axis=0)


def one_block(pair):
    rows = pair.shape[0] // 2
    lane = lax.broadcasted_iota(jnp.int32, (rows, LANES), 1)
    return jnp.where(lane < HEAD_DIM, pair[:rows], pair[rows:])


def at128(p, base=0):
    return pl.ds(pl.multiple_of(base + p * LANES, LANES), LANES)


def put_stat(stat, p, pair):
    rows = pair.shape[0] // 2
    lane = lax.broadcasted_iota(jnp.int32, stat.shape, 1)
    stat = jnp.where(lane == 2 * p, pair[:rows], stat)
    return jnp.where(lane == 2 * p + 1, pair[rows:], stat)


def normalise(values):
    center = values - jnp.mean(values, axis=-1, keepdims=True)
    spread = jnp.mean(center * center, axis=-1, keepdims=True)
    return center * lax.rsqrt(spread + 1e-05)


def forward(r, me, nz):
    rows, d = r.tokens.shape
    items, frames = r.kv.shape[:2]
    pairs = d // LANES

    def weight(k, n, size=WIDE):
        return r.wg[k, :, :, :, :, :, n * size : (n + 1) * size].reshape(d, size)

    def product(x, k, sink):
        sink(dot(x, weight(k, 0, d)))

    def ln(values, i):
        return normalise(values) * r.gs[i : i + 1, :] + r.gs[4 + i : 5 + i, :]

    def norms_in():
        for g in range(2 * nz):
            total = r.ng[g // 2, g % 2, 0, 0, 0:16, :].astype(F32)
            for f in range(1, 4):
                total = total + r.ng[g // 2, g % 2, f // 2, f % 2, 0:16, :].astype(F32)
            r.gs[:, g * LANES : (g + 1) * LANES] = total

    def norm_one():
        pltpu.make_async_copy(r.tokens, r.first, r.own_sem.at[1]).wait()
        r.xb[...] = ln(r.first[...], 0).astype(BF16)
        r.n1t[...] = r.xb[...].T

    def joint(q):
        def sink(v):
            r.joint[:, q * d : (q + 1) * d] = v.astype(BF16)

        product(r.xb[...], q, sink)

    def self_attention(half):
        row = lax.rem(lax.broadcasted_iota(jnp.int32, (2 * rows, rows), 0), rows)
        causal = row >= lax.broadcasted_iota(jnp.int32, (2 * rows, rows), 1)

        def body(p, stat):
            q2 = two_heads(r.joint[:, at128(p)] * jnp.asarray(HEAD_DIM**-0.5, BF16))
            s = dot_nt(q2, r.joint[:, at128(p, d)])
            s = jnp.where(causal, s, -1e30)
            m = jnp.max(s, axis=-1, keepdims=True)
            e = jnp.exp(s - m)
            total = jnp.sum(e, axis=-1, keepdims=True)
            o2 = dot(e.astype(BF16), r.joint[:, at128(p, 2 * d)]) / total
            r.xb[:, at128(p)] = one_block(o2).astype(BF16)
            return put_stat(stat, p, m + jnp.log(total))

        first = jnp.zeros((rows, LANES), F32) if half == 0 else r.wcol[...]
        stat = lax.fori_loop(half * pairs // 2, (half + 1) * pairs // 2, body, first)
        if half == 0:
            r.wcol[...] = stat
        else:
            r.slse[...] = stat.T[0:16]
            r.smixt[...] = r.xb[...].T

    def self_out():
        def sink(v):
            r.branch[...] = v

        product(r.xb[...], 3, sink)
        r.first[...] = r.first[...] + r.branch[...]
        squares(1, r.branch[...])
        r.xb[...] = ln(r.first[...], 1).astype(BF16)
        r.n2t[...] = r.xb[...].T

    def squares(i, values):
        ok = lax.broadcasted_iota(jnp.int32, (rows, 1), 0) < r.tl[0]
        total = jnp.sum(jnp.where(ok, values * values, 0.0))
        line = lax.broadcasted_iota(jnp.int32, r.sq.shape, 0)
        r.sq[...] = jnp.where(line == i, total, r.sq[...])

    def start_counts():
        line = lax.broadcasted_iota(jnp.int32, r.sq.shape, 0)
        r.sq[...] = jnp.where(line == 4, r.tl[0].astype(F32), 0.0)

    def queries():
        def sink(v):
            r.qa[me.fr] = v.astype(BF16)

        product(r.xb[...], 4, sink)

    def q_copy(f, s, device):
        return remote(r.qa.at[f], r.qa.at[f], r.q_send.at[s], r.q_recv.at[s], device)

    fx, fs, fd = (1 - me.x) * 2 + me.c, me.x * 2 + 1 - me.c, (1 - me.x) * 2 + 1 - me.c

    def q_start():
        q_copy(me.fr, 0, me.xn).start()
        q_copy(me.fr, 1, me.sib).start()

    def q_forward():
        q_copy(fx, 0, me.xn).wait_recv()
        q_copy(fx, 2, me.sib).start()

    def q_done():
        q_copy(fs, 1, me.sib).wait_recv()
        q_copy(fd, 2, me.sib).wait_recv()

    def mem_copy(t):
        return pltpu.make_async_copy(r.memory.at[t], r.rc.at[t % 2, 0 : r.memory.shape[1]], r.m_sem.at[t % 2])

    def memory_part(which, t):
        mem_copy(t).wait()
        stage = r.rc.at[t % 2, 0 : r.memory.shape[1]]
        for n in range(d // WIDE):
            v = dot(stage[...].reshape(frames, d), weight(5 + which, n))
            r.kv[t, :, which * d + n * WIDE : which * d + (n + 1) * WIDE] = v.astype(BF16)
        if which == 0:
            r.memt[:, t * frames : (t + 1) * frames] = stage[...].reshape(frames, d).T
        if t + 2 < items or which == 0:
            mem_copy((t + 2) % items).start()

    def mem_start():
        for t in range(min(2, items)):
            mem_copy(t).start()

    def cross_half(t, half):
        def body(p, stat):
            q2 = two_heads(r.qa[t, :, at128(p)] * jnp.asarray(HEAD_DIM**-0.5, BF16))
            s = dot_nt(q2, r.kv[t, :, at128(p)]) + r.bias[pl.ds(t, 1), :]
            m = jnp.max(s, axis=-1, keepdims=True)
            e = jnp.exp(s - m)
            total = jnp.sum(e, axis=-1, keepdims=True)
            o2 = dot(e.astype(BF16), r.kv[t, :, at128(p, d)]) / total
            r.op[t, :, at128(p)] = one_block(o2).astype(BF16)
            return put_stat(stat, p, m + jnp.log(total))

        first = jnp.zeros((rows, LANES), F32) if half == 0 else r.wcol[...]
        stat = lax.fori_loop(half * pairs // 2, (half + 1) * pairs // 2, body, first)
        if half == 0:
            r.wcol[...] = stat
        else:
            r.opl[t] = stat.T[0:16]

    def o_copies(t, slot, device):
        return (
            remote(r.op.at[t], r.orv.at[slot], r.o_send.at[slot], r.o_recv.at[slot], device),
            remote(r.opl.at[t], r.orl.at[slot], r.o_send.at[3 + slot], r.o_recv.at[3 + slot], device),
        )

    def o_start(t, slot, device):
        for cp in o_copies(t, slot, device):
            cp.start()

    def o_wait(t, slot, device):
        for cp in o_copies(t, slot, device):
            cp.wait_recv()

    def merge(parts, sink):
        lses = [lse[...] for _, lse in parts]
        top = functools.reduce(jnp.maximum, lses)
        shares = [jnp.exp(v - top) for v in lses]
        total = functools.reduce(jnp.add, shares)
        flat = jnp.concatenate([v / total for v in shares] + [jnp.zeros((LANES - 16 * len(parts), LANES), F32)], axis=0)
        r.wcol[...] = flat.T
        lane = lax.broadcasted_iota(jnp.int32, (rows, LANES), 1)
        for p in range(pairs):
            value = jnp.zeros((rows, LANES), F32)
            for i, (mix, _) in enumerate(parts):
                left = r.wcol[:, 16 * i + 2 * p : 16 * i + 2 * p + 1]
                right = r.wcol[:, 16 * i + 2 * p + 1 : 16 * i + 2 * p + 2]
                share = jnp.where(lane < HEAD_DIM, left, right)
                value = value + share * mix[:, p * LANES : (p + 1) * LANES].astype(F32)
            sink(p, value)
        return top + jnp.log(total)

    def send_far():
        o_start(fd, 0, me.sib)

    def send_side():
        o_start(fs, 1, me.sib)

    def merge_across():
        o_wait(fd, 0, me.sib)

        def sink(p, v):
            r.op[fx, :, p * LANES : (p + 1) * LANES] = v.astype(BF16)

        r.opl[fx] = merge([(r.op.at[fx], r.opl.at[fx]), (r.orv.at[0], r.orl.at[0])], sink)
        o_start(fx, 2, me.xn)

    def merge_own():
        o_wait(fs, 1, me.sib)
        o_wait(fx, 2, me.xn)

        def sink(p, v):
            r.xb[:, p * LANES : (p + 1) * LANES] = v.astype(BF16)

        parts = [(r.op.at[me.fr], r.opl.at[me.fr]), (r.orv.at[1], r.orl.at[1]), (r.orv.at[2], r.orl.at[2])]
        r.clse[...] = merge(parts, sink)
        r.cmixt[...] = r.xb[...].T

    def cross_out():
        def sink(v):
            r.branch[...] = v

        product(r.xb[...], 7, sink)
        squares(2, r.branch[...])
        r.second[...] = r.first[...] + r.branch[...]
        r.xb[...] = ln(r.second[...], 2).astype(BF16)
        r.n3t[...] = r.xb[...].T

    def expand(q):
        for n in range(d // WIDE):
            v = dot(r.xb[...], weight(8 + q, n))
            at = slice(q * d + n * WIDE, q * d + (n + 1) * WIDE)
            half = 0.5 * (1.0 + lax.erf(v * (2.0**-0.5)))
            r.active[:, at] = (v * half).astype(BF16)
            r.slope[:, at] = (half + v * jnp.exp(-0.5 * v * v) * 0.3989422804014327).astype(BF16)
        r.activet[q * d : (q + 1) * d, :] = r.active[:, q * d : (q + 1) * d].T

    def contract(q, fresh=False):
        def sink(v):
            r.branch[...] = v if fresh else r.branch[...] + v

        product(r.active[:, q * d : (q + 1) * d], 12 + q, sink)

    def finish():
        squares(3, r.branch[...])
        r.third[...] = r.second[...] + r.branch[...]
        squares(0, r.third[...])
        ok = lax.broadcasted_iota(jnp.int32, (rows, 1), 0) < r.tl[0]
        r.branch[...] = jnp.where(ok, ln(r.third[...], 3), 0.0)
        pltpu.make_async_copy(r.branch, r.result, r.own_sem.at[3]).start()

    part = functools.partial

    def item(t):
        return [part(cross_half, t, 0), part(cross_half, t, 1)]

    tasks = {
        0: [start_counts, mem_start],
        2: [norms_in, norm_one],
        4: [part(joint, 0)],
        5: [part(joint, 1)],
        6: [part(joint, 2), part(self_attention, 0), part(self_attention, 1)],
        7: [self_out],
        8: [queries, q_start],
        9: [part(memory_part, 0, t) for t in range(items)],
        10: [q_forward] + [part(memory_part, 1, t) for t in range(items)],
        11: [q_done, *item(fd), send_far, *item(fs), send_side],
        12: [*item(fx), merge_across],
        13: item(me.fr),
        14: [merge_own, cross_out, part(expand, 0), part(expand, 1), part(contract, LATE[0] - 12, True)],
        15: [part(expand, 2), part(expand, 3), part(contract, LATE[1] - 12)],
        16: [part(contract, LATE[2] - 12), part(contract, 0), finish],
    }

    def drain():
        q_copy(me.fr, 0, me.xn).wait_send()
        q_copy(me.fr, 1, me.sib).wait_send()
        q_copy(fx, 2, me.sib).wait_send()
        for t, slot, device in ((fd, 0, me.sib), (fs, 1, me.sib), (fx, 2, me.xn)):
            for cp in o_copies(t, slot, device):
                cp.wait_send()

    return tasks, drain, (fx, fs, fd)


def ln_back(values, gain_row, grad):
    center = values - jnp.mean(values, axis=-1, keepdims=True)
    scale = lax.rsqrt(jnp.mean(center * center, axis=-1, keepdims=True) + 1e-05)
    unit = center * scale
    gain_grad = jnp.sum(grad * unit, axis=0, keepdims=True)
    shift_grad = jnp.sum(grad, axis=0, keepdims=True)
    lifted = grad * gain_row
    inner = jnp.mean(lifted * unit, axis=-1, keepdims=True)
    back = scale * (lifted - jnp.mean(lifted, axis=-1, keepdims=True) - unit * inner)
    return back, gain_grad, shift_grad


def backward(r, me, nz, fronts):
    rows, d = r.first.shape
    items, frames = r.kv.shape[:2]
    pairs = d // LANES
    fx, fs, fd = fronts
    t = {}

    def grad_into(k, left, right, into=None):
        for n in range(d // WIDE):
            v = dot(left, right(n * WIDE, (n + 1) * WIDE)).astype(BF16)
            at = slice(n * WIDE, (n + 1) * WIDE)
            r.wg[k if into is None else into, :, :, :, :, :, at] = v.reshape(nz, 2, 2, 2, d // (8 * nz), WIDE)

    def through(k, grad):
        return dot_nt(grad, r.wg[k].reshape(d, d))

    def ln_step(i, values, grad, first=False):
        back, gain, shift = ln_back(values, r.gs[i : i + 1, :], grad)
        r.gr[...] = back if first else r.gr[...] + back
        r.nrow[i : i + 1, :] = gain
        r.nrow[4 + i : 5 + i, :] = shift

    def start():
        pltpu.make_async_copy(r.cotangent, r.gr, r.own_sem.at[2]).wait()
        r.biast[...] = jnp.concatenate([r.bias[...], jnp.zeros((LANES - r.bias.shape[0], frames), F32)], axis=0).T
        for g in range(d // LANES):
            r.nrow[8:16, g * LANES : (g + 1) * LANES] = r.sq[...]
        ok = lax.broadcasted_iota(jnp.int32, (rows, 1), 0) < r.tl[0]
        ln_step(3, r.third[...], jnp.where(ok, r.gr[...], 0.0), True)
        r.xb[...] = r.gr[...].astype(BF16)
        pltpu.make_async_copy(r.tokens, r.third, r.own_sem.at[1]).start()

    def contract(q):
        at = slice(q * d, (q + 1) * d)
        r.active[:, at] = (through(12 + q, r.xb[...]) * r.slope[:, at].astype(F32)).astype(BF16)

    def contract_grad(q):
        grad_into(12 + q, r.activet[q * d : (q + 1) * d, :], lambda lo, hi: r.xb[:, lo:hi])

    def onto(fresh, value):
        r.branch[...] = value if fresh else r.branch[...] + value

    def expand(q):
        if q == 0:
            pltpu.make_async_copy(r.branch, r.result, r.own_sem.at[3]).wait()
        onto(q == 0, through(8 + q, r.active[:, q * d : (q + 1) * d]))

    def expand_grad(q):
        grad_into(8 + q, r.n3t[...], lambda lo, hi: r.active[:, q * d + lo : q * d + hi])

    def cross_out():
        ln_step(2, r.second[...], r.branch[...])
        r.xb[...] = r.gr[...].astype(BF16)
        r.ga[me.fr] = through(7, r.xb[...]).astype(BF16)
        r.gl[me.fr, 0:16] = r.clse[...]

        def body(p, carry):
            left, right = row_dots(r.ga[me.fr, :, at128(p)], r.cmixt[at128(p), :])
            r.gl[me.fr, pl.ds(16 + 2 * p, 1), :] = left
            r.gl[me.fr, pl.ds(17 + 2 * p, 1), :] = right
            return carry

        lax.fori_loop(0, pairs, body, 0)

    def cross_out_grad():
        grad_into(7, r.cmixt[...], lambda lo, hi: r.xb[:, lo:hi])

    def row_dots(grad, mixt):
        prod = grad.astype(F32).T * mixt.astype(F32)
        return jnp.sum(prod[:HEAD_DIM], axis=0, keepdims=True), jnp.sum(prod[HEAD_DIM:], axis=0, keepdims=True)

    def g_copies(f, s, device):
        return (
            remote(r.ga.at[f], r.ga.at[f], r.g2_send.at[s], r.g2_recv.at[s], device),
            remote(r.gl.at[f], r.gl.at[f], r.g2_send.at[3 + s], r.g2_recv.at[3 + s], device),
        )

    def each(copies, what):
        for cp in copies:
            getattr(cp, what)()

    def g_start():
        each(g_copies(me.fr, 0, me.xn), "start")
        each(g_copies(me.fr, 1, me.sib), "start")

    def g_forward():
        each(g_copies(fx, 0, me.xn), "wait_recv")
        each(g_copies(fx, 2, me.sib), "start")

    def g_drain():
        each(g_copies(me.fr, 0, me.xn), "wait_send")
        each(g_copies(me.fr, 1, me.sib), "wait_send")
        each(g_copies(fx, 2, me.sib), "wait_send")

    scale = HEAD_DIM**-0.5

    def pair_back(q, k, v, g, hide, lse, dots):
        q2, g2 = two_heads(q * jnp.asarray(scale, BF16)), two_heads(g)
        probs = jnp.exp(hide(dot_nt(k, q2)) - lse)
        ds = (probs * (dot_nt(v, g2) - dots)).astype(BF16)
        dq = one_block(dot(ds.T, k)) * scale
        return dq, dot(ds, q2), dot(probs.astype(BF16), g2)

    def cross_half(f, half):
        lane = lax.broadcasted_iota(jnp.int32, (frames, LANES), 1)
        column = jnp.sum(jnp.where(lane == f, r.biast[...], 0.0), axis=-1, keepdims=True)

        def body(p, carry):
            stats = [
                jnp.concatenate([r.gl[f, pl.ds(b + 2 * p, 1), :], r.gl[f, pl.ds(b + 1 + 2 * p, 1), :]], axis=1)
                for b in (0, 16)
            ]
            dq, dk, dv = pair_back(
                r.qa[f, :, at128(p)],
                r.kv[f, :, at128(p)],
                r.kv[f, :, at128(p, d)],
                r.ga[f, :, at128(p)],
                lambda s: s + column,
                *stats,
            )
            r.op[f, :, at128(p)] = dq.astype(BF16)
            r.kv[f, :, at128(p)] = dk.astype(BF16)
            r.kv[f, :, at128(p, d)] = dv.astype(BF16)
            return carry

        lax.fori_loop(half * pairs // 2, (half + 1) * pairs // 2, body, 0)

    def d_copy(f, slot, device):
        return remote(r.op.at[f], r.orv.at[slot], r.o2_send.at[slot], r.o2_recv.at[slot], device)

    def side_ready():
        each(g_copies(fs, 1, me.sib), "wait_recv")

    def send_side():
        d_copy(fs, 1, me.sib).start()

    def far_ready():
        each(g_copies(fd, 2, me.sib), "wait_recv")

    def send_far():
        d_copy(fd, 0, me.sib).start()

    def send_across():
        d_copy(fd, 0, me.sib).wait_recv()
        r.op[fx] = (r.op[fx].astype(F32) + r.orv[0].astype(F32)).astype(BF16)
        d_copy(fx, 2, me.xn).start()

    def tile_copy(n):
        f, h = n // 2, n % 2
        return pltpu.make_async_copy(
            r.mst.at[n % 2, 0 : r.memory_grad.shape[1]],
            r.memory_grad.at[f, :, h * WIDE : (h + 1) * WIDE],
            r.t_sem.at[n % 2],
        )

    def memory_grad(n):
        f, h = n // 2, n % 2
        if n >= 2:
            tile_copy(n - 2).wait()
        layers = slice(h * nz // 2, (h + 1) * nz // 2)
        keys, values = (r.wg[k, layers].reshape(WIDE, d) for k in (5, 6))
        r.mst[n % 2] = dot_nt(r.kv[f, :, 0:d], keys) + dot_nt(r.kv[f, :, d : 2 * d], values)
        tile_copy(n).start()

    def memory_done():
        for n in (2 * items - 2, 2 * items - 1):
            tile_copy(n).wait()

    def memory_weights(which, into):
        def rows_of(lo, hi):
            return r.kv[:, :, which * d + lo : which * d + hi].reshape(items * frames, hi - lo)

        grad_into(5 + which, r.memt[...], rows_of, into)

    def query():
        d_copy(fs, 1, me.sib).wait_recv()
        d_copy(fx, 2, me.xn).wait_recv()
        r.xb[...] = (r.op[me.fr].astype(F32) + r.orv[1].astype(F32) + r.orv[2].astype(F32)).astype(BF16)
        onto(True, through(4, r.xb[...]))
        grad_into(4, r.n2t[...], lambda lo, hi: r.xb[:, lo:hi])

    def d_drain():
        for f, slot, device in ((fd, 0, me.sib), (fs, 1, me.sib), (fx, 2, me.xn)):
            d_copy(f, slot, device).wait_send()

    def self_out():
        ln_step(1, r.first[...], r.branch[...])
        r.xb[...] = r.gr[...].astype(BF16)
        r.ga[me.fr] = through(3, r.xb[...]).astype(BF16)
        grad_into(3, r.smixt[...], lambda lo, hi: r.xb[:, lo:hi])

    def self_attention(half):
        key = lax.broadcasted_iota(jnp.int32, (rows, 2 * rows), 0)
        causal = key <= lax.rem(lax.broadcasted_iota(jnp.int32, (rows, 2 * rows), 1), rows)

        def body(p, carry):
            g = r.ga[me.fr, :, at128(p)]
            lse = jnp.concatenate([r.slse[pl.ds(2 * p, 1), :], r.slse[pl.ds(2 * p + 1, 1), :]], axis=1)
            dots = jnp.concatenate(row_dots(g, r.smixt[at128(p), :]), axis=1)
            dq, dk, dv = pair_back(
                r.joint[:, at128(p)],
                r.joint[:, at128(p, d)],
                r.joint[:, at128(p, 2 * d)],
                g,
                lambda s: jnp.where(causal, s, -1e30),
                lse,
                dots,
            )
            r.joint[:, at128(p)] = dq.astype(BF16)
            r.joint[:, at128(p, d)] = dk.astype(BF16)
            r.joint[:, at128(p, 2 * d)] = dv.astype(BF16)
            return carry

        lax.fori_loop(half * pairs // 2, (half + 1) * pairs // 2, body, 0)

    def project(q):
        onto(q == 0, through(q, r.joint[:, q * d : (q + 1) * d]))

    def project_grad(q):
        grad_into(q, r.n1t[...], lambda lo, hi: r.joint[:, q * d + lo : q * d + hi])

    def finish():
        pltpu.make_async_copy(r.tokens, r.third, r.own_sem.at[1]).wait()
        ln_step(0, r.third[...], r.branch[...])
        pltpu.make_async_copy(r.gr, r.tokens_grad, r.own_sem.at[2]).start()
        for g in range(d // LANES):
            for f in range(4):
                r.nw[g // 2, g % 2, f // 2, f % 2] = r.nrow[:, g * LANES : (g + 1) * LANES]

    def close():
        pltpu.make_async_copy(r.gr, r.tokens_grad, r.own_sem.at[2]).wait()

    return SimpleNamespace(**{k: v for k, v in locals().items() if callable(v)})


GRAD_ORDER = (12, 13, 14, 15, 8, 9, 10, 11, 7, 5, 6, 4, 3, 0, 1, 2)
SLOTS = 2


LATE = (13, 14, 15)
LATE_TICKS = (1, 4, 8)
TILT = (5, 9)
EARLY = (1, 3, 5)
EARLY_TICKS = (1, 4, 7)
ROWS = 7
SEND_ROWS = 7
INTO = {5: 12, 6: 14}


def own_blocks(r):
    slab, d = r.self_output.shape
    blocks = {}
    for k in range(3):
        blocks[k] = (r.self_project.at[:, k * d : (k + 1) * d], r.self_project_grad.at[:, k * d : (k + 1) * d])
    for k in range(2):
        blocks[5 + k] = (r.cross_memory.at[:, k * d : (k + 1) * d], r.cross_memory_grad.at[:, k * d : (k + 1) * d])
    blocks[3] = (r.self_output, r.self_output_grad)
    blocks[4] = (r.cross_query, r.cross_query_grad)
    blocks[7] = (r.cross_output, r.cross_output_grad)
    for k in range(4):
        blocks[12 + k] = tuple(a.at[k * slab : (k + 1) * slab] for a in (r.contract, r.contract_grad))
    return blocks


def deal(r, put):
    slab = r.expand.shape[0]
    ways = LANES // slab

    def body(g, carry):
        lane = lax.div(lax.broadcasted_iota(jnp.int32, (slab, LANES), 1), slab)
        source = [r.expand[:, at128(ways * g + a)].astype(F32) for a in range(ways)]
        for q in range(ways):
            total = source[q]
            for a in range(ways):
                if a != q:
                    total = jnp.where(lane == a, pltpu.roll(source[a], (slab * (a - q)) % LANES, 1), total)
            put(q, at128(g), total.astype(BF16))
        return carry

    lax.fori_loop(0, r.expand.shape[1] // (ways * LANES), body, 0)


def undeal(r, q, total):
    slab = total.shape[0]
    ways = LANES // slab
    lane = lax.div(lax.broadcasted_iota(jnp.int32, (slab, LANES), 1), slab)
    for g in range(total.shape[1] // LANES):
        block = total[:, g * LANES : (g + 1) * LANES]
        for a in range(ways):
            line, column = divmod((ways * g + a) * LANES, total.shape[1])
            at = (slice(line * slab, (line + 1) * slab), slice(column, column + LANES))
            moved = block if a == q else pltpu.roll(block, (slab * (q - a)) % LANES, 1)
            r.second[at] = jnp.where(lane == q, moved, r.second[at])


def run(r, nz, chunks):
    me = place()
    barrier = pltpu.get_barrier_semaphore()
    peers = [me.xn, me.yn, me.sib, me.diag]
    peers += [me.dev(lax.rem(me.z + dz, nz), me.y, me.x, me.c) for dz in range(1, nz)]
    for device in peers:
        pl.semaphore_signal(barrier, inc=1, device_id=device, device_id_type=MESH)
    blocks = own_blocks(r)
    owns = {
        k: pltpu.make_async_copy(blocks[k][0], r.wg.at[k, me.z, me.y, me.x, me.c], r.w_sem.at[k]) for k in sorted(blocks)
    }
    for k in (0, 1, *LATE):
        owns[k].start()
    for k in owns:
        if k not in (0, 1, *LATE):
            owns[k].start()
    pltpu.make_async_copy(r.tokens, r.first, r.own_sem.at[1]).start()
    pltpu.make_async_copy(r.cotangent, r.gr, r.own_sem.at[2]).start()
    slab = r.expand.shape[0]
    lane = lax.div(lax.broadcasted_iota(jnp.int32, (8, LANES), 1), slab)
    both = jnp.concatenate([r.norm_gains[...].astype(F32), r.norm_shifts[...].astype(F32)], axis=0)
    wide = jnp.where(lane == me.fr, jnp.concatenate([both] * (LANES // slab), axis=1), 0.0)
    r.ng[me.z, me.y, me.x, me.c] = jnp.concatenate([wide, jnp.zeros((24, LANES), F32)], axis=0).astype(BF16)

    def put(q, at, v):
        r.wg[8 + q, me.z, me.y, me.x, me.c, :, at] = v

    early = [k for k in range(chunks) if k not in LATE]
    count = len(early)
    norm = gather_steps(me, r.ng, r.g_send.at[ROWS], r.g_recv.at[ROWS], nz)
    steps = []
    for k in range(chunks):
        row = ROWS + 1 + LATE.index(k) if k in LATE else early.index(k) % ROWS
        sems = (r.g_send.at[row], r.g_recv.at[row])
        if k in LATE:
            steps.append(gather_late_steps(me, r.wg.at[k], *sems, nz))
        else:
            steps.append(gather_steps(me, r.wg.at[k], *sems, nz, k in TILT))

    def mix(steps, pieces):
        for i, step in enumerate(steps):
            step()
            for piece in pieces[i * len(pieces) // len(steps) : (i + 1) * len(pieces) // len(steps)]:
                piece()

    part = functools.partial
    pl.semaphore_wait(barrier, len(peers))
    norm.z()
    owns[0].wait()
    steps[0].z()
    for k in LATE:
        owns[k].wait()
        steps[k].near()
    for k in owns:
        if k != 0 and k not in LATE:
            owns[k].wait()
    for k in LATE:
        steps[k].far()
    steps[0].relay()
    tasks, drain, fronts = forward(r, me, nz)
    lines = {tick: [] for tick in range(count + 4)}
    for tick in lines:
        for step, t in (
            ("done", tick - 4),
            ("near", tick),
            ("drain", tick - 4),
            ("z", tick + 2),
            ("relay", tick + 1),
            ("far", tick - 1),
            ("last", tick - 2),
        ):
            if tick == 0 and step == "z":
                lines[tick].append(steps[early[1]].z)
            if 0 <= t < count:
                lines[tick].append(getattr(steps[early[t]], step))
    lines[0][1:1] = [norm.relay, norm.near]
    lines[0].append(norm.far)
    lines[1] += [norm.last] + [steps[k].square for k in LATE]
    lines[2].insert(0, norm.done)
    for k, first in zip(LATE, LATE_TICKS):
        for dz, go, come in ((2, first, first + 3), (1, first + 2, first + 6), (3, first + 2, first + 6)):
            lines[go].append(part(steps[k].z, dz))
            lines[come].append(part(steps[k].pass_on, dz))
        lines[first + 8].insert(0, steps[k].done)
    tasks[0] = tasks.get(0, []) + [part(deal, r, put)]
    for tick in lines:
        mix(lines[tick], tasks.get(tick, []))
    drain()
    norm.drain()
    for k in LATE:
        steps[k].drain()

    b = backward(r, me, nz, fronts)

    plain = [m for m in range(chunks) if m not in EARLY]
    spots = {m: i if i < len(EARLY) + 3 else i + 1 for i, m in enumerate(plain)}
    ends = {m: t + 4.0 for m, t in spots.items()}
    ends.update({m: EARLY_TICKS[i] + 5.5 for i, m in enumerate(EARLY)})
    direct = sorted((m for m, k in enumerate(GRAD_ORDER) if k in blocks), key=ends.get)

    def out_copy(i):
        return pltpu.make_async_copy(r.ost.at[i % 2], blocks[GRAD_ORDER[direct[i]]][1], r.e_sem.at[i % 2])

    def keep(turn):
        k = GRAD_ORDER[turn]

        def sink(total):
            if k not in blocks:
                undeal(r, k - 8, total)
                return
            i = direct.index(turn)
            if i >= 2:
                out_copy(i - 2).wait()
            r.ost[i % 2] = total
            out_copy(i).start()

        return sink

    def keep_norms(total):
        rms = jnp.sqrt(total / (total[12:13] * r.first.shape[1]))
        line = lax.broadcasted_iota(jnp.int32, total.shape, 0)
        r.norm_out[...] = jnp.where(line < 8, total, rms)

    boxes = (r.rc, r.y1, r.x1, r.x2, r.y2, r.zs, r.zr, r.total)
    fast_boxes = (r.rc, r.fy1, r.fx1, r.fx2, r.fy2, r.fzs, r.fzr)
    norm_boxes = (r.nrc, r.ny1, r.nx1, r.nx2, r.ny2, r.nzs, r.nzr, r.ntotal)
    adds = {}
    for m, k in enumerate(GRAD_ORDER):
        w = r.wg.at[INTO.get(k, k)]
        if m in EARLY:
            build, box, turn = scatter_early_steps, fast_boxes, (EARLY.index(m), 1, len(EARLY))
            at = SEND_ROWS + EARLY.index(m), SLOTS
        else:
            build, box, turn = scatter_steps, boxes, (plain.index(m), SLOTS, len(plain))
            at = turn[0] % SEND_ROWS, turn[0] % SLOTS
        sems = (r.s_send.at[at[0]], r.s_recv.at[at[1]], r.core_recv.at[m % SLOTS])
        adds[m] = build(me, w, box, sems, r.credit, nz, (m, SLOTS, chunks), turn, keep(m))
    once = (0, 1, 1)
    sems = (r.s_send.at[SEND_ROWS + len(EARLY)], r.s_recv.at[SLOTS + 1], r.core_recv.at[SLOTS])
    adds[chunks] = scatter_steps(me, r.nw, norm_boxes, sems, r.credit, nz, once, once, keep_norms)
    wide_copies = [
        pltpu.make_async_copy(
            r.second.at[i * slab : (i + 1) * slab],
            r.expand_grad.at[:, i * r.second.shape[1] : (i + 1) * r.second.shape[1]],
            r.x_sem.at[i],
        )
        for i in range(4)
    ]

    def wide_start():
        for cp in wide_copies:
            cp.start()

    def pair(f):
        return [part(b.cross_half, f, 0), part(b.cross_half, f, 1)]

    fx, fs, fd = fronts
    mg = [part(b.memory_grad, n) for n in range(8)]
    work = {
        -1: [b.start, part(b.contract, 0), part(b.contract_grad, 0), adds[0].a],
        0: [
            part(b.contract, 1),
            part(b.contract_grad, 1),
            adds[1].a,
            part(b.contract, 2),
            part(b.contract_grad, 2),
            adds[2].a,
            part(b.contract, 3),
            part(b.contract_grad, 3),
        ],
        1: [
            adds[3].a,
            part(b.expand, 0),
            part(b.expand_grad, 0),
            adds[4].a,
            part(b.expand, 1),
            part(b.expand_grad, 1),
            part(b.expand, 2),
            part(b.expand_grad, 2),
        ],
        2: [adds[5].a, part(b.expand, 3), part(b.expand_grad, 3), adds[6].a, b.cross_out, b.g_start, b.cross_out_grad],
        3: [adds[7].a, *pair(me.fr), adds[8].a, b.side_ready, part(b.cross_half, fs, 0)],
        4: [part(b.cross_half, fs, 1), b.send_side, b.g_forward, b.far_ready, part(b.cross_half, fd, 0)],
        5: [part(b.cross_half, fd, 1), b.send_far, *pair(fx)],
        6: [b.send_across, part(b.memory_weights, 0, INTO[5]), adds[9].a, b.g_drain],
        7: [part(b.memory_weights, 1, INTO[6]), adds[10].a, mg[0]],
        8: [b.query, adds[11].a, mg[1], mg[2]],
        9: [b.d_drain, b.self_out, adds[12].a, mg[3]],
        10: [part(b.self_attention, 0), part(b.self_attention, 1), part(b.project, 0), part(b.project_grad, 0), adds[13].a],
        11: [part(b.project, 1), part(b.project_grad, 1), adds[14].a, mg[4]],
        12: [part(b.project, 2), part(b.project_grad, 2), adds[15].a, b.finish, adds[16].a],
        13: [mg[5]],
        14: [mg[6], mg[7]],
        16: [b.memory_done],
    }
    named = {}
    spots[chunks] = max(spots.values())
    for m, spot in spots.items():
        for late, name in enumerate("bcdre"):
            named.setdefault(spot + late, {}).setdefault(name, []).append(getattr(adds[m], name))
    for i, m in enumerate(EARLY):
        named[i + 1]["b"].insert(0, adds[m].b)
        for late, name in enumerate(("z", "r", None, "c", "d", "e")):
            if name:
                named[EARLY_TICKS[i] + late].setdefault("also", []).append(getattr(adds[m], name))
    for i, m in enumerate(plain[: len(plain) - SEND_ROWS]):
        named[spots[m] + 5].setdefault("drain", []).append(adds[m].drain)

    def all_of(actions):
        for action in actions:
            action()

    for tick in range(-1, spots[chunks] + 5):
        by = named.get(tick, {})
        line = [part(all_of, by.get("drain", []) + by.get("b", []))]
        line += [step for name in ("e", "r", "c", "d", "also") for step in by.get(name, [])]
        mix(line, work.get(tick, []))
        if tick == 13:
            wide_start()
    b.close()
    for cp in wide_copies:
        cp.wait()
    out_copy(len(direct) - 2).wait()
    out_copy(len(direct) - 1).wait()
    for m in (*plain[len(plain) - SEND_ROWS :], *EARLY, chunks):
        adds[m].drain()


VMEM_BYTES = 127 * 2**19


INPUTS = (
    "tl",
    "tokens",
    "cotangent",
    "memory",
    "self_project",
    "self_output",
    "cross_query",
    "cross_memory",
    "cross_output",
    "expand",
    "contract",
    "norm_gains",
    "norm_shifts",
    "bias",
)
GRADS = ("self_project", "self_output", "cross_query", "cross_memory", "cross_output", "expand", "contract")


def at(space):
    return pl.BlockSpec(memory_space=space)


def fused(nz, chunks, frame_count, **given):
    rows, d = given["tokens"].shape
    items, parts = given["memory"].shape[:2]
    slab = given["self_output"].shape[0]
    padded = parts * 4 * slab
    half = slab // 2
    outs = dict(
        result=((rows, d), pl.ANY),
        tokens_grad=((rows, d), pl.ANY),
        memory_grad=((items, frame_count, d), pl.ANY),
        **{k + "_grad": (given[k].shape, pl.ANY) for k in GRADS},
        norm_out=((16, LANES), pltpu.VMEM),
    )
    vm = pltpu.VMEM
    dma = pltpu.SemaphoreType.DMA
    scratch = dict(
        wg=vm((chunks, nz, 2, 2, 2, slab, d), BF16),
        ng=vm((nz, 2, 2, 2, 32, LANES), BF16),
        gs=vm((16, d), F32),
        n1t=vm((d, rows), BF16),
        joint=vm((rows, 3 * d), BF16),
        smixt=vm((d, rows), BF16),
        slse=vm((16, LANES), F32),
        first=vm((rows, d), F32),
        n2t=vm((d, rows), BF16),
        qa=vm((items, rows, d), BF16),
        kv=vm((items, padded, 2 * d), BF16),
        memt=vm((d, items * padded), BF16),
        clse=vm((16, LANES), F32),
        second=vm((rows, d), F32),
        n3t=vm((d, rows), BF16),
        activet=vm((4 * d, rows), BF16),
        active=vm((rows, 4 * d), BF16),
        slope=vm((rows, 4 * d), BF16),
        third=vm((rows, d), F32),
        sq=vm((8, LANES), F32),
        xb=vm((rows, d), BF16),
        branch=vm((rows, d), F32),
        op=vm((items, rows, d), BF16),
        opl=vm((items, 16, LANES), F32),
        orv=vm((3, rows, d), BF16),
        orl=vm((3, 16, LANES), F32),
        wcol=vm((LANES, LANES), F32),
        cmixt=vm((d, rows), BF16),
        gr=vm((rows, d), F32),
        ga=vm((items, rows, d), BF16),
        gl=vm((items, 32, LANES), F32),
        nrow=vm((16, d), F32),
        biast=vm((padded, LANES), F32),
        mst=vm((2, padded, WIDE), F32),
        ost=vm((2, slab, d), F32),
        nw=vm((nz, 2, 2, 2, 16, LANES), F32),
        rc=vm((SLOTS, nz, 2, 2, slab, d), BF16),
        y1=vm((SLOTS, nz, 2, half, d), BF16),
        x1=vm((SLOTS, nz, 2, half, d), BF16),
        x2=vm((SLOTS, nz, half, d), BF16),
        y2=vm((SLOTS, nz, half, d), BF16),
        zs=vm((SLOTS, nz - 1, slab, d), BF16),
        zr=vm((SLOTS, slab, d), BF16),
        total=vm((slab, d), F32),
        fzr=vm((1, 2, 2, slab, d), BF16),
        nzr=vm((1, 16, LANES), F32),
        ntotal=vm((16, LANES), F32),
        fy1=vm((1, 2, half, d), BF16),
        fx1=vm((1, 2, half, d), BF16),
        fx2=vm((1, half, d), BF16),
        fy2=vm((1, half, d), BF16),
        fzs=vm((1, nz - 1, 2, 2, slab, d), BF16),
        nrc=vm((1, nz, 2, 2, 16, LANES), F32),
        ny1=vm((1, nz, 2, 8, LANES), F32),
        nx1=vm((1, nz, 2, 8, LANES), F32),
        nx2=vm((1, nz, 8, LANES), F32),
        ny2=vm((1, nz, 8, LANES), F32),
        nzs=vm((1, nz - 1, 16, LANES), F32),
        own_sem=dma((4,)),
        x_sem=dma((4,)),
        w_sem=dma((chunks,)),
        m_sem=dma((2,)),
        t_sem=dma((2,)),
        e_sem=dma((2,)),
        g_send=dma((ROWS + 1 + len(LATE), nz + 8)),
        g_recv=dma((ROWS + 1 + len(LATE), nz + 7)),
        s_send=dma((SEND_ROWS + len(EARLY) + 1, nz + 5)),
        s_recv=dma((SLOTS + 2, nz + 4)),
        core_recv=dma((SLOTS + 1,)),
        credit=pltpu.SemaphoreType.REGULAR((3 * nz + 9,)),
        q_send=dma((3,)),
        q_recv=dma((3,)),
        o_send=dma((6,)),
        o_recv=dma((6,)),
        g2_send=dma((6,)),
        g2_recv=dma((6,)),
        o2_send=dma((3,)),
        o2_recv=dma((3,)),
    )
    names = list(INPUTS) + list(outs) + list(scratch)

    def kernel(*refs):
        run(SimpleNamespace(**dict(zip(names, refs))), nz, chunks)

    spaces = {"tl": pltpu.SMEM, "expand": pltpu.VMEM, "norm_gains": pltpu.VMEM, "norm_shifts": pltpu.VMEM, "bias": pltpu.VMEM}
    res = pl.pallas_call(
        kernel,
        out_shape=[jax.ShapeDtypeStruct(s, F32) for s, _ in outs.values()],
        in_specs=[at(spaces.get(k, pl.ANY)) for k in INPUTS],
        out_specs=[at(s) for _, s in outs.values()],
        scratch_shapes=list(scratch.values()),
        compiler_params=pltpu.CompilerParams(collective_id=0, has_side_effects=True, vmem_limit_bytes=VMEM_BYTES),
    )(*(given[k] for k in INPUTS))
    return dict(zip(outs, res))


def settle(arrays, norm_out, width):
    count = len(arrays)
    pieces = []
    for i, a in enumerate(arrays):
        pieces += [(i, k) for k in range(a.shape[0])] if a.ndim == 3 else [(i, None)]

    def kernel(*refs):
        sources, (table, scalars) = refs[:count], refs[count : count + 2]
        targets = refs[count + 2 : 2 * count + 2]
        gains, shifts, rms = refs[2 * count + 2 : 2 * count + 5]
        held = refs[2 * count + 5 : 3 * count + 5]
        in_sem, out_sem = refs[3 * count + 5 :]

        def pick(ref, k):
            return ref if k is None else ref.at[k]

        ins = [pltpu.make_async_copy(pick(sources[i], k), pick(held[i], k), in_sem.at[n]) for n, (i, k) in enumerate(pieces)]
        outs = [pltpu.make_async_copy(pick(held[i], k), pick(targets[i], k), out_sem.at[n]) for n, (i, k) in enumerate(pieces)]
        for cp in ins:
            cp.start()
        fr = lax.axis_index("frames")
        mine = jnp.zeros((8, width), F32)
        for f in range(LANES // width):
            mine = jnp.where(fr == f, table[0:8, f * width : (f + 1) * width], mine)
        gains[...] = mine[0:4]
        shifts[...] = mine[4:8]
        for i in range(4):
            rms[i] = scalars[8 + i, 0]
        for a, b in zip(ins, outs):
            a.wait()
            b.start()
        for b in outs:
            b.wait()

    small = jax.ShapeDtypeStruct((4, width), F32)
    return pl.pallas_call(
        kernel,
        out_shape=[jax.ShapeDtypeStruct(a.shape, a.dtype) for a in arrays] + [small, small, jax.ShapeDtypeStruct((4,), F32)],
        in_specs=[at(pl.ANY)] * count + [at(pltpu.VMEM), at(pltpu.SMEM)],
        out_specs=[at(pl.ANY)] * count + [at(pltpu.VMEM)] * 2 + [at(pltpu.SMEM)],
        scratch_shapes=[pltpu.VMEM(a.shape, a.dtype) for a in arrays]
        + [pltpu.SemaphoreType.DMA((len(pieces),)), pltpu.SemaphoreType.DMA((len(pieces),))],
        compiler_params=pltpu.CompilerParams(vmem_limit_bytes=VMEM_BYTES),
    )(*arrays, norm_out, norm_out)


CHUNKS = 16
Z_CHIPS = 4


def frame_bias(cross_mask, memory_length, frame_count, padded):
    start = lax.axis_index("frames") * frame_count
    items = cross_mask.shape[0]
    wide = jnp.pad(cross_mask, ((0, 8 - items), (0, padded - frame_count)))
    mask = lax.dynamic_slice_in_dim(wide, start, padded, 1)
    lengths = jnp.pad(memory_length, (0, 8 - items))
    offset = jnp.arange(padded)[None]
    at = start + offset
    ok = (offset < frame_count) & (at < lengths[:, None]) & ((mask == 1) | (at == 0))
    return jnp.where(ok, 0.0, -1e30).astype(F32)


def local_fused(
    tokens,
    memory,
    cotangent,
    self_project,
    self_output,
    cross_query,
    cross_memory,
    cross_output,
    expand,
    contract,
    norm_gains,
    norm_shifts,
    target_length,
    memory_length,
    cross_mask,
):
    items, frame_count, d = memory.shape
    slab = self_output.shape[0]
    group = 4 * slab
    parts = -(-frame_count // group)
    padded = parts * group
    rolled = jnp.pad(memory, ((0, 0), (0, padded - frame_count), (0, 0))).reshape(items, parts, 2, 2, slab, d)
    o = fused(
        Z_CHIPS,
        CHUNKS,
        frame_count,
        tl=target_length,
        tokens=tokens[0],
        cotangent=cotangent[0],
        memory=rolled,
        self_project=self_project,
        self_output=self_output,
        cross_query=cross_query,
        cross_memory=cross_memory,
        cross_output=cross_output,
        expand=expand,
        contract=contract,
        norm_gains=norm_gains,
        norm_shifts=norm_shifts,
        bias=frame_bias(cross_mask, memory_length, frame_count, padded),
    )
    large = [o[k] for k in ("result", "tokens_grad", "memory_grad")] + [o[k + "_grad"] for k in GRADS]
    done = settle(large, o["norm_out"], norm_gains.shape[1])
    return (done[0][None], done[1][None], *done[2:])


block_heads = 4


def layer_norm(values, gain_row, shift_row):
    center = values - jnp.mean(values, axis=-1, keepdims=True)
    spread = jnp.mean(center * center, axis=-1, keepdims=True)
    return center * lax.rsqrt(spread + 1e-05) * gain_row + shift_row


def exact_gelu(values):
    return jax.nn.gelu(values, approximate=False)


def matmul(left_side, right_side):
    return jnp.dot(left_side, right_side, preferred_element_type=jnp.float32)


def split_heads(rows):
    return rows.reshape(rows.shape[:-1] + (rows.shape[-1] // HEAD_DIM, HEAD_DIM))


def to_blocks(rows):
    row_count, head_count, head_width = rows.shape
    return rows.reshape(row_count, head_count // block_heads, block_heads, head_width).transpose(
        1, 0, 2, 3
    )


def from_blocks(blocks):
    group_count, row_count, head_count, head_width = blocks.shape
    return blocks.transpose(1, 0, 2, 3).reshape(row_count, group_count * head_count * head_width)


def block_scores(query_block, key_block, allowed):
    factor = query_block.shape[-1] ** (-0.5)
    raw_scores = (
        jnp.einsum("shd,fhd->hsf", query_block, key_block, preferred_element_type=jnp.float32)
        * factor
    )
    return jnp.where(allowed[None], raw_scores, -1e30)


def block_probs(query_block, key_block, allowed, max_block, total_block):
    scores = block_scores(query_block, key_block, allowed)
    shifted = jnp.where(allowed[None], jnp.exp(scores - max_block[..., None]), 0.0)
    return shifted / total_block[..., None]


def block_grads(query_block, key_block, grad_block, probs, grad_probs, row_dot):
    factor = query_block.shape[-1] ** (-0.5)
    score_grad = (probs * (grad_probs - row_dot)).astype(jnp.bfloat16)
    query_grad = (
        jnp.einsum("hsf,fhd->shd", score_grad, key_block, preferred_element_type=jnp.float32)
        * factor
    )
    key_grad = (
        jnp.einsum("hsf,shd->fhd", score_grad, query_block, preferred_element_type=jnp.float32)
        * factor
    )
    value_grad = jnp.einsum(
        "hsf,shd->fhd", probs.astype(jnp.bfloat16), grad_block, preferred_element_type=jnp.float32
    )
    return (query_grad, key_grad, value_grad)


def attend_whole(query_rows, key_rows, value_rows, allowed):

    def one_group(blocks):
        query_block, key_block, value_block = blocks
        scores = block_scores(query_block, key_block, allowed)
        max_block = jnp.max(scores, axis=-1)
        shifted = jnp.where(allowed[None], jnp.exp(scores - max_block[..., None]), 0.0)
        total_block = jnp.sum(shifted, axis=-1)
        weights = (shifted / total_block[..., None]).astype(jnp.bfloat16)
        mixture = jnp.einsum(
            "hsf,fhd->shd", weights, value_block, preferred_element_type=jnp.float32
        )
        return (mixture, max_block, total_block)

    mixture, row_max, totals = lax.map(
        one_group, (to_blocks(query_rows), to_blocks(key_rows), to_blocks(value_rows))
    )
    return (from_blocks(mixture), row_max, totals)


def attend_whole_back(query_rows, key_rows, value_rows, allowed, grad_rows, row_max, totals):

    def one_group(blocks):
        query_block, key_block, value_block, grad_block, max_block, total_block = blocks
        probs = block_probs(query_block, key_block, allowed, max_block, total_block)
        grad_probs = jnp.einsum(
            "shd,fhd->hsf", grad_block, value_block, preferred_element_type=jnp.float32
        )
        row_dot = jnp.sum(probs * grad_probs, axis=-1, keepdims=True)
        return block_grads(query_block, key_block, grad_block, probs, grad_probs, row_dot)

    query_grad, key_grad, value_grad = lax.map(
        one_group,
        (
            to_blocks(query_rows),
            to_blocks(key_rows),
            to_blocks(value_rows),
            to_blocks(grad_rows),
            row_max,
            totals,
        ),
    )
    return (from_blocks(query_grad), from_blocks(key_grad), from_blocks(value_grad))


def cross_stats(query_rows, key_rows, allowed):

    def one_group(blocks):
        query_block, key_block = blocks
        scores = block_scores(query_block, key_block, allowed)
        max_block = jnp.max(scores, axis=-1)
        total_block = jnp.sum(
            jnp.where(allowed[None], jnp.exp(scores - max_block[..., None]), 0.0), axis=-1
        )
        return (max_block, total_block)

    return lax.map(one_group, (to_blocks(query_rows), to_blocks(key_rows)))


def cross_partial(query_rows, key_rows, value_rows, allowed, row_max, totals):

    def one_group(blocks):
        query_block, key_block, value_block, max_block, total_block = blocks
        probs = block_probs(query_block, key_block, allowed, max_block, total_block)
        return jnp.einsum(
            "hsf,fhd->shd",
            probs.astype(jnp.bfloat16),
            value_block,
            preferred_element_type=jnp.float32,
        )

    return from_blocks(
        lax.map(
            one_group,
            (to_blocks(query_rows), to_blocks(key_rows), to_blocks(value_rows), row_max, totals),
        )
    )


def cross_row_dot(query_rows, key_rows, value_rows, allowed, grad_rows, row_max, totals):

    def one_group(blocks):
        query_block, key_block, value_block, grad_block, max_block, total_block = blocks
        probs = block_probs(query_block, key_block, allowed, max_block, total_block)
        grad_probs = jnp.einsum(
            "shd,fhd->hsf", grad_block, value_block, preferred_element_type=jnp.float32
        )
        return jnp.sum(probs * grad_probs, axis=-1)

    return lax.map(
        one_group,
        (
            to_blocks(query_rows),
            to_blocks(key_rows),
            to_blocks(value_rows),
            to_blocks(grad_rows),
            row_max,
            totals,
        ),
    )


def cross_partial_grads(
    query_rows, key_rows, value_rows, allowed, grad_rows, row_max, totals, row_dot
):

    def one_group(blocks):
        query_block, key_block, value_block, grad_block, max_block, total_block, dot_block = blocks
        probs = block_probs(query_block, key_block, allowed, max_block, total_block)
        grad_probs = jnp.einsum(
            "shd,fhd->hsf", grad_block, value_block, preferred_element_type=jnp.float32
        )
        return block_grads(
            query_block, key_block, grad_block, probs, grad_probs, dot_block[..., None]
        )

    query_grad, key_grad, value_grad = lax.map(
        one_group,
        (
            to_blocks(query_rows),
            to_blocks(key_rows),
            to_blocks(value_rows),
            to_blocks(grad_rows),
            row_max,
            totals,
            row_dot,
        ),
    )
    return (from_blocks(query_grad), from_blocks(key_grad), from_blocks(value_grad))


def local(
    tokens,
    memory,
    cotangent,
    self_project,
    self_output,
    cross_query,
    cross_memory,
    cross_output,
    expand,
    contract,
    norm_gains,
    norm_shifts,
    target_length,
    memory_length,
    cross_mask,
):
    gathered = (
        lax.all_gather(self_project, ("dp", "frames"), axis=0, tiled=True),
        lax.all_gather(self_output, ("dp", "frames"), axis=0, tiled=True),
        lax.all_gather(cross_query, ("dp", "frames"), axis=0, tiled=True),
        lax.all_gather(cross_memory, ("dp", "frames"), axis=0, tiled=True),
        lax.all_gather(cross_output, ("dp", "frames"), axis=0, tiled=True),
        lax.all_gather(expand, ("dp", "frames"), axis=0, tiled=True),
        lax.all_gather(contract, ("dp", "frames"), axis=0, tiled=True),
        lax.all_gather(norm_gains, ("dp", "frames"), axis=1, tiled=True),
        lax.all_gather(norm_shifts, ("dp", "frames"), axis=1, tiled=True),
    )
    (
        w_self,
        w_self_out,
        w_query,
        w_memory,
        w_cross_out,
        w_expand,
        w_contract,
        gains_low,
        shifts_low,
    ) = gathered
    gains = gains_low.astype(jnp.float32)
    shifts = shifts_low.astype(jnp.float32)
    model_width = w_self_out.shape[0]
    residual_in = tokens[0]
    length = residual_in.shape[0]
    positions = jnp.arange(length)
    row_valid = positions < target_length[0]
    causal = positions[:, None] >= positions[None, :]
    item_count = memory.shape[0]
    frame_count = memory.shape[1]
    own_item = lax.axis_index("frames")
    normed_one_f, back_one = jax.vjp(layer_norm, residual_in, gains[0], shifts[0])
    normed_one = normed_one_f.astype(jnp.bfloat16)
    joint_rows = matmul(normed_one, w_self).astype(jnp.bfloat16)
    self_queries = split_heads(joint_rows[:, :model_width])
    self_keys = split_heads(joint_rows[:, model_width : 2 * model_width])
    self_values = split_heads(joint_rows[:, 2 * model_width :])
    self_mix, self_max, self_totals = attend_whole(self_queries, self_keys, self_values, causal)
    self_mix_low = self_mix.astype(jnp.bfloat16)
    self_branch = matmul(self_mix_low, w_self_out)
    first_sum = residual_in + self_branch
    normed_two_f, back_two = jax.vjp(layer_norm, first_sum, gains[1], shifts[1])
    normed_two = normed_two_f.astype(jnp.bfloat16)
    cross_queries = matmul(normed_two, w_query).astype(jnp.bfloat16)
    every_query = lax.all_gather(cross_queries[None], "frames", axis=0, tiled=True)
    query_heads = split_heads(every_query)
    frame_start = own_item * frame_count
    local_frames = frame_start + jnp.arange(frame_count)
    local_mask = lax.dynamic_slice_in_dim(cross_mask, frame_start, frame_count, 1)
    frame_ok = (local_frames[None, :] < memory_length[:, None]) & (
        (local_mask == 1) | (local_frames[None, :] == 0)
    )
    memory_rows = matmul(memory.reshape(item_count * frame_count, model_width), w_memory).astype(
        jnp.bfloat16
    )
    memory_rows = memory_rows.reshape(item_count, frame_count, 2 * model_width)
    memory_keys = split_heads(memory_rows[..., :model_width])
    memory_values = split_heads(memory_rows[..., model_width:])

    def item_stats(inputs):
        query_item, key_item, frame_item = inputs
        return cross_stats(
            query_item, key_item, jnp.broadcast_to(frame_item[None, :], (length, frame_count))
        )

    local_max, local_totals = lax.map(item_stats, (query_heads, memory_keys, frame_ok))
    cross_max = lax.pmax(local_max.astype(jnp.bfloat16), "frames").astype(local_max.dtype)
    cross_totals = lax.psum(
        (local_totals * jnp.exp(local_max - cross_max)).astype(jnp.bfloat16), "frames"
    ).astype(jnp.float32)

    def item_partial(inputs):
        query_item, key_item, value_item, frame_item, max_item, total_item = inputs
        allowed = jnp.broadcast_to(frame_item[None, :], (length, frame_count))
        return cross_partial(query_item, key_item, value_item, allowed, max_item, total_item)

    partial_mix = lax.map(
        item_partial, (query_heads, memory_keys, memory_values, frame_ok, cross_max, cross_totals)
    )
    cross_mix = lax.psum_scatter(
        partial_mix.astype(jnp.bfloat16), "frames", scatter_dimension=0, tiled=True
    ).astype(jnp.float32)[0]
    cross_mix_low = cross_mix.astype(jnp.bfloat16)
    cross_branch = matmul(cross_mix_low, w_cross_out)
    second_sum = first_sum + cross_branch
    normed_three_f, back_three = jax.vjp(layer_norm, second_sum, gains[2], shifts[2])
    normed_three = normed_three_f.astype(jnp.bfloat16)
    hidden = matmul(normed_three, w_expand)
    active_f, gelu_back = jax.vjp(exact_gelu, hidden)
    active = active_f.astype(jnp.bfloat16)
    feed_branch = matmul(active, w_contract)
    third_sum = second_sum + feed_branch
    final_rows, back_final = jax.vjp(layer_norm, third_sum, gains[3], shifts[3])
    result = jnp.where(row_valid[:, None], final_rows, 0.0)
    row_weight = row_valid.astype(jnp.float32)[:, None]
    squares = jnp.stack(
        [
            jnp.sum(row_weight * member * member)
            for member in (third_sum, self_branch, cross_branch, feed_branch)
        ]
    )
    squares_all, counted = lax.psum((squares, jnp.sum(row_weight)), ("dp", "frames"))
    branch_rms = jnp.sqrt(squares_all / (counted * model_width))
    grad_result = jnp.where(row_valid[:, None], cotangent[0], 0.0)
    grad_third, gain_grad_three, shift_grad_three = back_final(grad_result)
    feed_low = grad_third.astype(jnp.bfloat16)
    contract_grad = matmul(active.T, feed_low)
    grad_active = matmul(feed_low, w_contract.T)
    grad_hidden = gelu_back(grad_active)[0].astype(jnp.bfloat16)
    expand_grad = matmul(normed_three.T, grad_hidden)
    grad_normed_three = matmul(grad_hidden, w_expand.T)
    grad_second_part, gain_grad_two, shift_grad_two = back_three(grad_normed_three)
    grad_second = grad_third + grad_second_part
    cross_low = grad_second.astype(jnp.bfloat16)
    cross_output_grad = matmul(cross_mix_low.T, cross_low)
    grad_cross_mix = matmul(cross_low, w_cross_out.T).astype(jnp.bfloat16)
    every_grad = split_heads(lax.all_gather(grad_cross_mix[None], "frames", axis=0, tiled=True))

    def item_dot(inputs):
        query_item, key_item, value_item, frame_item, grad_item, max_item, total_item = inputs
        allowed = jnp.broadcast_to(frame_item[None, :], (length, frame_count))
        return cross_row_dot(
            query_item, key_item, value_item, allowed, grad_item, max_item, total_item
        )

    local_dot = lax.map(
        item_dot,
        (query_heads, memory_keys, memory_values, frame_ok, every_grad, cross_max, cross_totals),
    )
    row_dot = lax.psum(local_dot.astype(jnp.bfloat16), "frames").astype(jnp.float32)

    def item_grads(inputs):
        query_item, key_item, value_item, frame_item, grad_item, max_item, total_item, dot_item = (
            inputs
        )
        allowed = jnp.broadcast_to(frame_item[None, :], (length, frame_count))
        return cross_partial_grads(
            query_item, key_item, value_item, allowed, grad_item, max_item, total_item, dot_item
        )

    query_parts, key_parts, value_parts = lax.map(
        item_grads,
        (
            query_heads,
            memory_keys,
            memory_values,
            frame_ok,
            every_grad,
            cross_max,
            cross_totals,
            row_dot,
        ),
    )
    query_grad = lax.psum_scatter(
        query_parts.astype(jnp.bfloat16), "frames", scatter_dimension=0, tiled=True
    ).astype(jnp.float32)[0]
    memory_low = (
        jnp.concatenate([key_parts, value_parts], axis=2)
        .astype(jnp.bfloat16)
        .reshape(item_count * frame_count, 2 * model_width)
    )
    cross_memory_grad = matmul(memory.reshape(item_count * frame_count, model_width).T, memory_low)
    memory_grad = matmul(memory_low, w_memory.T).reshape(item_count, frame_count, model_width)
    query_low = query_grad.astype(jnp.bfloat16)
    cross_query_grad = matmul(normed_two.T, query_low)
    grad_normed_two = matmul(query_low, w_query.T)
    grad_first_part, gain_grad_one, shift_grad_one = back_two(grad_normed_two)
    grad_first = grad_second + grad_first_part
    self_low = grad_first.astype(jnp.bfloat16)
    self_output_grad = matmul(self_mix_low.T, self_low)
    grad_self_mix = matmul(self_low, w_self_out.T).astype(jnp.bfloat16)
    self_query_grad, self_key_grad, self_value_grad = attend_whole_back(
        self_queries,
        self_keys,
        self_values,
        causal,
        split_heads(grad_self_mix),
        self_max,
        self_totals,
    )
    joint_grad = jnp.concatenate([self_query_grad, self_key_grad, self_value_grad], axis=1).astype(
        jnp.bfloat16
    )
    self_project_grad = matmul(normed_one.T, joint_grad)
    grad_normed_one = matmul(joint_grad, w_self.T)
    grad_input_part, gain_grad_zero, shift_grad_zero = back_one(grad_normed_one)
    tokens_grad = grad_first + grad_input_part
    gain_grads = jnp.stack([gain_grad_zero, gain_grad_one, gain_grad_two, gain_grad_three])
    shift_grads = jnp.stack([shift_grad_zero, shift_grad_one, shift_grad_two, shift_grad_three])
    reduced = (
        lax.psum_scatter(self_project_grad, ("dp", "frames"), scatter_dimension=0, tiled=True),
        lax.psum_scatter(self_output_grad, ("dp", "frames"), scatter_dimension=0, tiled=True),
        lax.psum_scatter(cross_query_grad, ("dp", "frames"), scatter_dimension=0, tiled=True),
        lax.psum_scatter(cross_memory_grad, ("dp", "frames"), scatter_dimension=0, tiled=True),
        lax.psum_scatter(cross_output_grad, ("dp", "frames"), scatter_dimension=0, tiled=True),
        lax.psum_scatter(expand_grad, ("dp", "frames"), scatter_dimension=0, tiled=True),
        lax.psum_scatter(contract_grad, ("dp", "frames"), scatter_dimension=0, tiled=True),
        lax.psum_scatter(gain_grads, ("dp", "frames"), scatter_dimension=1, tiled=True),
        lax.psum_scatter(shift_grads, ("dp", "frames"), scatter_dimension=1, tiled=True),
    )
    (
        project_part,
        output_part,
        query_part,
        memory_part,
        cross_out_part,
        expand_part,
        contract_part,
        gains_part,
        shifts_part,
    ) = reduced
    return (
        result[None],
        tokens_grad[None],
        memory_grad,
        project_part,
        output_part,
        query_part,
        memory_part,
        cross_out_part,
        expand_part,
        contract_part,
        gains_part,
        shifts_part,
        branch_rms,
    )


def solution(mesh):
    fits = (mesh.shape["dp"], mesh.shape["frames"]) == (2 * Z_CHIPS, 4)
    return jax.shard_map(
        local_fused if fits else local,
        mesh=mesh,
        in_specs=(
            P(("dp", "frames"), None, None),
            P("dp", "frames", None),
            P(("dp", "frames"), None, None),
            P(("dp", "frames"), None),
            P(("dp", "frames"), None),
            P(("dp", "frames"), None),
            P(("dp", "frames"), None),
            P(("dp", "frames"), None),
            P(("dp", "frames"), None),
            P(("dp", "frames"), None),
            P(None, ("dp", "frames")),
            P(None, ("dp", "frames")),
            P(("dp", "frames")),
            P("dp"),
            P("dp", None),
        ),
        out_specs=(
            P(("dp", "frames"), None, None),
            P(("dp", "frames"), None, None),
            P("dp", "frames", None),
            P(("dp", "frames"), None),
            P(("dp", "frames"), None),
            P(("dp", "frames"), None),
            P(("dp", "frames"), None),
            P(("dp", "frames"), None),
            P(("dp", "frames"), None),
            P(("dp", "frames"), None),
            P(None, ("dp", "frames")),
            P(None, ("dp", "frames")),
            P(),
        ),
        check_vma=False,
    )
```

```python
import functools
from types import SimpleNamespace

import jax
import jax.numpy as jnp
from jax import lax
from jax.experimental import pallas as pl
from jax.experimental.pallas import tpu as pltpu
from jax.sharding import PartitionSpec as P

MESH = pl.DeviceIdType.MESH
F32 = jnp.float32
BF16 = jnp.bfloat16
HEAD_DIM = 64
LANES = 128
WIDE = 512


def dot(a, b):
    return jnp.dot(a, b, preferred_element_type=F32)


def dot_nt(a, b):
    return lax.dot_general(a, b, (((1,), (1,)), ((), ())), preferred_element_type=F32)


def place():
    dp, fr = lax.axis_index("dp"), lax.axis_index("frames")
    z, y = lax.div(dp, 2), lax.rem(dp, 2)
    x, c = lax.div(fr, 2), lax.rem(fr, 2)

    def dev(zz, yy, xx, cc):
        return {"dp": zz * 2 + yy, "frames": xx * 2 + cc}

    me = SimpleNamespace(z=z, y=y, x=x, c=c, fr=fr, dev=dev)
    me.xn = dev(z, y, 1 - x, c)
    me.yn = dev(z, 1 - y, x, c)
    me.sib = dev(z, y, x, 1 - c)
    me.diag = dev(z, y, 1 - x, 1 - c)
    return me


def remote(src, dst, send, recv, device):
    return pltpu.make_async_remote_copy(
        src_ref=src, dst_ref=dst, send_sem=send, recv_sem=recv, device_id=device, device_id_type=MESH
    )


def z_ways(me, nz):
    sends = {dz: (me.z != nz - 1) if dz == 1 else (me.z != 0) if dz == nz - 1 else None for dz in range(1, nz)}
    inner = (me.z == 1) | (me.z == 2)
    upper = me.z == 2
    return sends, inner, lax.rem(me.z + 2, nz), jnp.where(upper, nz - 1, 0), jnp.where(upper, nz - 1, 1)


def when(condition, action):
    if condition is None:
        action()
    else:
        pl.when(condition)(action)


def gather_steps(me, w, send, recv, nz, tilt=False):
    half = w.shape[4] if tilt else w.shape[4] // 2
    xo, yo, co = 1 - me.x, 1 - me.y, 1 - me.c

    def cp(view, s, device):
        return remote(view, view, send.at[s], recv.at[s], device)

    def spot(y, x, c):
        return w.at[:, y, x, c]

    def one(dz, y, x):
        return w.at[lax.rem(me.z + nz - dz, nz), y, x, me.c]

    def part(y, x, lower):
        return w.at[:, y, x, me.c, 0:half] if lower else w.at[:, y, x, me.c, half:]

    sends, inner, source, target, distance = z_ways(me, nz)
    passed = w.at[source, me.y, me.x, me.c]

    def pass_copy():
        to = me.dev(target, me.y, me.x, me.c)
        return remote(passed, passed, send.at[nz + 7], recv.at[distance - 1], to)

    def z_copy(dz):
        return cp(one(0, me.y, me.x), dz - 1, me.dev(lax.rem(me.z + dz, nz), me.y, me.x, me.c))

    def z_arrived(dz):
        cp(one(dz, me.y, me.x), dz - 1, me.xn).wait_recv()

    def step_z():
        for dz in range(1, nz):
            when(sends[dz], lambda: z_copy(dz).start())

    def step_relay():
        @pl.when(inner)
        def _():
            z_arrived(2)
            pass_copy().start()

    def step_near():
        z_arrived(1)
        z_arrived(3)
        pl.when(jnp.logical_not(inner))(lambda: z_arrived(2))
        cp(spot(me.y, me.x, me.c), nz - 1, me.xn).start()
        cp(spot(me.y, me.x, me.c), nz, me.yn).start()
        cp(spot(me.y, me.x, me.c), nz + 1, me.sib).start()

    def step_far():
        cp(spot(me.y, xo, me.c), nz - 1, me.xn).wait_recv()
        cp(part(me.y, xo, True), nz + 2, me.yn).start()
        cp(spot(me.y, xo, me.c), nz + 3, me.sib).start()
        cp(spot(yo, me.x, me.c), nz, me.yn).wait_recv()
        if not tilt:
            cp(part(yo, me.x, False), nz + 4, me.xn).start()
        cp(spot(yo, me.x, me.c), nz + 5, me.sib).start()

    def step_last():
        cp(part(yo, xo, True), nz + 2, me.yn).wait_recv()
        if not tilt:
            cp(part(yo, xo, False), nz + 4, me.xn).wait_recv()
        cp(spot(yo, xo, me.c), nz + 6, me.sib).start()

    def step_done():
        for y, x, s in ((me.y, me.x, nz + 1), (me.y, xo, nz + 3), (yo, me.x, nz + 5), (yo, xo, nz + 6)):
            cp(spot(y, x, co), s, me.sib).wait_recv()

    def drain():
        for dz in range(1, nz):
            when(sends[dz], lambda: z_copy(dz).wait_send())
        pl.when(inner)(lambda: pass_copy().wait_send())
        for s in (nz - 1, nz):
            cp(spot(me.y, me.x, me.c), s, me.xn).wait_send()
        for y, x, s in ((me.y, me.x, nz + 1), (me.y, xo, nz + 3), (yo, me.x, nz + 5), (yo, xo, nz + 6)):
            cp(spot(y, x, me.c), s, me.xn).wait_send()
        cp(part(me.y, xo, True), nz + 2, me.xn).wait_send()
        if not tilt:
            cp(part(yo, me.x, False), nz + 4, me.xn).wait_send()

    return SimpleNamespace(
        z=step_z, relay=step_relay, near=step_near, far=step_far, last=step_last, done=step_done, drain=drain
    )


def gather_late_steps(me, w, send, recv, nz):
    half = w.shape[4] // 2
    xo, yo, co = 1 - me.x, 1 - me.y, 1 - me.c

    def cp(view, s, device):
        return remote(view, view, send.at[s], recv.at[s], device)

    def one(y, x):
        return w.at[me.z, y, x, me.c]

    def part(y, x, lower):
        return w.at[me.z, y, x, me.c, 0:half] if lower else w.at[me.z, y, x, me.c, half:]

    def layer(dz, c):
        return w.at[lax.rem(me.z + nz - dz, nz), :, :, c]

    def step_near():
        cp(one(me.y, me.x), 0, me.xn).start()
        cp(one(me.y, me.x), 1, me.yn).start()

    def step_far():
        cp(one(me.y, xo), 0, me.xn).wait_recv()
        cp(part(me.y, xo, True), 2, me.yn).start()
        cp(one(yo, me.x), 1, me.yn).wait_recv()
        cp(part(yo, me.x, False), 3, me.xn).start()

    def step_square():
        cp(part(yo, xo, True), 2, me.yn).wait_recv()
        cp(part(yo, xo, False), 3, me.xn).wait_recv()
        cp(layer(0, me.c), 4, me.sib).start()

    sends, inner, source, target, distance = z_ways(me, nz)
    passed = w.at[source, :, :, me.c]

    def pass_copy():
        to = me.dev(target, me.y, me.x, me.c)
        return remote(passed, passed, send.at[nz + 7], recv.at[4 + distance], to)

    def z_copy(dz):
        return cp(layer(0, me.c), 4 + dz, me.dev(lax.rem(me.z + dz, nz), me.y, me.x, me.c))

    def step_z(dz):
        when(sends[dz], lambda: z_copy(dz).start())

    def step_pass(dz):
        cp(layer(dz, me.c), 4 + dz, me.xn).wait_recv()
        if dz == 2:
            pl.when(inner)(lambda: pass_copy().start())
        cp(layer(dz, me.c), 3 + nz + dz, me.sib).start()

    def step_done():
        cp(layer(0, co), 4, me.sib).wait_recv()
        for dz in range(1, nz):
            cp(layer(dz, co), 3 + nz + dz, me.sib).wait_recv()

    def drain():
        cp(one(me.y, me.x), 0, me.xn).wait_send()
        cp(one(me.y, me.x), 1, me.xn).wait_send()
        cp(part(me.y, xo, True), 2, me.xn).wait_send()
        cp(part(yo, me.x, False), 3, me.xn).wait_send()
        cp(layer(0, me.c), 4, me.xn).wait_send()
        for dz in range(1, nz):
            when(sends[dz], lambda: z_copy(dz).wait_send())
            cp(layer(dz, me.c), 3 + nz + dz, me.xn).wait_send()
        pl.when(inner)(lambda: pass_copy().wait_send())

    return SimpleNamespace(
        near=step_near, far=step_far, square=step_square, z=step_z, pass_on=step_pass, done=step_done, drain=drain
    )


class Moves:
    def __init__(self, moves, send, recv, core_recv):
        self.moves, self.send, self.recv, self.core_recv = moves, send, recv, core_recv

    def cp(self, i):
        src, dst, to = self.moves[i][:3]
        return remote(src, dst, self.send.at[i], self.recv.at[i - 1] if i else self.core_recv, to)

    def go(self, i):
        _, _, _, _, credit, turn, slots, _, sends, _ = self.moves[i]

        def action():
            if turn >= slots:
                pl.semaphore_wait(credit, 1)
            self.cp(i).start()

        when(sends, action)

    def free(self, i):
        _, _, _, giver, credit, turn, slots, turns, _, receives = self.moves[i]
        if turn + slots < turns:
            when(receives, lambda: pl.semaphore_signal(credit, inc=1, device_id=giver, device_id_type=MESH))

    def arrive(self, *at):
        for i in at:
            when(self.moves[i][9], lambda: self.cp(i).wait_recv())

    def drain(self):
        for i in range(len(self.moves)):
            when(self.moves[i][8], lambda: self.cp(i).wait_send())


def add(view, arrived):
    view[...] = (view[...].astype(F32) + arrived[...].astype(F32)).astype(view.dtype)


def add_core(me, w, core, nz):
    def body(zz, carry):
        for y in range(2):
            for x in range(2):
                add(w.at[zz, y, x, me.c], core.at[zz, y, x])
        return carry

    lax.fori_loop(0, nz, body, 0)


RELAY = 8


def z_moves(me, nz, layer, zs, relay, credit, turn):
    last = nz - 1
    outer = (me.z == 0) | (me.z == last)

    def at_z(zz):
        return me.dev(zz, me.y, me.x, me.c)

    moves = []
    for dz in range(1, nz):
        to, giver = lax.rem(me.z + dz, nz), lax.rem(me.z + nz - dz, nz)
        sends = {1: me.z != last, last: me.z != 0}.get(dz)
        receives = {1: me.z != 0, last: me.z != last}.get(dz)
        moves.append((layer(to), zs.at[dz - 1], at_z(to), at_z(giver), credit.at[dz - 1], *turn, sends, receives))
    near = jnp.where(me.z == last, last - 1, 1)
    back = jnp.where(me.z == last - 1, last, 0)
    moves.append(
        (layer(last - me.z), relay, at_z(near), at_z(back), credit.at[nz - 1], *turn, outer, jnp.logical_not(outer))
    )
    return moves, outer, jnp.where(me.z == last - 1, 0, last)


def scatter_steps(me, w, box, sems, credit, nz, core_turn, turn, sink):
    half = w.shape[4] // 2
    xo, yo, co = 1 - me.x, 1 - me.y, 1 - me.c
    core = box[0].at[core_turn[0] % core_turn[1]]
    y1, x1, x2, y2, zs, relay = (b.at[turn[0] % turn[1]] for b in box[1:7])
    total = box[7]
    both = (None, None)

    def layer(zz):
        return w.at[zz, me.y, me.x, me.c]

    moves = [
        (w.at[:, :, :, co], core, me.sib, me.sib, credit.at[0], *core_turn, *both),
        (w.at[:, yo, :, me.c, 0:half], y1, me.yn, me.yn, credit.at[1], *turn, *both),
        (w.at[:, :, xo, me.c, half:], x1, me.xn, me.xn, credit.at[2], *turn, *both),
        (w.at[:, me.y, xo, me.c, 0:half], x2, me.xn, me.xn, credit.at[3], *turn, *both),
        (w.at[:, yo, me.x, me.c, half:], y2, me.yn, me.yn, credit.at[4], *turn, *both),
    ]
    along, outer, handed = z_moves(me, nz, layer, zs, relay, credit.at[5 : 5 + nz], turn)
    m = Moves(moves + along, *sems)

    def step_a():
        m.go(0)

    def step_b():
        m.arrive(0)
        add_core(me, w, core, nz)
        m.free(0)
        m.go(1)
        m.go(2)

    def step_c():
        m.arrive(1, 2)

        def body(zz, carry):
            for o in range(2):
                add(w.at[zz, me.y, o, me.c, 0:half], y1.at[zz, o])
                add(w.at[zz, o, me.x, me.c, half:], x1.at[zz, o])
            return carry

        lax.fori_loop(0, nz, body, 0)
        m.free(1)
        m.free(2)
        m.go(3)
        m.go(4)

    def step_d():
        m.arrive(3, 4)

        def body(zz, carry):
            add(w.at[zz, me.y, me.x, me.c, 0:half], x2.at[zz])
            add(w.at[zz, me.y, me.x, me.c, half:], y2.at[zz])
            return carry

        lax.fori_loop(0, nz, body, 0)
        m.free(3)
        m.free(4)
        m.go(RELAY)
        m.go(5)
        m.go(7)
        pl.when(outer)(lambda: m.go(6))

    def step_r():
        @pl.when(jnp.logical_not(outer))
        def _():
            m.cp(RELAY).wait_recv()
            add(layer(handed), relay)
            m.go(6)

        m.free(RELAY)

    def step_e():
        m.arrive(5, 6, 7)
        total[...] = layer(me.z)[...].astype(F32) + zs[1].astype(F32)

        @pl.when(me.z != 0)
        def _():
            total[...] += zs[0].astype(F32)

        @pl.when(me.z != nz - 1)
        def _():
            total[...] += zs[2].astype(F32)

        sink(total[...])
        for i in (5, 6, 7):
            m.free(i)

    return SimpleNamespace(a=step_a, b=step_b, c=step_c, d=step_d, r=step_r, e=step_e, drain=m.drain)


def scatter_early_steps(me, w, box, sems, credit, nz, core_turn, turn, sink):
    half = w.shape[4] // 2
    xo, yo, co = 1 - me.x, 1 - me.y, 1 - me.c
    core = box[0].at[core_turn[0] % core_turn[1]]
    y1, x1, x2, y2, zs, relay = (b.at[turn[0] % turn[1]] for b in box[1:7])
    both = (None, None)
    base = 5 + nz

    def layer(zz):
        return w.at[zz, :, :, me.c]

    moves = [
        (w.at[:, :, :, co], core, me.sib, me.sib, credit.at[0], *core_turn, *both),
        (w.at[me.z, yo, :, me.c, 0:half], y1, me.yn, me.yn, credit.at[base], *turn, *both),
        (w.at[me.z, :, xo, me.c, half:], x1, me.xn, me.xn, credit.at[base + 1], *turn, *both),
        (w.at[me.z, me.y, xo, me.c, 0:half], x2, me.xn, me.xn, credit.at[base + 2], *turn, *both),
        (w.at[me.z, yo, me.x, me.c, half:], y2, me.yn, me.yn, credit.at[base + 3], *turn, *both),
    ]
    along, outer, handed = z_moves(me, nz, layer, zs, relay, credit.at[base + 4 : base + 4 + nz], turn)
    m = Moves(moves + along, *sems)

    def add_layer(zz, arrived):
        for y in range(2):
            for x in range(2):
                add(w.at[zz, y, x, me.c], arrived.at[y, x])

    def step_a():
        m.go(0)

    def step_b():
        m.arrive(0)
        add_core(me, w, core, nz)
        m.free(0)

    def step_z():
        m.go(RELAY)
        m.go(5)
        m.go(7)
        pl.when(outer)(lambda: m.go(6))

    def step_r():
        @pl.when(jnp.logical_not(outer))
        def _():
            m.cp(RELAY).wait_recv()
            add_layer(handed, relay)
            m.go(6)

        m.free(RELAY)

    def step_c():
        m.arrive(5, 6, 7)
        add_layer(me.z, zs.at[1])
        pl.when(me.z != 0)(lambda: add_layer(me.z, zs.at[0]))
        pl.when(me.z != nz - 1)(lambda: add_layer(me.z, zs.at[2]))
        for i in (5, 6, 7):
            m.free(i)
        m.go(1)
        m.go(2)

    def step_d():
        m.arrive(1, 2)
        for o in range(2):
            add(w.at[me.z, me.y, o, me.c, 0:half], y1.at[o])
            add(w.at[me.z, o, me.x, me.c, half:], x1.at[o])
        m.free(1)
        m.free(2)
        m.go(3)
        m.go(4)

    def step_e():
        m.arrive(3, 4)
        late = jnp.concatenate([x2[...].astype(F32), y2[...].astype(F32)], axis=0)
        sink(w[me.z, me.y, me.x, me.c].astype(F32) + late)
        m.free(3)
        m.free(4)

    return SimpleNamespace(a=step_a, b=step_b, z=step_z, r=step_r, c=step_c, d=step_d, e=step_e, drain=m.drain)


def lane_masks():
    lane = lax.broadcasted_iota(jnp.int32, (1, LANES), 1)
    left = jnp.where(lane < HEAD_DIM, 1.0, 0.0).astype(BF16)
    return left, (1.0 - left.astype(F32)).astype(BF16)


def two_heads(block):
    left, right = lane_masks()
    return jnp.concatenate([block * left, block * right], axis=0)


def one_block(pair):
    rows = pair.shape[0] // 2
    lane = lax.broadcasted_iota(jnp.int32, (rows, LANES), 1)
    return jnp.where(lane < HEAD_DIM, pair[:rows], pair[rows:])


def at128(p, base=0):
    return pl.ds(pl.multiple_of(base + p * LANES, LANES), LANES)


def put_stat(stat, p, pair):
    rows = pair.shape[0] // 2
    lane = lax.broadcasted_iota(jnp.int32, stat.shape, 1)
    stat = jnp.where(lane == 2 * p, pair[:rows], stat)
    return jnp.where(lane == 2 * p + 1, pair[rows:], stat)


def normalise(values):
    center = values - jnp.mean(values, axis=-1, keepdims=True)
    spread = jnp.mean(center * center, axis=-1, keepdims=True)
    return center * lax.rsqrt(spread + 1e-05)


def forward(r, me, nz):
    rows, d = r.tokens.shape
    items, frames = r.kv.shape[:2]
    pairs = d // LANES

    def weight(k, n, size=WIDE):
        return r.wg[k, :, :, :, :, :, n * size : (n + 1) * size].reshape(d, size)

    def product(x, k, sink):
        sink(dot(x, weight(k, 0, d)))

    def ln(values, i):
        return normalise(values) * r.gs[i : i + 1, :] + r.gs[4 + i : 5 + i, :]

    def norms_in():
        for g in range(2 * nz):
            total = r.ng[g // 2, g % 2, 0, 0, 0:16, :].astype(F32)
            for f in range(1, 4):
                total = total + r.ng[g // 2, g % 2, f // 2, f % 2, 0:16, :].astype(F32)
            r.gs[:, g * LANES : (g + 1) * LANES] = total

    def norm_one():
        pltpu.make_async_copy(r.tokens, r.first, r.own_sem.at[1]).wait()
        r.xb[...] = ln(r.first[...], 0).astype(BF16)
        r.n1t[...] = r.xb[...].T

    def joint(q):
        def sink(v):
            r.joint[:, q * d : (q + 1) * d] = v.astype(BF16)

        product(r.xb[...], q, sink)

    def self_attention(half):
        row = lax.rem(lax.broadcasted_iota(jnp.int32, (2 * rows, rows), 0), rows)
        causal = row >= lax.broadcasted_iota(jnp.int32, (2 * rows, rows), 1)

        def body(p, stat):
            q2 = two_heads(r.joint[:, at128(p)] * jnp.asarray(HEAD_DIM**-0.5, BF16))
            s = dot_nt(q2, r.joint[:, at128(p, d)])
            s = jnp.where(causal, s, -1e30)
            m = jnp.max(s, axis=-1, keepdims=True)
            e = jnp.exp(s - m)
            total = jnp.sum(e, axis=-1, keepdims=True)
            o2 = dot(e.astype(BF16), r.joint[:, at128(p, 2 * d)]) / total
            r.xb[:, at128(p)] = one_block(o2).astype(BF16)
            return put_stat(stat, p, m + jnp.log(total))

        first = jnp.zeros((rows, LANES), F32) if half == 0 else r.wcol[...]
        stat = lax.fori_loop(half * pairs // 2, (half + 1) * pairs // 2, body, first)
        if half == 0:
            r.wcol[...] = stat
        else:
            r.slse[...] = stat.T[0:16]
            r.smixt[...] = r.xb[...].T

    def self_out():
        def sink(v):
            r.branch[...] = v

        product(r.xb[...], 3, sink)
        r.first[...] = r.first[...] + r.branch[...]
        squares(1, r.branch[...])
        r.xb[...] = ln(r.first[...], 1).astype(BF16)
        r.n2t[...] = r.xb[...].T

    def squares(i, values):
        ok = lax.broadcasted_iota(jnp.int32, (rows, 1), 0) < r.tl[0]
        total = jnp.sum(jnp.where(ok, values * values, 0.0))
        line = lax.broadcasted_iota(jnp.int32, r.sq.shape, 0)
        r.sq[...] = jnp.where(line == i, total, r.sq[...])

    def start_counts():
        line = lax.broadcasted_iota(jnp.int32, r.sq.shape, 0)
        r.sq[...] = jnp.where(line == 4, r.tl[0].astype(F32), 0.0)

    def queries():
        def sink(v):
            r.qa[me.fr] = v.astype(BF16)

        product(r.xb[...], 4, sink)

    def q_copy(f, s, device):
        return remote(r.qa.at[f], r.qa.at[f], r.q_send.at[s], r.q_recv.at[s], device)

    fx, fs, fd = (1 - me.x) * 2 + me.c, me.x * 2 + 1 - me.c, (1 - me.x) * 2 + 1 - me.c

    def q_start():
        q_copy(me.fr, 0, me.xn).start()
        q_copy(me.fr, 1, me.sib).start()

    def q_forward():
        q_copy(fx, 0, me.xn).wait_recv()
        q_copy(fx, 2, me.sib).start()

    def q_done():
        q_copy(fs, 1, me.sib).wait_recv()
        q_copy(fd, 2, me.sib).wait_recv()

    def mem_copy(t):
        return pltpu.make_async_copy(r.memory.at[t], r.rc.at[t % 2, 0 : r.memory.shape[1]], r.m_sem.at[t % 2])

    def memory_part(which, t):
        mem_copy(t).wait()
        stage = r.rc.at[t % 2, 0 : r.memory.shape[1]]
        for n in range(d // WIDE):
            v = dot(stage[...].reshape(frames, d), weight(5 + which, n))
            r.kv[t, :, which * d + n * WIDE : which * d + (n + 1) * WIDE] = v.astype(BF16)
        if which == 0:
            r.memt[:, t * frames : (t + 1) * frames] = stage[...].reshape(frames, d).T
        if t + 2 < items or which == 0:
            mem_copy((t + 2) % items).start()

    def mem_start():
        for t in range(min(2, items)):
            mem_copy(t).start()

    def cross_half(t, half):
        def body(p, stat):
            q2 = two_heads(r.qa[t, :, at128(p)] * jnp.asarray(HEAD_DIM**-0.5, BF16))
            s = dot_nt(q2, r.kv[t, :, at128(p)]) + r.bias[pl.ds(t, 1), :]
            m = jnp.max(s, axis=-1, keepdims=True)
            e = jnp.exp(s - m)
            total = jnp.sum(e, axis=-1, keepdims=True)
            o2 = dot(e.astype(BF16), r.kv[t, :, at128(p, d)]) / total
            r.op[t, :, at128(p)] = one_block(o2).astype(BF16)
            return put_stat(stat, p, m + jnp.log(total))

        first = jnp.zeros((rows, LANES), F32) if half == 0 else r.wcol[...]
        stat = lax.fori_loop(half * pairs // 2, (half + 1) * pairs // 2, body, first)
        if half == 0:
            r.wcol[...] = stat
        else:
            r.opl[t] = stat.T[0:16]

    def o_copies(t, slot, device):
        return (
            remote(r.op.at[t], r.orv.at[slot], r.o_send.at[slot], r.o_recv.at[slot], device),
            remote(r.opl.at[t], r.orl.at[slot], r.o_send.at[3 + slot], r.o_recv.at[3 + slot], device),
        )

    def o_start(t, slot, device):
        for cp in o_copies(t, slot, device):
            cp.start()

    def o_wait(t, slot, device):
        for cp in o_copies(t, slot, device):
            cp.wait_recv()

    def merge(parts, sink):
        lses = [lse[...] for _, lse in parts]
        top = functools.reduce(jnp.maximum, lses)
        shares = [jnp.exp(v - top) for v in lses]
        total = functools.reduce(jnp.add, shares)
        flat = jnp.concatenate([v / total for v in shares] + [jnp.zeros((LANES - 16 * len(parts), LANES), F32)], axis=0)
        r.wcol[...] = flat.T
        lane = lax.broadcasted_iota(jnp.int32, (rows, LANES), 1)
        for p in range(pairs):
            value = jnp.zeros((rows, LANES), F32)
            for i, (mix, _) in enumerate(parts):
                left = r.wcol[:, 16 * i + 2 * p : 16 * i + 2 * p + 1]
                right = r.wcol[:, 16 * i + 2 * p + 1 : 16 * i + 2 * p + 2]
                share = jnp.where(lane < HEAD_DIM, left, right)
                value = value + share * mix[:, p * LANES : (p + 1) * LANES].astype(F32)
            sink(p, value)
        return top + jnp.log(total)

    def send_far():
        o_start(fd, 0, me.sib)

    def send_side():
        o_start(fs, 1, me.sib)

    def merge_across():
        o_wait(fd, 0, me.sib)

        def sink(p, v):
            r.op[fx, :, p * LANES : (p + 1) * LANES] = v.astype(BF16)

        r.opl[fx] = merge([(r.op.at[fx], r.opl.at[fx]), (r.orv.at[0], r.orl.at[0])], sink)
        o_start(fx, 2, me.xn)

    def merge_own():
        o_wait(fs, 1, me.sib)
        o_wait(fx, 2, me.xn)

        def sink(p, v):
            r.xb[:, p * LANES : (p + 1) * LANES] = v.astype(BF16)

        parts = [(r.op.at[me.fr], r.opl.at[me.fr]), (r.orv.at[1], r.orl.at[1]), (r.orv.at[2], r.orl.at[2])]
        r.clse[...] = merge(parts, sink)
        r.cmixt[...] = r.xb[...].T

    def cross_out():
        def sink(v):
            r.branch[...] = v

        product(r.xb[...], 7, sink)
        squares(2, r.branch[...])
        r.second[...] = r.first[...] + r.branch[...]
        r.xb[...] = ln(r.second[...], 2).astype(BF16)
        r.n3t[...] = r.xb[...].T

    def expand(q):
        for n in range(d // WIDE):
            v = dot(r.xb[...], weight(8 + q, n))
            at = slice(q * d + n * WIDE, q * d + (n + 1) * WIDE)
            half = 0.5 * (1.0 + lax.erf(v * (2.0**-0.5)))
            r.active[:, at] = (v * half).astype(BF16)
            r.slope[:, at] = (half + v * jnp.exp(-0.5 * v * v) * 0.3989422804014327).astype(BF16)
        r.activet[q * d : (q + 1) * d, :] = r.active[:, q * d : (q + 1) * d].T

    def contract(q, fresh=False):
        def sink(v):
            r.branch[...] = v if fresh else r.branch[...] + v

        product(r.active[:, q * d : (q + 1) * d], 12 + q, sink)

    def finish():
        squares(3, r.branch[...])
        r.third[...] = r.second[...] + r.branch[...]
        squares(0, r.third[...])
        ok = lax.broadcasted_iota(jnp.int32, (rows, 1), 0) < r.tl[0]
        r.branch[...] = jnp.where(ok, ln(r.third[...], 3), 0.0)
        pltpu.make_async_copy(r.branch, r.result, r.own_sem.at[3]).start()

    part = functools.partial

    def item(t):
        return [part(cross_half, t, 0), part(cross_half, t, 1)]

    tasks = {
        0: [start_counts, mem_start],
        2: [norms_in, norm_one],
        4: [part(joint, 0)],
        5: [part(joint, 1)],
        6: [part(joint, 2), part(self_attention, 0), part(self_attention, 1)],
        7: [self_out],
        8: [queries, q_start],
        9: [part(memory_part, 0, t) for t in range(items)],
        10: [q_forward] + [part(memory_part, 1, t) for t in range(items)],
        11: [q_done, *item(fd), send_far, *item(fs), send_side],
        12: [*item(fx), merge_across],
        13: item(me.fr),
        14: [merge_own, cross_out, part(expand, 0), part(expand, 1), part(contract, LATE[0] - 12, True)],
        15: [part(expand, 2), part(expand, 3), part(contract, LATE[1] - 12)],
        16: [part(contract, LATE[2] - 12), part(contract, 0), finish],
    }

    def drain():
        q_copy(me.fr, 0, me.xn).wait_send()
        q_copy(me.fr, 1, me.sib).wait_send()
        q_copy(fx, 2, me.sib).wait_send()
        for t, slot, device in ((fd, 0, me.sib), (fs, 1, me.sib), (fx, 2, me.xn)):
            for cp in o_copies(t, slot, device):
                cp.wait_send()

    return tasks, drain, (fx, fs, fd)


def ln_back(values, gain_row, grad):
    center = values - jnp.mean(values, axis=-1, keepdims=True)
    scale = lax.rsqrt(jnp.mean(center * center, axis=-1, keepdims=True) + 1e-05)
    unit = center * scale
    gain_grad = jnp.sum(grad * unit, axis=0, keepdims=True)
    shift_grad = jnp.sum(grad, axis=0, keepdims=True)
    lifted = grad * gain_row
    inner = jnp.mean(lifted * unit, axis=-1, keepdims=True)
    back = scale * (lifted - jnp.mean(lifted, axis=-1, keepdims=True) - unit * inner)
    return back, gain_grad, shift_grad


def backward(r, me, nz, fronts):
    rows, d = r.first.shape
    items, frames = r.kv.shape[:2]
    pairs = d // LANES
    fx, fs, fd = fronts
    t = {}

    def grad_into(k, left, right, into=None):
        for n in range(d // WIDE):
            v = dot(left, right(n * WIDE, (n + 1) * WIDE)).astype(BF16)
            at = slice(n * WIDE, (n + 1) * WIDE)
            r.wg[k if into is None else into, :, :, :, :, :, at] = v.reshape(nz, 2, 2, 2, d // (8 * nz), WIDE)

    def through(k, grad):
        return dot_nt(grad, r.wg[k].reshape(d, d))

    def ln_step(i, values, grad, first=False):
        back, gain, shift = ln_back(values, r.gs[i : i + 1, :], grad)
        r.gr[...] = back if first else r.gr[...] + back
        r.nrow[i : i + 1, :] = gain
        r.nrow[4 + i : 5 + i, :] = shift

    def start():
        pltpu.make_async_copy(r.cotangent, r.gr, r.own_sem.at[2]).wait()
        r.biast[...] = jnp.concatenate([r.bias[...], jnp.zeros((LANES - r.bias.shape[0], frames), F32)], axis=0).T
        for g in range(d // LANES):
            r.nrow[8:16, g * LANES : (g + 1) * LANES] = r.sq[...]
        ok = lax.broadcasted_iota(jnp.int32, (rows, 1), 0) < r.tl[0]
        ln_step(3, r.third[...], jnp.where(ok, r.gr[...], 0.0), True)
        r.xb[...] = r.gr[...].astype(BF16)
        pltpu.make_async_copy(r.tokens, r.third, r.own_sem.at[1]).start()

    def contract(q):
        at = slice(q * d, (q + 1) * d)
        r.active[:, at] = (through(12 + q, r.xb[...]) * r.slope[:, at].astype(F32)).astype(BF16)

    def contract_grad(q):
        grad_into(12 + q, r.activet[q * d : (q + 1) * d, :], lambda lo, hi: r.xb[:, lo:hi])

    def onto(fresh, value):
        r.branch[...] = value if fresh else r.branch[...] + value

    def expand(q):
        if q == 0:
            pltpu.make_async_copy(r.branch, r.result, r.own_sem.at[3]).wait()
        onto(q == 0, through(8 + q, r.active[:, q * d : (q + 1) * d]))

    def expand_grad(q):
        grad_into(8 + q, r.n3t[...], lambda lo, hi: r.active[:, q * d + lo : q * d + hi])

    def cross_out():
        ln_step(2, r.second[...], r.branch[...])
        r.xb[...] = r.gr[...].astype(BF16)
        r.ga[me.fr] = through(7, r.xb[...]).astype(BF16)
        r.gl[me.fr, 0:16] = r.clse[...]

        def body(p, carry):
            left, right = row_dots(r.ga[me.fr, :, at128(p)], r.cmixt[at128(p), :])
            r.gl[me.fr, pl.ds(16 + 2 * p, 1), :] = left
            r.gl[me.fr, pl.ds(17 + 2 * p, 1), :] = right
            return carry

        lax.fori_loop(0, pairs, body, 0)

    def cross_out_grad():
        grad_into(7, r.cmixt[...], lambda lo, hi: r.xb[:, lo:hi])

    def row_dots(grad, mixt):
        prod = grad.astype(F32).T * mixt.astype(F32)
        return jnp.sum(prod[:HEAD_DIM], axis=0, keepdims=True), jnp.sum(prod[HEAD_DIM:], axis=0, keepdims=True)

    def g_copies(f, s, device):
        return (
            remote(r.ga.at[f], r.ga.at[f], r.g2_send.at[s], r.g2_recv.at[s], device),
            remote(r.gl.at[f], r.gl.at[f], r.g2_send.at[3 + s], r.g2_recv.at[3 + s], device),
        )

    def each(copies, what):
        for cp in copies:
            getattr(cp, what)()

    def g_start():
        each(g_copies(me.fr, 0, me.xn), "start")
        each(g_copies(me.fr, 1, me.sib), "start")

    def g_forward():
        each(g_copies(fx, 0, me.xn), "wait_recv")
        each(g_copies(fx, 2, me.sib), "start")

    def g_drain():
        each(g_copies(me.fr, 0, me.xn), "wait_send")
        each(g_copies(me.fr, 1, me.sib), "wait_send")
        each(g_copies(fx, 2, me.sib), "wait_send")

    scale = HEAD_DIM**-0.5

    def pair_back(q, k, v, g, hide, lse, dots):
        q2, g2 = two_heads(q * jnp.asarray(scale, BF16)), two_heads(g)
        probs = jnp.exp(hide(dot_nt(k, q2)) - lse)
        ds = (probs * (dot_nt(v, g2) - dots)).astype(BF16)
        dq = one_block(dot(ds.T, k)) * scale
        return dq, dot(ds, q2), dot(probs.astype(BF16), g2)

    def cross_half(f, half):
        lane = lax.broadcasted_iota(jnp.int32, (frames, LANES), 1)
        column = jnp.sum(jnp.where(lane == f, r.biast[...], 0.0), axis=-1, keepdims=True)

        def body(p, carry):
            stats = [
                jnp.concatenate([r.gl[f, pl.ds(b + 2 * p, 1), :], r.gl[f, pl.ds(b + 1 + 2 * p, 1), :]], axis=1)
                for b in (0, 16)
            ]
            dq, dk, dv = pair_back(
                r.qa[f, :, at128(p)],
                r.kv[f, :, at128(p)],
                r.kv[f, :, at128(p, d)],
                r.ga[f, :, at128(p)],
                lambda s: s + column,
                *stats,
            )
            r.op[f, :, at128(p)] = dq.astype(BF16)
            r.kv[f, :, at128(p)] = dk.astype(BF16)
            r.kv[f, :, at128(p, d)] = dv.astype(BF16)
            return carry

        lax.fori_loop(half * pairs // 2, (half + 1) * pairs // 2, body, 0)

    def d_copy(f, slot, device):
        return remote(r.op.at[f], r.orv.at[slot], r.o2_send.at[slot], r.o2_recv.at[slot], device)

    def side_ready():
        each(g_copies(fs, 1, me.sib), "wait_recv")

    def send_side():
        d_copy(fs, 1, me.sib).start()

    def far_ready():
        each(g_copies(fd, 2, me.sib), "wait_recv")

    def send_far():
        d_copy(fd, 0, me.sib).start()

    def send_across():
        d_copy(fd, 0, me.sib).wait_recv()
        r.op[fx] = (r.op[fx].astype(F32) + r.orv[0].astype(F32)).astype(BF16)
        d_copy(fx, 2, me.xn).start()

    def tile_copy(n):
        f, h = n // 2, n % 2
        return pltpu.make_async_copy(
            r.mst.at[n % 2, 0 : r.memory_grad.shape[1]],
            r.memory_grad.at[f, :, h * WIDE : (h + 1) * WIDE],
            r.t_sem.at[n % 2],
        )

    def memory_grad(n):
        f, h = n // 2, n % 2
        if n >= 2:
            tile_copy(n - 2).wait()
        layers = slice(h * nz // 2, (h + 1) * nz // 2)
        keys, values = (r.wg[k, layers].reshape(WIDE, d) for k in (5, 6))
        r.mst[n % 2] = dot_nt(r.kv[f, :, 0:d], keys) + dot_nt(r.kv[f, :, d : 2 * d], values)
        tile_copy(n).start()

    def memory_done():
        for n in (2 * items - 2, 2 * items - 1):
            tile_copy(n).wait()

    def memory_weights(which, into):
        def rows_of(lo, hi):
            return r.kv[:, :, which * d + lo : which * d + hi].reshape(items * frames, hi - lo)

        grad_into(5 + which, r.memt[...], rows_of, into)

    def query():
        d_copy(fs, 1, me.sib).wait_recv()
        d_copy(fx, 2, me.xn).wait_recv()
        r.xb[...] = (r.op[me.fr].astype(F32) + r.orv[1].astype(F32) + r.orv[2].astype(F32)).astype(BF16)
        onto(True, through(4, r.xb[...]))
        grad_into(4, r.n2t[...], lambda lo, hi: r.xb[:, lo:hi])

    def d_drain():
        for f, slot, device in ((fd, 0, me.sib), (fs, 1, me.sib), (fx, 2, me.xn)):
            d_copy(f, slot, device).wait_send()

    def self_out():
        ln_step(1, r.first[...], r.branch[...])
        r.xb[...] = r.gr[...].astype(BF16)
        r.ga[me.fr] = through(3, r.xb[...]).astype(BF16)
        grad_into(3, r.smixt[...], lambda lo, hi: r.xb[:, lo:hi])

    def self_attention(half):
        key = lax.broadcasted_iota(jnp.int32, (rows, 2 * rows), 0)
        causal = key <= lax.rem(lax.broadcasted_iota(jnp.int32, (rows, 2 * rows), 1), rows)

        def body(p, carry):
            g = r.ga[me.fr, :, at128(p)]
            lse = jnp.concatenate([r.slse[pl.ds(2 * p, 1), :], r.slse[pl.ds(2 * p + 1, 1), :]], axis=1)
            dots = jnp.concatenate(row_dots(g, r.smixt[at128(p), :]), axis=1)
            dq, dk, dv = pair_back(
                r.joint[:, at128(p)],
                r.joint[:, at128(p, d)],
                r.joint[:, at128(p, 2 * d)],
                g,
                lambda s: jnp.where(causal, s, -1e30),
                lse,
                dots,
            )
            r.joint[:, at128(p)] = dq.astype(BF16)
            r.joint[:, at128(p, d)] = dk.astype(BF16)
            r.joint[:, at128(p, 2 * d)] = dv.astype(BF16)
            return carry

        lax.fori_loop(half * pairs // 2, (half + 1) * pairs // 2, body, 0)

    def project(q):
        onto(q == 0, through(q, r.joint[:, q * d : (q + 1) * d]))

    def project_grad(q):
        grad_into(q, r.n1t[...], lambda lo, hi: r.joint[:, q * d + lo : q * d + hi])

    def finish():
        pltpu.make_async_copy(r.tokens, r.third, r.own_sem.at[1]).wait()
        ln_step(0, r.third[...], r.branch[...])
        pltpu.make_async_copy(r.gr, r.tokens_grad, r.own_sem.at[2]).start()
        for g in range(d // LANES):
            for f in range(4):
                r.nw[g // 2, g % 2, f // 2, f % 2] = r.nrow[:, g * LANES : (g + 1) * LANES]

    def close():
        pltpu.make_async_copy(r.gr, r.tokens_grad, r.own_sem.at[2]).wait()

    return SimpleNamespace(**{k: v for k, v in locals().items() if callable(v)})


GRAD_ORDER = (12, 13, 14, 15, 8, 9, 10, 11, 7, 5, 6, 4, 3, 0, 1, 2)
SLOTS = 2


LATE = (13, 14, 15)
LATE_TICKS = (1, 4, 8)
TILT = (5, 9)
EARLY = (1, 3, 5)
EARLY_TICKS = (1, 4, 7)
ROWS = 7
SEND_ROWS = 7
INTO = {5: 12, 6: 14}


def own_blocks(r):
    slab, d = r.self_output.shape
    blocks = {}
    for k in range(3):
        blocks[k] = (r.self_project.at[:, k * d : (k + 1) * d], r.self_project_grad.at[:, k * d : (k + 1) * d])
    for k in range(2):
        blocks[5 + k] = (r.cross_memory.at[:, k * d : (k + 1) * d], r.cross_memory_grad.at[:, k * d : (k + 1) * d])
    blocks[3] = (r.self_output, r.self_output_grad)
    blocks[4] = (r.cross_query, r.cross_query_grad)
    blocks[7] = (r.cross_output, r.cross_output_grad)
    for k in range(4):
        blocks[12 + k] = tuple(a.at[k * slab : (k + 1) * slab] for a in (r.contract, r.contract_grad))
    return blocks


def deal(r, put):
    slab = r.expand.shape[0]
    ways = LANES // slab

    def body(g, carry):
        lane = lax.div(lax.broadcasted_iota(jnp.int32, (slab, LANES), 1), slab)
        source = [r.expand[:, at128(ways * g + a)].astype(F32) for a in range(ways)]
        for q in range(ways):
            total = source[q]
            for a in range(ways):
                if a != q:
                    total = jnp.where(lane == a, pltpu.roll(source[a], (slab * (a - q)) % LANES, 1), total)
            put(q, at128(g), total.astype(BF16))
        return carry

    lax.fori_loop(0, r.expand.shape[1] // (ways * LANES), body, 0)


def undeal(r, q, total):
    slab = total.shape[0]
    ways = LANES // slab
    lane = lax.div(lax.broadcasted_iota(jnp.int32, (slab, LANES), 1), slab)
    for g in range(total.shape[1] // LANES):
        block = total[:, g * LANES : (g + 1) * LANES]
        for a in range(ways):
            line, column = divmod((ways * g + a) * LANES, total.shape[1])
            at = (slice(line * slab, (line + 1) * slab), slice(column, column + LANES))
            moved = block if a == q else pltpu.roll(block, (slab * (q - a)) % LANES, 1)
            r.second[at] = jnp.where(lane == q, moved, r.second[at])


def hide_frames(r, me):
    items, total = r.cross_mask.shape
    count = r.memory_grad.shape[1]
    mask = r.cross_mask[:, 0:count]
    for f in range(1, total // count):
        mask = jnp.where(me.fr == f, r.cross_mask[:, f * count : (f + 1) * count], mask)
    frame = me.fr * count + lax.broadcasted_iota(jnp.int32, (items, count), 1)
    line = lax.broadcasted_iota(jnp.int32, (items, count), 0)
    length = jnp.zeros((items, count), jnp.int32)
    for t in range(items):
        length = jnp.where(line == t, r.memory_length[t], length)
    ok = (frame < length) & ((mask == 1) | (frame == 0))
    r.bias[...] = jnp.full(r.bias.shape, -1e30, F32)
    r.bias[0:items, 0:count] = jnp.where(ok, 0.0, -1e30)


def run(r, nz, chunks):
    me = place()
    barrier = pltpu.get_barrier_semaphore()
    peers = [me.xn, me.yn, me.sib, me.diag]
    peers += [me.dev(lax.rem(me.z + dz, nz), me.y, me.x, me.c) for dz in range(1, nz)]
    for device in peers:
        pl.semaphore_signal(barrier, inc=1, device_id=device, device_id_type=MESH)
    blocks = own_blocks(r)
    owns = {
        k: pltpu.make_async_copy(blocks[k][0], r.wg.at[k, me.z, me.y, me.x, me.c], r.w_sem.at[k]) for k in sorted(blocks)
    }
    for k in (0, 1, *LATE):
        owns[k].start()
    for k in owns:
        if k not in (0, 1, *LATE):
            owns[k].start()
    pltpu.make_async_copy(r.tokens, r.first, r.own_sem.at[1]).start()
    pltpu.make_async_copy(r.cotangent, r.gr, r.own_sem.at[2]).start()
    slab = r.expand.shape[0]
    lane = lax.div(lax.broadcasted_iota(jnp.int32, (8, LANES), 1), slab)
    both = jnp.concatenate([r.norm_gains[...].astype(F32), r.norm_shifts[...].astype(F32)], axis=0)
    wide = jnp.where(lane == me.fr, jnp.concatenate([both] * (LANES // slab), axis=1), 0.0)
    r.ng[me.z, me.y, me.x, me.c] = jnp.concatenate([wide, jnp.zeros((24, LANES), F32)], axis=0).astype(BF16)

    def put(q, at, v):
        r.wg[8 + q, me.z, me.y, me.x, me.c, :, at] = v

    early = [k for k in range(chunks) if k not in LATE]
    count = len(early)
    norm = gather_steps(me, r.ng, r.g_send.at[ROWS], r.g_recv.at[ROWS], nz)
    steps = []
    for k in range(chunks):
        row = ROWS + 1 + LATE.index(k) if k in LATE else early.index(k) % ROWS
        sems = (r.g_send.at[row], r.g_recv.at[row])
        if k in LATE:
            steps.append(gather_late_steps(me, r.wg.at[k], *sems, nz))
        else:
            steps.append(gather_steps(me, r.wg.at[k], *sems, nz, k in TILT))

    def mix(steps, pieces):
        for i, step in enumerate(steps):
            step()
            for piece in pieces[i * len(pieces) // len(steps) : (i + 1) * len(pieces) // len(steps)]:
                piece()

    part = functools.partial
    pl.semaphore_wait(barrier, len(peers))
    norm.z()
    owns[0].wait()
    steps[0].z()
    for k in LATE:
        owns[k].wait()
        steps[k].near()
    for k in owns:
        if k != 0 and k not in LATE:
            owns[k].wait()
    for k in LATE:
        steps[k].far()
    steps[0].relay()
    tasks, drain, fronts = forward(r, me, nz)
    lines = {tick: [] for tick in range(count + 4)}
    for tick in lines:
        for step, t in (
            ("done", tick - 4),
            ("near", tick),
            ("drain", tick - 4),
            ("z", tick + 2),
            ("relay", tick + 1),
            ("far", tick - 1),
            ("last", tick - 2),
        ):
            if tick == 0 and step == "z":
                lines[tick].append(steps[early[1]].z)
            if 0 <= t < count:
                lines[tick].append(getattr(steps[early[t]], step))
    lines[0][1:1] = [norm.relay, norm.near]
    lines[0].append(norm.far)
    lines[1] += [norm.last] + [steps[k].square for k in LATE]
    lines[2].insert(0, norm.done)
    for k, first in zip(LATE, LATE_TICKS):
        for dz, go, come in ((2, first, first + 3), (1, first + 2, first + 6), (3, first + 2, first + 6)):
            lines[go].append(part(steps[k].z, dz))
            lines[come].append(part(steps[k].pass_on, dz))
        lines[first + 8].insert(0, steps[k].done)
    tasks[0] = tasks.get(0, []) + [part(deal, r, put), part(hide_frames, r, me)]
    for tick in lines:
        mix(lines[tick], tasks.get(tick, []))
    drain()
    norm.drain()
    for k in LATE:
        steps[k].drain()

    b = backward(r, me, nz, fronts)

    plain = [m for m in range(chunks) if m not in EARLY]
    spots = {m: i if i < len(EARLY) + 3 else i + 1 for i, m in enumerate(plain)}
    ends = {m: t + 4.0 for m, t in spots.items()}
    ends.update({m: EARLY_TICKS[i] + 5.5 for i, m in enumerate(EARLY)})
    direct = sorted((m for m, k in enumerate(GRAD_ORDER) if k in blocks), key=ends.get)

    def out_copy(i):
        return pltpu.make_async_copy(r.ost.at[i % 2], blocks[GRAD_ORDER[direct[i]]][1], r.e_sem.at[i % 2])

    def keep(turn):
        k = GRAD_ORDER[turn]

        def sink(total):
            if k not in blocks:
                undeal(r, k - 8, total)
                return
            i = direct.index(turn)
            if i >= 2:
                out_copy(i - 2).wait()
            r.ost[i % 2] = total
            out_copy(i).start()

        return sink

    def keep_norms(total):
        rms = jnp.sqrt(total / (total[12:13] * r.first.shape[1]))
        line = lax.broadcasted_iota(jnp.int32, total.shape, 0)
        r.norm_out[...] = jnp.where(line < 8, total, rms)

    boxes = (r.rc, r.y1, r.x1, r.x2, r.y2, r.zs, r.zr, r.total)
    fast_boxes = (r.rc, r.fy1, r.fx1, r.fx2, r.fy2, r.fzs, r.fzr)
    norm_boxes = (r.nrc, r.ny1, r.nx1, r.nx2, r.ny2, r.nzs, r.nzr, r.ntotal)
    adds = {}
    for m, k in enumerate(GRAD_ORDER):
        w = r.wg.at[INTO.get(k, k)]
        if m in EARLY:
            build, box, turn = scatter_early_steps, fast_boxes, (EARLY.index(m), 1, len(EARLY))
            at = SEND_ROWS + EARLY.index(m), SLOTS
        else:
            build, box, turn = scatter_steps, boxes, (plain.index(m), SLOTS, len(plain))
            at = turn[0] % SEND_ROWS, turn[0] % SLOTS
        sems = (r.s_send.at[at[0]], r.s_recv.at[at[1]], r.core_recv.at[m % SLOTS])
        adds[m] = build(me, w, box, sems, r.credit, nz, (m, SLOTS, chunks), turn, keep(m))
    once = (0, 1, 1)
    sems = (r.s_send.at[SEND_ROWS + len(EARLY)], r.s_recv.at[SLOTS + 1], r.core_recv.at[SLOTS])
    adds[chunks] = scatter_steps(me, r.nw, norm_boxes, sems, r.credit, nz, once, once, keep_norms)
    wide_copies = [
        pltpu.make_async_copy(
            r.second.at[i * slab : (i + 1) * slab],
            r.expand_grad.at[:, i * r.second.shape[1] : (i + 1) * r.second.shape[1]],
            r.x_sem.at[i],
        )
        for i in range(4)
    ]

    def wide_start():
        for cp in wide_copies:
            cp.start()

    def pair(f):
        return [part(b.cross_half, f, 0), part(b.cross_half, f, 1)]

    fx, fs, fd = fronts
    mg = [part(b.memory_grad, n) for n in range(8)]
    work = {
        -1: [b.start, part(b.contract, 0), part(b.contract_grad, 0), adds[0].a],
        0: [
            part(b.contract, 1),
            part(b.contract_grad, 1),
            adds[1].a,
            part(b.contract, 2),
            part(b.contract_grad, 2),
            adds[2].a,
            part(b.contract, 3),
            part(b.contract_grad, 3),
        ],
        1: [
            adds[3].a,
            part(b.expand, 0),
            part(b.expand_grad, 0),
            adds[4].a,
            part(b.expand, 1),
            part(b.expand_grad, 1),
            part(b.expand, 2),
            part(b.expand_grad, 2),
        ],
        2: [adds[5].a, part(b.expand, 3), part(b.expand_grad, 3), adds[6].a, b.cross_out, b.g_start, b.cross_out_grad],
        3: [adds[7].a, *pair(me.fr), adds[8].a, b.side_ready, part(b.cross_half, fs, 0)],
        4: [part(b.cross_half, fs, 1), b.send_side, b.g_forward, b.far_ready, part(b.cross_half, fd, 0)],
        5: [part(b.cross_half, fd, 1), b.send_far, *pair(fx)],
        6: [b.send_across, part(b.memory_weights, 0, INTO[5]), adds[9].a, b.g_drain],
        7: [part(b.memory_weights, 1, INTO[6]), adds[10].a, mg[0]],
        8: [b.query, adds[11].a, mg[1], mg[2]],
        9: [b.d_drain, b.self_out, adds[12].a, mg[3]],
        10: [part(b.self_attention, 0), part(b.self_attention, 1), part(b.project, 0), part(b.project_grad, 0), adds[13].a],
        11: [part(b.project, 1), part(b.project_grad, 1), adds[14].a, mg[4]],
        12: [part(b.project, 2), part(b.project_grad, 2), adds[15].a, b.finish, adds[16].a],
        13: [mg[5]],
        14: [mg[6], mg[7]],
        16: [b.memory_done],
    }
    named = {}
    spots[chunks] = max(spots.values())
    for m, spot in spots.items():
        for late, name in enumerate("bcdre"):
            named.setdefault(spot + late, {}).setdefault(name, []).append(getattr(adds[m], name))
    for i, m in enumerate(EARLY):
        named[i + 1]["b"].insert(0, adds[m].b)
        for late, name in enumerate(("z", "r", None, "c", "d", "e")):
            if name:
                named[EARLY_TICKS[i] + late].setdefault("also", []).append(getattr(adds[m], name))
    for i, m in enumerate(plain[: len(plain) - SEND_ROWS]):
        named[spots[m] + 5].setdefault("drain", []).append(adds[m].drain)

    def all_of(actions):
        for action in actions:
            action()

    for tick in range(-1, spots[chunks] + 5):
        by = named.get(tick, {})
        line = [part(all_of, by.get("drain", []) + by.get("b", []))]
        line += [step for name in ("e", "r", "c", "d", "also") for step in by.get(name, [])]
        mix(line, work.get(tick, []))
        if tick == 13:
            wide_start()
    b.close()
    for cp in wide_copies:
        cp.wait()
    out_copy(len(direct) - 2).wait()
    out_copy(len(direct) - 1).wait()
    for m in (*plain[len(plain) - SEND_ROWS :], *EARLY, chunks):
        adds[m].drain()


VMEM_BYTES = 127 * 2**19


INPUTS = (
    "tl",
    "tokens",
    "cotangent",
    "memory",
    "self_project",
    "self_output",
    "cross_query",
    "cross_memory",
    "cross_output",
    "expand",
    "contract",
    "norm_gains",
    "norm_shifts",
    "memory_length",
    "cross_mask",
)
GRADS = ("self_project", "self_output", "cross_query", "cross_memory", "cross_output", "expand", "contract")


def at(space):
    return pl.BlockSpec(memory_space=space)


def fused(nz, chunks, frame_count, **given):
    rows, d = given["tokens"].shape
    items, parts = given["memory"].shape[:2]
    slab = given["self_output"].shape[0]
    padded = parts * 4 * slab
    half = slab // 2
    outs = dict(
        result=((rows, d), pl.ANY),
        tokens_grad=((rows, d), pl.ANY),
        memory_grad=((items, frame_count, d), pl.ANY),
        **{k + "_grad": (given[k].shape, pl.ANY) for k in GRADS},
        norm_out=((16, LANES), pltpu.VMEM),
    )
    vm = pltpu.VMEM
    dma = pltpu.SemaphoreType.DMA
    scratch = dict(
        wg=vm((chunks, nz, 2, 2, 2, slab, d), BF16),
        ng=vm((nz, 2, 2, 2, 32, LANES), BF16),
        gs=vm((16, d), F32),
        n1t=vm((d, rows), BF16),
        joint=vm((rows, 3 * d), BF16),
        smixt=vm((d, rows), BF16),
        slse=vm((16, LANES), F32),
        first=vm((rows, d), F32),
        n2t=vm((d, rows), BF16),
        qa=vm((items, rows, d), BF16),
        kv=vm((items, padded, 2 * d), BF16),
        memt=vm((d, items * padded), BF16),
        clse=vm((16, LANES), F32),
        second=vm((rows, d), F32),
        n3t=vm((d, rows), BF16),
        activet=vm((4 * d, rows), BF16),
        active=vm((rows, 4 * d), BF16),
        slope=vm((rows, 4 * d), BF16),
        third=vm((rows, d), F32),
        sq=vm((8, LANES), F32),
        xb=vm((rows, d), BF16),
        branch=vm((rows, d), F32),
        op=vm((items, rows, d), BF16),
        opl=vm((items, 16, LANES), F32),
        orv=vm((3, rows, d), BF16),
        orl=vm((3, 16, LANES), F32),
        wcol=vm((LANES, LANES), F32),
        cmixt=vm((d, rows), BF16),
        gr=vm((rows, d), F32),
        ga=vm((items, rows, d), BF16),
        gl=vm((items, 32, LANES), F32),
        nrow=vm((16, d), F32),
        bias=vm((8, padded), F32),
        biast=vm((padded, LANES), F32),
        mst=vm((2, padded, WIDE), F32),
        ost=vm((2, slab, d), F32),
        nw=vm((nz, 2, 2, 2, 16, LANES), F32),
        rc=vm((SLOTS, nz, 2, 2, slab, d), BF16),
        y1=vm((SLOTS, nz, 2, half, d), BF16),
        x1=vm((SLOTS, nz, 2, half, d), BF16),
        x2=vm((SLOTS, nz, half, d), BF16),
        y2=vm((SLOTS, nz, half, d), BF16),
        zs=vm((SLOTS, nz - 1, slab, d), BF16),
        zr=vm((SLOTS, slab, d), BF16),
        total=vm((slab, d), F32),
        fzr=vm((1, 2, 2, slab, d), BF16),
        nzr=vm((1, 16, LANES), F32),
        ntotal=vm((16, LANES), F32),
        fy1=vm((1, 2, half, d), BF16),
        fx1=vm((1, 2, half, d), BF16),
        fx2=vm((1, half, d), BF16),
        fy2=vm((1, half, d), BF16),
        fzs=vm((1, nz - 1, 2, 2, slab, d), BF16),
        nrc=vm((1, nz, 2, 2, 16, LANES), F32),
        ny1=vm((1, nz, 2, 8, LANES), F32),
        nx1=vm((1, nz, 2, 8, LANES), F32),
        nx2=vm((1, nz, 8, LANES), F32),
        ny2=vm((1, nz, 8, LANES), F32),
        nzs=vm((1, nz - 1, 16, LANES), F32),
        own_sem=dma((4,)),
        x_sem=dma((4,)),
        w_sem=dma((chunks,)),
        m_sem=dma((2,)),
        t_sem=dma((2,)),
        e_sem=dma((2,)),
        g_send=dma((ROWS + 1 + len(LATE), nz + 8)),
        g_recv=dma((ROWS + 1 + len(LATE), nz + 7)),
        s_send=dma((SEND_ROWS + len(EARLY) + 1, nz + 5)),
        s_recv=dma((SLOTS + 2, nz + 4)),
        core_recv=dma((SLOTS + 1,)),
        credit=pltpu.SemaphoreType.REGULAR((3 * nz + 9,)),
        q_send=dma((3,)),
        q_recv=dma((3,)),
        o_send=dma((6,)),
        o_recv=dma((6,)),
        g2_send=dma((6,)),
        g2_recv=dma((6,)),
        o2_send=dma((3,)),
        o2_recv=dma((3,)),
    )
    names = list(INPUTS) + list(outs) + list(scratch)

    def kernel(*refs):
        run(SimpleNamespace(**dict(zip(names, refs))), nz, chunks)

    spaces = {"tl": pltpu.SMEM, "expand": pltpu.VMEM, "norm_gains": pltpu.VMEM, "norm_shifts": pltpu.VMEM}
    spaces.update({"memory_length": pltpu.SMEM, "cross_mask": pltpu.VMEM})
    res = pl.pallas_call(
        kernel,
        out_shape=[jax.ShapeDtypeStruct(s, F32) for s, _ in outs.values()],
        in_specs=[at(spaces.get(k, pl.ANY)) for k in INPUTS],
        out_specs=[at(s) for _, s in outs.values()],
        scratch_shapes=list(scratch.values()),
        compiler_params=pltpu.CompilerParams(collective_id=0, has_side_effects=True, vmem_limit_bytes=VMEM_BYTES),
    )(*(given[k] for k in INPUTS))
    return dict(zip(outs, res))


def settle(arrays, norm_out, width):
    count = len(arrays)
    pieces = []
    for i, a in enumerate(arrays):
        pieces += [(i, k) for k in range(a.shape[0])] if a.ndim == 3 else [(i, None)]

    def kernel(*refs):
        sources, (table, scalars) = refs[:count], refs[count : count + 2]
        targets = refs[count + 2 : 2 * count + 2]
        gains, shifts, rms = refs[2 * count + 2 : 2 * count + 5]
        held = refs[2 * count + 5 : 3 * count + 5]
        in_sem, out_sem = refs[3 * count + 5 :]

        def pick(ref, k):
            return ref if k is None else ref.at[k]

        ins = [pltpu.make_async_copy(pick(sources[i], k), pick(held[i], k), in_sem.at[n]) for n, (i, k) in enumerate(pieces)]
        outs = [pltpu.make_async_copy(pick(held[i], k), pick(targets[i], k), out_sem.at[n]) for n, (i, k) in enumerate(pieces)]
        for cp in ins:
            cp.start()
        fr = lax.axis_index("frames")
        mine = jnp.zeros((8, width), F32)
        for f in range(LANES // width):
            mine = jnp.where(fr == f, table[0:8, f * width : (f + 1) * width], mine)
        gains[...] = mine[0:4]
        shifts[...] = mine[4:8]
        for i in range(4):
            rms[i] = scalars[8 + i, 0]
        for a, b in zip(ins, outs):
            a.wait()
            b.start()
        for b in outs:
            b.wait()

    small = jax.ShapeDtypeStruct((4, width), F32)
    return pl.pallas_call(
        kernel,
        out_shape=[jax.ShapeDtypeStruct(a.shape, a.dtype) for a in arrays] + [small, small, jax.ShapeDtypeStruct((4,), F32)],
        in_specs=[at(pl.ANY)] * count + [at(pltpu.VMEM), at(pltpu.SMEM)],
        out_specs=[at(pl.ANY)] * count + [at(pltpu.VMEM)] * 2 + [at(pltpu.SMEM)],
        scratch_shapes=[pltpu.VMEM(a.shape, a.dtype) for a in arrays]
        + [pltpu.SemaphoreType.DMA((len(pieces),)), pltpu.SemaphoreType.DMA((len(pieces),))],
        compiler_params=pltpu.CompilerParams(vmem_limit_bytes=VMEM_BYTES),
    )(*arrays, norm_out, norm_out)


CHUNKS = 16
Z_CHIPS = 4


def local_fused(
    tokens,
    memory,
    cotangent,
    self_project,
    self_output,
    cross_query,
    cross_memory,
    cross_output,
    expand,
    contract,
    norm_gains,
    norm_shifts,
    target_length,
    memory_length,
    cross_mask,
):
    items, frame_count, d = memory.shape
    slab = self_output.shape[0]
    group = 4 * slab
    parts = -(-frame_count // group)
    padded = parts * group
    rolled = jnp.pad(memory, ((0, 0), (0, padded - frame_count), (0, 0))).reshape(items, parts, 2, 2, slab, d)
    o = fused(
        Z_CHIPS,
        CHUNKS,
        frame_count,
        tl=target_length,
        tokens=tokens[0],
        cotangent=cotangent[0],
        memory=rolled,
        self_project=self_project,
        self_output=self_output,
        cross_query=cross_query,
        cross_memory=cross_memory,
        cross_output=cross_output,
        expand=expand,
        contract=contract,
        norm_gains=norm_gains,
        norm_shifts=norm_shifts,
        memory_length=memory_length,
        cross_mask=cross_mask,
    )
    large = [o[k] for k in ("result", "tokens_grad", "memory_grad")] + [o[k + "_grad"] for k in GRADS]
    done = settle(large, o["norm_out"], norm_gains.shape[1])
    return (done[0][None], done[1][None], *done[2:])


block_heads = 4


def layer_norm(values, gain_row, shift_row):
    center = values - jnp.mean(values, axis=-1, keepdims=True)
    spread = jnp.mean(center * center, axis=-1, keepdims=True)
    return center * lax.rsqrt(spread + 1e-05) * gain_row + shift_row


def exact_gelu(values):
    return jax.nn.gelu(values, approximate=False)


def matmul(left_side, right_side):
    return jnp.dot(left_side, right_side, preferred_element_type=jnp.float32)


def split_heads(rows):
    return rows.reshape(rows.shape[:-1] + (rows.shape[-1] // HEAD_DIM, HEAD_DIM))


def to_blocks(rows):
    row_count, head_count, head_width = rows.shape
    return rows.reshape(row_count, head_count // block_heads, block_heads, head_width).transpose(
        1, 0, 2, 3
    )


def from_blocks(blocks):
    group_count, row_count, head_count, head_width = blocks.shape
    return blocks.transpose(1, 0, 2, 3).reshape(row_count, group_count * head_count * head_width)


def block_scores(query_block, key_block, allowed):
    factor = query_block.shape[-1] ** (-0.5)
    raw_scores = (
        jnp.einsum("shd,fhd->hsf", query_block, key_block, preferred_element_type=jnp.float32)
        * factor
    )
    return jnp.where(allowed[None], raw_scores, -1e30)


def block_probs(query_block, key_block, allowed, max_block, total_block):
    scores = block_scores(query_block, key_block, allowed)
    shifted = jnp.where(allowed[None], jnp.exp(scores - max_block[..., None]), 0.0)
    return shifted / total_block[..., None]


def block_grads(query_block, key_block, grad_block, probs, grad_probs, row_dot):
    factor = query_block.shape[-1] ** (-0.5)
    score_grad = (probs * (grad_probs - row_dot)).astype(jnp.bfloat16)
    query_grad = (
        jnp.einsum("hsf,fhd->shd", score_grad, key_block, preferred_element_type=jnp.float32)
        * factor
    )
    key_grad = (
        jnp.einsum("hsf,shd->fhd", score_grad, query_block, preferred_element_type=jnp.float32)
        * factor
    )
    value_grad = jnp.einsum(
        "hsf,shd->fhd", probs.astype(jnp.bfloat16), grad_block, preferred_element_type=jnp.float32
    )
    return (query_grad, key_grad, value_grad)


def attend_whole(query_rows, key_rows, value_rows, allowed):

    def one_group(blocks):
        query_block, key_block, value_block = blocks
        scores = block_scores(query_block, key_block, allowed)
        max_block = jnp.max(scores, axis=-1)
        shifted = jnp.where(allowed[None], jnp.exp(scores - max_block[..., None]), 0.0)
        total_block = jnp.sum(shifted, axis=-1)
        weights = (shifted / total_block[..., None]).astype(jnp.bfloat16)
        mixture = jnp.einsum(
            "hsf,fhd->shd", weights, value_block, preferred_element_type=jnp.float32
        )
        return (mixture, max_block, total_block)

    mixture, row_max, totals = lax.map(
        one_group, (to_blocks(query_rows), to_blocks(key_rows), to_blocks(value_rows))
    )
    return (from_blocks(mixture), row_max, totals)


def attend_whole_back(query_rows, key_rows, value_rows, allowed, grad_rows, row_max, totals):

    def one_group(blocks):
        query_block, key_block, value_block, grad_block, max_block, total_block = blocks
        probs = block_probs(query_block, key_block, allowed, max_block, total_block)
        grad_probs = jnp.einsum(
            "shd,fhd->hsf", grad_block, value_block, preferred_element_type=jnp.float32
        )
        row_dot = jnp.sum(probs * grad_probs, axis=-1, keepdims=True)
        return block_grads(query_block, key_block, grad_block, probs, grad_probs, row_dot)

    query_grad, key_grad, value_grad = lax.map(
        one_group,
        (
            to_blocks(query_rows),
            to_blocks(key_rows),
            to_blocks(value_rows),
            to_blocks(grad_rows),
            row_max,
            totals,
        ),
    )
    return (from_blocks(query_grad), from_blocks(key_grad), from_blocks(value_grad))


def cross_stats(query_rows, key_rows, allowed):

    def one_group(blocks):
        query_block, key_block = blocks
        scores = block_scores(query_block, key_block, allowed)
        max_block = jnp.max(scores, axis=-1)
        total_block = jnp.sum(
            jnp.where(allowed[None], jnp.exp(scores - max_block[..., None]), 0.0), axis=-1
        )
        return (max_block, total_block)

    return lax.map(one_group, (to_blocks(query_rows), to_blocks(key_rows)))


def cross_partial(query_rows, key_rows, value_rows, allowed, row_max, totals):

    def one_group(blocks):
        query_block, key_block, value_block, max_block, total_block = blocks
        probs = block_probs(query_block, key_block, allowed, max_block, total_block)
        return jnp.einsum(
            "hsf,fhd->shd",
            probs.astype(jnp.bfloat16),
            value_block,
            preferred_element_type=jnp.float32,
        )

    return from_blocks(
        lax.map(
            one_group,
            (to_blocks(query_rows), to_blocks(key_rows), to_blocks(value_rows), row_max, totals),
        )
    )


def cross_row_dot(query_rows, key_rows, value_rows, allowed, grad_rows, row_max, totals):

    def one_group(blocks):
        query_block, key_block, value_block, grad_block, max_block, total_block = blocks
        probs = block_probs(query_block, key_block, allowed, max_block, total_block)
        grad_probs = jnp.einsum(
            "shd,fhd->hsf", grad_block, value_block, preferred_element_type=jnp.float32
        )
        return jnp.sum(probs * grad_probs, axis=-1)

    return lax.map(
        one_group,
        (
            to_blocks(query_rows),
            to_blocks(key_rows),
            to_blocks(value_rows),
            to_blocks(grad_rows),
            row_max,
            totals,
        ),
    )


def cross_partial_grads(
    query_rows, key_rows, value_rows, allowed, grad_rows, row_max, totals, row_dot
):

    def one_group(blocks):
        query_block, key_block, value_block, grad_block, max_block, total_block, dot_block = blocks
        probs = block_probs(query_block, key_block, allowed, max_block, total_block)
        grad_probs = jnp.einsum(
            "shd,fhd->hsf", grad_block, value_block, preferred_element_type=jnp.float32
        )
        return block_grads(
            query_block, key_block, grad_block, probs, grad_probs, dot_block[..., None]
        )

    query_grad, key_grad, value_grad = lax.map(
        one_group,
        (
            to_blocks(query_rows),
            to_blocks(key_rows),
            to_blocks(value_rows),
            to_blocks(grad_rows),
            row_max,
            totals,
            row_dot,
        ),
    )
    return (from_blocks(query_grad), from_blocks(key_grad), from_blocks(value_grad))


def local(
    tokens,
    memory,
    cotangent,
    self_project,
    self_output,
    cross_query,
    cross_memory,
    cross_output,
    expand,
    contract,
    norm_gains,
    norm_shifts,
    target_length,
    memory_length,
    cross_mask,
):
    gathered = (
        lax.all_gather(self_project, ("dp", "frames"), axis=0, tiled=True),
        lax.all_gather(self_output, ("dp", "frames"), axis=0, tiled=True),
        lax.all_gather(cross_query, ("dp", "frames"), axis=0, tiled=True),
        lax.all_gather(cross_memory, ("dp", "frames"), axis=0, tiled=True),
        lax.all_gather(cross_output, ("dp", "frames"), axis=0, tiled=True),
        lax.all_gather(expand, ("dp", "frames"), axis=0, tiled=True),
        lax.all_gather(contract, ("dp", "frames"), axis=0, tiled=True),
        lax.all_gather(norm_gains, ("dp", "frames"), axis=1, tiled=True),
        lax.all_gather(norm_shifts, ("dp", "frames"), axis=1, tiled=True),
    )
    (
        w_self,
        w_self_out,
        w_query,
        w_memory,
        w_cross_out,
        w_expand,
        w_contract,
        gains_low,
        shifts_low,
    ) = gathered
    gains = gains_low.astype(jnp.float32)
    shifts = shifts_low.astype(jnp.float32)
    model_width = w_self_out.shape[0]
    residual_in = tokens[0]
    length = residual_in.shape[0]
    positions = jnp.arange(length)
    row_valid = positions < target_length[0]
    causal = positions[:, None] >= positions[None, :]
    item_count = memory.shape[0]
    frame_count = memory.shape[1]
    own_item = lax.axis_index("frames")
    normed_one_f, back_one = jax.vjp(layer_norm, residual_in, gains[0], shifts[0])
    normed_one = normed_one_f.astype(jnp.bfloat16)
    joint_rows = matmul(normed_one, w_self).astype(jnp.bfloat16)
    self_queries = split_heads(joint_rows[:, :model_width])
    self_keys = split_heads(joint_rows[:, model_width : 2 * model_width])
    self_values = split_heads(joint_rows[:, 2 * model_width :])
    self_mix, self_max, self_totals = attend_whole(self_queries, self_keys, self_values, causal)
    self_mix_low = self_mix.astype(jnp.bfloat16)
    self_branch = matmul(self_mix_low, w_self_out)
    first_sum = residual_in + self_branch
    normed_two_f, back_two = jax.vjp(layer_norm, first_sum, gains[1], shifts[1])
    normed_two = normed_two_f.astype(jnp.bfloat16)
    cross_queries = matmul(normed_two, w_query).astype(jnp.bfloat16)
    every_query = lax.all_gather(cross_queries[None], "frames", axis=0, tiled=True)
    query_heads = split_heads(every_query)
    frame_start = own_item * frame_count
    local_frames = frame_start + jnp.arange(frame_count)
    local_mask = lax.dynamic_slice_in_dim(cross_mask, frame_start, frame_count, 1)
    frame_ok = (local_frames[None, :] < memory_length[:, None]) & (
        (local_mask == 1) | (local_frames[None, :] == 0)
    )
    memory_rows = matmul(memory.reshape(item_count * frame_count, model_width), w_memory).astype(
        jnp.bfloat16
    )
    memory_rows = memory_rows.reshape(item_count, frame_count, 2 * model_width)
    memory_keys = split_heads(memory_rows[..., :model_width])
    memory_values = split_heads(memory_rows[..., model_width:])

    def item_stats(inputs):
        query_item, key_item, frame_item = inputs
        return cross_stats(
            query_item, key_item, jnp.broadcast_to(frame_item[None, :], (length, frame_count))
        )

    local_max, local_totals = lax.map(item_stats, (query_heads, memory_keys, frame_ok))
    cross_max = lax.pmax(local_max.astype(jnp.bfloat16), "frames").astype(local_max.dtype)
    cross_totals = lax.psum(
        (local_totals * jnp.exp(local_max - cross_max)).astype(jnp.bfloat16), "frames"
    ).astype(jnp.float32)

    def item_partial(inputs):
        query_item, key_item, value_item, frame_item, max_item, total_item = inputs
        allowed = jnp.broadcast_to(frame_item[None, :], (length, frame_count))
        return cross_partial(query_item, key_item, value_item, allowed, max_item, total_item)

    partial_mix = lax.map(
        item_partial, (query_heads, memory_keys, memory_values, frame_ok, cross_max, cross_totals)
    )
    cross_mix = lax.psum_scatter(
        partial_mix.astype(jnp.bfloat16), "frames", scatter_dimension=0, tiled=True
    ).astype(jnp.float32)[0]
    cross_mix_low = cross_mix.astype(jnp.bfloat16)
    cross_branch = matmul(cross_mix_low, w_cross_out)
    second_sum = first_sum + cross_branch
    normed_three_f, back_three = jax.vjp(layer_norm, second_sum, gains[2], shifts[2])
    normed_three = normed_three_f.astype(jnp.bfloat16)
    hidden = matmul(normed_three, w_expand)
    active_f, gelu_back = jax.vjp(exact_gelu, hidden)
    active = active_f.astype(jnp.bfloat16)
    feed_branch = matmul(active, w_contract)
    third_sum = second_sum + feed_branch
    final_rows, back_final = jax.vjp(layer_norm, third_sum, gains[3], shifts[3])
    result = jnp.where(row_valid[:, None], final_rows, 0.0)
    row_weight = row_valid.astype(jnp.float32)[:, None]
    squares = jnp.stack(
        [
            jnp.sum(row_weight * member * member)
            for member in (third_sum, self_branch, cross_branch, feed_branch)
        ]
    )
    squares_all, counted = lax.psum((squares, jnp.sum(row_weight)), ("dp", "frames"))
    branch_rms = jnp.sqrt(squares_all / (counted * model_width))
    grad_result = jnp.where(row_valid[:, None], cotangent[0], 0.0)
    grad_third, gain_grad_three, shift_grad_three = back_final(grad_result)
    feed_low = grad_third.astype(jnp.bfloat16)
    contract_grad = matmul(active.T, feed_low)
    grad_active = matmul(feed_low, w_contract.T)
    grad_hidden = gelu_back(grad_active)[0].astype(jnp.bfloat16)
    expand_grad = matmul(normed_three.T, grad_hidden)
    grad_normed_three = matmul(grad_hidden, w_expand.T)
    grad_second_part, gain_grad_two, shift_grad_two = back_three(grad_normed_three)
    grad_second = grad_third + grad_second_part
    cross_low = grad_second.astype(jnp.bfloat16)
    cross_output_grad = matmul(cross_mix_low.T, cross_low)
    grad_cross_mix = matmul(cross_low, w_cross_out.T).astype(jnp.bfloat16)
    every_grad = split_heads(lax.all_gather(grad_cross_mix[None], "frames", axis=0, tiled=True))

    def item_dot(inputs):
        query_item, key_item, value_item, frame_item, grad_item, max_item, total_item = inputs
        allowed = jnp.broadcast_to(frame_item[None, :], (length, frame_count))
        return cross_row_dot(
            query_item, key_item, value_item, allowed, grad_item, max_item, total_item
        )

    local_dot = lax.map(
        item_dot,
        (query_heads, memory_keys, memory_values, frame_ok, every_grad, cross_max, cross_totals),
    )
    row_dot = lax.psum(local_dot.astype(jnp.bfloat16), "frames").astype(jnp.float32)

    def item_grads(inputs):
        query_item, key_item, value_item, frame_item, grad_item, max_item, total_item, dot_item = (
            inputs
        )
        allowed = jnp.broadcast_to(frame_item[None, :], (length, frame_count))
        return cross_partial_grads(
            query_item, key_item, value_item, allowed, grad_item, max_item, total_item, dot_item
        )

    query_parts, key_parts, value_parts = lax.map(
        item_grads,
        (
            query_heads,
            memory_keys,
            memory_values,
            frame_ok,
            every_grad,
            cross_max,
            cross_totals,
            row_dot,
        ),
    )
    query_grad = lax.psum_scatter(
        query_parts.astype(jnp.bfloat16), "frames", scatter_dimension=0, tiled=True
    ).astype(jnp.float32)[0]
    memory_low = (
        jnp.concatenate([key_parts, value_parts], axis=2)
        .astype(jnp.bfloat16)
        .reshape(item_count * frame_count, 2 * model_width)
    )
    cross_memory_grad = matmul(memory.reshape(item_count * frame_count, model_width).T, memory_low)
    memory_grad = matmul(memory_low, w_memory.T).reshape(item_count, frame_count, model_width)
    query_low = query_grad.astype(jnp.bfloat16)
    cross_query_grad = matmul(normed_two.T, query_low)
    grad_normed_two = matmul(query_low, w_query.T)
    grad_first_part, gain_grad_one, shift_grad_one = back_two(grad_normed_two)
    grad_first = grad_second + grad_first_part
    self_low = grad_first.astype(jnp.bfloat16)
    self_output_grad = matmul(self_mix_low.T, self_low)
    grad_self_mix = matmul(self_low, w_self_out.T).astype(jnp.bfloat16)
    self_query_grad, self_key_grad, self_value_grad = attend_whole_back(
        self_queries,
        self_keys,
        self_values,
        causal,
        split_heads(grad_self_mix),
        self_max,
        self_totals,
    )
    joint_grad = jnp.concatenate([self_query_grad, self_key_grad, self_value_grad], axis=1).astype(
        jnp.bfloat16
    )
    self_project_grad = matmul(normed_one.T, joint_grad)
    grad_normed_one = matmul(joint_grad, w_self.T)
    grad_input_part, gain_grad_zero, shift_grad_zero = back_one(grad_normed_one)
    tokens_grad = grad_first + grad_input_part
    gain_grads = jnp.stack([gain_grad_zero, gain_grad_one, gain_grad_two, gain_grad_three])
    shift_grads = jnp.stack([shift_grad_zero, shift_grad_one, shift_grad_two, shift_grad_three])
    reduced = (
        lax.psum_scatter(self_project_grad, ("dp", "frames"), scatter_dimension=0, tiled=True),
        lax.psum_scatter(self_output_grad, ("dp", "frames"), scatter_dimension=0, tiled=True),
        lax.psum_scatter(cross_query_grad, ("dp", "frames"), scatter_dimension=0, tiled=True),
        lax.psum_scatter(cross_memory_grad, ("dp", "frames"), scatter_dimension=0, tiled=True),
        lax.psum_scatter(cross_output_grad, ("dp", "frames"), scatter_dimension=0, tiled=True),
        lax.psum_scatter(expand_grad, ("dp", "frames"), scatter_dimension=0, tiled=True),
        lax.psum_scatter(contract_grad, ("dp", "frames"), scatter_dimension=0, tiled=True),
        lax.psum_scatter(gain_grads, ("dp", "frames"), scatter_dimension=1, tiled=True),
        lax.psum_scatter(shift_grads, ("dp", "frames"), scatter_dimension=1, tiled=True),
    )
    (
        project_part,
        output_part,
        query_part,
        memory_part,
        cross_out_part,
        expand_part,
        contract_part,
        gains_part,
        shifts_part,
    ) = reduced
    return (
        result[None],
        tokens_grad[None],
        memory_grad,
        project_part,
        output_part,
        query_part,
        memory_part,
        cross_out_part,
        expand_part,
        contract_part,
        gains_part,
        shifts_part,
        branch_rms,
    )


def solution(mesh):
    fits = (mesh.shape["dp"], mesh.shape["frames"]) == (2 * Z_CHIPS, 4)
    return jax.shard_map(
        local_fused if fits else local,
        mesh=mesh,
        in_specs=(
            P(("dp", "frames"), None, None),
            P("dp", "frames", None),
            P(("dp", "frames"), None, None),
            P(("dp", "frames"), None),
            P(("dp", "frames"), None),
            P(("dp", "frames"), None),
            P(("dp", "frames"), None),
            P(("dp", "frames"), None),
            P(("dp", "frames"), None),
            P(("dp", "frames"), None),
            P(None, ("dp", "frames")),
            P(None, ("dp", "frames")),
            P(("dp", "frames")),
            P("dp"),
            P("dp", None),
        ),
        out_specs=(
            P(("dp", "frames"), None, None),
            P(("dp", "frames"), None, None),
            P("dp", "frames", None),
            P(("dp", "frames"), None),
            P(("dp", "frames"), None),
            P(("dp", "frames"), None),
            P(("dp", "frames"), None),
            P(("dp", "frames"), None),
            P(("dp", "frames"), None),
            P(("dp", "frames"), None),
            P(None, ("dp", "frames")),
            P(None, ("dp", "frames")),
            P(),
        ),
        check_vma=False,
    )
```
